32 devices in a mesh: blk: 8 (over z, y), clip: 4 (over x, core).
Axes of the slice: x: 2, y: 2, z: 4, core: 2. Of those that a mesh axis runs over, the one named last changes fastest.
Arguments:
- tokens: bfloat16 [4, 16, 128, 1024], P('clip', 'blk'), may hold values from -6 to 6
- noise_levels: int32 [4, 16], P('clip'), may hold values from 0 to 999, as said below
- group_map: int32 [16], replicated, may hold values from 0 to 15, as said below
- noise_table: bfloat16 [1000, 1024], replicated, may hold values from -6 to 6
- mod_weight: bfloat16 [1024, 6144], replicated, may hold values from -0.1875 to 0.1875
- mod_bias: bfloat16 [6144], replicated, may hold values from -3 to 3
- qkv_weight: bfloat16 [1024, 3072], replicated, may hold values from -0.1875 to 0.1875
- out_weight: bfloat16 [1024, 1024], replicated, may hold values from -6 to 6
- fc1_weight: bfloat16 [1024, 4096], replicated, may hold values from -0.1875 to 0.1875
- fc2_weight: bfloat16 [4096, 1024], replicated, may hold values from -0.09375 to 0.09375
- out_cotangent: bfloat16 [4, 16, 128, 1024], P('clip', 'blk'), may hold values from -6 to 6
Outputs:
- layer_out: bfloat16 [4, 16, 128, 1024], P('clip', 'blk')
- tokens_grad: bfloat16 [4, 16, 128, 1024], P('clip', 'blk')
- noise_table_grad: float32 [1000, 1024], P(None, ('blk', 'clip'))
- mod_weight_grad: float32 [1024, 6144], P(('blk', 'clip'))
- mod_bias_grad: float32 [6144], P(('blk', 'clip'))
- qkv_weight_grad: float32 [1024, 3072], P(('blk', 'clip'))
- out_weight_grad: float32 [1024, 1024], P(('blk', 'clip'))
- fc1_weight_grad: float32 [1024, 4096], P(('blk', 'clip'))
- fc2_weight_grad: float32 [4096, 1024], P(('blk', 'clip'))
The draws below stay inside these ranges and needn't reach their ends.
Inputs may be any that keep to these rules, and one draw needn't show every extreme that they name: `group_map`: A permutation of the frames; slots 2 i and 2 i + 1 hold some frame f and 15 - f, in either order. `noise_levels`: in each clip one frame has level 0 and another level 999.
All inputs are finite; a program needn't handle non-finite values.
Results may differ from the reference program's by a relative error of at most 0.014.
The reference program's roundings to bfloat16 on the way count: a program that leaves them out, or rounds other values in their place, can miss the bound.
Values may be sent and summed in bfloat16 or wider, within the bound.
No kernel may reach another device: no remote copies, remote signals or barrier semaphores. Data moves between devices by JAX's collectives and lax.ppermute only.
A program may use at most 256 MiB of HBM per device.

```python
import jax
import jax.numpy as jnp
from jax import lax

D = 1024
FF = 4096
HEAD = 64
HEADS = 16
LEVELS = 1000
GRID_H = 8
GRID_W = 16
PATCHES = 128
FRAMES = 16
CLIPS = 4


def draw_group_map(key, part):
    key = jax.random.fold_in(key, 11)
    pair_key, flip_key = jax.random.split(key)
    pair_count = FRAMES // 2
    pair_order = jax.random.permutation(pair_key, pair_count).astype(jnp.int32)
    flipped = jax.random.randint(flip_key, (pair_count,), 0, 2)
    mirror = FRAMES - 1 - pair_order
    leading = jnp.where(flipped == 1, mirror, pair_order)
    trailing = jnp.where(flipped == 1, pair_order, mirror)
    return jnp.stack([leading, trailing], axis=1).reshape(FRAMES).astype(jnp.int32)


def draw_noise_levels(key, part):
    key = jax.random.fold_in(key, 23)
    subkeys = jax.random.split(key, 5)
    grid_shape = (CLIPS, FRAMES)
    levels_drawn = jax.random.randint(subkeys[0], grid_shape, 0, LEVELS)
    levels_drawn = jnp.maximum(levels_drawn, jax.random.randint(subkeys[1], grid_shape, 0, LEVELS))
    levels_drawn = jnp.maximum(levels_drawn, jax.random.randint(subkeys[2], grid_shape, 0, LEVELS))
    top_at = jax.random.randint(subkeys[3], (CLIPS, 1), 0, FRAMES)
    low_at = (top_at + 1 + jax.random.randint(subkeys[4], (CLIPS, 1), 0, FRAMES - 1)) % FRAMES
    column = jnp.arange(FRAMES, dtype=jnp.int32)[None, :]
    levels_drawn = jnp.where(column == top_at, LEVELS - 1, levels_drawn)
    levels_drawn = jnp.where(column == low_at, 0, levels_drawn)
    return levels_drawn.astype(jnp.int32)


def shard_levels(rng, dims, cuts, least, largest):
    gain = 1.0
    for dim, blocks in cuts:
        heights = jax.random.uniform(jax.random.fold_in(jax.random.fold_in(rng, 6), dim), (blocks,), jnp.float32, least / len(cuts), largest / len(cuts))
        gain = gain * jnp.repeat(jnp.exp(heights), dims[dim] // blocks).reshape((-1,) + (1,) * (len(dims) - 1 - dim))
    return gain


def gaussian(own_key, extent, deviation, limit, cuts=(), kind=jnp.bfloat16):
    entries = deviation * jax.random.normal(own_key, extent, jnp.float32)
    if cuts:
        entries = entries * shard_levels(own_key, extent, cuts, -0.22, 0.18)
    return jnp.clip(entries, -limit, limit).astype(kind)


def setup_inputs(seed: int = 0) -> dict:
    splits = jax.random.split(jax.random.key(seed), 12)
    tokens = gaussian(splits[0], (CLIPS, FRAMES, PATCHES, D), 1.0, 6.0, ((0, 4), (1, 8)))
    noise_levels = draw_noise_levels(jax.random.fold_in(splits[11], 71), 0)
    group_map = draw_group_map(jax.random.fold_in(splits[11], 71), 0)
    noise_table = gaussian(splits[3], (LEVELS, D), 1.0, 6.0)
    mod_weight = gaussian(splits[4], (D, 6 * D), D ** -0.5, 0.1875)
    mod_bias = gaussian(splits[5], (6 * D,), 0.5, 3.0)
    qkv_weight = gaussian(splits[6], (D, 3 * D), D ** -0.5, 0.1875)
    out_weight = gaussian(splits[7], (D, D), 1 ** -0.5, 6.0)
    fc1_weight = gaussian(splits[8], (D, FF), D ** -0.5, 0.1875)
    fc2_weight = gaussian(splits[9], (FF, D), FF ** -0.5, 0.09375)
    out_cotangent = gaussian(splits[10], (CLIPS, FRAMES, PATCHES, D), 1.0, 6.0, ((0, 4), (1, 8)))
    return {"tokens": tokens, "noise_levels": noise_levels, "group_map": group_map, "noise_table": noise_table, "mod_weight": mod_weight, "mod_bias": mod_bias, "qkv_weight": qkv_weight, "out_weight": out_weight, "fc1_weight": fc1_weight, "fc2_weight": fc2_weight, "out_cotangent": out_cotangent}


SCALE = 0.125
EPSILON = 1e-06
ROPE_BASE = 10000.0
HIGHEST = lax.Precision.HIGHEST

@jax.custom_vjp
def low(v):
    return lax.optimization_barrier(v.astype(jnp.bfloat16)).astype(jnp.float32)

@jax.custom_vjp
def low_back(v):
    return v

def low_keep(v):
    return (low(v), None)

def low_pass(kept, grad):
    return (grad,)

def back_keep(v):
    return (v, None)

def back_low(kept, grad):
    return (low(grad),)
low.defvjp(low_keep, low_pass)
low_back.defvjp(back_keep, back_low)

def token_positions(frame_ids):
    slot_count = frame_ids.shape[0]
    total_rows = slot_count * GRID_H * GRID_W
    patch_ids = jnp.arange(total_rows, dtype=jnp.int32) % (GRID_H * GRID_W)
    frame_pos = jnp.repeat(frame_ids, GRID_H * GRID_W, total_repeat_length=total_rows)
    return (frame_pos, patch_ids // GRID_W, patch_ids % GRID_W)

def rope_angles(frame_pos, row_pos, col_pos):
    angle_list = []
    for position, comp_width in ((frame_pos, 16), (row_pos, 24), (col_pos, 24)):
        half_width = comp_width // 2
        frequency = ROPE_BASE ** (-2.0 * jnp.arange(half_width, dtype=jnp.float32) / comp_width)
        angle_list.append(position.astype(jnp.float32)[:, None] * frequency[None, :])
    return angle_list

def rotate(values, angle_list, direction):
    pieces = []
    offset = 0
    for angles in angle_list:
        half_width = angles.shape[1]
        first_half = values[:, :, offset:offset + half_width]
        second_half = values[:, :, offset + half_width:offset + 2 * half_width]
        cosine = jnp.cos(angles)[:, None, :]
        sine_part = direction * jnp.sin(angles)[:, None, :]
        pieces.append(first_half * cosine - second_half * sine_part)
        pieces.append(first_half * sine_part + second_half * cosine)
        offset = offset + 2 * half_width
    return jnp.concatenate(pieces, axis=2)

def normalize(values):
    center = values - lax.optimization_barrier(jnp.mean(values, axis=-1, keepdims=True))
    inverse = lax.rsqrt(lax.optimization_barrier(jnp.mean(center * center, axis=-1, keepdims=True)) + EPSILON)
    return (center * inverse, inverse)

def layer_clip(params, clip_tokens, clip_levels, frame_ids):
    noise_table, mod_weight, mod_bias, qkv_weight, out_weight, fc1_weight, fc2_weight = params
    slot_count = frame_ids.shape[0]
    token_count = slot_count * GRID_H * GRID_W
    embedded = noise_table[clip_levels[frame_ids]]
    activated = low(jax.nn.silu(embedded))
    modulation = low_back(jnp.dot(activated, mod_weight, precision=HIGHEST)) + mod_bias
    shift_one, scale_one, gate_one, shift_two, scale_two, gate_two = [modulation[:, member * D:(member + 1) * D][:, None, :] for member in range(6)]
    normed_one, unused_one = normalize(clip_tokens)
    first_in = low(normed_one * (1.0 + scale_one) + shift_one).reshape(token_count, D)
    qkv_lin = low_back(jnp.dot(first_in, qkv_weight, precision=HIGHEST))
    frame_pos, row_pos, col_pos = token_positions(frame_ids)
    angle_list = rope_angles(frame_pos, row_pos, col_pos)
    query = low(low_back(rotate(qkv_lin[:, :D].reshape(token_count, HEADS, HEAD), angle_list, 1.0)))
    key_all = low(low_back(rotate(qkv_lin[:, D:2 * D].reshape(token_count, HEADS, HEAD), angle_list, 1.0)))
    value_all = low(low_back(qkv_lin[:, 2 * D:].reshape(token_count, HEADS, HEAD)))

    @jax.checkpoint
    def attend_slot(inputs):
        query_slot, slot_frame = inputs
        raw_scores = low_back(jnp.einsum('qhd,khd->hqk', query_slot, key_all, precision=HIGHEST))
        allowed = (frame_pos <= slot_frame)[None, None, :]
        weights = low(jax.nn.softmax(jnp.where(allowed, raw_scores * SCALE, -jnp.inf), axis=-1))
        return jnp.einsum('hqk,khd->qhd', weights, value_all, precision=HIGHEST)
    attended = lax.map(attend_slot, (query.reshape(slot_count, GRID_H * GRID_W, HEADS, HEAD), frame_ids))
    attended = low(low_back(attended.reshape(token_count, D)))
    attn_out = low_back(jnp.dot(attended, out_weight, precision=HIGHEST)).reshape(clip_tokens.shape)
    middle = clip_tokens + gate_one * attn_out
    normed_two, unused_two = normalize(middle)
    second_in = low(normed_two * (1.0 + scale_two) + shift_two).reshape(token_count, D)
    up_lin = low_back(jnp.dot(second_in, fc1_weight, precision=HIGHEST))
    hidden = low(jax.nn.gelu(up_lin, approximate=False))
    mlp_out = low_back(jnp.dot(hidden, fc2_weight, precision=HIGHEST)).reshape(clip_tokens.shape)
    return middle + gate_two * mlp_out

def reference(tokens, noise_levels, group_map, noise_table, mod_weight, mod_bias, qkv_weight, out_weight, fc1_weight, fc2_weight, out_cotangent):
    params = tuple((weight.astype(jnp.float32) for weight in (noise_table, mod_weight, mod_bias, qkv_weight, out_weight, fc1_weight, fc2_weight)))

    def per_clip(totals, inputs):
        clip_tokens, clip_levels, clip_cotangent = inputs

        def forward(weights, values):
            return layer_clip(weights, values, clip_levels, group_map)
        result, pullback = jax.vjp(forward, params, clip_tokens.astype(jnp.float32))
        weight_grads, token_grad = pullback(clip_cotangent.astype(jnp.float32))
        totals = jax.tree.map(jnp.add, totals, weight_grads)
        return (totals, (result.astype(jnp.bfloat16), token_grad.astype(jnp.bfloat16)))
    zeros_start = jax.tree.map(jnp.zeros_like, params)
    totals, (layer_out, tokens_grad) = lax.scan(per_clip, zeros_start, (tokens, noise_levels, out_cotangent))
    table_grad, modw_grad, bias_grad, qkv_grad, outw_grad, upper_grad, lower_grad = totals
    return (layer_out, tokens_grad, table_grad, modw_grad, bias_grad, qkv_grad, outw_grad, upper_grad, lower_grad)
```

```python
from functools import partial

import jax
import jax.numpy as jnp
from jax import lax
from jax.experimental import pallas as pl
from jax.experimental.pallas import tpu as pltpu
from jax.sharding import PartitionSpec as P

D = 1024
HEAD = 64
HEADS = 16
LEVELS = 1000
GRID_H = 8
GRID_W = 16
PATCHES = 128


SCALE = 0.125
EPSILON = 1e-06
ROPE_BASE = 10000.0
NEG_LARGE = -1e30


def token_positions(frame_ids):
    slot_count = frame_ids.shape[0]
    total_rows = slot_count * GRID_H * GRID_W
    patch_ids = jnp.arange(total_rows, dtype=jnp.int32) % (GRID_H * GRID_W)
    frame_pos = jnp.repeat(frame_ids, GRID_H * GRID_W, total_repeat_length=total_rows)
    return (frame_pos, patch_ids // GRID_W, patch_ids % GRID_W)


def rope_angles(frame_pos, row_pos, col_pos):
    angle_list = []
    for position, comp_width in ((frame_pos, 16), (row_pos, 24), (col_pos, 24)):
        half_width = comp_width // 2
        frequency = ROPE_BASE ** (-2.0 * jnp.arange(half_width, dtype=jnp.float32) / comp_width)
        angle_list.append(position.astype(jnp.float32)[:, None] * frequency[None, :])
    return angle_list


def rotate(values, angle_list, direction):
    pieces = []
    offset = 0
    for angles in angle_list:
        half_width = angles.shape[1]
        first_half = values[:, :, offset : offset + half_width]
        second_half = values[:, :, offset + half_width : offset + 2 * half_width]
        cosine = jnp.cos(angles)[:, None, :]
        sine_part = direction * jnp.sin(angles)[:, None, :]
        pieces.append(first_half * cosine - second_half * sine_part)
        pieces.append(first_half * sine_part + second_half * cosine)
        offset = offset + 2 * half_width
    return jnp.concatenate(pieces, axis=2)


def normalize(values):
    center = values - jnp.mean(values, axis=-1, keepdims=True)
    inverse = lax.rsqrt(jnp.mean(center * center, axis=-1, keepdims=True) + EPSILON)
    return (center * inverse, inverse)


def norm_backward(grad_in, normed, inverse):
    return inverse * (
        grad_in
        - jnp.mean(grad_in, axis=-1, keepdims=True)
        - normed * jnp.mean(grad_in * normed, axis=-1, keepdims=True)
    )


def frames_of(group_map, first_row, row_count):
    slot_frames = lax.dynamic_slice_in_dim(group_map, first_row // PATCHES, row_count // PATCHES)
    return jnp.repeat(slot_frames, PATCHES, total_repeat_length=row_count)


def block_size(row_count, shard_rows):
    return 2 * shard_rows if row_count // shard_rows % 2 == 0 else shard_rows


def keep_same(values):
    return values


def local(
    tokens,
    noise_levels,
    group_map,
    noise_table,
    mod_weight,
    mod_bias,
    qkv_weight,
    out_weight,
    fc1_weight,
    fc2_weight,
    out_cotangent,
):
    rows_here = 2 * PATCHES
    my_frames = lax.dynamic_slice_in_dim(group_map, 2 * lax.axis_index("blk"), 2)
    frame_hot = (
        jnp.arange(group_map.shape[0], dtype=jnp.int32)[None, :] == my_frames[:, None]
    ).astype(jnp.int32)
    my_levels = jnp.sum(frame_hot * noise_levels[0][None, :], axis=1)
    level_hot = jnp.arange(LEVELS, dtype=jnp.int32)[None, :] == my_levels[:, None]
    embedded = jnp.dot(
        level_hot.astype(jnp.bfloat16), noise_table, preferred_element_type=jnp.float32
    )
    activated = jax.nn.silu(embedded).astype(jnp.bfloat16)
    modulation = (
        jnp.dot(activated, mod_weight, preferred_element_type=jnp.float32)
        + mod_bias.astype(jnp.float32)[None, :]
    )
    shift_one, scale_one, gate_one, shift_two, scale_two, gate_two = [
        modulation[:, member * D : (member + 1) * D][:, None, :] for member in range(6)
    ]
    inputs_here = tokens[0].astype(jnp.float32)
    normed_one, inverse_one = normalize(inputs_here)
    first_in = (
        (normed_one * (1.0 + scale_one) + shift_one).astype(jnp.bfloat16).reshape(rows_here, D)
    )
    qkv_lin = jnp.dot(first_in, qkv_weight, preferred_element_type=jnp.float32)
    token_frames, row_pos, col_pos = token_positions(my_frames)
    angle_list = rope_angles(token_frames, row_pos, col_pos)
    query = rotate(qkv_lin[:, :D].reshape(rows_here, HEADS, HEAD), angle_list, 1.0).astype(
        jnp.bfloat16
    )
    key_part = rotate(
        qkv_lin[:, D : 2 * D].reshape(rows_here, HEADS, HEAD), angle_list, 1.0
    ).astype(jnp.bfloat16)
    value_part = qkv_lin[:, 2 * D :].reshape(rows_here, HEADS, HEAD).astype(jnp.bfloat16)
    top_frame = jnp.max(my_frames)
    own_lowest = jnp.min(my_frames)
    forward_start = (
        jnp.full((HEADS, rows_here), NEG_LARGE, jnp.float32),
        jnp.zeros((HEADS, rows_here), jnp.float32),
        jnp.zeros((rows_here, HEADS, HEAD), jnp.float32),
    )
    first_row = jnp.int32(0)
    keys_piece = lax.all_gather(key_part, "blk", axis=0, tiled=True)
    values_piece = lax.all_gather(value_part, "blk", axis=0, tiled=True)
    piece_rows = keys_piece.shape[0]
    block_rows = block_size(piece_rows, rows_here)

    def forward_advance(turn_index, running):
        offset = turn_index * block_rows
        keys_block = lax.dynamic_slice_in_dim(keys_piece, offset, block_rows)
        values_block = lax.dynamic_slice_in_dim(values_piece, offset, block_rows)
        block_frames = frames_of(group_map, first_row + offset, block_rows)

        def attend(previous):
            top_scores, totals, accumulated = previous
            scores = (
                jnp.einsum("qhd,khd->hqk", query, keys_block, preferred_element_type=jnp.float32)
                * SCALE
            )
            allowed = block_frames[None, None, :] <= token_frames[None, :, None]
            new_top = jnp.maximum(
                top_scores, jnp.max(jnp.where(allowed, scores, NEG_LARGE), axis=2)
            )
            weights = jnp.where(allowed, jnp.exp(scores - new_top[:, :, None]), 0.0)
            factor = jnp.exp(top_scores - new_top)
            update = jnp.einsum(
                "hqk,khd->qhd",
                weights.astype(jnp.bfloat16),
                values_block,
                preferred_element_type=jnp.float32,
            )
            return (
                new_top,
                totals * factor + jnp.sum(weights, axis=2),
                accumulated * factor.T[:, :, None] + update,
            )

        return lax.cond(jnp.min(block_frames) > top_frame, keep_same, attend, running)

    top_scores, totals, accumulated = lax.fori_loop(
        0, piece_rows // block_rows, forward_advance, forward_start
    )
    attended = accumulated / totals.T[:, :, None]
    log_total = top_scores + jnp.log(totals)
    attended_low = attended.astype(jnp.bfloat16).reshape(rows_here, D)
    attn_out = jnp.dot(attended_low, out_weight, preferred_element_type=jnp.float32).reshape(
        2, PATCHES, D
    )
    middle = inputs_here + gate_one * attn_out
    normed_two, inverse_two = normalize(middle)
    second_in = (
        (normed_two * (1.0 + scale_two) + shift_two).astype(jnp.bfloat16).reshape(rows_here, D)
    )
    up_lin = jnp.dot(second_in, fc1_weight, preferred_element_type=jnp.float32)
    hidden = jax.nn.gelu(up_lin, approximate=False).astype(jnp.bfloat16)
    mlp_out = jnp.dot(hidden, fc2_weight, preferred_element_type=jnp.float32).reshape(2, PATCHES, D)
    layer_out = (middle + gate_two * mlp_out).astype(jnp.bfloat16)[None]
    cotangent = out_cotangent[0].astype(jnp.float32)
    d_gate_two = jnp.sum(cotangent * mlp_out, axis=1)
    d_mlp = (cotangent * gate_two).astype(jnp.bfloat16).reshape(rows_here, D)
    lower_part = jnp.einsum("rf,rd->fd", hidden, d_mlp, preferred_element_type=jnp.float32)
    d_hidden = jnp.einsum("rd,fd->rf", d_mlp, fc2_weight, preferred_element_type=jnp.float32)
    unused_value, gelu_pull = jax.vjp(partial(jax.nn.gelu, approximate=False), up_lin)
    d_up = gelu_pull(d_hidden)[0].astype(jnp.bfloat16)
    upper_part = jnp.einsum("rc,rf->cf", second_in, d_up, preferred_element_type=jnp.float32)
    d_second = jnp.einsum(
        "rf,cf->rc", d_up, fc1_weight, preferred_element_type=jnp.float32
    ).reshape(2, PATCHES, D)
    d_shift_two = jnp.sum(d_second, axis=1)
    d_scale_two = jnp.sum(d_second * normed_two, axis=1)
    d_middle = cotangent + norm_backward(d_second * (1.0 + scale_two), normed_two, inverse_two)
    d_gate_one = jnp.sum(d_middle * attn_out, axis=1)
    d_attn = (d_middle * gate_one).astype(jnp.bfloat16).reshape(rows_here, D)
    outw_part = jnp.einsum("rc,rd->cd", attended_low, d_attn, preferred_element_type=jnp.float32)
    d_attended = (
        jnp.einsum("rd,cd->rc", d_attn, out_weight, preferred_element_type=jnp.float32)
        .astype(jnp.bfloat16)
        .reshape(rows_here, HEADS, HEAD)
    )
    delta = jnp.sum(d_attended.astype(jnp.float32) * attended, axis=2).T
    grad_start = jnp.zeros((rows_here, HEADS, HEAD), jnp.float32)
    query_first_row = jnp.int32(0)
    query_keys_piece = lax.all_gather(key_part, "blk", axis=0, tiled=True)
    query_values_piece = lax.all_gather(value_part, "blk", axis=0, tiled=True)
    piece_rows = query_keys_piece.shape[0]
    query_block_rows = block_size(piece_rows, rows_here)

    def query_advance(turn_index, running):
        offset = turn_index * query_block_rows
        keys_block = lax.dynamic_slice_in_dim(query_keys_piece, offset, query_block_rows)
        values_block = lax.dynamic_slice_in_dim(query_values_piece, offset, query_block_rows)
        block_frames = frames_of(group_map, query_first_row + offset, query_block_rows)

        def query_accumulate(previous):
            scores = (
                jnp.einsum("qhd,khd->hqk", query, keys_block, preferred_element_type=jnp.float32)
                * SCALE
            )
            allowed = block_frames[None, None, :] <= token_frames[None, :, None]
            weights = jnp.where(allowed, jnp.exp(scores - log_total[:, :, None]), 0.0)
            weight_grad = jnp.einsum(
                "qhd,khd->hqk", d_attended, values_block, preferred_element_type=jnp.float32
            )
            score_grad = (weights * (weight_grad - delta[:, :, None]) * SCALE).astype(jnp.bfloat16)
            return previous + jnp.einsum(
                "hqk,khd->qhd", score_grad, keys_block, preferred_element_type=jnp.float32
            )

        return lax.cond(jnp.min(block_frames) > top_frame, keep_same, query_accumulate, running)

    query_grad = lax.fori_loop(0, piece_rows // query_block_rows, query_advance, grad_start)
    stats_lse, stats_delta = (
        lax.all_gather(log_total.T, "blk", axis=0, tiled=True),
        lax.all_gather(delta.T, "blk", axis=0, tiled=True),
    )
    key_first_row = jnp.int32(0)
    queries_piece = lax.all_gather(query, "blk", axis=0, tiled=True)
    grads_piece = lax.all_gather(d_attended, "blk", axis=0, tiled=True)
    piece_rows = queries_piece.shape[0]
    key_block_rows = block_size(piece_rows, rows_here)

    def key_advance(turn_index, running):
        offset = turn_index * key_block_rows
        query_block = lax.dynamic_slice_in_dim(queries_piece, offset, key_block_rows)
        grad_block = lax.dynamic_slice_in_dim(grads_piece, offset, key_block_rows)
        lse_block = lax.dynamic_slice_in_dim(stats_lse, key_first_row + offset, key_block_rows).T
        delta_block = lax.dynamic_slice_in_dim(
            stats_delta, key_first_row + offset, key_block_rows
        ).T
        block_frames = frames_of(group_map, key_first_row + offset, key_block_rows)

        def key_accumulate(previous):
            key_total, value_total = previous
            scores = (
                jnp.einsum(
                    "qhd,khd->hqk", query_block, key_part, preferred_element_type=jnp.float32
                )
                * SCALE
            )
            allowed = token_frames[None, None, :] <= block_frames[None, :, None]
            weights = jnp.where(allowed, jnp.exp(scores - lse_block[:, :, None]), 0.0)
            value_total = value_total + jnp.einsum(
                "hqk,qhd->khd",
                weights.astype(jnp.bfloat16),
                grad_block,
                preferred_element_type=jnp.float32,
            )
            weight_grad = jnp.einsum(
                "qhd,khd->hqk", grad_block, value_part, preferred_element_type=jnp.float32
            )
            score_grad = (weights * (weight_grad - delta_block[:, :, None]) * SCALE).astype(
                jnp.bfloat16
            )
            key_total = key_total + jnp.einsum(
                "hqk,qhd->khd", score_grad, query_block, preferred_element_type=jnp.float32
            )
            return (key_total, value_total)

        return lax.cond(jnp.max(block_frames) < own_lowest, keep_same, key_accumulate, running)

    key_grad, value_grad = lax.fori_loop(
        0, piece_rows // key_block_rows, key_advance, (grad_start, grad_start)
    )
    query_low = lax.optimization_barrier(query_grad.astype(jnp.bfloat16)).astype(jnp.float32)
    key_low = lax.optimization_barrier(key_grad.astype(jnp.bfloat16)).astype(jnp.float32)
    query_back = rotate(query_low, angle_list, -1.0).reshape(rows_here, D)
    key_back = rotate(key_low, angle_list, -1.0).reshape(rows_here, D)
    d_qkv = jnp.concatenate(
        [query_back, key_back, value_grad.reshape(rows_here, D)], axis=1
    ).astype(jnp.bfloat16)
    qkv_part = jnp.einsum("rc,rk->ck", first_in, d_qkv, preferred_element_type=jnp.float32)
    d_first = jnp.einsum(
        "rk,ck->rc", d_qkv, qkv_weight, preferred_element_type=jnp.float32
    ).reshape(2, PATCHES, D)
    d_shift_one = jnp.sum(d_first, axis=1)
    d_scale_one = jnp.sum(d_first * normed_one, axis=1)
    tokens_grad = (
        d_middle + norm_backward(d_first * (1.0 + scale_one), normed_one, inverse_one)
    ).astype(jnp.bfloat16)[None]
    d_mod = jnp.concatenate(
        [d_shift_one, d_scale_one, d_gate_one, d_shift_two, d_scale_two, d_gate_two], axis=1
    )
    bias_part = jnp.sum(d_mod, axis=0)
    d_mod_low = d_mod.astype(jnp.bfloat16)
    d_activated = jnp.einsum("sk,ck->sc", d_mod_low, mod_weight, preferred_element_type=jnp.float32)
    unused_silu, silu_pull = jax.vjp(jax.nn.silu, embedded)
    d_embedded = silu_pull(d_activated)[0]
    table_part = jnp.einsum(
        "sl,sc->cl", level_hot.astype(jnp.float32), d_embedded, precision=lax.Precision.HIGHEST
    )
    activated_all, d_mod_all = (
        lax.all_gather(activated, ("blk", "clip"), axis=0, tiled=True),
        lax.all_gather(d_mod_low, ("blk", "clip"), axis=0, tiled=True),
    )
    share_rows = D // lax.axis_size(("blk", "clip"))
    my_columns = lax.dynamic_slice_in_dim(
        activated_all, lax.axis_index(("blk", "clip")) * share_rows, share_rows, 1
    )
    modw_share = jnp.einsum("sc,sk->ck", my_columns, d_mod_all, preferred_element_type=jnp.float32)
    summed = (
        lax.psum_scatter(table_part, ("blk", "clip"), scatter_dimension=0, tiled=True),
        lax.psum_scatter(bias_part, ("blk", "clip"), scatter_dimension=0, tiled=True),
        lax.psum_scatter(qkv_part, ("blk", "clip"), scatter_dimension=0, tiled=True),
        lax.psum_scatter(outw_part, ("blk", "clip"), scatter_dimension=0, tiled=True),
        lax.psum_scatter(upper_part, ("blk", "clip"), scatter_dimension=0, tiled=True),
        lax.psum_scatter(lower_part, ("blk", "clip"), scatter_dimension=0, tiled=True),
    )
    return (
        layer_out,
        tokens_grad,
        summed[0].T,
        modw_share,
        summed[1],
        summed[2],
        summed[3],
        summed[4],
        summed[5],
    )


LANES = 128
FF = 4096
AXES = ("blk", "clip")
EXP_SCALE = SCALE * 1.4426950408889634
VMEM_LIMIT = 56 * 1024 * 1024
NT = (((1,), (1,)), ((), ()))
NN = (((1,), (0,)), ((), ()))


def full_block(shape):
    return pl.BlockSpec(shape, lambda *ids: (0,) * len(shape))


def rope_tables(frame_count):
    lane = jnp.arange(LANES, dtype=jnp.int32) % HEAD
    pieces = []
    for comp_width in (16, 24, 24):
        half_width = comp_width // 2
        frequency = ROPE_BASE ** (-2.0 * jnp.arange(half_width, dtype=jnp.float32) / comp_width)
        pieces += [frequency, frequency]
    frequency = jnp.tile(jnp.concatenate(pieces), LANES // HEAD)[None, :]
    first = (lane < 8) | ((lane >= 16) & (lane < 28)) | ((lane >= 40) & (lane < 52))
    sign = jnp.where(first, -1.0, 1.0)[None, :]
    in_frame = (lane < 16)[None, :]
    in_row = (lane < 40)[None, :]
    frame_angle = jnp.arange(frame_count, dtype=jnp.float32)[:, None] * frequency
    patch = jnp.arange(PATCHES, dtype=jnp.int32)[:, None]
    place = jnp.where(in_row, patch // GRID_W, patch % GRID_W).astype(jnp.float32)
    place_angle = place * frequency
    return (
        jnp.where(in_frame, jnp.cos(frame_angle), 0.0),
        jnp.where(in_frame, sign * jnp.sin(frame_angle), 0.0),
        jnp.where(in_frame, 0.0, jnp.cos(place_angle)),
        jnp.where(in_frame, 0.0, sign * jnp.sin(place_angle)),
    )


def partner_lanes(values):
    lane = lax.broadcasted_iota(jnp.int32, values.shape, 1) % HEAD
    ahead_eight = pltpu.roll(values, LANES - 8, 1)
    behind_eight = pltpu.roll(values, 8, 1)
    ahead_twelve = pltpu.roll(values, LANES - 12, 1)
    behind_twelve = pltpu.roll(values, 12, 1)
    ahead = ((lane >= 16) & (lane < 28)) | ((lane >= 40) & (lane < 52))
    return jnp.where(
        lane < 8,
        ahead_eight,
        jnp.where(lane < 16, behind_eight, jnp.where(ahead, ahead_twelve, behind_twelve)),
    )


def qkv_kernel(
    frames_ref,
    tokens_ref,
    mod_ref,
    qw_ref,
    kw_ref,
    vw_ref,
    fcos_ref,
    fsin_ref,
    pcos_ref,
    psin_ref,
    out_ref,
    first_ref,
):
    @pl.when(pl.program_id(0) == 0)
    def _():
        for slot in range(2):
            rows = slice(slot * PATCHES, (slot + 1) * PATCHES)
            normed, unused = normalize(tokens_ref[rows, :].astype(jnp.float32))
            shift = mod_ref[slot : slot + 1, :D]
            scale = mod_ref[slot : slot + 1, D : 2 * D]
            first_ref[rows, :] = (normed * (1.0 + scale) + shift).astype(jnp.bfloat16)

    first = first_ref[...]
    linear = [
        lax.dot_general(first, ref[...], NN, preferred_element_type=jnp.float32)
        for ref in (qw_ref, kw_ref, vw_ref)
    ]
    for slot in range(2):
        rows = slice(slot * PATCHES, (slot + 1) * PATCHES)
        frame = frames_ref[slot]
        cosine = pcos_ref[...] + fcos_ref[pl.ds(frame, 1), :]
        sine = psin_ref[...] + fsin_ref[pl.ds(frame, 1), :]
        for part in range(2):
            values = linear[part][rows, :]
            turned = values * cosine + partner_lanes(values) * sine
            out_ref[0, rows, part * LANES : (part + 1) * LANES] = turned.astype(jnp.bfloat16)
        out_ref[0, rows, 2 * LANES :] = linear[2][rows, :].astype(jnp.bfloat16)


def project_qkv(my_frames, tokens_here, mod_first, qkv_weight, tables):
    groups = D // LANES
    rows = tokens_here.shape[0]
    weight_specs = [
        pl.BlockSpec((D, LANES), lambda g, frames, part=part: (0, part * groups + g))
        for part in range(3)
    ]
    return pl.pallas_call(
        qkv_kernel,
        grid_spec=pltpu.PrefetchScalarGridSpec(
            num_scalar_prefetch=1,
            grid=(groups,),
            in_specs=[full_block((rows, D)), full_block(mod_first.shape)]
            + weight_specs
            + [full_block(table.shape) for table in tables],
            out_specs=[
                pl.BlockSpec((1, rows, 3 * LANES), lambda g, frames: (g, 0, 0)),
                full_block((rows, D)),
            ],
        ),
        out_shape=[
            jax.ShapeDtypeStruct((groups, rows, 3 * LANES), jnp.bfloat16),
            jax.ShapeDtypeStruct((rows, D), jnp.bfloat16),
        ],
        compiler_params=pltpu.CompilerParams(
            vmem_limit_bytes=VMEM_LIMIT, dimension_semantics=("arbitrary",)
        ),
        name="project_qkv",
    )(my_frames, tokens_here, mod_first, qkv_weight, qkv_weight, qkv_weight, *tables)


def head_stack(values):
    lane = lax.broadcasted_iota(jnp.int32, values.shape, 1)
    zero = jnp.zeros_like(values)
    return jnp.concatenate(
        [jnp.where(lane < HEAD, values, zero), jnp.where(lane < HEAD, zero, values)], axis=0
    )


def hidden_keys(shape):
    key_row = lax.broadcasted_iota(jnp.int32, shape, 0)
    query_column = lax.broadcasted_iota(jnp.int32, shape, 1) % (2 * PATCHES)
    return (key_row >= PATCHES) & (query_column < PATCHES)


def own_heads(values):
    rows = 2 * PATCHES
    return jnp.concatenate([values[:HEAD, :rows], values[HEAD:LANES, rows:]], axis=0)


def by_frame(frames_ref, source_ref, target_refs):
    for slot in range(source_ref.shape[0] // PATCHES):
        rows = pl.ds(pl.multiple_of(frames_ref[slot] * PATCHES, PATCHES), PATCHES)
        for part, target in enumerate(target_refs):
            target[rows, :] = source_ref[
                slot * PATCHES : (slot + 1) * PATCHES, part * LANES : (part + 1) * LANES
            ]


def attend_kernel(
    frames_ref, slots_ref, qkv_ref, att_ref, ot_ref, lse_ref, q_ref, k_ref, v_ref, vt_ref
):
    token_count = qkv_ref.shape[0]
    by_frame(frames_ref, qkv_ref, (q_ref, k_ref, v_ref))
    vt_ref[:LANES, :] = v_ref[...].T
    vt_ref[LANES:, :] = jnp.ones((vt_ref.shape[0] - LANES, token_count), jnp.bfloat16)
    step = 2 * PATCHES
    for turn in range(token_count // step):
        here = slice(turn * step, (turn + 1) * step)
        queries = head_stack(q_ref[here, :])
        ranges = [here] if turn == 0 else [slice(0, turn * step), here]
        raw = [
            lax.dot_general(k_ref[keys, :], queries, NT, preferred_element_type=jnp.float32)
            for keys in ranges
        ]
        raw[-1] = jnp.where(hidden_keys(raw[-1].shape), NEG_LARGE, raw[-1])
        top = jnp.max(raw[-1], axis=0, keepdims=True)
        for part in raw[:-1]:
            top = jnp.maximum(top, jnp.max(part, axis=0, keepdims=True))
        top = top * EXP_SCALE
        summed = None
        for keys, part in zip(ranges, raw):
            weights = jnp.exp2(part * EXP_SCALE - top).astype(jnp.bfloat16)
            update = lax.dot_general(
                vt_ref[:, keys], weights, NN, preferred_element_type=jnp.float32
            )
            summed = update if summed is None else summed + update
        totals = summed[LANES : LANES + 1, :]
        lse_ref[turn : turn + 1, :] = top + jnp.log2(totals)
        out = own_heads(summed[:LANES, :] / totals)
        ot_ref[:, here] = out
        rounded = out.T.astype(jnp.bfloat16)
        for half in range(2):
            slot = slots_ref[2 * turn + half]
            rows = pl.ds(pl.multiple_of(slot * PATCHES, PATCHES), PATCHES)
            att_ref[rows, :] = rounded[half * PATCHES : (half + 1) * PATCHES, :]


def attend(frames, slots, qkv):
    token_count = qkv.shape[0]
    turns = token_count // (2 * PATCHES)
    return pl.pallas_call(
        attend_kernel,
        in_specs=[
            pl.BlockSpec(memory_space=pltpu.SMEM),
            pl.BlockSpec(memory_space=pltpu.SMEM),
            pl.BlockSpec(memory_space=pltpu.VMEM),
        ],
        out_specs=[pl.BlockSpec(memory_space=pltpu.VMEM)] * 3,
        out_shape=[
            jax.ShapeDtypeStruct((token_count, LANES), jnp.bfloat16),
            jax.ShapeDtypeStruct((LANES, token_count), jnp.float32),
            jax.ShapeDtypeStruct((turns, 4 * PATCHES), jnp.float32),
        ],
        scratch_shapes=[pltpu.VMEM((token_count, LANES), jnp.bfloat16)] * 3
        + [pltpu.VMEM((LANES + 16, token_count), jnp.bfloat16)],
        compiler_params=pltpu.CompilerParams(vmem_limit_bytes=VMEM_LIMIT),
        name="attend",
    )(frames, slots, qkv)


def attend_back_kernel(
    frames_ref,
    slots_ref,
    qkv_ref,
    grad_ref,
    ot_ref,
    lse_ref,
    fcos_ref,
    fsin_ref,
    pcos_ref,
    psin_ref,
    out_ref,
    q_ref,
    k_ref,
    v_ref,
    d_ref,
    kt_ref,
    dk_ref,
    dv_ref,
):
    token_count = qkv_ref.shape[0]
    by_frame(frames_ref, qkv_ref, (q_ref, k_ref, v_ref))
    by_frame(frames_ref, grad_ref, (d_ref,))
    kt_ref[...] = k_ref[...].T
    step = 2 * PATCHES

    def put(frame, part, values):
        rows = pl.ds(pl.multiple_of(slots_ref[frame] * PATCHES, PATCHES), PATCHES)
        out_ref[rows, part * LANES : (part + 1) * LANES] = values

    def turn_back(frame, values):
        values = values.astype(jnp.bfloat16).astype(jnp.float32)
        cosine = pcos_ref[...] + fcos_ref[frame : frame + 1, :]
        sine = psin_ref[...] + fsin_ref[frame : frame + 1, :]
        return (values * cosine - partner_lanes(values) * sine).astype(jnp.bfloat16)

    for turn in range(token_count // step):
        here = slice(turn * step, (turn + 1) * step)
        queries = head_stack(q_ref[here, :])
        grads_here = d_ref[here, :]
        grads = head_stack(grads_here)
        product = grads_here.astype(jnp.float32).T * ot_ref[:, here]
        delta = jnp.concatenate(
            [
                jnp.sum(product[:HEAD, :], axis=0, keepdims=True),
                jnp.sum(product[HEAD:, :], axis=0, keepdims=True),
            ],
            axis=1,
        )
        lse = lse_ref[turn : turn + 1, :]
        ranges = [here] if turn == 0 else [here, slice(0, turn * step)]
        total = None
        for keys in ranges:
            raw = lax.dot_general(
                k_ref[keys, :], queries, NT, preferred_element_type=jnp.float32
            )
            weights = jnp.exp2(raw * EXP_SCALE - lse)
            if keys is here:
                weights = jnp.where(hidden_keys(weights.shape), 0.0, weights)
            weight_grad = lax.dot_general(
                v_ref[keys, :], grads, NT, preferred_element_type=jnp.float32
            )
            score_grad = (weights * (weight_grad - delta)).astype(jnp.bfloat16)
            value_part = lax.dot_general(
                weights.astype(jnp.bfloat16), grads, NN, preferred_element_type=jnp.float32
            )
            key_part = lax.dot_general(
                score_grad, queries, NN, preferred_element_type=jnp.float32
            )
            if keys is here:
                dv_ref[keys, :] = value_part
                dk_ref[keys, :] = key_part
            else:
                dv_ref[keys, :] += value_part
                dk_ref[keys, :] += key_part
            update = lax.dot_general(
                kt_ref[:, keys], score_grad, NN, preferred_element_type=jnp.float32
            )
            total = update if total is None else total + update
        query_grad = own_heads(total).T * SCALE
        for half in range(2):
            put(
                2 * turn + half,
                0,
                turn_back(2 * turn + half, query_grad[half * PATCHES : (half + 1) * PATCHES, :]),
            )
    for frame in range(token_count // PATCHES):
        rows = slice(frame * PATCHES, (frame + 1) * PATCHES)
        put(frame, 1, turn_back(frame, dk_ref[rows, :] * SCALE))
        put(frame, 2, dv_ref[rows, :].astype(jnp.bfloat16))


def attend_back(frames, slots, qkv, grads, ot, lse, tables):
    token_count = qkv.shape[0]
    smem = pl.BlockSpec(memory_space=pltpu.SMEM)
    vmem = pl.BlockSpec(memory_space=pltpu.VMEM)
    return pl.pallas_call(
        attend_back_kernel,
        in_specs=[smem, smem] + [vmem] * 8,
        out_specs=vmem,
        out_shape=jax.ShapeDtypeStruct((token_count, 3 * LANES), jnp.bfloat16),
        scratch_shapes=[pltpu.VMEM((token_count, LANES), jnp.bfloat16)] * 4
        + [pltpu.VMEM((LANES, token_count), jnp.bfloat16)]
        + [pltpu.VMEM((token_count, LANES), jnp.float32)] * 2,
        compiler_params=pltpu.CompilerParams(vmem_limit_bytes=VMEM_LIMIT),
        name="attend_back",
    )(frames, slots, qkv, grads, ot, lse, *tables)


def swap(values, bit):
    count = lax.axis_size(AXES)
    return lax.ppermute(values, AXES, [(index, index ^ bit) for index in range(count)])


def gather_pairs(values):
    bit = 1
    while bit < lax.axis_size(AXES):
        values = jnp.concatenate([values, swap(values, bit)], axis=0)
        bit *= 2
    return values


def halving_sum(values, order):
    index = lax.axis_index(AXES)
    left = sorted(order)
    for position, bit in enumerate(order):
        place = left.index(bit)
        above = 2 ** (len(left) - 1 - place)
        split = values.reshape((above, 2, 2**place) + values.shape[1:])
        mine = (index >> bit) & 1
        keep = lax.dynamic_index_in_dim(split, mine, 1, keepdims=False)
        send = lax.dynamic_index_in_dim(split, 1 - mine, 1, keepdims=False)
        got = swap(send, 2**bit)
        total = keep.astype(jnp.float32) + got.astype(jnp.float32)
        if position < len(order) - 1:
            total = total.astype(jnp.bfloat16)
        values = total.reshape((above * 2**place,) + values.shape[1:])
        left.remove(bit)
    return values[0]


def sum_shares(values):
    count = lax.axis_size(AXES)
    rows, columns = values.shape
    blocks = values.reshape(count, rows // count, columns)
    bits = list(range(count.bit_length() - 1))
    other = [0, 2, 1] + bits[3:]
    half = columns // 2
    return jnp.concatenate(
        [halving_sum(blocks[:, :, :half], bits), halving_sum(blocks[:, :, half:], other)], axis=1
    )


def local_heads(
    tokens,
    noise_levels,
    group_map,
    noise_table,
    mod_weight,
    mod_bias,
    qkv_weight,
    out_weight,
    fc1_weight,
    fc2_weight,
    out_cotangent,
):
    rows_here = 2 * PATCHES
    frame_count = group_map.shape[0]
    groups = D // LANES
    clips = lax.axis_size("clip")
    device_count = lax.axis_size(AXES)
    index = lax.axis_index(AXES)
    slots = jnp.argsort(group_map).astype(jnp.int32)
    my_frames = lax.dynamic_slice_in_dim(group_map, 2 * lax.axis_index("blk"), 2)
    tables = rope_tables(frame_count)
    embedded = jnp.concatenate(
        [
            lax.dynamic_slice_in_dim(noise_table, noise_levels[0, my_frames[slot]], 1)
            for slot in range(2)
        ]
    ).astype(jnp.float32)
    activated = jax.nn.silu(embedded).astype(jnp.bfloat16)
    modulation = (
        jnp.dot(activated, mod_weight, preferred_element_type=jnp.float32)
        + mod_bias.astype(jnp.float32)[None, :]
    )
    shift_one, scale_one, gate_one, shift_two, scale_two, gate_two = [
        modulation[:, member * D : (member + 1) * D][:, None, :] for member in range(6)
    ]
    qkv_out, first_in = project_qkv(
        my_frames, tokens.reshape(rows_here, D), modulation[:, : 2 * D], qkv_weight, tables
    )
    qkv_heads = lax.all_to_all(qkv_out, "blk", 0, 0, tiled=True).reshape(-1, 3 * LANES)
    att_heads, ot, lse = attend(group_map, slots, qkv_heads)
    attended_low = (
        lax.all_to_all(att_heads.reshape(groups, rows_here, LANES), "blk", 0, 0, tiled=True)
        .transpose(1, 0, 2)
        .reshape(rows_here, D)
    )
    inputs_here = tokens[0].astype(jnp.float32)
    attn_out = jnp.dot(attended_low, out_weight, preferred_element_type=jnp.float32).reshape(
        2, PATCHES, D
    )
    middle = inputs_here + gate_one * attn_out
    normed_two, inverse_two = normalize(middle)
    second_in = (
        (normed_two * (1.0 + scale_two) + shift_two).astype(jnp.bfloat16).reshape(rows_here, D)
    )
    up_lin = jnp.dot(second_in, fc1_weight, preferred_element_type=jnp.float32)
    hidden = jax.nn.gelu(up_lin, approximate=False).astype(jnp.bfloat16)
    mlp_out = jnp.dot(hidden, fc2_weight, preferred_element_type=jnp.float32).reshape(2, PATCHES, D)
    layer_out = (middle + gate_two * mlp_out).astype(jnp.bfloat16)[None]
    cotangent = out_cotangent[0].astype(jnp.float32)
    d_gate_two = jnp.sum(cotangent * mlp_out, axis=1)
    d_mlp = (cotangent * gate_two).astype(jnp.bfloat16).reshape(rows_here, D)
    lower_part = jnp.einsum("rf,rd->fd", hidden, d_mlp, preferred_element_type=jnp.float32)
    lower_share = sum_shares(lower_part.astype(jnp.bfloat16))
    d_hidden = jnp.einsum("rd,fd->rf", d_mlp, fc2_weight, preferred_element_type=jnp.float32)
    unused_value, gelu_pull = jax.vjp(partial(jax.nn.gelu, approximate=False), up_lin)
    d_up = gelu_pull(d_hidden)[0].astype(jnp.bfloat16)
    upper_part = jnp.einsum("rc,rf->cf", second_in, d_up, preferred_element_type=jnp.float32)
    upper_share = sum_shares(upper_part.astype(jnp.bfloat16))
    d_second = jnp.einsum(
        "rf,cf->rc", d_up, fc1_weight, preferred_element_type=jnp.float32
    ).reshape(2, PATCHES, D)
    d_shift_two = jnp.sum(d_second, axis=1)
    d_scale_two = jnp.sum(d_second * normed_two, axis=1)
    d_middle = cotangent + norm_backward(d_second * (1.0 + scale_two), normed_two, inverse_two)
    d_gate_one = jnp.sum(d_middle * attn_out, axis=1)
    d_attn = (d_middle * gate_one).astype(jnp.bfloat16).reshape(rows_here, D)
    outw_part = jnp.einsum("rc,rd->cd", attended_low, d_attn, preferred_element_type=jnp.float32)
    outw_share = sum_shares(outw_part.astype(jnp.bfloat16))
    d_attended = jnp.einsum(
        "rd,cd->rc", d_attn, out_weight, preferred_element_type=jnp.float32
    ).astype(jnp.bfloat16)
    early_all = gather_pairs(
        jnp.concatenate([d_gate_one, d_shift_two, d_scale_two, d_gate_two], axis=1).astype(
            jnp.bfloat16
        )[None]
    )
    grad_heads = lax.all_to_all(
        d_attended.reshape(rows_here, groups, LANES).transpose(1, 0, 2), "blk", 0, 0, tiled=True
    ).reshape(-1, LANES)
    d_heads = attend_back(group_map, slots, qkv_heads, grad_heads, ot, lse, tables)
    d_qkv = (
        lax.all_to_all(d_heads.reshape(groups, rows_here, 3 * LANES), "blk", 0, 0, tiled=True)
        .reshape(groups, rows_here, 3, LANES)
        .transpose(1, 2, 0, 3)
        .reshape(rows_here, 3 * D)
    )
    qkv_part = jnp.einsum("rc,rk->ck", first_in, d_qkv, preferred_element_type=jnp.float32)
    qkv_share = sum_shares(qkv_part.astype(jnp.bfloat16))
    d_first = jnp.einsum(
        "rk,ck->rc", d_qkv, qkv_weight, preferred_element_type=jnp.float32
    ).reshape(2, PATCHES, D)
    normed_one, inverse_one = normalize(inputs_here)
    d_shift_one = jnp.sum(d_first, axis=1)
    d_scale_one = jnp.sum(d_first * normed_one, axis=1)
    tokens_grad = (
        d_middle + norm_backward(d_first * (1.0 + scale_one), normed_one, inverse_one)
    ).astype(jnp.bfloat16)[None]
    late_all = gather_pairs(
        jnp.concatenate([d_shift_one, d_scale_one], axis=1).astype(jnp.bfloat16)[None]
    )
    d_mod_all = jnp.concatenate([late_all, early_all], axis=2).reshape(2 * device_count, 6 * D)
    member_index = index ^ jnp.arange(device_count, dtype=jnp.int32)
    levels_all = gather_pairs(
        lax.dynamic_slice_in_dim(
            jnp.broadcast_to(noise_levels[0][my_frames][:, None], (2, LANES)), 0, 2
        )[None]
    )[:, :, 0].reshape(2 * device_count)
    share = D // device_count
    level_hot = jnp.arange(LEVELS, dtype=jnp.int32)[:, None] == levels_all[None, :]
    table_columns = lax.dynamic_slice_in_dim(noise_table, index * share, share, 1)
    embedded_columns = jnp.einsum(
        "ls,lc->sc",
        level_hot.astype(jnp.bfloat16),
        table_columns,
        preferred_element_type=jnp.float32,
    )
    activated_columns, silu_pull = jax.vjp(jax.nn.silu, embedded_columns)
    modw_share = jnp.einsum(
        "sc,sk->ck",
        activated_columns.astype(jnp.bfloat16),
        d_mod_all,
        preferred_element_type=jnp.float32,
    )
    weight_rows = lax.dynamic_slice_in_dim(mod_weight, index * share, share, 0)
    d_activated = jnp.einsum("sk,ck->sc", d_mod_all, weight_rows, preferred_element_type=jnp.float32)
    d_embedded = silu_pull(d_activated)[0]
    table_share = jnp.dot(
        level_hot.astype(jnp.float32), d_embedded, precision=lax.Precision.HIGHEST
    )
    bias_columns = 6 * D // device_count
    bias_share = jnp.sum(
        lax.dynamic_slice_in_dim(d_mod_all, index * bias_columns, bias_columns, 1).astype(
            jnp.float32
        ),
        axis=0,
    )
    return (
        layer_out,
        tokens_grad,
        table_share,
        modw_share,
        bias_share,
        qkv_share,
        outw_share,
        upper_share,
        lower_share,
    )


def solution(mesh):
    pair_split = mesh.shape["blk"] * LANES == D
    return jax.shard_map(
        local_heads if pair_split else local,
        mesh=mesh,
        in_specs=(
            P("clip", "blk", None, None),
            P("clip", None),
            P(),
            P(),
            P(),
            P(),
            P(),
            P(),
            P(),
            P(),
            P("clip", "blk", None, None),
        ),
        out_specs=(
            P("clip", "blk", None, None),
            P("clip", "blk", None, None),
            P(None, ("blk", "clip")),
            P(("blk", "clip"), None),
            P(("blk", "clip")),
            P(("blk", "clip"), None),
            P(("blk", "clip"), None),
            P(("blk", "clip"), None),
            P(("blk", "clip"), None),
        ),
        check_vma=False,
    )
```

```python
from functools import partial

import jax
import jax.numpy as jnp
from jax import lax
from jax.experimental import pallas as pl
from jax.experimental.pallas import tpu as pltpu
from jax.sharding import PartitionSpec as P

D = 1024
HEAD = 64
HEADS = 16
LEVELS = 1000
GRID_H = 8
GRID_W = 16
PATCHES = 128


SCALE = 0.125
EPSILON = 1e-06
ROPE_BASE = 10000.0
NEG_LARGE = -1e30


def token_positions(frame_ids):
    slot_count = frame_ids.shape[0]
    total_rows = slot_count * GRID_H * GRID_W
    patch_ids = jnp.arange(total_rows, dtype=jnp.int32) % (GRID_H * GRID_W)
    frame_pos = jnp.repeat(frame_ids, GRID_H * GRID_W, total_repeat_length=total_rows)
    return (frame_pos, patch_ids // GRID_W, patch_ids % GRID_W)


def rope_angles(frame_pos, row_pos, col_pos):
    angle_list = []
    for position, comp_width in ((frame_pos, 16), (row_pos, 24), (col_pos, 24)):
        half_width = comp_width // 2
        frequency = ROPE_BASE ** (-2.0 * jnp.arange(half_width, dtype=jnp.float32) / comp_width)
        angle_list.append(position.astype(jnp.float32)[:, None] * frequency[None, :])
    return angle_list


def rotate(values, angle_list, direction):
    pieces = []
    offset = 0
    for angles in angle_list:
        half_width = angles.shape[1]
        first_half = values[:, :, offset : offset + half_width]
        second_half = values[:, :, offset + half_width : offset + 2 * half_width]
        cosine = jnp.cos(angles)[:, None, :]
        sine_part = direction * jnp.sin(angles)[:, None, :]
        pieces.append(first_half * cosine - second_half * sine_part)
        pieces.append(first_half * sine_part + second_half * cosine)
        offset = offset + 2 * half_width
    return jnp.concatenate(pieces, axis=2)


def normalize(values):
    center = values - jnp.mean(values, axis=-1, keepdims=True)
    inverse = lax.rsqrt(jnp.mean(center * center, axis=-1, keepdims=True) + EPSILON)
    return (center * inverse, inverse)


def norm_backward(grad_in, normed, inverse):
    return inverse * (
        grad_in
        - jnp.mean(grad_in, axis=-1, keepdims=True)
        - normed * jnp.mean(grad_in * normed, axis=-1, keepdims=True)
    )


def frames_of(group_map, first_row, row_count):
    slot_frames = lax.dynamic_slice_in_dim(group_map, first_row // PATCHES, row_count // PATCHES)
    return jnp.repeat(slot_frames, PATCHES, total_repeat_length=row_count)


def block_size(row_count, shard_rows):
    return 2 * shard_rows if row_count // shard_rows % 2 == 0 else shard_rows


def keep_same(values):
    return values


def local(
    tokens,
    noise_levels,
    group_map,
    noise_table,
    mod_weight,
    mod_bias,
    qkv_weight,
    out_weight,
    fc1_weight,
    fc2_weight,
    out_cotangent,
):
    rows_here = 2 * PATCHES
    my_frames = lax.dynamic_slice_in_dim(group_map, 2 * lax.axis_index("blk"), 2)
    frame_hot = (
        jnp.arange(group_map.shape[0], dtype=jnp.int32)[None, :] == my_frames[:, None]
    ).astype(jnp.int32)
    my_levels = jnp.sum(frame_hot * noise_levels[0][None, :], axis=1)
    level_hot = jnp.arange(LEVELS, dtype=jnp.int32)[None, :] == my_levels[:, None]
    embedded = jnp.dot(
        level_hot.astype(jnp.bfloat16), noise_table, preferred_element_type=jnp.float32
    )
    activated = jax.nn.silu(embedded).astype(jnp.bfloat16)
    modulation = (
        jnp.dot(activated, mod_weight, preferred_element_type=jnp.float32)
        + mod_bias.astype(jnp.float32)[None, :]
    )
    shift_one, scale_one, gate_one, shift_two, scale_two, gate_two = [
        modulation[:, member * D : (member + 1) * D][:, None, :] for member in range(6)
    ]
    inputs_here = tokens[0].astype(jnp.float32)
    normed_one, inverse_one = normalize(inputs_here)
    first_in = (
        (normed_one * (1.0 + scale_one) + shift_one).astype(jnp.bfloat16).reshape(rows_here, D)
    )
    qkv_lin = jnp.dot(first_in, qkv_weight, preferred_element_type=jnp.float32)
    token_frames, row_pos, col_pos = token_positions(my_frames)
    angle_list = rope_angles(token_frames, row_pos, col_pos)
    query = rotate(qkv_lin[:, :D].reshape(rows_here, HEADS, HEAD), angle_list, 1.0).astype(
        jnp.bfloat16
    )
    key_part = rotate(
        qkv_lin[:, D : 2 * D].reshape(rows_here, HEADS, HEAD), angle_list, 1.0
    ).astype(jnp.bfloat16)
    value_part = qkv_lin[:, 2 * D :].reshape(rows_here, HEADS, HEAD).astype(jnp.bfloat16)
    top_frame = jnp.max(my_frames)
    own_lowest = jnp.min(my_frames)
    forward_start = (
        jnp.full((HEADS, rows_here), NEG_LARGE, jnp.float32),
        jnp.zeros((HEADS, rows_here), jnp.float32),
        jnp.zeros((rows_here, HEADS, HEAD), jnp.float32),
    )
    first_row = jnp.int32(0)
    keys_piece = lax.all_gather(key_part, "blk", axis=0, tiled=True)
    values_piece = lax.all_gather(value_part, "blk", axis=0, tiled=True)
    piece_rows = keys_piece.shape[0]
    block_rows = block_size(piece_rows, rows_here)

    def forward_advance(turn_index, running):
        offset = turn_index * block_rows
        keys_block = lax.dynamic_slice_in_dim(keys_piece, offset, block_rows)
        values_block = lax.dynamic_slice_in_dim(values_piece, offset, block_rows)
        block_frames = frames_of(group_map, first_row + offset, block_rows)

        def attend(previous):
            top_scores, totals, accumulated = previous
            scores = (
                jnp.einsum("qhd,khd->hqk", query, keys_block, preferred_element_type=jnp.float32)
                * SCALE
            )
            allowed = block_frames[None, None, :] <= token_frames[None, :, None]
            new_top = jnp.maximum(
                top_scores, jnp.max(jnp.where(allowed, scores, NEG_LARGE), axis=2)
            )
            weights = jnp.where(allowed, jnp.exp(scores - new_top[:, :, None]), 0.0)
            factor = jnp.exp(top_scores - new_top)
            update = jnp.einsum(
                "hqk,khd->qhd",
                weights.astype(jnp.bfloat16),
                values_block,
                preferred_element_type=jnp.float32,
            )
            return (
                new_top,
                totals * factor + jnp.sum(weights, axis=2),
                accumulated * factor.T[:, :, None] + update,
            )

        return lax.cond(jnp.min(block_frames) > top_frame, keep_same, attend, running)

    top_scores, totals, accumulated = lax.fori_loop(
        0, piece_rows // block_rows, forward_advance, forward_start
    )
    attended = accumulated / totals.T[:, :, None]
    log_total = top_scores + jnp.log(totals)
    attended_low = attended.astype(jnp.bfloat16).reshape(rows_here, D)
    attn_out = jnp.dot(attended_low, out_weight, preferred_element_type=jnp.float32).reshape(
        2, PATCHES, D
    )
    middle = inputs_here + gate_one * attn_out
    normed_two, inverse_two = normalize(middle)
    second_in = (
        (normed_two * (1.0 + scale_two) + shift_two).astype(jnp.bfloat16).reshape(rows_here, D)
    )
    up_lin = jnp.dot(second_in, fc1_weight, preferred_element_type=jnp.float32)
    hidden = jax.nn.gelu(up_lin, approximate=False).astype(jnp.bfloat16)
    mlp_out = jnp.dot(hidden, fc2_weight, preferred_element_type=jnp.float32).reshape(2, PATCHES, D)
    layer_out = (middle + gate_two * mlp_out).astype(jnp.bfloat16)[None]
    cotangent = out_cotangent[0].astype(jnp.float32)
    d_gate_two = jnp.sum(cotangent * mlp_out, axis=1)
    d_mlp = (cotangent * gate_two).astype(jnp.bfloat16).reshape(rows_here, D)
    lower_part = jnp.einsum("rf,rd->fd", hidden, d_mlp, preferred_element_type=jnp.float32)
    d_hidden = jnp.einsum("rd,fd->rf", d_mlp, fc2_weight, preferred_element_type=jnp.float32)
    unused_value, gelu_pull = jax.vjp(partial(jax.nn.gelu, approximate=False), up_lin)
    d_up = gelu_pull(d_hidden)[0].astype(jnp.bfloat16)
    upper_part = jnp.einsum("rc,rf->cf", second_in, d_up, preferred_element_type=jnp.float32)
    d_second = jnp.einsum(
        "rf,cf->rc", d_up, fc1_weight, preferred_element_type=jnp.float32
    ).reshape(2, PATCHES, D)
    d_shift_two = jnp.sum(d_second, axis=1)
    d_scale_two = jnp.sum(d_second * normed_two, axis=1)
    d_middle = cotangent + norm_backward(d_second * (1.0 + scale_two), normed_two, inverse_two)
    d_gate_one = jnp.sum(d_middle * attn_out, axis=1)
    d_attn = (d_middle * gate_one).astype(jnp.bfloat16).reshape(rows_here, D)
    outw_part = jnp.einsum("rc,rd->cd", attended_low, d_attn, preferred_element_type=jnp.float32)
    d_attended = (
        jnp.einsum("rd,cd->rc", d_attn, out_weight, preferred_element_type=jnp.float32)
        .astype(jnp.bfloat16)
        .reshape(rows_here, HEADS, HEAD)
    )
    delta = jnp.sum(d_attended.astype(jnp.float32) * attended, axis=2).T
    grad_start = jnp.zeros((rows_here, HEADS, HEAD), jnp.float32)
    query_first_row = jnp.int32(0)
    query_keys_piece = lax.all_gather(key_part, "blk", axis=0, tiled=True)
    query_values_piece = lax.all_gather(value_part, "blk", axis=0, tiled=True)
    piece_rows = query_keys_piece.shape[0]
    query_block_rows = block_size(piece_rows, rows_here)

    def query_advance(turn_index, running):
        offset = turn_index * query_block_rows
        keys_block = lax.dynamic_slice_in_dim(query_keys_piece, offset, query_block_rows)
        values_block = lax.dynamic_slice_in_dim(query_values_piece, offset, query_block_rows)
        block_frames = frames_of(group_map, query_first_row + offset, query_block_rows)

        def query_accumulate(previous):
            scores = (
                jnp.einsum("qhd,khd->hqk", query, keys_block, preferred_element_type=jnp.float32)
                * SCALE
            )
            allowed = block_frames[None, None, :] <= token_frames[None, :, None]
            weights = jnp.where(allowed, jnp.exp(scores - log_total[:, :, None]), 0.0)
            weight_grad = jnp.einsum(
                "qhd,khd->hqk", d_attended, values_block, preferred_element_type=jnp.float32
            )
            score_grad = (weights * (weight_grad - delta[:, :, None]) * SCALE).astype(jnp.bfloat16)
            return previous + jnp.einsum(
                "hqk,khd->qhd", score_grad, keys_block, preferred_element_type=jnp.float32
            )

        return lax.cond(jnp.min(block_frames) > top_frame, keep_same, query_accumulate, running)

    query_grad = lax.fori_loop(0, piece_rows // query_block_rows, query_advance, grad_start)
    stats_lse, stats_delta = (
        lax.all_gather(log_total.T, "blk", axis=0, tiled=True),
        lax.all_gather(delta.T, "blk", axis=0, tiled=True),
    )
    key_first_row = jnp.int32(0)
    queries_piece = lax.all_gather(query, "blk", axis=0, tiled=True)
    grads_piece = lax.all_gather(d_attended, "blk", axis=0, tiled=True)
    piece_rows = queries_piece.shape[0]
    key_block_rows = block_size(piece_rows, rows_here)

    def key_advance(turn_index, running):
        offset = turn_index * key_block_rows
        query_block = lax.dynamic_slice_in_dim(queries_piece, offset, key_block_rows)
        grad_block = lax.dynamic_slice_in_dim(grads_piece, offset, key_block_rows)
        lse_block = lax.dynamic_slice_in_dim(stats_lse, key_first_row + offset, key_block_rows).T
        delta_block = lax.dynamic_slice_in_dim(
            stats_delta, key_first_row + offset, key_block_rows
        ).T
        block_frames = frames_of(group_map, key_first_row + offset, key_block_rows)

        def key_accumulate(previous):
            key_total, value_total = previous
            scores = (
                jnp.einsum(
                    "qhd,khd->hqk", query_block, key_part, preferred_element_type=jnp.float32
                )
                * SCALE
            )
            allowed = token_frames[None, None, :] <= block_frames[None, :, None]
            weights = jnp.where(allowed, jnp.exp(scores - lse_block[:, :, None]), 0.0)
            value_total = value_total + jnp.einsum(
                "hqk,qhd->khd",
                weights.astype(jnp.bfloat16),
                grad_block,
                preferred_element_type=jnp.float32,
            )
            weight_grad = jnp.einsum(
                "qhd,khd->hqk", grad_block, value_part, preferred_element_type=jnp.float32
            )
            score_grad = (weights * (weight_grad - delta_block[:, :, None]) * SCALE).astype(
                jnp.bfloat16
            )
            key_total = key_total + jnp.einsum(
                "hqk,qhd->khd", score_grad, query_block, preferred_element_type=jnp.float32
            )
            return (key_total, value_total)

        return lax.cond(jnp.max(block_frames) < own_lowest, keep_same, key_accumulate, running)

    key_grad, value_grad = lax.fori_loop(
        0, piece_rows // key_block_rows, key_advance, (grad_start, grad_start)
    )
    query_low = lax.optimization_barrier(query_grad.astype(jnp.bfloat16)).astype(jnp.float32)
    key_low = lax.optimization_barrier(key_grad.astype(jnp.bfloat16)).astype(jnp.float32)
    query_back = rotate(query_low, angle_list, -1.0).reshape(rows_here, D)
    key_back = rotate(key_low, angle_list, -1.0).reshape(rows_here, D)
    d_qkv = jnp.concatenate(
        [query_back, key_back, value_grad.reshape(rows_here, D)], axis=1
    ).astype(jnp.bfloat16)
    qkv_part = jnp.einsum("rc,rk->ck", first_in, d_qkv, preferred_element_type=jnp.float32)
    d_first = jnp.einsum(
        "rk,ck->rc", d_qkv, qkv_weight, preferred_element_type=jnp.float32
    ).reshape(2, PATCHES, D)
    d_shift_one = jnp.sum(d_first, axis=1)
    d_scale_one = jnp.sum(d_first * normed_one, axis=1)
    tokens_grad = (
        d_middle + norm_backward(d_first * (1.0 + scale_one), normed_one, inverse_one)
    ).astype(jnp.bfloat16)[None]
    d_mod = jnp.concatenate(
        [d_shift_one, d_scale_one, d_gate_one, d_shift_two, d_scale_two, d_gate_two], axis=1
    )
    bias_part = jnp.sum(d_mod, axis=0)
    d_mod_low = d_mod.astype(jnp.bfloat16)
    d_activated = jnp.einsum("sk,ck->sc", d_mod_low, mod_weight, preferred_element_type=jnp.float32)
    unused_silu, silu_pull = jax.vjp(jax.nn.silu, embedded)
    d_embedded = silu_pull(d_activated)[0]
    table_part = jnp.einsum(
        "sl,sc->cl", level_hot.astype(jnp.float32), d_embedded, precision=lax.Precision.HIGHEST
    )
    activated_all, d_mod_all = (
        lax.all_gather(activated, ("blk", "clip"), axis=0, tiled=True),
        lax.all_gather(d_mod_low, ("blk", "clip"), axis=0, tiled=True),
    )
    share_rows = D // lax.axis_size(("blk", "clip"))
    my_columns = lax.dynamic_slice_in_dim(
        activated_all, lax.axis_index(("blk", "clip")) * share_rows, share_rows, 1
    )
    modw_share = jnp.einsum("sc,sk->ck", my_columns, d_mod_all, preferred_element_type=jnp.float32)
    summed = (
        lax.psum_scatter(table_part, ("blk", "clip"), scatter_dimension=0, tiled=True),
        lax.psum_scatter(bias_part, ("blk", "clip"), scatter_dimension=0, tiled=True),
        lax.psum_scatter(qkv_part, ("blk", "clip"), scatter_dimension=0, tiled=True),
        lax.psum_scatter(outw_part, ("blk", "clip"), scatter_dimension=0, tiled=True),
        lax.psum_scatter(upper_part, ("blk", "clip"), scatter_dimension=0, tiled=True),
        lax.psum_scatter(lower_part, ("blk", "clip"), scatter_dimension=0, tiled=True),
    )
    return (
        layer_out,
        tokens_grad,
        summed[0].T,
        modw_share,
        summed[1],
        summed[2],
        summed[3],
        summed[4],
        summed[5],
    )


LANES = 128
FF = 4096
AXES = ("blk", "clip")
EXP_SCALE = SCALE * 1.4426950408889634
VMEM_LIMIT = 56 * 1024 * 1024
NT = (((1,), (1,)), ((), ()))
NN = (((1,), (0,)), ((), ()))


def cost(microseconds):
    return pl.CostEstimate(
        flops=int(microseconds * 1e9), bytes_accessed=int(microseconds * 3e6), transcendentals=0
    )


ANYWHERE = pl.BlockSpec(memory_space=pl.ANY)


def full_block(shape):
    return pl.BlockSpec(shape, lambda *ids: (0,) * len(shape))


def rope_tables(frame_count):
    lane = jnp.arange(LANES, dtype=jnp.int32) % HEAD
    pieces = []
    for comp_width in (16, 24, 24):
        half_width = comp_width // 2
        frequency = ROPE_BASE ** (-2.0 * jnp.arange(half_width, dtype=jnp.float32) / comp_width)
        pieces += [frequency, frequency]
    frequency = jnp.tile(jnp.concatenate(pieces), LANES // HEAD)[None, :]
    first = (lane < 8) | ((lane >= 16) & (lane < 28)) | ((lane >= 40) & (lane < 52))
    sign = jnp.where(first, -1.0, 1.0)[None, :]
    in_frame = (lane < 16)[None, :]
    in_row = (lane < 40)[None, :]
    frame_angle = jnp.arange(frame_count, dtype=jnp.float32)[:, None] * frequency
    patch = jnp.arange(PATCHES, dtype=jnp.int32)[:, None]
    place = jnp.where(in_row, patch // GRID_W, patch % GRID_W).astype(jnp.float32)
    place_angle = place * frequency
    return (
        jnp.where(in_frame, jnp.cos(frame_angle), 0.0),
        jnp.where(in_frame, sign * jnp.sin(frame_angle), 0.0),
        jnp.where(in_frame, 0.0, jnp.cos(place_angle)),
        jnp.where(in_frame, 0.0, sign * jnp.sin(place_angle)),
    )


def partner_lanes(values):
    lane = lax.broadcasted_iota(jnp.int32, values.shape, 1) % HEAD
    ahead_eight = pltpu.roll(values, LANES - 8, 1)
    behind_eight = pltpu.roll(values, 8, 1)
    ahead_twelve = pltpu.roll(values, LANES - 12, 1)
    behind_twelve = pltpu.roll(values, 12, 1)
    ahead = ((lane >= 16) & (lane < 28)) | ((lane >= 40) & (lane < 52))
    return jnp.where(
        lane < 8,
        ahead_eight,
        jnp.where(lane < 16, behind_eight, jnp.where(ahead, ahead_twelve, behind_twelve)),
    )


def qkv_kernel(
    frames_ref,
    tokens_ref,
    mod_ref,
    qw_ref,
    kw_ref,
    vw_ref,
    fcos_ref,
    fsin_ref,
    pcos_ref,
    psin_ref,
    out_ref,
    first_ref,
):
    @pl.when(pl.program_id(0) == 0)
    def _():
        for slot in range(2):
            rows = slice(slot * PATCHES, (slot + 1) * PATCHES)
            normed, unused = normalize(tokens_ref[rows, :].astype(jnp.float32))
            shift = mod_ref[slot : slot + 1, :D]
            scale = mod_ref[slot : slot + 1, D : 2 * D]
            first_ref[rows, :] = (normed * (1.0 + scale) + shift).astype(jnp.bfloat16)

    first = first_ref[...]
    linear = [
        lax.dot_general(first, ref[...], NN, preferred_element_type=jnp.float32)
        for ref in (qw_ref, kw_ref, vw_ref)
    ]
    for slot in range(2):
        rows = slice(slot * PATCHES, (slot + 1) * PATCHES)
        frame = frames_ref[slot]
        cosine = pcos_ref[...] + fcos_ref[pl.ds(frame, 1), :]
        sine = psin_ref[...] + fsin_ref[pl.ds(frame, 1), :]
        for part in range(2):
            values = linear[part][rows, :]
            turned = values * cosine + partner_lanes(values) * sine
            out_ref[0, rows, part * LANES : (part + 1) * LANES] = turned.astype(jnp.bfloat16)
        out_ref[0, rows, 2 * LANES :] = linear[2][rows, :].astype(jnp.bfloat16)


def project_qkv(my_frames, tokens_here, mod_first, qkv_weight, tables):
    groups = D // LANES
    rows = tokens_here.shape[0]
    weight_specs = [
        pl.BlockSpec((D, LANES), lambda g, frames, part=part: (0, part * groups + g))
        for part in range(3)
    ]
    return pl.pallas_call(
        qkv_kernel,
        grid_spec=pltpu.PrefetchScalarGridSpec(
            num_scalar_prefetch=1,
            grid=(groups,),
            in_specs=[full_block((rows, D)), full_block(mod_first.shape)]
            + weight_specs
            + [full_block(table.shape) for table in tables],
            out_specs=[
                pl.BlockSpec((1, rows, 3 * LANES), lambda g, frames: (g, 0, 0)),
                full_block((rows, D)),
            ],
        ),
        out_shape=[
            jax.ShapeDtypeStruct((groups, rows, 3 * LANES), jnp.bfloat16),
            jax.ShapeDtypeStruct((rows, D), jnp.bfloat16),
        ],
        compiler_params=pltpu.CompilerParams(
            vmem_limit_bytes=VMEM_LIMIT, dimension_semantics=("arbitrary",)
        ),
        cost_estimate=cost(8),
        name="project_qkv",
    )(my_frames, tokens_here, mod_first, qkv_weight, qkv_weight, qkv_weight, *tables)


def head_stack(values):
    lane = lax.broadcasted_iota(jnp.int32, values.shape, 1)
    zero = jnp.zeros_like(values)
    return jnp.concatenate(
        [jnp.where(lane < HEAD, values, zero), jnp.where(lane < HEAD, zero, values)], axis=0
    )


def hidden_keys(shape):
    key_row = lax.broadcasted_iota(jnp.int32, shape, 0)
    query_column = lax.broadcasted_iota(jnp.int32, shape, 1) % (2 * PATCHES)
    return (key_row >= PATCHES) & (query_column < PATCHES)


def own_heads(values):
    rows = 2 * PATCHES
    return jnp.concatenate([values[:HEAD, :rows], values[HEAD:LANES, rows:]], axis=0)


def by_frame(frames_ref, source_ref, target_refs):
    for slot in range(source_ref.shape[0] // PATCHES):
        rows = pl.ds(pl.multiple_of(frames_ref[slot] * PATCHES, PATCHES), PATCHES)
        for part, target in enumerate(target_refs):
            target[rows, :] = source_ref[
                slot * PATCHES : (slot + 1) * PATCHES, part * LANES : (part + 1) * LANES
            ]


def attend_kernel(
    frames_ref,
    slots_ref,
    qkv_ref,
    first_ref,
    after_ref,
    att_ref,
    ot_ref,
    lse_ref,
    copy_ref,
    q_ref,
    k_ref,
    v_ref,
    vt_ref,
):
    token_count = qkv_ref.shape[0]
    copy_ref[...] = first_ref[...]
    by_frame(frames_ref, qkv_ref, (q_ref, k_ref, v_ref))
    vt_ref[:LANES, :] = v_ref[...].T
    vt_ref[LANES:, :] = jnp.ones((vt_ref.shape[0] - LANES, token_count), jnp.bfloat16)
    step = 2 * PATCHES
    for turn in range(token_count // step):
        here = slice(turn * step, (turn + 1) * step)
        queries = head_stack(q_ref[here, :])
        ranges = [here] if turn == 0 else [slice(0, turn * step), here]
        raw = [
            lax.dot_general(k_ref[keys, :], queries, NT, preferred_element_type=jnp.float32)
            for keys in ranges
        ]
        raw[-1] = jnp.where(hidden_keys(raw[-1].shape), NEG_LARGE, raw[-1])
        top = jnp.max(raw[-1], axis=0, keepdims=True)
        for part in raw[:-1]:
            top = jnp.maximum(top, jnp.max(part, axis=0, keepdims=True))
        top = top * EXP_SCALE
        summed = None
        for keys, part in zip(ranges, raw):
            weights = jnp.exp2(part * EXP_SCALE - top).astype(jnp.bfloat16)
            update = lax.dot_general(
                vt_ref[:, keys], weights, NN, preferred_element_type=jnp.float32
            )
            summed = update if summed is None else summed + update
        totals = summed[LANES : LANES + 1, :]
        lse_ref[turn : turn + 1, :] = top + jnp.log2(totals)
        out = own_heads(summed[:LANES, :] / totals)
        ot_ref[:, here] = out
        rounded = out.T.astype(jnp.bfloat16)
        for half in range(2):
            slot = slots_ref[2 * turn + half]
            rows = pl.ds(pl.multiple_of(slot % 2 * PATCHES, PATCHES), PATCHES)
            att_ref[slot // 2, rows, :] = rounded[half * PATCHES : (half + 1) * PATCHES, :]


def attend(frames, slots, qkv, first_in, after):
    token_count = qkv.shape[0]
    turns = token_count // (2 * PATCHES)
    return pl.pallas_call(
        attend_kernel,
        in_specs=[
            pl.BlockSpec(memory_space=pltpu.SMEM),
            pl.BlockSpec(memory_space=pltpu.SMEM),
            pl.BlockSpec(memory_space=pltpu.VMEM),
            pl.BlockSpec(memory_space=pltpu.VMEM),
            ANYWHERE,
        ],
        out_specs=[pl.BlockSpec(memory_space=pltpu.VMEM)] * 4,
        out_shape=[
            jax.ShapeDtypeStruct((turns, 2 * PATCHES, LANES), jnp.bfloat16),
            jax.ShapeDtypeStruct((LANES, token_count), jnp.float32),
            jax.ShapeDtypeStruct((turns, 4 * PATCHES), jnp.float32),
            jax.ShapeDtypeStruct(first_in.shape, jnp.bfloat16),
        ],
        scratch_shapes=[pltpu.VMEM((token_count, LANES), jnp.bfloat16)] * 3
        + [pltpu.VMEM((LANES + 16, token_count), jnp.bfloat16)],
        compiler_params=pltpu.CompilerParams(vmem_limit_bytes=VMEM_LIMIT),
        cost_estimate=cost(10),
        name="attend",
    )(frames, slots, qkv, first_in, after)


def attend_back_kernel(
    frames_ref,
    slots_ref,
    qkv_ref,
    grad_ref,
    ot_ref,
    lse_ref,
    fcos_ref,
    fsin_ref,
    pcos_ref,
    psin_ref,
    after_ref,
    out_ref,
    q_ref,
    k_ref,
    v_ref,
    d_ref,
    kt_ref,
    dk_ref,
    dv_ref,
):
    token_count = qkv_ref.shape[0]
    by_frame(frames_ref, qkv_ref, (q_ref, k_ref, v_ref))
    by_frame(frames_ref, grad_ref, (d_ref,))
    kt_ref[...] = k_ref[...].T
    step = 2 * PATCHES

    def put(frame, part, values):
        slot = slots_ref[frame]
        rows = pl.ds(pl.multiple_of(slot % 2 * PATCHES, PATCHES), PATCHES)
        out_ref[slot // 2, rows, part * LANES : (part + 1) * LANES] = values

    def turn_back(frame, values):
        values = values.astype(jnp.bfloat16).astype(jnp.float32)
        cosine = pcos_ref[...] + fcos_ref[frame : frame + 1, :]
        sine = psin_ref[...] + fsin_ref[frame : frame + 1, :]
        return (values * cosine - partner_lanes(values) * sine).astype(jnp.bfloat16)

    for turn in range(token_count // step):
        here = slice(turn * step, (turn + 1) * step)
        queries = head_stack(q_ref[here, :])
        grads_here = d_ref[here, :]
        grads = head_stack(grads_here)
        product = grads_here.astype(jnp.float32).T * ot_ref[:, here]
        delta = jnp.concatenate(
            [
                jnp.sum(product[:HEAD, :], axis=0, keepdims=True),
                jnp.sum(product[HEAD:, :], axis=0, keepdims=True),
            ],
            axis=1,
        )
        lse = lse_ref[turn : turn + 1, :]
        ranges = [here] if turn == 0 else [here, slice(0, turn * step)]
        total = None
        for keys in ranges:
            raw = lax.dot_general(
                k_ref[keys, :], queries, NT, preferred_element_type=jnp.float32
            )
            weights = jnp.exp2(raw * EXP_SCALE - lse)
            if keys is here:
                weights = jnp.where(hidden_keys(weights.shape), 0.0, weights)
            weight_grad = lax.dot_general(
                v_ref[keys, :], grads, NT, preferred_element_type=jnp.float32
            )
            score_grad = (weights * (weight_grad - delta)).astype(jnp.bfloat16)
            value_part = lax.dot_general(
                weights.astype(jnp.bfloat16), grads, NN, preferred_element_type=jnp.float32
            )
            key_part = lax.dot_general(
                score_grad, queries, NN, preferred_element_type=jnp.float32
            )
            if keys is here:
                dv_ref[keys, :] = value_part
                dk_ref[keys, :] = key_part
            else:
                dv_ref[keys, :] += value_part
                dk_ref[keys, :] += key_part
            update = lax.dot_general(
                kt_ref[:, keys], score_grad, NN, preferred_element_type=jnp.float32
            )
            total = update if total is None else total + update
        query_grad = own_heads(total).T * SCALE
        for half in range(2):
            put(
                2 * turn + half,
                0,
                turn_back(2 * turn + half, query_grad[half * PATCHES : (half + 1) * PATCHES, :]),
            )
    for frame in range(token_count // PATCHES):
        rows = slice(frame * PATCHES, (frame + 1) * PATCHES)
        put(frame, 1, turn_back(frame, dk_ref[rows, :] * SCALE))
        put(frame, 2, dv_ref[rows, :].astype(jnp.bfloat16))


def attend_back(frames, slots, qkv, grads, ot, lse, tables, after):
    token_count = qkv.shape[0]
    smem = pl.BlockSpec(memory_space=pltpu.SMEM)
    vmem = pl.BlockSpec(memory_space=pltpu.VMEM)
    return pl.pallas_call(
        attend_back_kernel,
        in_specs=[smem, smem] + [vmem] * 8 + [ANYWHERE],
        out_specs=vmem,
        out_shape=jax.ShapeDtypeStruct(
            (token_count // (2 * PATCHES), 2 * PATCHES, 3 * LANES), jnp.bfloat16
        ),
        scratch_shapes=[pltpu.VMEM((token_count, LANES), jnp.bfloat16)] * 4
        + [pltpu.VMEM((LANES, token_count), jnp.bfloat16)]
        + [pltpu.VMEM((token_count, LANES), jnp.float32)] * 2,
        compiler_params=pltpu.CompilerParams(vmem_limit_bytes=VMEM_LIMIT),
        cost_estimate=cost(15),
        name="attend_back",
    )(frames, slots, qkv, grads, ot, lse, *tables, after)


def swap(values, bit):
    count = lax.axis_size(AXES)
    return lax.ppermute(values, AXES, [(index, index ^ bit) for index in range(count)])


def gather_pairs(values):
    bit = lax.axis_size(AXES) // 2
    while bit:
        values = jnp.concatenate([values, swap(values, bit)], axis=0)
        bit //= 2
    return values


HIDDEN_AT, UP_AT, SECOND_AT, MLP_AT, ATTENDED_AT, ATTN_AT, ACTS = (
    0,
    FF,
    2 * FF,
    2 * FF + D,
    2 * FF + 2 * D,
    2 * FF + 3 * D,
    2 * FF + 4 * D,
)
FF_TILE = 512


def middle_kernel(
    att_ref,
    tokens_ref,
    cot_ref,
    mod_ref,
    ow_ref,
    up_ref,
    down_ref,
    layer_ref,
    acts_ref,
    datt_ref,
    dmid_ref,
    dmod_ref,
    attn_ref,
    mid_ref,
    mlp_ref,
    dsec_ref,
):
    step = pl.program_id(0)
    slot_rows = [slice(slot * PATCHES, (slot + 1) * PATCHES) for slot in range(2)]

    def member(slot, which):
        return mod_ref[slot : slot + 1, which * D : (which + 1) * D]

    @pl.when(step == 0)
    def _():
        for group in range(D // LANES):
            acts_ref[:, ATTENDED_AT + group * LANES : ATTENDED_AT + (group + 1) * LANES] = att_ref[
                group
            ]
        attn_ref[...] = lax.dot_general(
            acts_ref[:, ATTENDED_AT : ATTENDED_AT + D],
            ow_ref[...],
            NN,
            preferred_element_type=jnp.float32,
        )
        for slot, rows in enumerate(slot_rows):
            middle = tokens_ref[rows, :].astype(jnp.float32) + member(slot, 2) * attn_ref[rows, :]
            mid_ref[rows, :] = middle
            normed, unused = normalize(middle)
            acts_ref[rows, SECOND_AT : SECOND_AT + D] = (
                normed * (1.0 + member(slot, 4)) + member(slot, 3)
            ).astype(jnp.bfloat16)
            acts_ref[rows, MLP_AT : MLP_AT + D] = (
                cot_ref[rows, :].astype(jnp.float32) * member(slot, 5)
            ).astype(jnp.bfloat16)
        mlp_ref[...] = jnp.zeros_like(mlp_ref)
        dsec_ref[...] = jnp.zeros_like(dsec_ref)

    up_lin = lax.dot_general(
        acts_ref[:, SECOND_AT : SECOND_AT + D],
        up_ref[...],
        NN,
        preferred_element_type=jnp.float32,
    )
    below = 0.5 + 0.5 * lax.erf(up_lin * 0.7071067811865476)
    density = jnp.exp(up_lin * up_lin * -0.5) * 0.3989422804014327
    hidden = (up_lin * below).astype(jnp.bfloat16)
    d_hidden = lax.dot_general(
        acts_ref[:, MLP_AT : MLP_AT + D], down_ref[...], NT, preferred_element_type=jnp.float32
    )
    d_up = (d_hidden * (below + up_lin * density)).astype(jnp.bfloat16)
    acts_ref[:, pl.ds(pl.multiple_of(HIDDEN_AT + step * FF_TILE, FF_TILE), FF_TILE)] = hidden
    acts_ref[:, pl.ds(pl.multiple_of(UP_AT + step * FF_TILE, FF_TILE), FF_TILE)] = d_up
    mlp_ref[...] += lax.dot_general(
        hidden, down_ref[...], NN, preferred_element_type=jnp.float32
    )
    dsec_ref[...] += lax.dot_general(d_up, up_ref[...], NT, preferred_element_type=jnp.float32)

    @pl.when(step == pl.num_programs(0) - 1)
    def _():
        for slot, rows in enumerate(slot_rows):
            middle = mid_ref[rows, :]
            mlp_out = mlp_ref[rows, :]
            cotangent = cot_ref[rows, :].astype(jnp.float32)
            layer_ref[rows, :] = (middle + member(slot, 5) * mlp_out).astype(jnp.bfloat16)
            normed, inverse = normalize(middle)
            d_second = dsec_ref[rows, :]
            d_middle = cotangent + norm_backward(
                d_second * (1.0 + member(slot, 4)), normed, inverse
            )
            dmid_ref[rows, :] = d_middle
            acts_ref[rows, ATTN_AT : ATTN_AT + D] = (d_middle * member(slot, 2)).astype(
                jnp.bfloat16
            )
            for place, values in enumerate(
                (d_middle * attn_ref[rows, :], d_second, d_second * normed, cotangent * mlp_out)
            ):
                dmod_ref[slot : slot + 1, place * D : (place + 1) * D] = jnp.sum(
                    values, axis=0, keepdims=True
                )
        d_attended = lax.dot_general(
            acts_ref[:, ATTN_AT : ATTN_AT + D],
            ow_ref[...],
            NT,
            preferred_element_type=jnp.float32,
        ).astype(jnp.bfloat16)
        for group in range(D // LANES):
            datt_ref[group] = d_attended[:, group * LANES : (group + 1) * LANES]


def middle_block(att, tokens_here, cot_here, modulation, out_weight, fc1_weight, fc2_weight):
    rows = tokens_here.shape[0]
    return pl.pallas_call(
        middle_kernel,
        grid=(FF // FF_TILE,),
        in_specs=[
            full_block(att.shape),
            full_block((rows, D)),
            full_block((rows, D)),
            full_block(modulation.shape),
            full_block((D, D)),
            pl.BlockSpec((D, FF_TILE), lambda f: (0, f)),
            pl.BlockSpec((FF_TILE, D), lambda f: (f, 0)),
        ],
        out_specs=[
            full_block((rows, D)),
            full_block((rows, ACTS)),
            full_block(att.shape),
            full_block((rows, D)),
            full_block((2, 4 * D)),
        ],
        out_shape=[
            jax.ShapeDtypeStruct((rows, D), jnp.bfloat16),
            jax.ShapeDtypeStruct((rows, ACTS), jnp.bfloat16),
            jax.ShapeDtypeStruct(att.shape, jnp.bfloat16),
            jax.ShapeDtypeStruct((rows, D), jnp.float32),
            jax.ShapeDtypeStruct((2, 4 * D), jnp.float32),
        ],
        scratch_shapes=[pltpu.VMEM((rows, D), jnp.float32)] * 4,
        compiler_params=pltpu.CompilerParams(
            vmem_limit_bytes=VMEM_LIMIT, dimension_semantics=("arbitrary",)
        ),
        cost_estimate=cost(21),
        name="middle_block",
    )(att, tokens_here, cot_here, modulation, out_weight, fc1_weight, fc2_weight)


CHIPS = 16
TILE = 256
SHARE_ROWS = (FF + 4 * D + D) // TILE * D // CHIPS // 4


def weight_kernel(
    bits_ref, mine_ref, theirs_ref, keep_a, send_a, keep_b, send_b, left1_ref, left2_ref, left3_ref
):
    core, xbit, ybit = bits_ref[0], bits_ref[1], bits_ref[2]
    rows = mine_ref.shape[0]
    small = D // CHIPS // 2
    for place, ref in enumerate((mine_ref, theirs_ref)):
        columns = slice(place * rows, (place + 1) * rows)
        for source, target in ((SECOND_AT, left1_ref), (ATTENDED_AT, left3_ref)):
            turned = ref[:, source : source + D].T.reshape(CHIPS, 2, small, rows)
            target[:, columns] = jnp.where(core == 0, turned[:, 0], turned[:, 1]).reshape(
                D // 2, rows
            )
        for chip in range(CHIPS):
            source = pl.multiple_of(HIDDEN_AT + (2 * chip + core) * LANES, LANES)
            left2_ref[chip * LANES : (chip + 1) * LANES, columns] = ref[:, pl.ds(source, LANES)].T

    jobs = []
    at = [0, 0]
    for left, right_at, width, height in (
        (left1_ref, UP_AT, FF, small),
        (left2_ref, MLP_AT, D, LANES),
        (left3_ref, ATTN_AT, D, small),
    ):
        tiles = width // TILE
        for tile in range(tiles):
            second = tile >= tiles // 2
            jobs.append((left, right_at + tile * TILE, height, second, at[second]))
            at[second] += height
    for left, source, height, second, place in jobs:
        right = jnp.concatenate(
            [mine_ref[:, source : source + TILE], theirs_ref[:, source : source + TILE]], axis=0
        )
        part = lax.dot_general(
            left[...], right, NN, preferred_element_type=jnp.float32
        ).astype(jnp.bfloat16)
        out_rows = slice(place, place + height)
        if second:
            part = part.reshape(CHIPS // 4, 2, 2, height, TILE)
            low, high, chosen = part[:, 0], part[:, 1], ybit
            keep_b[:, :, out_rows, :] = jnp.where(chosen == 0, low, high)
            send_b[:, :, out_rows, :] = jnp.where(chosen == 0, high, low)
        else:
            part = part.reshape(CHIPS // 2, 2, height, TILE)
            low, high, chosen = part[:, 0], part[:, 1], xbit
            keep_a[:, out_rows, :] = jnp.where(chosen == 0, low, high)
            send_a[:, out_rows, :] = jnp.where(chosen == 0, high, low)


def weight_parts(bits, mine, theirs):
    rows = mine.shape[0]
    vmem = pl.BlockSpec(memory_space=pltpu.VMEM)
    first = jax.ShapeDtypeStruct((CHIPS // 2, SHARE_ROWS, TILE), jnp.bfloat16)
    second = jax.ShapeDtypeStruct((CHIPS // 4, 2, SHARE_ROWS, TILE), jnp.bfloat16)
    return pl.pallas_call(
        weight_kernel,
        in_specs=[pl.BlockSpec(memory_space=pltpu.SMEM), vmem, vmem],
        out_specs=[vmem] * 4,
        out_shape=[first, first, second, second],
        scratch_shapes=[
            pltpu.VMEM((D // 2, 2 * rows), jnp.bfloat16),
            pltpu.VMEM((FF // 2, 2 * rows), jnp.bfloat16),
            pltpu.VMEM((D // 2, 2 * rows), jnp.bfloat16),
        ],
        compiler_params=pltpu.CompilerParams(vmem_limit_bytes=VMEM_LIMIT),
        cost_estimate=cost(13),
        name="weight_parts",
    )(bits, mine, theirs)


def first_back_kernel(
    dqkv_ref,
    tokens_ref,
    mod_ref,
    dmid_ref,
    qw_ref,
    kw_ref,
    vw_ref,
    after_ref,
    grad_ref,
    late_ref,
    total_ref,
):
    step = pl.program_id(0)
    weights = jnp.concatenate([qw_ref[...], kw_ref[...], vw_ref[...]], axis=1)
    update = lax.dot_general(dqkv_ref[0], weights, NT, preferred_element_type=jnp.float32)

    @pl.when(step == 0)
    def _():
        total_ref[...] = update

    @pl.when(step > 0)
    def _():
        total_ref[...] += update

    @pl.when(step == pl.num_programs(0) - 1)
    def _():
        for slot in range(2):
            rows = slice(slot * PATCHES, (slot + 1) * PATCHES)
            normed, inverse = normalize(tokens_ref[rows, :].astype(jnp.float32))
            d_first = total_ref[rows, :]
            scale = mod_ref[slot : slot + 1, D : 2 * D]
            grad_ref[rows, :] = (
                dmid_ref[rows, :] + norm_backward(d_first * (1.0 + scale), normed, inverse)
            ).astype(jnp.bfloat16)
            late_ref[slot : slot + 1, :D] = jnp.sum(d_first, axis=0, keepdims=True)
            late_ref[slot : slot + 1, D:] = jnp.sum(d_first * normed, axis=0, keepdims=True)


def first_back(d_qkv, tokens_here, modulation, d_middle, qkv_weight, after):
    groups, rows, width = d_qkv.shape
    weight_specs = [
        pl.BlockSpec((D, LANES), lambda g, part=part: (0, part * groups + g)) for part in range(3)
    ]
    return pl.pallas_call(
        first_back_kernel,
        grid=(groups,),
        in_specs=[
            pl.BlockSpec((1, rows, width), lambda g: (g, 0, 0)),
            full_block((rows, D)),
            full_block(modulation.shape),
            full_block((rows, D)),
        ]
        + weight_specs
        + [ANYWHERE],
        out_specs=[full_block((rows, D)), full_block((2, 2 * D))],
        out_shape=[
            jax.ShapeDtypeStruct((rows, D), jnp.bfloat16),
            jax.ShapeDtypeStruct((2, 2 * D), jnp.float32),
        ],
        scratch_shapes=[pltpu.VMEM((rows, D), jnp.float32)],
        compiler_params=pltpu.CompilerParams(
            vmem_limit_bytes=VMEM_LIMIT, dimension_semantics=("arbitrary",)
        ),
        cost_estimate=cost(9),
        name="first_back",
    )(d_qkv, tokens_here, modulation, d_middle, qkv_weight, qkv_weight, qkv_weight, after)


def add_split(keep, got, axis, bit):
    def pick(which):
        return (
            lax.dynamic_index_in_dim(keep, which, axis, keepdims=False).astype(jnp.float32)
            + lax.dynamic_index_in_dim(got, which, axis, keepdims=False).astype(jnp.float32)
        ).astype(jnp.bfloat16)

    return pick(bit), pick(1 - bit)


def qkv_part_kernel(core_ref, first_ref, grad_ref, after_ref, keep_ref, send_ref, total_ref):
    step = pl.program_id(0)
    update = lax.dot_general(
        first_ref[...], grad_ref[...], (((0,), (0,)), ((), ())), preferred_element_type=jnp.float32
    )

    @pl.when(step == 0)
    def _():
        total_ref[...] = update

    @pl.when(step > 0)
    def _():
        total_ref[...] += update

    @pl.when(step == pl.num_programs(0) - 1)
    def _():
        groups, clip_pairs, share, width = keep_ref.shape
        split = total_ref[...].astype(jnp.bfloat16).reshape(groups, clip_pairs, 2, share, width)
        low, high = split[:, :, 0], split[:, :, 1]
        keep_ref[...] = jnp.where(core_ref[0] == 0, low, high)
        send_ref[...] = jnp.where(core_ref[0] == 0, high, low)


def qkv_parts(core, first_all, d_heads, share, after):
    rows, width = d_heads.shape
    tile = 512
    shape = (D // LANES, 2, share, width)
    return pl.pallas_call(
        qkv_part_kernel,
        grid_spec=pltpu.PrefetchScalarGridSpec(
            num_scalar_prefetch=1,
            grid=(rows // tile,),
            in_specs=[
                pl.BlockSpec((tile, D), lambda i, core: (i, 0)),
                pl.BlockSpec((tile, width), lambda i, core: (i, 0)),
                ANYWHERE,
            ],
            out_specs=[full_block(shape)] * 2,
            scratch_shapes=[pltpu.VMEM((D, width), jnp.float32)],
        ),
        out_shape=[jax.ShapeDtypeStruct(shape, jnp.bfloat16)] * 2,
        compiler_params=pltpu.CompilerParams(
            vmem_limit_bytes=VMEM_LIMIT, dimension_semantics=("arbitrary",)
        ),
        cost_estimate=cost(5),
        name="qkv_parts",
    )(core, first_all, d_heads, after)


def fold_kernel(bits_ref, keep_a, got_a, keep_b, got_b, after_ref, *out_refs):
    for place, (keep, got) in enumerate(((keep_a, got_a), (keep_b, got_b))):
        low, high = (
            (
                keep[0, half].astype(jnp.float32) + got[0, half].astype(jnp.float32)
            ).astype(jnp.bfloat16)
            for half in range(2)
        )
        kept, sent = out_refs[2 * place : 2 * place + 2]
        kept[0] = jnp.where(bits_ref[place] == 0, low, high)
        sent[0] = jnp.where(bits_ref[place] == 0, high, low)


def fold(bits, keep_a, got_a, keep_b, got_b, after):
    count, unused, rows, columns = keep_a.shape
    parts = 1 if count > 1 else 3
    in_block = pl.BlockSpec((1, 2, rows // parts, columns), lambda i, j, bits: (i, 0, j, 0))
    out_block = pl.BlockSpec((1, rows // parts, columns), lambda i, j, bits: (i, j, 0))
    out = jax.ShapeDtypeStruct((count, rows, columns), jnp.bfloat16)
    return pl.pallas_call(
        fold_kernel,
        grid_spec=pltpu.PrefetchScalarGridSpec(
            num_scalar_prefetch=1,
            grid=(count, parts),
            in_specs=[in_block] * 4 + [ANYWHERE],
            out_specs=[out_block] * 4,
        ),
        out_shape=[out] * 4,
        compiler_params=pltpu.CompilerParams(
            vmem_limit_bytes=VMEM_LIMIT, dimension_semantics=("arbitrary", "arbitrary")
        ),
        cost_estimate=cost(1 + count),
        name="fold",
    )(jnp.stack(bits), keep_a, got_a, keep_b, got_b, after)


def finish_kernel(keep_a, got_a, keep_b, got_b, upper_ref, lower_ref, outw_ref):
    for place, (keep, got) in enumerate(((keep_a, got_a), (keep_b, got_b))):
        row = 0
        for target in (upper_ref, lower_ref, outw_ref):
            height, width = target.shape
            tiles = width // 2 // TILE
            for tile in range(tiles):
                column = (place * tiles + tile) * TILE
                target[:, column : column + TILE] = keep[row : row + height, :].astype(
                    jnp.float32
                ) + got[row : row + height, :].astype(jnp.float32)
                row += height


def finish(share, keep_a, got_a, keep_b, got_b):
    vmem = pl.BlockSpec(memory_space=pltpu.VMEM)
    return pl.pallas_call(
        finish_kernel,
        in_specs=[vmem] * 4,
        out_specs=[vmem] * 3,
        out_shape=[
            jax.ShapeDtypeStruct((share, FF), jnp.float32),
            jax.ShapeDtypeStruct((FF * share // D, D), jnp.float32),
            jax.ShapeDtypeStruct((share, D), jnp.float32),
        ],
        compiler_params=pltpu.CompilerParams(vmem_limit_bytes=VMEM_LIMIT),
        cost_estimate=cost(2),
        name="finish",
    )(keep_a, got_a, keep_b, got_b)


def local_heads(
    tokens,
    noise_levels,
    group_map,
    noise_table,
    mod_weight,
    mod_bias,
    qkv_weight,
    out_weight,
    fc1_weight,
    fc2_weight,
    out_cotangent,
):
    rows_here = 2 * PATCHES
    frame_count = group_map.shape[0]
    groups = D // LANES
    device_count = lax.axis_size(AXES)
    index = lax.axis_index(AXES)
    bits = [(index >> place) & 1 for place in range(5)]
    slots = jnp.argsort(group_map).astype(jnp.int32)
    my_frames = lax.dynamic_slice_in_dim(group_map, 2 * lax.axis_index("blk"), 2)
    tables = rope_tables(frame_count)
    clip_levels = noise_levels
    for bit in (1, 2):
        clip_levels = jnp.concatenate([clip_levels, swap(clip_levels, bit)], axis=0)
    members = jnp.zeros((1,), jnp.int32)
    for bit in (16, 8, 4, 2, 1):
        members = jnp.concatenate([members, members ^ bit])
    member_slots = (2 * ((index ^ members) >> 2))[:, None] + jnp.arange(2, dtype=jnp.int32)[None, :]
    levels_all = clip_levels[(members & 3)[:, None], group_map[member_slots]].reshape(
        2 * device_count
    )
    tokens_here = tokens.reshape(rows_here, D)
    embedded = jnp.concatenate(
        [
            lax.dynamic_slice_in_dim(noise_table, noise_levels[0, my_frames[slot]], 1)
            for slot in range(2)
        ]
    ).astype(jnp.float32)
    activated = jax.nn.silu(embedded).astype(jnp.bfloat16)
    modulation = (
        jnp.dot(activated, mod_weight, preferred_element_type=jnp.float32)
        + mod_bias.astype(jnp.float32)[None, :]
    )
    qkv_out, first_in = project_qkv(
        my_frames, tokens_here, modulation[:, : 2 * D], qkv_weight, tables
    )
    qkv_heads = lax.all_to_all(qkv_out, "blk", 0, 0, tiled=True).reshape(-1, 3 * LANES)
    att_heads, ot, lse, first_in = attend(group_map, slots, qkv_heads, first_in, levels_all)
    att = lax.all_to_all(att_heads, "blk", 0, 0, tiled=True)
    first_all = lax.all_gather(first_in, "blk", axis=0, tiled=True)
    layer_out, acts, d_att, d_middle, d_mod_early = middle_block(
        att,
        tokens_here,
        out_cotangent.reshape(rows_here, D),
        modulation,
        out_weight,
        fc1_weight,
        fc2_weight,
    )
    grad_heads = lax.all_to_all(d_att, "blk", 0, 0, tiled=True).reshape(-1, LANES)
    acts_other = swap(acts, 1)
    keep_a, send_a, keep_b, send_b = weight_parts(jnp.stack(bits[:3]), acts, acts_other)
    got_a, got_b = swap(send_a, 2), swap(send_b, 4)
    d_heads = attend_back(group_map, slots, qkv_heads, grad_heads, ot, lse, tables, send_a)
    d_qkv = lax.all_to_all(d_heads, "blk", 0, 0, tiled=True)
    share = D // device_count
    split = (-1, 2, SHARE_ROWS, TILE)
    keep_a, send_a, keep_b, send_b = fold(
        [bits[2], bits[1]],
        keep_a.reshape(split),
        got_a.reshape(split),
        keep_b,
        got_b,
        d_heads,
    )
    got_a, got_b = swap(send_a, 4), swap(send_b, 2)
    tokens_grad, d_mod_late = first_back(
        d_qkv, tokens_here, modulation, d_middle, qkv_weight, send_a
    )
    qkv_keep, qkv_send = qkv_parts(
        bits[0].reshape(1), first_all, d_heads.reshape(-1, 3 * LANES), share, d_mod_late
    )
    qkv_keep, qkv_send = add_split(qkv_keep, swap(qkv_send, 1), 1, bits[1])
    qkv_got = swap(qkv_send, 2)
    qkv_sum = (qkv_keep.astype(jnp.float32) + qkv_got.astype(jnp.float32)).astype(jnp.bfloat16)
    qkv_share = (
        lax.all_to_all(qkv_sum, "blk", 0, 0, tiled=True)
        .reshape(groups, share, 3, LANES)
        .transpose(1, 2, 0, 3)
        .reshape(share, 3 * D)
        .astype(jnp.float32)
    )
    for bit in (8, 16):
        place = bit.bit_length() - 1
        keep_a, send_a, keep_b, send_b = fold(
            [bits[place], bits[place]],
            *(part.reshape(split) for part in (keep_a, got_a, keep_b, got_b)),
            d_mod_late,
        )
        got_a, got_b = swap(send_a, bit), swap(send_b, bit)
    upper_share, lower_share, outw_share = finish(
        share, *(part.reshape(SHARE_ROWS, TILE) for part in (keep_a, got_a, keep_b, got_b))
    )
    d_mod = jnp.concatenate([d_mod_late, d_mod_early], axis=1).astype(jnp.bfloat16)
    d_mod_all = gather_pairs(d_mod[None]).reshape(2 * device_count, 6 * D)
    level_hot = jnp.arange(LEVELS, dtype=jnp.int32)[:, None] == levels_all[None, :]
    table_columns = lax.dynamic_slice_in_dim(noise_table, index * share, share, 1)
    embedded_columns = jnp.einsum(
        "ls,lc->sc",
        level_hot.astype(jnp.bfloat16),
        table_columns,
        preferred_element_type=jnp.float32,
    )
    activated_columns, silu_pull = jax.vjp(jax.nn.silu, embedded_columns)
    modw_share = jnp.einsum(
        "sc,sk->ck",
        activated_columns.astype(jnp.bfloat16),
        d_mod_all,
        preferred_element_type=jnp.float32,
    )
    weight_rows = lax.dynamic_slice_in_dim(mod_weight, index * share, share, 0)
    d_activated = jnp.einsum("sk,ck->sc", d_mod_all, weight_rows, preferred_element_type=jnp.float32)
    d_embedded = silu_pull(d_activated)[0]
    table_share = jnp.dot(
        level_hot.astype(jnp.float32), d_embedded, precision=lax.Precision.HIGHEST
    )
    bias_columns = 6 * D // device_count
    bias_share = jnp.sum(
        lax.dynamic_slice_in_dim(d_mod_all, index * bias_columns, bias_columns, 1).astype(
            jnp.float32
        ),
        axis=0,
    )
    return (
        layer_out[None].reshape(1, 2, PATCHES, D),
        tokens_grad.reshape(1, 2, PATCHES, D),
        table_share,
        modw_share,
        bias_share,
        qkv_share,
        outw_share,
        upper_share,
        lower_share,
    )


def solution(mesh):
    pair_split = mesh.shape["blk"] * LANES == D and mesh.shape["clip"] == 4
    return jax.shard_map(
        local_heads if pair_split else local,
        mesh=mesh,
        in_specs=(
            P("clip", "blk", None, None),
            P("clip", None),
            P(),
            P(),
            P(),
            P(),
            P(),
            P(),
            P(),
            P(),
            P("clip", "blk", None, None),
        ),
        out_specs=(
            P("clip", "blk", None, None),
            P("clip", "blk", None, None),
            P(None, ("blk", "clip")),
            P(("blk", "clip"), None),
            P(("blk", "clip")),
            P(("blk", "clip"), None),
            P(("blk", "clip"), None),
            P(("blk", "clip"), None),
            P(("blk", "clip"), None),
        ),
        check_vma=False,
    )
```

```python
from functools import partial

import jax
import jax.numpy as jnp
import numpy as np
from jax import lax
from jax.experimental import pallas as pl
from jax.experimental.pallas import tpu as pltpu
from jax.sharding import PartitionSpec as P

D = 1024
HEAD = 64
HEADS = 16
LEVELS = 1000
GRID_H = 8
GRID_W = 16
PATCHES = 128


SCALE = 0.125
EPSILON = 1e-06
ROPE_BASE = 10000.0
NEG_LARGE = -1e30


def token_positions(frame_ids):
    slot_count = frame_ids.shape[0]
    total_rows = slot_count * GRID_H * GRID_W
    patch_ids = jnp.arange(total_rows, dtype=jnp.int32) % (GRID_H * GRID_W)
    frame_pos = jnp.repeat(frame_ids, GRID_H * GRID_W, total_repeat_length=total_rows)
    return (frame_pos, patch_ids // GRID_W, patch_ids % GRID_W)


def rope_angles(frame_pos, row_pos, col_pos):
    angle_list = []
    for position, comp_width in ((frame_pos, 16), (row_pos, 24), (col_pos, 24)):
        half_width = comp_width // 2
        frequency = ROPE_BASE ** (-2.0 * jnp.arange(half_width, dtype=jnp.float32) / comp_width)
        angle_list.append(position.astype(jnp.float32)[:, None] * frequency[None, :])
    return angle_list


def rotate(values, angle_list, direction):
    pieces = []
    offset = 0
    for angles in angle_list:
        half_width = angles.shape[1]
        first_half = values[:, :, offset : offset + half_width]
        second_half = values[:, :, offset + half_width : offset + 2 * half_width]
        cosine = jnp.cos(angles)[:, None, :]
        sine_part = direction * jnp.sin(angles)[:, None, :]
        pieces.append(first_half * cosine - second_half * sine_part)
        pieces.append(first_half * sine_part + second_half * cosine)
        offset = offset + 2 * half_width
    return jnp.concatenate(pieces, axis=2)


def normalize(values):
    center = values - jnp.mean(values, axis=-1, keepdims=True)
    inverse = lax.rsqrt(jnp.mean(center * center, axis=-1, keepdims=True) + EPSILON)
    return (center * inverse, inverse)


def norm_backward(grad_in, normed, inverse):
    return inverse * (
        grad_in
        - jnp.mean(grad_in, axis=-1, keepdims=True)
        - normed * jnp.mean(grad_in * normed, axis=-1, keepdims=True)
    )


def frames_of(group_map, first_row, row_count):
    slot_frames = lax.dynamic_slice_in_dim(group_map, first_row // PATCHES, row_count // PATCHES)
    return jnp.repeat(slot_frames, PATCHES, total_repeat_length=row_count)


def block_size(row_count, shard_rows):
    return 2 * shard_rows if row_count // shard_rows % 2 == 0 else shard_rows


def keep_same(values):
    return values


def local(
    tokens,
    noise_levels,
    group_map,
    noise_table,
    mod_weight,
    mod_bias,
    qkv_weight,
    out_weight,
    fc1_weight,
    fc2_weight,
    out_cotangent,
):
    rows_here = 2 * PATCHES
    my_frames = lax.dynamic_slice_in_dim(group_map, 2 * lax.axis_index("blk"), 2)
    frame_hot = (
        jnp.arange(group_map.shape[0], dtype=jnp.int32)[None, :] == my_frames[:, None]
    ).astype(jnp.int32)
    my_levels = jnp.sum(frame_hot * noise_levels[0][None, :], axis=1)
    level_hot = jnp.arange(LEVELS, dtype=jnp.int32)[None, :] == my_levels[:, None]
    embedded = jnp.dot(
        level_hot.astype(jnp.bfloat16), noise_table, preferred_element_type=jnp.float32
    )
    activated = jax.nn.silu(embedded).astype(jnp.bfloat16)
    modulation = (
        jnp.dot(activated, mod_weight, preferred_element_type=jnp.float32)
        + mod_bias.astype(jnp.float32)[None, :]
    )
    shift_one, scale_one, gate_one, shift_two, scale_two, gate_two = [
        modulation[:, member * D : (member + 1) * D][:, None, :] for member in range(6)
    ]
    inputs_here = tokens[0].astype(jnp.float32)
    normed_one, inverse_one = normalize(inputs_here)
    first_in = (
        (normed_one * (1.0 + scale_one) + shift_one).astype(jnp.bfloat16).reshape(rows_here, D)
    )
    qkv_lin = jnp.dot(first_in, qkv_weight, preferred_element_type=jnp.float32)
    token_frames, row_pos, col_pos = token_positions(my_frames)
    angle_list = rope_angles(token_frames, row_pos, col_pos)
    query = rotate(qkv_lin[:, :D].reshape(rows_here, HEADS, HEAD), angle_list, 1.0).astype(
        jnp.bfloat16
    )
    key_part = rotate(
        qkv_lin[:, D : 2 * D].reshape(rows_here, HEADS, HEAD), angle_list, 1.0
    ).astype(jnp.bfloat16)
    value_part = qkv_lin[:, 2 * D :].reshape(rows_here, HEADS, HEAD).astype(jnp.bfloat16)
    top_frame = jnp.max(my_frames)
    own_lowest = jnp.min(my_frames)
    forward_start = (
        jnp.full((HEADS, rows_here), NEG_LARGE, jnp.float32),
        jnp.zeros((HEADS, rows_here), jnp.float32),
        jnp.zeros((rows_here, HEADS, HEAD), jnp.float32),
    )
    first_row = jnp.int32(0)
    keys_piece = lax.all_gather(key_part, "blk", axis=0, tiled=True)
    values_piece = lax.all_gather(value_part, "blk", axis=0, tiled=True)
    piece_rows = keys_piece.shape[0]
    block_rows = block_size(piece_rows, rows_here)

    def forward_advance(turn_index, running):
        offset = turn_index * block_rows
        keys_block = lax.dynamic_slice_in_dim(keys_piece, offset, block_rows)
        values_block = lax.dynamic_slice_in_dim(values_piece, offset, block_rows)
        block_frames = frames_of(group_map, first_row + offset, block_rows)

        def attend(previous):
            top_scores, totals, accumulated = previous
            scores = (
                jnp.einsum("qhd,khd->hqk", query, keys_block, preferred_element_type=jnp.float32)
                * SCALE
            )
            allowed = block_frames[None, None, :] <= token_frames[None, :, None]
            new_top = jnp.maximum(
                top_scores, jnp.max(jnp.where(allowed, scores, NEG_LARGE), axis=2)
            )
            weights = jnp.where(allowed, jnp.exp(scores - new_top[:, :, None]), 0.0)
            factor = jnp.exp(top_scores - new_top)
            update = jnp.einsum(
                "hqk,khd->qhd",
                weights.astype(jnp.bfloat16),
                values_block,
                preferred_element_type=jnp.float32,
            )
            return (
                new_top,
                totals * factor + jnp.sum(weights, axis=2),
                accumulated * factor.T[:, :, None] + update,
            )

        return lax.cond(jnp.min(block_frames) > top_frame, keep_same, attend, running)

    top_scores, totals, accumulated = lax.fori_loop(
        0, piece_rows // block_rows, forward_advance, forward_start
    )
    attended = accumulated / totals.T[:, :, None]
    log_total = top_scores + jnp.log(totals)
    attended_low = attended.astype(jnp.bfloat16).reshape(rows_here, D)
    attn_out = jnp.dot(attended_low, out_weight, preferred_element_type=jnp.float32).reshape(
        2, PATCHES, D
    )
    middle = inputs_here + gate_one * attn_out
    normed_two, inverse_two = normalize(middle)
    second_in = (
        (normed_two * (1.0 + scale_two) + shift_two).astype(jnp.bfloat16).reshape(rows_here, D)
    )
    up_lin = jnp.dot(second_in, fc1_weight, preferred_element_type=jnp.float32)
    hidden = jax.nn.gelu(up_lin, approximate=False).astype(jnp.bfloat16)
    mlp_out = jnp.dot(hidden, fc2_weight, preferred_element_type=jnp.float32).reshape(2, PATCHES, D)
    layer_out = (middle + gate_two * mlp_out).astype(jnp.bfloat16)[None]
    cotangent = out_cotangent[0].astype(jnp.float32)
    d_gate_two = jnp.sum(cotangent * mlp_out, axis=1)
    d_mlp = (cotangent * gate_two).astype(jnp.bfloat16).reshape(rows_here, D)
    lower_part = jnp.einsum("rf,rd->fd", hidden, d_mlp, preferred_element_type=jnp.float32)
    d_hidden = jnp.einsum("rd,fd->rf", d_mlp, fc2_weight, preferred_element_type=jnp.float32)
    unused_value, gelu_pull = jax.vjp(partial(jax.nn.gelu, approximate=False), up_lin)
    d_up = gelu_pull(d_hidden)[0].astype(jnp.bfloat16)
    upper_part = jnp.einsum("rc,rf->cf", second_in, d_up, preferred_element_type=jnp.float32)
    d_second = jnp.einsum(
        "rf,cf->rc", d_up, fc1_weight, preferred_element_type=jnp.float32
    ).reshape(2, PATCHES, D)
    d_shift_two = jnp.sum(d_second, axis=1)
    d_scale_two = jnp.sum(d_second * normed_two, axis=1)
    d_middle = cotangent + norm_backward(d_second * (1.0 + scale_two), normed_two, inverse_two)
    d_gate_one = jnp.sum(d_middle * attn_out, axis=1)
    d_attn = (d_middle * gate_one).astype(jnp.bfloat16).reshape(rows_here, D)
    outw_part = jnp.einsum("rc,rd->cd", attended_low, d_attn, preferred_element_type=jnp.float32)
    d_attended = (
        jnp.einsum("rd,cd->rc", d_attn, out_weight, preferred_element_type=jnp.float32)
        .astype(jnp.bfloat16)
        .reshape(rows_here, HEADS, HEAD)
    )
    delta = jnp.sum(d_attended.astype(jnp.float32) * attended, axis=2).T
    grad_start = jnp.zeros((rows_here, HEADS, HEAD), jnp.float32)
    query_first_row = jnp.int32(0)
    query_keys_piece = lax.all_gather(key_part, "blk", axis=0, tiled=True)
    query_values_piece = lax.all_gather(value_part, "blk", axis=0, tiled=True)
    piece_rows = query_keys_piece.shape[0]
    query_block_rows = block_size(piece_rows, rows_here)

    def query_advance(turn_index, running):
        offset = turn_index * query_block_rows
        keys_block = lax.dynamic_slice_in_dim(query_keys_piece, offset, query_block_rows)
        values_block = lax.dynamic_slice_in_dim(query_values_piece, offset, query_block_rows)
        block_frames = frames_of(group_map, query_first_row + offset, query_block_rows)

        def query_accumulate(previous):
            scores = (
                jnp.einsum("qhd,khd->hqk", query, keys_block, preferred_element_type=jnp.float32)
                * SCALE
            )
            allowed = block_frames[None, None, :] <= token_frames[None, :, None]
            weights = jnp.where(allowed, jnp.exp(scores - log_total[:, :, None]), 0.0)
            weight_grad = jnp.einsum(
                "qhd,khd->hqk", d_attended, values_block, preferred_element_type=jnp.float32
            )
            score_grad = (weights * (weight_grad - delta[:, :, None]) * SCALE).astype(jnp.bfloat16)
            return previous + jnp.einsum(
                "hqk,khd->qhd", score_grad, keys_block, preferred_element_type=jnp.float32
            )

        return lax.cond(jnp.min(block_frames) > top_frame, keep_same, query_accumulate, running)

    query_grad = lax.fori_loop(0, piece_rows // query_block_rows, query_advance, grad_start)
    stats_lse, stats_delta = (
        lax.all_gather(log_total.T, "blk", axis=0, tiled=True),
        lax.all_gather(delta.T, "blk", axis=0, tiled=True),
    )
    key_first_row = jnp.int32(0)
    queries_piece = lax.all_gather(query, "blk", axis=0, tiled=True)
    grads_piece = lax.all_gather(d_attended, "blk", axis=0, tiled=True)
    piece_rows = queries_piece.shape[0]
    key_block_rows = block_size(piece_rows, rows_here)

    def key_advance(turn_index, running):
        offset = turn_index * key_block_rows
        query_block = lax.dynamic_slice_in_dim(queries_piece, offset, key_block_rows)
        grad_block = lax.dynamic_slice_in_dim(grads_piece, offset, key_block_rows)
        lse_block = lax.dynamic_slice_in_dim(stats_lse, key_first_row + offset, key_block_rows).T
        delta_block = lax.dynamic_slice_in_dim(
            stats_delta, key_first_row + offset, key_block_rows
        ).T
        block_frames = frames_of(group_map, key_first_row + offset, key_block_rows)

        def key_accumulate(previous):
            key_total, value_total = previous
            scores = (
                jnp.einsum(
                    "qhd,khd->hqk", query_block, key_part, preferred_element_type=jnp.float32
                )
                * SCALE
            )
            allowed = token_frames[None, None, :] <= block_frames[None, :, None]
            weights = jnp.where(allowed, jnp.exp(scores - lse_block[:, :, None]), 0.0)
            value_total = value_total + jnp.einsum(
                "hqk,qhd->khd",
                weights.astype(jnp.bfloat16),
                grad_block,
                preferred_element_type=jnp.float32,
            )
            weight_grad = jnp.einsum(
                "qhd,khd->hqk", grad_block, value_part, preferred_element_type=jnp.float32
            )
            score_grad = (weights * (weight_grad - delta_block[:, :, None]) * SCALE).astype(
                jnp.bfloat16
            )
            key_total = key_total + jnp.einsum(
                "hqk,qhd->khd", score_grad, query_block, preferred_element_type=jnp.float32
            )
            return (key_total, value_total)

        return lax.cond(jnp.max(block_frames) < own_lowest, keep_same, key_accumulate, running)

    key_grad, value_grad = lax.fori_loop(
        0, piece_rows // key_block_rows, key_advance, (grad_start, grad_start)
    )
    query_low = lax.optimization_barrier(query_grad.astype(jnp.bfloat16)).astype(jnp.float32)
    key_low = lax.optimization_barrier(key_grad.astype(jnp.bfloat16)).astype(jnp.float32)
    query_back = rotate(query_low, angle_list, -1.0).reshape(rows_here, D)
    key_back = rotate(key_low, angle_list, -1.0).reshape(rows_here, D)
    d_qkv = jnp.concatenate(
        [query_back, key_back, value_grad.reshape(rows_here, D)], axis=1
    ).astype(jnp.bfloat16)
    qkv_part = jnp.einsum("rc,rk->ck", first_in, d_qkv, preferred_element_type=jnp.float32)
    d_first = jnp.einsum(
        "rk,ck->rc", d_qkv, qkv_weight, preferred_element_type=jnp.float32
    ).reshape(2, PATCHES, D)
    d_shift_one = jnp.sum(d_first, axis=1)
    d_scale_one = jnp.sum(d_first * normed_one, axis=1)
    tokens_grad = (
        d_middle + norm_backward(d_first * (1.0 + scale_one), normed_one, inverse_one)
    ).astype(jnp.bfloat16)[None]
    d_mod = jnp.concatenate(
        [d_shift_one, d_scale_one, d_gate_one, d_shift_two, d_scale_two, d_gate_two], axis=1
    )
    bias_part = jnp.sum(d_mod, axis=0)
    d_mod_low = d_mod.astype(jnp.bfloat16)
    d_activated = jnp.einsum("sk,ck->sc", d_mod_low, mod_weight, preferred_element_type=jnp.float32)
    unused_silu, silu_pull = jax.vjp(jax.nn.silu, embedded)
    d_embedded = silu_pull(d_activated)[0]
    table_part = jnp.einsum(
        "sl,sc->cl", level_hot.astype(jnp.float32), d_embedded, precision=lax.Precision.HIGHEST
    )
    activated_all, d_mod_all = (
        lax.all_gather(activated, ("blk", "clip"), axis=0, tiled=True),
        lax.all_gather(d_mod_low, ("blk", "clip"), axis=0, tiled=True),
    )
    share_rows = D // lax.axis_size(("blk", "clip"))
    my_columns = lax.dynamic_slice_in_dim(
        activated_all, lax.axis_index(("blk", "clip")) * share_rows, share_rows, 1
    )
    modw_share = jnp.einsum("sc,sk->ck", my_columns, d_mod_all, preferred_element_type=jnp.float32)
    summed = (
        lax.psum_scatter(table_part, ("blk", "clip"), scatter_dimension=0, tiled=True),
        lax.psum_scatter(bias_part, ("blk", "clip"), scatter_dimension=0, tiled=True),
        lax.psum_scatter(qkv_part, ("blk", "clip"), scatter_dimension=0, tiled=True),
        lax.psum_scatter(outw_part, ("blk", "clip"), scatter_dimension=0, tiled=True),
        lax.psum_scatter(upper_part, ("blk", "clip"), scatter_dimension=0, tiled=True),
        lax.psum_scatter(lower_part, ("blk", "clip"), scatter_dimension=0, tiled=True),
    )
    return (
        layer_out,
        tokens_grad,
        summed[0].T,
        modw_share,
        summed[1],
        summed[2],
        summed[3],
        summed[4],
        summed[5],
    )


LANES = 128
FF = 4096
AXES = ("blk", "clip")
EXP_SCALE = SCALE * 1.4426950408889634
VMEM_LIMIT = 56 * 1024 * 1024
NT = (((1,), (1,)), ((), ()))
NN = (((1,), (0,)), ((), ()))


def cost(microseconds):
    return pl.CostEstimate(
        flops=int(microseconds * 1e9), bytes_accessed=int(microseconds * 3e6), transcendentals=0
    )


class Shifted:
    def __init__(self, ref, start):
        self.ref, self.start = ref, start

    def __getitem__(self, place):
        return self.ref[self.start + place]


FRAME_COUNT = 2 * D // LANES
BITS_AT, ORDER_AT = 0, 5
FRAMES_AT = ORDER_AT + D // LANES
SLOTS_AT = FRAMES_AT + FRAME_COUNT
GROUP_AT = SLOTS_AT + FRAME_COUNT
MINE_AT = GROUP_AT + FRAME_COUNT
ANYWHERE = pl.BlockSpec(memory_space=pl.ANY)


def full_block(shape):
    return pl.BlockSpec(shape, lambda *ids: (0,) * len(shape))


def rope_tables(frame_count):
    lane = np.arange(LANES) % HEAD
    pieces = []
    for comp_width in (16, 24, 24):
        half_width = comp_width // 2
        frequency = ROPE_BASE ** (-2.0 * np.arange(half_width) / comp_width)
        pieces += [frequency, frequency]
    frequency = np.tile(np.concatenate(pieces), LANES // HEAD)[None, :]
    first = (lane < 8) | ((lane >= 16) & (lane < 28)) | ((lane >= 40) & (lane < 52))
    sign = np.where(first, -1.0, 1.0)[None, :]
    in_frame = (lane < 16)[None, :]
    in_row = (lane < 40)[None, :]
    frame_angle = np.arange(frame_count)[:, None] * frequency
    patch = np.arange(PATCHES)[:, None]
    place_angle = np.where(in_row, patch // GRID_W, patch % GRID_W) * frequency
    tables = (
        np.where(in_frame, np.cos(frame_angle), 0.0),
        np.where(in_frame, sign * np.sin(frame_angle), 0.0),
        np.where(in_frame, 0.0, np.cos(place_angle)),
        np.where(in_frame, 0.0, sign * np.sin(place_angle)),
    )
    return tuple(jnp.asarray(table, jnp.float32) for table in tables)


def partner_lanes(values):
    lane = lax.broadcasted_iota(jnp.int32, values.shape, 1) % HEAD
    ahead_eight = pltpu.roll(values, LANES - 8, 1)
    behind_eight = pltpu.roll(values, 8, 1)
    ahead_twelve = pltpu.roll(values, LANES - 12, 1)
    behind_twelve = pltpu.roll(values, 12, 1)
    ahead = ((lane >= 16) & (lane < 28)) | ((lane >= 40) & (lane < 52))
    return jnp.where(
        lane < 8,
        ahead_eight,
        jnp.where(lane < 16, behind_eight, jnp.where(ahead, ahead_twelve, behind_twelve)),
    )


def modulation_kernel(levels_ref, table_ref, weight_ref, bias_ref, out_ref, activated_ref):
    @pl.when(pl.program_id(0) == 0)
    def _():
        count = levels_ref.shape[1]
        hot = lax.broadcasted_iota(jnp.int32, (LEVELS, count), 0) == levels_ref[...]
        embedded = lax.dot_general(
            jnp.where(hot, 1.0, 0.0).astype(jnp.bfloat16),
            table_ref[...],
            (((0,), (0,)), ((), ())),
            preferred_element_type=jnp.float32,
        )
        activated_ref[...] = jax.nn.silu(embedded).astype(jnp.bfloat16)

    out_ref[...] = lax.dot_general(
        activated_ref[...], weight_ref[...], NN, preferred_element_type=jnp.float32
    ) + bias_ref[...].astype(jnp.float32)[None, :]


def modulate(levels, noise_table, mod_weight, mod_bias):
    frame_count = levels.shape[1]
    return pl.pallas_call(
        modulation_kernel,
        grid=(6,),
        in_specs=[
            full_block(levels.shape),
            full_block(noise_table.shape),
            pl.BlockSpec((D, D), lambda i: (0, i)),
            pl.BlockSpec((D,), lambda i: (i,)),
        ],
        out_specs=pl.BlockSpec((frame_count, D), lambda i: (0, i)),
        out_shape=jax.ShapeDtypeStruct((frame_count, 6 * D), jnp.float32),
        scratch_shapes=[pltpu.VMEM((frame_count, D), jnp.bfloat16)],
        compiler_params=pltpu.CompilerParams(
            vmem_limit_bytes=VMEM_LIMIT, dimension_semantics=("arbitrary",)
        ),
        cost_estimate=cost(7),
        name="modulate",
    )(levels, noise_table, mod_weight, mod_bias)


def copy_kernel(info_ref, source_ref, target_ref):
    target_ref[...] = source_ref[...]


def own_columns(info, weight):
    return pl.pallas_call(
        copy_kernel,
        grid_spec=pltpu.PrefetchScalarGridSpec(
            num_scalar_prefetch=1,
            grid=(3,),
            in_specs=[
                pl.BlockSpec((D, LANES), lambda i, info: (0, i * (D // LANES) + info[ORDER_AT]))
            ],
            out_specs=pl.BlockSpec((D, LANES), lambda i, info: (0, i)),
        ),
        out_shape=jax.ShapeDtypeStruct((D, 3 * LANES), jnp.bfloat16),
        compiler_params=pltpu.CompilerParams(dimension_semantics=("arbitrary",)),
        cost_estimate=cost(2),
        name="own_columns",
    )(info, weight)


def project_kernel(
    count,
    first_piece,
    info_ref,
    mod_ref,
    weight_ref,
    fcos_ref,
    fsin_ref,
    pcos_ref,
    psin_ref,
    *refs,
):
    frames_ref = Shifted(info_ref, FRAMES_AT)
    halves, out_ref, first_ref = refs[: 2 * count], refs[-2], refs[-1]
    for piece in range(count):
        for half in range(2):
            source, place = halves[2 * piece + half]
            rows = slice(half * PATCHES, (half + 1) * PATCHES)
            frame = frames_ref[2 * (first_piece + piece) + half]
            normed, unused = normalize(
                source[place * PATCHES : (place + 1) * PATCHES, :].astype(jnp.float32)
            )
            shift = mod_ref[pl.ds(frame, 1), :D]
            scale = mod_ref[pl.ds(frame, 1), D : 2 * D]
            first_ref[piece, rows, :] = (normed * (1.0 + scale) + shift).astype(jnp.bfloat16)
        linear = lax.dot_general(
            first_ref[piece], weight_ref[...], NN, preferred_element_type=jnp.float32
        )
        for half in range(2):
            rows = slice(half * PATCHES, (half + 1) * PATCHES)
            frame = frames_ref[2 * (first_piece + piece) + half]
            cosine = pcos_ref[...] + fcos_ref[pl.ds(frame, 1), :]
            sine = psin_ref[...] + fsin_ref[pl.ds(frame, 1), :]
            for part in range(2):
                columns = slice(part * LANES, (part + 1) * LANES)
                values = linear[rows, columns]
                turned = values * cosine + partner_lanes(values) * sine
                out_ref[piece, rows, columns] = turned.astype(jnp.bfloat16)
            out_ref[piece, rows, 2 * LANES :] = linear[rows, 2 * LANES :].astype(jnp.bfloat16)


def project(info, modulation, weight, tables, first_piece, pieces):
    vmem = pl.BlockSpec(memory_space=pltpu.VMEM)
    count = len(pieces)
    arrays, sources = [], []
    for piece in pieces:
        if isinstance(piece, tuple):
            sources += [(len(arrays), 0), (len(arrays) + 1, 0)]
            arrays += list(piece)
        else:
            sources += [(len(arrays), 0), (len(arrays), 1)]
            arrays.append(piece)

    def kernel(*refs):
        inputs = refs[7 : 7 + len(arrays)]
        halves = [(inputs[which], place) for which, place in sources]
        project_kernel(count, first_piece, *refs[:7], *halves, *refs[7 + len(arrays) :])

    rows = 2 * PATCHES
    return pl.pallas_call(
        kernel,
        in_specs=[pl.BlockSpec(memory_space=pltpu.SMEM)] + [vmem] * (6 + len(arrays)),
        out_specs=[vmem] * 2,
        out_shape=[
            jax.ShapeDtypeStruct((count, rows, 3 * LANES), jnp.bfloat16),
            jax.ShapeDtypeStruct((count, rows, D), jnp.bfloat16),
        ],
        compiler_params=pltpu.CompilerParams(vmem_limit_bytes=VMEM_LIMIT),
        cost_estimate=cost(2 * count),
        name="project",
    )(info, modulation, weight, *tables, *arrays)


def head_stack(values):
    lane = lax.broadcasted_iota(jnp.int32, values.shape, 1)
    zero = jnp.zeros_like(values)
    return jnp.concatenate(
        [jnp.where(lane < HEAD, values, zero), jnp.where(lane < HEAD, zero, values)], axis=0
    )


def hidden_keys(shape):
    key_row = lax.broadcasted_iota(jnp.int32, shape, 0)
    query_column = lax.broadcasted_iota(jnp.int32, shape, 1) % (2 * PATCHES)
    return (key_row >= PATCHES) & (query_column < PATCHES)


def own_heads(values):
    rows = 2 * PATCHES
    return jnp.concatenate([values[:HEAD, :rows], values[HEAD:LANES, rows:]], axis=0)


def by_frame(frames_ref, source_refs, target_refs):
    pieces = [(ref, piece) for ref in source_refs for piece in range(ref.shape[0])]
    for place, (ref, piece) in enumerate(pieces):
        for half in range(2):
            frame = frames_ref[2 * place + half]
            rows = pl.ds(pl.multiple_of(frame * PATCHES, PATCHES), PATCHES)
            for part, target in enumerate(target_refs):
                target[rows, :] = ref[
                    piece,
                    half * PATCHES : (half + 1) * PATCHES,
                    part * LANES : (part + 1) * LANES,
                ]


def attend_kernel(info_ref, qkv_refs, att_ref, ot_ref, lse_ref, q_ref, k_ref, v_ref, vt_ref):
    token_count = q_ref.shape[0]
    frames_ref, slots_ref = Shifted(info_ref, FRAMES_AT), Shifted(info_ref, SLOTS_AT)
    by_frame(frames_ref, qkv_refs, (q_ref, k_ref, v_ref))
    vt_ref[:LANES, :] = v_ref[...].T
    vt_ref[LANES:, :] = jnp.ones((vt_ref.shape[0] - LANES, token_count), jnp.bfloat16)
    step = 2 * PATCHES
    for turn in range(token_count // step):
        here = slice(turn * step, (turn + 1) * step)
        queries = head_stack(q_ref[here, :])
        ranges = [here] if turn == 0 else [slice(0, turn * step), here]
        raw = [
            lax.dot_general(k_ref[keys, :], queries, NT, preferred_element_type=jnp.float32)
            for keys in ranges
        ]
        raw[-1] = jnp.where(hidden_keys(raw[-1].shape), NEG_LARGE, raw[-1])
        top = jnp.max(raw[-1], axis=0, keepdims=True)
        for part in raw[:-1]:
            top = jnp.maximum(top, jnp.max(part, axis=0, keepdims=True))
        top = top * EXP_SCALE
        summed = None
        for keys, part in zip(ranges, raw):
            weights = jnp.exp2(part * EXP_SCALE - top).astype(jnp.bfloat16)
            update = lax.dot_general(
                vt_ref[:, keys], weights, NN, preferred_element_type=jnp.float32
            )
            summed = update if summed is None else summed + update
        totals = summed[LANES : LANES + 1, :]
        lse_ref[turn : turn + 1, :] = top + jnp.log2(totals)
        out = own_heads(summed[:LANES, :] / totals)
        ot_ref[:, here] = out
        rounded = out.T.astype(jnp.bfloat16)
        for half in range(2):
            slot = slots_ref[2 * turn + half]
            rows = pl.ds(pl.multiple_of(slot % 2 * PATCHES, PATCHES), PATCHES)
            att_ref[slot // 2, rows, :] = rounded[half * PATCHES : (half + 1) * PATCHES, :]


def attend(info, qkv, after):
    token_count = FRAME_COUNT * PATCHES
    turns = token_count // (2 * PATCHES)
    vmem = pl.BlockSpec(memory_space=pltpu.VMEM)

    def kernel(info_ref, *refs):
        attend_kernel(info_ref, refs[: len(qkv)], *refs[len(qkv) + 1 :])

    return pl.pallas_call(
        kernel,
        in_specs=[pl.BlockSpec(memory_space=pltpu.SMEM)] + [vmem] * len(qkv) + [ANYWHERE],
        out_specs=[vmem] * 3,
        out_shape=[
            jax.ShapeDtypeStruct((turns, 2 * PATCHES, LANES), jnp.bfloat16),
            jax.ShapeDtypeStruct((LANES, token_count), jnp.float32),
            jax.ShapeDtypeStruct((turns, 4 * PATCHES), jnp.float32),
        ],
        scratch_shapes=[pltpu.VMEM((token_count, LANES), jnp.bfloat16)] * 3
        + [pltpu.VMEM((LANES + 16, token_count), jnp.bfloat16)],
        compiler_params=pltpu.CompilerParams(vmem_limit_bytes=VMEM_LIMIT),
        cost_estimate=cost(10),
        name="attend",
    )(info, *qkv, after)


def attend_back_kernel(
    info_ref,
    grad_ref,
    ot_ref,
    lse_ref,
    fcos_ref,
    fsin_ref,
    pcos_ref,
    psin_ref,
    qkv_refs,
    out_ref,
    q_ref,
    k_ref,
    v_ref,
    d_ref,
    kt_ref,
    dk_ref,
    dv_ref,
):
    token_count = q_ref.shape[0]
    frames_ref, slot_frames_ref, slots_ref = (
        Shifted(info_ref, place) for place in (FRAMES_AT, GROUP_AT, SLOTS_AT)
    )
    by_frame(frames_ref, qkv_refs, (q_ref, k_ref, v_ref))
    by_frame(slot_frames_ref, (grad_ref,), (d_ref,))
    kt_ref[...] = k_ref[...].T
    step = 2 * PATCHES

    def put(frame, part, values):
        slot = slots_ref[frame]
        rows = pl.ds(pl.multiple_of(slot % 2 * PATCHES, PATCHES), PATCHES)
        out_ref[slot // 2, rows, part * LANES : (part + 1) * LANES] = values

    def turn_back(frame, values):
        values = values.astype(jnp.bfloat16).astype(jnp.float32)
        cosine = pcos_ref[...] + fcos_ref[frame : frame + 1, :]
        sine = psin_ref[...] + fsin_ref[frame : frame + 1, :]
        return (values * cosine - partner_lanes(values) * sine).astype(jnp.bfloat16)

    for turn in range(token_count // step):
        here = slice(turn * step, (turn + 1) * step)
        queries = head_stack(q_ref[here, :])
        grads_here = d_ref[here, :]
        grads = head_stack(grads_here)
        product = grads_here.astype(jnp.float32).T * ot_ref[:, here]
        delta = jnp.concatenate(
            [
                jnp.sum(product[:HEAD, :], axis=0, keepdims=True),
                jnp.sum(product[HEAD:, :], axis=0, keepdims=True),
            ],
            axis=1,
        )
        lse = lse_ref[turn : turn + 1, :]
        ranges = [here] if turn == 0 else [here, slice(0, turn * step)]
        total = None
        for keys in ranges:
            raw = lax.dot_general(
                k_ref[keys, :], queries, NT, preferred_element_type=jnp.float32
            )
            weights = jnp.exp2(raw * EXP_SCALE - lse)
            if keys is here:
                weights = jnp.where(hidden_keys(weights.shape), 0.0, weights)
            weight_grad = lax.dot_general(
                v_ref[keys, :], grads, NT, preferred_element_type=jnp.float32
            )
            score_grad = (weights * (weight_grad - delta)).astype(jnp.bfloat16)
            value_part = lax.dot_general(
                weights.astype(jnp.bfloat16), grads, NN, preferred_element_type=jnp.float32
            )
            key_part = lax.dot_general(
                score_grad, queries, NN, preferred_element_type=jnp.float32
            )
            if keys is here:
                dv_ref[keys, :] = value_part
                dk_ref[keys, :] = key_part
            else:
                dv_ref[keys, :] += value_part
                dk_ref[keys, :] += key_part
            update = lax.dot_general(
                kt_ref[:, keys], score_grad, NN, preferred_element_type=jnp.float32
            )
            total = update if total is None else total + update
        query_grad = own_heads(total).T * SCALE
        for half in range(2):
            put(
                2 * turn + half,
                0,
                turn_back(2 * turn + half, query_grad[half * PATCHES : (half + 1) * PATCHES, :]),
            )
    for frame in range(token_count // PATCHES):
        rows = slice(frame * PATCHES, (frame + 1) * PATCHES)
        put(frame, 1, turn_back(frame, dk_ref[rows, :] * SCALE))
        put(frame, 2, dv_ref[rows, :].astype(jnp.bfloat16))


def attend_back(info, qkv, grads, ot, lse, tables, after):
    token_count = FRAME_COUNT * PATCHES
    smem = pl.BlockSpec(memory_space=pltpu.SMEM)
    vmem = pl.BlockSpec(memory_space=pltpu.VMEM)

    def kernel(*refs):
        outs = 8 + len(qkv) + len(after)
        attend_back_kernel(*refs[:8], refs[8 : 8 + len(qkv)], *refs[outs:])

    return pl.pallas_call(
        kernel,
        in_specs=[smem] + [vmem] * (7 + len(qkv)) + [ANYWHERE] * len(after),
        out_specs=vmem,
        out_shape=jax.ShapeDtypeStruct(
            (token_count // (2 * PATCHES), 2 * PATCHES, 3 * LANES), jnp.bfloat16
        ),
        scratch_shapes=[pltpu.VMEM((token_count, LANES), jnp.bfloat16)] * 4
        + [pltpu.VMEM((LANES, token_count), jnp.bfloat16)]
        + [pltpu.VMEM((token_count, LANES), jnp.float32)] * 2,
        compiler_params=pltpu.CompilerParams(vmem_limit_bytes=VMEM_LIMIT),
        cost_estimate=cost(5),
        name="attend_back",
    )(info, grads, ot, lse, *tables, *qkv, *after)


def swap(values, bit):
    count = lax.axis_size(AXES)
    return lax.ppermute(values, AXES, [(index, index ^ bit) for index in range(count)])


PIECES = (0, 4, 2, 1, 5, 6, 3, 7)


def cross(values, bit):
    count = lax.axis_size("blk")
    return lax.ppermute(values, "blk", [(place, place ^ bit) for place in range(count)])


def gather_pairs(values):
    bit = lax.axis_size(AXES) // 2
    while bit:
        values = jnp.concatenate([values, swap(values, bit)], axis=0)
        bit //= 2
    return values


SECOND_AT, UP_AT, UP_ACTS = 0, D, D + FF
MLP_AT, ATTENDED_AT, ATTN_AT, HIDDEN_AT, DOWN_ACTS = 0, D, 2 * D, 3 * D, 3 * D + FF
FF_TILE = 512


def middle_kernel(
    info_ref,
    att_ref,
    tokens_ref,
    cot_ref,
    mod_ref,
    ow_ref,
    up_ref,
    down_ref,
    layer_ref,
    upper_ref,
    lower_ref,
    datt_ref,
    dmid_ref,
    dmod_ref,
    attn_ref,
    mid_ref,
    mlp_ref,
    dsec_ref,
):
    step = pl.program_id(0)
    slot_rows = [slice(slot * PATCHES, (slot + 1) * PATCHES) for slot in range(2)]

    def member(slot, which):
        return mod_ref[pl.ds(info_ref[MINE_AT + slot], 1), which * D : (which + 1) * D]

    @pl.when(step == 0)
    def _():
        for group in range(D // LANES):
            lower_ref[:, ATTENDED_AT + group * LANES : ATTENDED_AT + (group + 1) * LANES] = att_ref[
                group
            ]
        attn_ref[...] = lax.dot_general(
            lower_ref[:, ATTENDED_AT : ATTENDED_AT + D],
            ow_ref[...],
            NN,
            preferred_element_type=jnp.float32,
        )
        for slot, rows in enumerate(slot_rows):
            middle = tokens_ref[rows, :].astype(jnp.float32) + member(slot, 2) * attn_ref[rows, :]
            mid_ref[rows, :] = middle
            normed, unused = normalize(middle)
            upper_ref[rows, SECOND_AT : SECOND_AT + D] = (
                normed * (1.0 + member(slot, 4)) + member(slot, 3)
            ).astype(jnp.bfloat16)
            lower_ref[rows, MLP_AT : MLP_AT + D] = (
                cot_ref[rows, :].astype(jnp.float32) * member(slot, 5)
            ).astype(jnp.bfloat16)
        mlp_ref[...] = jnp.zeros_like(mlp_ref)
        dsec_ref[...] = jnp.zeros_like(dsec_ref)

    up_lin = lax.dot_general(
        upper_ref[:, SECOND_AT : SECOND_AT + D],
        up_ref[...],
        NN,
        preferred_element_type=jnp.float32,
    )
    below = 0.5 + 0.5 * lax.erf(up_lin * 0.7071067811865476)
    density = jnp.exp(up_lin * up_lin * -0.5) * 0.3989422804014327
    hidden = (up_lin * below).astype(jnp.bfloat16)
    d_hidden = lax.dot_general(
        lower_ref[:, MLP_AT : MLP_AT + D], down_ref[...], NT, preferred_element_type=jnp.float32
    )
    d_up = (d_hidden * (below + up_lin * density)).astype(jnp.bfloat16)
    lower_ref[:, pl.ds(pl.multiple_of(HIDDEN_AT + step * FF_TILE, FF_TILE), FF_TILE)] = hidden
    upper_ref[:, pl.ds(pl.multiple_of(UP_AT + step * FF_TILE, FF_TILE), FF_TILE)] = d_up
    mlp_ref[...] += lax.dot_general(
        hidden, down_ref[...], NN, preferred_element_type=jnp.float32
    )
    dsec_ref[...] += lax.dot_general(d_up, up_ref[...], NT, preferred_element_type=jnp.float32)

    @pl.when(step == pl.num_programs(0) - 1)
    def _():
        for slot, rows in enumerate(slot_rows):
            middle = mid_ref[rows, :]
            mlp_out = mlp_ref[rows, :]
            cotangent = cot_ref[rows, :].astype(jnp.float32)
            layer_ref[rows, :] = (middle + member(slot, 5) * mlp_out).astype(jnp.bfloat16)
            normed, inverse = normalize(middle)
            d_second = dsec_ref[rows, :]
            d_middle = cotangent + norm_backward(
                d_second * (1.0 + member(slot, 4)), normed, inverse
            )
            dmid_ref[rows, :] = d_middle
            lower_ref[rows, ATTN_AT : ATTN_AT + D] = (d_middle * member(slot, 2)).astype(
                jnp.bfloat16
            )
            for place, values in enumerate(
                (d_middle * attn_ref[rows, :], d_second, d_second * normed, cotangent * mlp_out)
            ):
                dmod_ref[slot : slot + 1, place * D : (place + 1) * D] = jnp.sum(
                    values, axis=0, keepdims=True
                )
        d_attended = lax.dot_general(
            lower_ref[:, ATTN_AT : ATTN_AT + D],
            ow_ref[...],
            NT,
            preferred_element_type=jnp.float32,
        ).astype(jnp.bfloat16)
        for group in range(D // LANES):
            datt_ref[group] = d_attended[:, group * LANES : (group + 1) * LANES]


def middle_block(info, att, tokens_here, cot_here, modulation, out_weight, fc1_weight, fc2_weight):
    rows = tokens_here.shape[0]
    return pl.pallas_call(
        middle_kernel,
        grid_spec=pltpu.PrefetchScalarGridSpec(
            num_scalar_prefetch=1,
            grid=(FF // FF_TILE,),
            in_specs=[
                full_block(att.shape),
                full_block((rows, D)),
                full_block((rows, D)),
                full_block(modulation.shape),
                full_block((D, D)),
                pl.BlockSpec((D, FF_TILE), lambda f, frames: (0, f)),
                pl.BlockSpec((FF_TILE, D), lambda f, frames: (f, 0)),
            ],
            out_specs=[
                full_block((rows, D)),
                full_block((rows, UP_ACTS)),
                full_block((rows, DOWN_ACTS)),
                full_block(att.shape),
                full_block((rows, D)),
                full_block((2, 4 * D)),
            ],
            scratch_shapes=[pltpu.VMEM((rows, D), jnp.float32)] * 4,
        ),
        out_shape=[
            jax.ShapeDtypeStruct((rows, D), jnp.bfloat16),
            jax.ShapeDtypeStruct((rows, UP_ACTS), jnp.bfloat16),
            jax.ShapeDtypeStruct((rows, DOWN_ACTS), jnp.bfloat16),
            jax.ShapeDtypeStruct(att.shape, jnp.bfloat16),
            jax.ShapeDtypeStruct((rows, D), jnp.float32),
            jax.ShapeDtypeStruct((2, 4 * D), jnp.float32),
        ],
        compiler_params=pltpu.CompilerParams(
            vmem_limit_bytes=VMEM_LIMIT, dimension_semantics=("arbitrary",)
        ),
        cost_estimate=cost(21),
        name="middle_block",
    )(info, att, tokens_here, cot_here, modulation, out_weight, fc1_weight, fc2_weight)


CHIPS = 16
TILE = 256
FINE = D // CHIPS // 2
UPPER_JOBS = ((SECOND_AT, FINE, UP_AT, FF, 10),)
LOWER_JOBS = ((HIDDEN_AT, LANES, MLP_AT, D, 3), (ATTENDED_AT, FINE, ATTN_AT, D, 2))


def rows_of(jobs):
    first = sum(height * tiles for unused, height, unused_at, width, tiles in jobs)
    return first, sum(job[1] * (job[3] // TILE) for job in jobs) - first


def weight_kernel(jobs, info_ref, mine_ref, theirs_ref, *refs):
    keep_a, send_a, keep_b, send_b = refs[-4 - len(jobs) : -len(jobs)]
    left_refs = refs[-len(jobs) :]
    core, xbit, ybit = (info_ref[BITS_AT + place] for place in range(3))
    rows = mine_ref.shape[0]
    row_a = row_b = 0
    for (left_at, height, right_at, width, tiles), left_ref in zip(jobs, left_refs):
        for place, ref in enumerate((mine_ref, theirs_ref)):
            columns = slice(place * rows, (place + 1) * rows)
            if height == LANES:
                for chip in range(CHIPS):
                    source = pl.multiple_of(left_at + (2 * chip + core) * LANES, LANES)
                    left_ref[chip * LANES : (chip + 1) * LANES, columns] = ref[
                        :, pl.ds(source, LANES)
                    ].T
            else:
                turned = ref[:, left_at : left_at + D].T.reshape(CHIPS, 2, height, rows)
                left_ref[:, columns] = jnp.where(core == 0, turned[:, 0], turned[:, 1]).reshape(
                    CHIPS * height, rows
                )
        for tile in range(width // TILE):
            source = right_at + tile * TILE
            right = jnp.concatenate(
                [mine_ref[:, source : source + TILE], theirs_ref[:, source : source + TILE]],
                axis=0,
            )
            part = lax.dot_general(
                left_ref[...], right, NN, preferred_element_type=jnp.float32
            ).astype(jnp.bfloat16)
            if tile < tiles:
                part = part.reshape(CHIPS // 2, 2, height, TILE)
                low, high = part[:, 0], part[:, 1]
                out_rows = slice(row_a, row_a + height)
                keep_a[:, out_rows, :] = jnp.where(xbit == 0, low, high)
                send_a[:, out_rows, :] = jnp.where(xbit == 0, high, low)
                row_a += height
            else:
                part = part.reshape(CHIPS // 4, 2, 2, height, TILE)
                low, high = part[:, 0], part[:, 1]
                out_rows = slice(row_b, row_b + height)
                keep_b[:, :, out_rows, :] = jnp.where(ybit == 0, low, high)
                send_b[:, :, out_rows, :] = jnp.where(ybit == 0, high, low)
                row_b += height


def weight_parts(jobs, info, mine, theirs, after):
    rows = mine.shape[0]
    vmem = pl.BlockSpec(memory_space=pltpu.VMEM)
    rows_a, rows_b = rows_of(jobs)
    first = jax.ShapeDtypeStruct((CHIPS // 2, rows_a, TILE), jnp.bfloat16)
    second = jax.ShapeDtypeStruct((CHIPS // 4, 2, rows_b, TILE), jnp.bfloat16)
    return pl.pallas_call(
        partial(weight_kernel, jobs),
        in_specs=[pl.BlockSpec(memory_space=pltpu.SMEM), vmem, vmem] + [ANYWHERE] * len(after),
        out_specs=[vmem] * 4,
        out_shape=[first, first, second, second],
        scratch_shapes=[pltpu.VMEM((CHIPS * job[1], 2 * rows), jnp.bfloat16) for job in jobs],
        compiler_params=pltpu.CompilerParams(vmem_limit_bytes=VMEM_LIMIT),
        cost_estimate=cost(3),
        name="weight_parts",
    )(info, mine, theirs, *after)


WEIGHT_ROWS = 256


def first_back_kernel(
    info_ref,
    dqkv_ref,
    tokens_ref,
    mod_ref,
    dmid_ref,
    weight_ref,
    *refs,
):
    grad_ref, late_ref, flat_ref, total_ref = refs[-4:]
    step = pl.program_id(0)

    @pl.when(step == 0)
    def _():
        for group in range(D // LANES):
            for part in range(3):
                column = part * D + group * LANES
                flat_ref[:, column : column + LANES] = dqkv_ref[
                    group, :, part * LANES : (part + 1) * LANES
                ]

    columns = pl.ds(pl.multiple_of(step * WEIGHT_ROWS, WEIGHT_ROWS), WEIGHT_ROWS)
    total_ref[:, columns] = lax.dot_general(
        flat_ref[...], weight_ref[...], NT, preferred_element_type=jnp.float32
    )

    @pl.when(step == pl.num_programs(0) - 1)
    def _():
        for slot in range(2):
            rows = slice(slot * PATCHES, (slot + 1) * PATCHES)
            normed, inverse = normalize(tokens_ref[rows, :].astype(jnp.float32))
            d_first = total_ref[rows, :]
            scale = mod_ref[pl.ds(info_ref[MINE_AT + slot], 1), D : 2 * D]
            grad_ref[rows, :] = (
                dmid_ref[rows, :] + norm_backward(d_first * (1.0 + scale), normed, inverse)
            ).astype(jnp.bfloat16)
            late_ref[slot : slot + 1, :D] = jnp.sum(d_first, axis=0, keepdims=True)
            late_ref[slot : slot + 1, D:] = jnp.sum(d_first * normed, axis=0, keepdims=True)


def first_back(info, d_qkv, tokens_here, modulation, d_middle, qkv_weight, after):
    rows = tokens_here.shape[0]
    return pl.pallas_call(
        first_back_kernel,
        grid_spec=pltpu.PrefetchScalarGridSpec(
            num_scalar_prefetch=1,
            grid=(D // WEIGHT_ROWS,),
            in_specs=[
                full_block(d_qkv.shape),
                full_block((rows, D)),
                full_block(modulation.shape),
                full_block((rows, D)),
                pl.BlockSpec((WEIGHT_ROWS, 3 * D), lambda i, frames: (i, 0)),
            ]
            + [ANYWHERE] * len(after),
            out_specs=[full_block((rows, D)), full_block((2, 2 * D))],
            scratch_shapes=[
                pltpu.VMEM((rows, 3 * D), jnp.bfloat16),
                pltpu.VMEM((rows, D), jnp.float32),
            ],
        ),
        out_shape=[
            jax.ShapeDtypeStruct((rows, D), jnp.bfloat16),
            jax.ShapeDtypeStruct((2, 2 * D), jnp.float32),
        ],
        compiler_params=pltpu.CompilerParams(
            vmem_limit_bytes=VMEM_LIMIT, dimension_semantics=("arbitrary",)
        ),
        cost_estimate=cost(6),
        name="first_back",
    )(info, d_qkv, tokens_here, modulation, d_middle, qkv_weight, *after)


def add_split(keep, got, axis, bit):
    def pick(which):
        return (
            lax.dynamic_index_in_dim(keep, which, axis, keepdims=False).astype(jnp.float32)
            + lax.dynamic_index_in_dim(got, which, axis, keepdims=False).astype(jnp.float32)
        ).astype(jnp.bfloat16)

    return pick(bit), pick(1 - bit)


def qkv_part_kernel(info_ref, first_refs, grad_ref, keep_ref, send_ref):
    pieces = [(ref, piece) for ref in first_refs for piece in range(ref.shape[0])]
    total = None
    for place, (ref, piece) in enumerate(pieces):
        update = lax.dot_general(
            ref[piece],
            grad_ref[info_ref[ORDER_AT + place]],
            (((0,), (0,)), ((), ())),
            preferred_element_type=jnp.float32,
        )
        total = update if total is None else total + update
    groups, clip_pairs, share, width = keep_ref.shape
    split = total.astype(jnp.bfloat16).reshape(groups, clip_pairs, 2, share, width)
    low, high = split[:, :, 0], split[:, :, 1]
    keep_ref[...] = jnp.where(info_ref[BITS_AT] == 0, low, high)
    send_ref[...] = jnp.where(info_ref[BITS_AT] == 0, high, low)


def qkv_parts(info, firsts, d_heads, share):
    vmem = pl.BlockSpec(memory_space=pltpu.VMEM)
    shape = (D // LANES, 2, share, d_heads.shape[2])

    def kernel(info_ref, *refs):
        count = len(firsts)
        qkv_part_kernel(info_ref, refs[:count], refs[count], *refs[count + 1 :])

    return pl.pallas_call(
        kernel,
        in_specs=[pl.BlockSpec(memory_space=pltpu.SMEM)]
        + [vmem] * (len(firsts) + 1),
        out_specs=[vmem] * 2,
        out_shape=[jax.ShapeDtypeStruct(shape, jnp.bfloat16)] * 2,
        compiler_params=pltpu.CompilerParams(vmem_limit_bytes=VMEM_LIMIT),
        cost_estimate=cost(2),
        name="qkv_parts",
    )(info, *firsts, d_heads)


def fold_kernel(bits, info_ref, keep_a, got_a, keep_b, got_b, *refs):
    out_refs = refs[-4:]
    for place, (keep, got) in enumerate(((keep_a, got_a), (keep_b, got_b))):
        low, high = (
            (
                keep[0, half].astype(jnp.float32) + got[0, half].astype(jnp.float32)
            ).astype(jnp.bfloat16)
            for half in range(2)
        )
        kept, sent = out_refs[2 * place : 2 * place + 2]
        bit = info_ref[BITS_AT + bits[place]]
        kept[0] = jnp.where(bit == 0, low, high)
        sent[0] = jnp.where(bit == 0, high, low)


def fold(info, bits, keep_a, got_a, keep_b, got_b, after):
    count = keep_a.shape[0]
    parts = 1 if count > 1 else 2
    in_specs, out_specs, out_shape = [], [], []
    for keep in (keep_a, keep_b):
        rows, columns = keep.shape[2:]
        block = (rows // parts, columns)
        in_specs += [pl.BlockSpec((1, 2) + block, lambda i, j, info: (i, 0, j, 0))] * 2
        out_specs += [pl.BlockSpec((1,) + block, lambda i, j, info: (i, j, 0))] * 2
        out_shape += [jax.ShapeDtypeStruct((count, rows, columns), jnp.bfloat16)] * 2
    return pl.pallas_call(
        partial(fold_kernel, bits),
        grid_spec=pltpu.PrefetchScalarGridSpec(
            num_scalar_prefetch=1,
            grid=(count, parts),
            in_specs=in_specs + [ANYWHERE] * len(after),
            out_specs=out_specs,
        ),
        out_shape=out_shape,
        compiler_params=pltpu.CompilerParams(
            vmem_limit_bytes=VMEM_LIMIT, dimension_semantics=("arbitrary", "arbitrary")
        ),
        cost_estimate=cost(15),
        name="fold",
    )(info, keep_a, got_a, keep_b, got_b, *after)


def add_kernel(keep_ref, got_ref, *refs):
    refs[-1][...] = (
        keep_ref[...].astype(jnp.float32) + got_ref[...].astype(jnp.float32)
    ).astype(jnp.bfloat16)


def add_pair(keep, got, after):
    vmem = pl.BlockSpec(memory_space=pltpu.VMEM)
    return pl.pallas_call(
        add_kernel,
        in_specs=[vmem, vmem] + [ANYWHERE] * len(after),
        out_specs=vmem,
        out_shape=jax.ShapeDtypeStruct(keep.shape, jnp.bfloat16),
        cost_estimate=cost(1),
        name="add_pair",
    )(keep, got, *after)


def finish_kernel(jobs, keep_a, got_a, keep_b, got_b, *refs):
    row = [0, 0]
    for (unused, height, unused_at, width, tiles), target in zip(jobs, refs[-len(jobs) :]):
        for tile in range(width // TILE):
            second = tile >= tiles
            keep, got = (keep_b, got_b) if second else (keep_a, got_a)
            rows = slice(row[second], row[second] + height)
            target[:, tile * TILE : (tile + 1) * TILE] = keep[rows, :].astype(
                jnp.float32
            ) + got[rows, :].astype(jnp.float32)
            row[second] += height


def finish(jobs, parts, after):
    vmem = pl.BlockSpec(memory_space=pltpu.VMEM)
    return pl.pallas_call(
        partial(finish_kernel, jobs),
        in_specs=[vmem] * 4 + [ANYWHERE] * len(after),
        out_specs=[vmem] * len(jobs),
        out_shape=[jax.ShapeDtypeStruct((job[1], job[3]), jnp.float32) for job in jobs],
        compiler_params=pltpu.CompilerParams(vmem_limit_bytes=VMEM_LIMIT),
        cost_estimate=cost(2),
        name="finish",
    )(*(part[0] for part in parts), *after)


def halve_once(info, parts, after, bit_a, bit_b):
    keep_a, got_a, keep_b, got_b = (
        part.reshape((-1, 2) + part.shape[-2:]) for part in parts
    )
    keep_a, send_a, keep_b, send_b = fold(
        info, (bit_a, bit_b), keep_a, got_a, keep_b, got_b, after
    )
    return keep_a, swap(send_a, 2**bit_a), keep_b, swap(send_b, 2**bit_b), send_a


def local_heads(
    tokens,
    noise_levels,
    group_map,
    noise_table,
    mod_weight,
    mod_bias,
    qkv_weight,
    out_weight,
    fc1_weight,
    fc2_weight,
    out_cotangent,
):
    rows_here = 2 * PATCHES
    frame_count = group_map.shape[0]
    groups = D // LANES
    device_count = lax.axis_size(AXES)
    index = lax.axis_index(AXES)
    bits = [(index >> place) & 1 for place in range(5)]
    tables = rope_tables(frame_count)
    clip_levels = noise_levels
    for bit in (1, 2):
        clip_levels = jnp.concatenate([clip_levels, swap(clip_levels, bit)], axis=0)
    members = jnp.zeros((1,), jnp.int32)
    for bit in (16, 8, 4, 2, 1):
        members = jnp.concatenate([members, members ^ bit])
    member_slots = (2 * ((index ^ members) >> 2))[:, None] + jnp.arange(2, dtype=jnp.int32)[None, :]
    levels_all = clip_levels[(members & 3)[:, None], group_map[member_slots]].reshape(
        2 * device_count
    )
    tokens_here = tokens.reshape(rows_here, D)
    block = lax.axis_index("blk")
    piece_at = block ^ jnp.array(PIECES, jnp.int32)
    places = jnp.arange(frame_count, dtype=jnp.int32)
    piece_slots = ((2 * piece_at)[:, None] + jnp.arange(2, dtype=jnp.int32)[None, :]).reshape(-1)
    frames = jnp.sum(
        jnp.where(piece_slots[:, None] == places[None, :], group_map[None, :], 0), axis=1
    )
    slots = jnp.sum(jnp.where(group_map[None, :] == places[:, None], places[None, :], 0), axis=1)
    info = jnp.concatenate(
        [jnp.stack(bits), piece_at, frames, slots, group_map, frames[:2]]
    ).astype(jnp.int32)
    far = cross(tokens_here, 4)
    side = cross(tokens_here, 1)
    near = cross(tokens_here, 2)
    far_side, far_near, near_side = cross(far, 1), cross(far, 2), cross(side, 2)
    last = (cross(far_near[:PATCHES], 1), cross(far_side[PATCHES:], 2))
    modulation = modulate(
        noise_levels, noise_table, mod_weight, mod_bias
    )
    weight_here = own_columns(info, qkv_weight)
    projected = []
    for first_piece, pieces in (
        (0, (tokens_here,)),
        (1, (far, near, side)),
        (4, (far_side, far_near, near_side)),
        (7, (last,)),
    ):
        projected.append(project(info, modulation, weight_here, tables, first_piece, pieces))
    qkv_heads = [pair[0] for pair in projected]
    firsts = [pair[1] for pair in projected]
    att_heads, ot, lse = attend(info, qkv_heads, levels_all)
    att = lax.all_to_all(att_heads, "blk", 0, 0, tiled=True)
    layer_out, up_acts, down_acts, d_att, d_middle, d_mod_early = middle_block(
        info,
        att,
        tokens_here,
        out_cotangent.reshape(rows_here, D),
        modulation,
        out_weight,
        fc1_weight,
        fc2_weight,
    )
    grad_heads = lax.all_to_all(d_att, "blk", 0, 0, tiled=True)
    halvings, sent = [], ()
    for jobs, acts in ((UPPER_JOBS, up_acts), (LOWER_JOBS, down_acts)):
        keep_a, send_a, keep_b, send_b = weight_parts(jobs, info, acts, swap(acts, 1), sent)
        halvings.append((keep_a, swap(send_a, 2), keep_b, swap(send_b, 4)))
        sent += (send_a,)
    d_heads = attend_back(
        info, qkv_heads, grad_heads, ot, lse, tables, sent
    )
    d_qkv = lax.all_to_all(d_heads, "blk", 0, 0, tiled=True)
    share = D // device_count
    qkv_keep, qkv_send = qkv_parts(info, firsts, d_heads, share)
    qkv_keep, qkv_send = add_split(qkv_keep, swap(qkv_send, 1), 1, bits[1])
    qkv_got = swap(qkv_send, 2)
    upper = halve_once(info, halvings[0], (d_heads,), 2, 1)
    lower = halve_once(info, halvings[1], (upper[4], qkv_send), 2, 1)
    tokens_grad, d_mod_late = first_back(
        info, d_qkv, tokens_here, modulation, d_middle, qkv_weight, (lower[4],)
    )
    upper = halve_once(info, upper[:4], (d_mod_late,), 3, 3)
    qkv_sum = add_pair(qkv_keep, qkv_got, (d_mod_late,))
    qkv_columns = lax.all_to_all(qkv_sum, "blk", 0, 0, tiled=True)
    qkv_share = (
        qkv_columns.reshape(groups, share, 3, LANES)
        .transpose(1, 2, 0, 3)
        .reshape(share, 3 * D)
        .astype(jnp.float32)
    )
    lower = halve_once(info, lower[:4], (upper[4],), 3, 3)
    upper = halve_once(info, upper[:4], (lower[4],), 4, 4)
    lower = halve_once(info, lower[:4], (upper[4], qkv_columns), 4, 4)
    d_mod = jnp.concatenate([d_mod_late, d_mod_early], axis=1).astype(jnp.bfloat16)
    d_mod_all = gather_pairs(d_mod[None]).reshape(2 * device_count, 6 * D)
    level_hot = jnp.arange(LEVELS, dtype=jnp.int32)[:, None] == levels_all[None, :]
    table_columns = lax.dynamic_slice_in_dim(noise_table, index * share, share, 1)
    embedded_columns = jnp.einsum(
        "ls,lc->sc",
        level_hot.astype(jnp.bfloat16),
        table_columns,
        preferred_element_type=jnp.float32,
    )
    activated_columns, silu_pull = jax.vjp(jax.nn.silu, embedded_columns)
    modw_share = jnp.einsum(
        "sc,sk->ck",
        activated_columns.astype(jnp.bfloat16),
        d_mod_all,
        preferred_element_type=jnp.float32,
    )
    weight_rows = lax.dynamic_slice_in_dim(mod_weight, index * share, share, 0)
    d_activated = jnp.einsum("sk,ck->sc", d_mod_all, weight_rows, preferred_element_type=jnp.float32)
    d_embedded = silu_pull(d_activated)[0]
    table_share = jnp.dot(
        level_hot.astype(jnp.float32), d_embedded, precision=lax.Precision.HIGHEST
    )
    bias_columns = 6 * D // device_count
    bias_share = jnp.sum(
        lax.dynamic_slice_in_dim(d_mod_all, index * bias_columns, bias_columns, 1).astype(
            jnp.float32
        ),
        axis=0,
    )
    (upper_share,) = finish(UPPER_JOBS, upper[:4], (table_share, modw_share, bias_share))
    lower_share, outw_share = finish(LOWER_JOBS, lower[:4], (upper_share,))
    return (
        layer_out[None].reshape(1, 2, PATCHES, D),
        tokens_grad.reshape(1, 2, PATCHES, D),
        table_share,
        modw_share,
        bias_share,
        qkv_share,
        outw_share,
        upper_share,
        lower_share,
    )


def solution(mesh):
    pair_split = mesh.shape["blk"] * LANES == D and mesh.shape["clip"] == 4
    return jax.shard_map(
        local_heads if pair_split else local,
        mesh=mesh,
        in_specs=(
            P("clip", "blk", None, None),
            P("clip", None),
            P(),
            P(),
            P(),
            P(),
            P(),
            P(),
            P(),
            P(),
            P("clip", "blk", None, None),
        ),
        out_specs=(
            P("clip", "blk", None, None),
            P("clip", "blk", None, None),
            P(None, ("blk", "clip")),
            P(("blk", "clip"), None),
            P(("blk", "clip")),
            P(("blk", "clip"), None),
            P(("blk", "clip"), None),
            P(("blk", "clip"), None),
            P(("blk", "clip"), None),
        ),
        check_vma=False,
    )
```

```python
from functools import partial

import jax
import jax.numpy as jnp
import numpy as np
from jax import lax
from jax.experimental import pallas as pl
from jax.experimental.pallas import tpu as pltpu
from jax.sharding import PartitionSpec as P

D = 1024
HEAD = 64
HEADS = 16
LEVELS = 1000
GRID_H = 8
GRID_W = 16
PATCHES = 128


SCALE = 0.125
EPSILON = 1e-06
ROPE_BASE = 10000.0
NEG_LARGE = -1e30


def token_positions(frame_ids):
    slot_count = frame_ids.shape[0]
    total_rows = slot_count * GRID_H * GRID_W
    patch_ids = jnp.arange(total_rows, dtype=jnp.int32) % (GRID_H * GRID_W)
    frame_pos = jnp.repeat(frame_ids, GRID_H * GRID_W, total_repeat_length=total_rows)
    return (frame_pos, patch_ids // GRID_W, patch_ids % GRID_W)


def rope_angles(frame_pos, row_pos, col_pos):
    angle_list = []
    for position, comp_width in ((frame_pos, 16), (row_pos, 24), (col_pos, 24)):
        half_width = comp_width // 2
        frequency = ROPE_BASE ** (-2.0 * jnp.arange(half_width, dtype=jnp.float32) / comp_width)
        angle_list.append(position.astype(jnp.float32)[:, None] * frequency[None, :])
    return angle_list


def rotate(values, angle_list, direction):
    pieces = []
    offset = 0
    for angles in angle_list:
        half_width = angles.shape[1]
        first_half = values[:, :, offset : offset + half_width]
        second_half = values[:, :, offset + half_width : offset + 2 * half_width]
        cosine = jnp.cos(angles)[:, None, :]
        sine_part = direction * jnp.sin(angles)[:, None, :]
        pieces.append(first_half * cosine - second_half * sine_part)
        pieces.append(first_half * sine_part + second_half * cosine)
        offset = offset + 2 * half_width
    return jnp.concatenate(pieces, axis=2)


def normalize(values):
    center = values - jnp.mean(values, axis=-1, keepdims=True)
    inverse = lax.rsqrt(jnp.mean(center * center, axis=-1, keepdims=True) + EPSILON)
    return (center * inverse, inverse)


def norm_backward(grad_in, normed, inverse):
    return inverse * (
        grad_in
        - jnp.mean(grad_in, axis=-1, keepdims=True)
        - normed * jnp.mean(grad_in * normed, axis=-1, keepdims=True)
    )


def frames_of(group_map, first_row, row_count):
    slot_frames = lax.dynamic_slice_in_dim(group_map, first_row // PATCHES, row_count // PATCHES)
    return jnp.repeat(slot_frames, PATCHES, total_repeat_length=row_count)


def block_size(row_count, shard_rows):
    return 2 * shard_rows if row_count // shard_rows % 2 == 0 else shard_rows


def keep_same(values):
    return values


def local(
    tokens,
    noise_levels,
    group_map,
    noise_table,
    mod_weight,
    mod_bias,
    qkv_weight,
    out_weight,
    fc1_weight,
    fc2_weight,
    out_cotangent,
):
    rows_here = 2 * PATCHES
    my_frames = lax.dynamic_slice_in_dim(group_map, 2 * lax.axis_index("blk"), 2)
    frame_hot = (
        jnp.arange(group_map.shape[0], dtype=jnp.int32)[None, :] == my_frames[:, None]
    ).astype(jnp.int32)
    my_levels = jnp.sum(frame_hot * noise_levels[0][None, :], axis=1)
    level_hot = jnp.arange(LEVELS, dtype=jnp.int32)[None, :] == my_levels[:, None]
    embedded = jnp.dot(
        level_hot.astype(jnp.bfloat16), noise_table, preferred_element_type=jnp.float32
    )
    activated = jax.nn.silu(embedded).astype(jnp.bfloat16)
    modulation = (
        jnp.dot(activated, mod_weight, preferred_element_type=jnp.float32)
        + mod_bias.astype(jnp.float32)[None, :]
    )
    shift_one, scale_one, gate_one, shift_two, scale_two, gate_two = [
        modulation[:, member * D : (member + 1) * D][:, None, :] for member in range(6)
    ]
    inputs_here = tokens[0].astype(jnp.float32)
    normed_one, inverse_one = normalize(inputs_here)
    first_in = (
        (normed_one * (1.0 + scale_one) + shift_one).astype(jnp.bfloat16).reshape(rows_here, D)
    )
    qkv_lin = jnp.dot(first_in, qkv_weight, preferred_element_type=jnp.float32)
    token_frames, row_pos, col_pos = token_positions(my_frames)
    angle_list = rope_angles(token_frames, row_pos, col_pos)
    query = rotate(qkv_lin[:, :D].reshape(rows_here, HEADS, HEAD), angle_list, 1.0).astype(
        jnp.bfloat16
    )
    key_part = rotate(
        qkv_lin[:, D : 2 * D].reshape(rows_here, HEADS, HEAD), angle_list, 1.0
    ).astype(jnp.bfloat16)
    value_part = qkv_lin[:, 2 * D :].reshape(rows_here, HEADS, HEAD).astype(jnp.bfloat16)
    top_frame = jnp.max(my_frames)
    own_lowest = jnp.min(my_frames)
    forward_start = (
        jnp.full((HEADS, rows_here), NEG_LARGE, jnp.float32),
        jnp.zeros((HEADS, rows_here), jnp.float32),
        jnp.zeros((rows_here, HEADS, HEAD), jnp.float32),
    )
    first_row = jnp.int32(0)
    keys_piece = lax.all_gather(key_part, "blk", axis=0, tiled=True)
    values_piece = lax.all_gather(value_part, "blk", axis=0, tiled=True)
    piece_rows = keys_piece.shape[0]
    block_rows = block_size(piece_rows, rows_here)

    def forward_advance(turn_index, running):
        offset = turn_index * block_rows
        keys_block = lax.dynamic_slice_in_dim(keys_piece, offset, block_rows)
        values_block = lax.dynamic_slice_in_dim(values_piece, offset, block_rows)
        block_frames = frames_of(group_map, first_row + offset, block_rows)

        def attend(previous):
            top_scores, totals, accumulated = previous
            scores = (
                jnp.einsum("qhd,khd->hqk", query, keys_block, preferred_element_type=jnp.float32)
                * SCALE
            )
            allowed = block_frames[None, None, :] <= token_frames[None, :, None]
            new_top = jnp.maximum(
                top_scores, jnp.max(jnp.where(allowed, scores, NEG_LARGE), axis=2)
            )
            weights = jnp.where(allowed, jnp.exp(scores - new_top[:, :, None]), 0.0)
            factor = jnp.exp(top_scores - new_top)
            update = jnp.einsum(
                "hqk,khd->qhd",
                weights.astype(jnp.bfloat16),
                values_block,
                preferred_element_type=jnp.float32,
            )
            return (
                new_top,
                totals * factor + jnp.sum(weights, axis=2),
                accumulated * factor.T[:, :, None] + update,
            )

        return lax.cond(jnp.min(block_frames) > top_frame, keep_same, attend, running)

    top_scores, totals, accumulated = lax.fori_loop(
        0, piece_rows // block_rows, forward_advance, forward_start
    )
    attended = accumulated / totals.T[:, :, None]
    log_total = top_scores + jnp.log(totals)
    attended_low = attended.astype(jnp.bfloat16).reshape(rows_here, D)
    attn_out = jnp.dot(attended_low, out_weight, preferred_element_type=jnp.float32).reshape(
        2, PATCHES, D
    )
    middle = inputs_here + gate_one * attn_out
    normed_two, inverse_two = normalize(middle)
    second_in = (
        (normed_two * (1.0 + scale_two) + shift_two).astype(jnp.bfloat16).reshape(rows_here, D)
    )
    up_lin = jnp.dot(second_in, fc1_weight, preferred_element_type=jnp.float32)
    hidden = jax.nn.gelu(up_lin, approximate=False).astype(jnp.bfloat16)
    mlp_out = jnp.dot(hidden, fc2_weight, preferred_element_type=jnp.float32).reshape(2, PATCHES, D)
    layer_out = (middle + gate_two * mlp_out).astype(jnp.bfloat16)[None]
    cotangent = out_cotangent[0].astype(jnp.float32)
    d_gate_two = jnp.sum(cotangent * mlp_out, axis=1)
    d_mlp = (cotangent * gate_two).astype(jnp.bfloat16).reshape(rows_here, D)
    lower_part = jnp.einsum("rf,rd->fd", hidden, d_mlp, preferred_element_type=jnp.float32)
    d_hidden = jnp.einsum("rd,fd->rf", d_mlp, fc2_weight, preferred_element_type=jnp.float32)
    unused_value, gelu_pull = jax.vjp(partial(jax.nn.gelu, approximate=False), up_lin)
    d_up = gelu_pull(d_hidden)[0].astype(jnp.bfloat16)
    upper_part = jnp.einsum("rc,rf->cf", second_in, d_up, preferred_element_type=jnp.float32)
    d_second = jnp.einsum(
        "rf,cf->rc", d_up, fc1_weight, preferred_element_type=jnp.float32
    ).reshape(2, PATCHES, D)
    d_shift_two = jnp.sum(d_second, axis=1)
    d_scale_two = jnp.sum(d_second * normed_two, axis=1)
    d_middle = cotangent + norm_backward(d_second * (1.0 + scale_two), normed_two, inverse_two)
    d_gate_one = jnp.sum(d_middle * attn_out, axis=1)
    d_attn = (d_middle * gate_one).astype(jnp.bfloat16).reshape(rows_here, D)
    outw_part = jnp.einsum("rc,rd->cd", attended_low, d_attn, preferred_element_type=jnp.float32)
    d_attended = (
        jnp.einsum("rd,cd->rc", d_attn, out_weight, preferred_element_type=jnp.float32)
        .astype(jnp.bfloat16)
        .reshape(rows_here, HEADS, HEAD)
    )
    delta = jnp.sum(d_attended.astype(jnp.float32) * attended, axis=2).T
    grad_start = jnp.zeros((rows_here, HEADS, HEAD), jnp.float32)
    query_first_row = jnp.int32(0)
    query_keys_piece = lax.all_gather(key_part, "blk", axis=0, tiled=True)
    query_values_piece = lax.all_gather(value_part, "blk", axis=0, tiled=True)
    piece_rows = query_keys_piece.shape[0]
    query_block_rows = block_size(piece_rows, rows_here)

    def query_advance(turn_index, running):
        offset = turn_index * query_block_rows
        keys_block = lax.dynamic_slice_in_dim(query_keys_piece, offset, query_block_rows)
        values_block = lax.dynamic_slice_in_dim(query_values_piece, offset, query_block_rows)
        block_frames = frames_of(group_map, query_first_row + offset, query_block_rows)

        def query_accumulate(previous):
            scores = (
                jnp.einsum("qhd,khd->hqk", query, keys_block, preferred_element_type=jnp.float32)
                * SCALE
            )
            allowed = block_frames[None, None, :] <= token_frames[None, :, None]
            weights = jnp.where(allowed, jnp.exp(scores - log_total[:, :, None]), 0.0)
            weight_grad = jnp.einsum(
                "qhd,khd->hqk", d_attended, values_block, preferred_element_type=jnp.float32
            )
            score_grad = (weights * (weight_grad - delta[:, :, None]) * SCALE).astype(jnp.bfloat16)
            return previous + jnp.einsum(
                "hqk,khd->qhd", score_grad, keys_block, preferred_element_type=jnp.float32
            )

        return lax.cond(jnp.min(block_frames) > top_frame, keep_same, query_accumulate, running)

    query_grad = lax.fori_loop(0, piece_rows // query_block_rows, query_advance, grad_start)
    stats_lse, stats_delta = (
        lax.all_gather(log_total.T, "blk", axis=0, tiled=True),
        lax.all_gather(delta.T, "blk", axis=0, tiled=True),
    )
    key_first_row = jnp.int32(0)
    queries_piece = lax.all_gather(query, "blk", axis=0, tiled=True)
    grads_piece = lax.all_gather(d_attended, "blk", axis=0, tiled=True)
    piece_rows = queries_piece.shape[0]
    key_block_rows = block_size(piece_rows, rows_here)

    def key_advance(turn_index, running):
        offset = turn_index * key_block_rows
        query_block = lax.dynamic_slice_in_dim(queries_piece, offset, key_block_rows)
        grad_block = lax.dynamic_slice_in_dim(grads_piece, offset, key_block_rows)
        lse_block = lax.dynamic_slice_in_dim(stats_lse, key_first_row + offset, key_block_rows).T
        delta_block = lax.dynamic_slice_in_dim(
            stats_delta, key_first_row + offset, key_block_rows
        ).T
        block_frames = frames_of(group_map, key_first_row + offset, key_block_rows)

        def key_accumulate(previous):
            key_total, value_total = previous
            scores = (
                jnp.einsum(
                    "qhd,khd->hqk", query_block, key_part, preferred_element_type=jnp.float32
                )
                * SCALE
            )
            allowed = token_frames[None, None, :] <= block_frames[None, :, None]
            weights = jnp.where(allowed, jnp.exp(scores - lse_block[:, :, None]), 0.0)
            value_total = value_total + jnp.einsum(
                "hqk,qhd->khd",
                weights.astype(jnp.bfloat16),
                grad_block,
                preferred_element_type=jnp.float32,
            )
            weight_grad = jnp.einsum(
                "qhd,khd->hqk", grad_block, value_part, preferred_element_type=jnp.float32
            )
            score_grad = (weights * (weight_grad - delta_block[:, :, None]) * SCALE).astype(
                jnp.bfloat16
            )
            key_total = key_total + jnp.einsum(
                "hqk,qhd->khd", score_grad, query_block, preferred_element_type=jnp.float32
            )
            return (key_total, value_total)

        return lax.cond(jnp.max(block_frames) < own_lowest, keep_same, key_accumulate, running)

    key_grad, value_grad = lax.fori_loop(
        0, piece_rows // key_block_rows, key_advance, (grad_start, grad_start)
    )
    query_low = lax.optimization_barrier(query_grad.astype(jnp.bfloat16)).astype(jnp.float32)
    key_low = lax.optimization_barrier(key_grad.astype(jnp.bfloat16)).astype(jnp.float32)
    query_back = rotate(query_low, angle_list, -1.0).reshape(rows_here, D)
    key_back = rotate(key_low, angle_list, -1.0).reshape(rows_here, D)
    d_qkv = jnp.concatenate(
        [query_back, key_back, value_grad.reshape(rows_here, D)], axis=1
    ).astype(jnp.bfloat16)
    qkv_part = jnp.einsum("rc,rk->ck", first_in, d_qkv, preferred_element_type=jnp.float32)
    d_first = jnp.einsum(
        "rk,ck->rc", d_qkv, qkv_weight, preferred_element_type=jnp.float32
    ).reshape(2, PATCHES, D)
    d_shift_one = jnp.sum(d_first, axis=1)
    d_scale_one = jnp.sum(d_first * normed_one, axis=1)
    tokens_grad = (
        d_middle + norm_backward(d_first * (1.0 + scale_one), normed_one, inverse_one)
    ).astype(jnp.bfloat16)[None]
    d_mod = jnp.concatenate(
        [d_shift_one, d_scale_one, d_gate_one, d_shift_two, d_scale_two, d_gate_two], axis=1
    )
    bias_part = jnp.sum(d_mod, axis=0)
    d_mod_low = d_mod.astype(jnp.bfloat16)
    d_activated = jnp.einsum("sk,ck->sc", d_mod_low, mod_weight, preferred_element_type=jnp.float32)
    unused_silu, silu_pull = jax.vjp(jax.nn.silu, embedded)
    d_embedded = silu_pull(d_activated)[0]
    table_part = jnp.einsum(
        "sl,sc->cl", level_hot.astype(jnp.float32), d_embedded, precision=lax.Precision.HIGHEST
    )
    activated_all, d_mod_all = (
        lax.all_gather(activated, ("blk", "clip"), axis=0, tiled=True),
        lax.all_gather(d_mod_low, ("blk", "clip"), axis=0, tiled=True),
    )
    share_rows = D // lax.axis_size(("blk", "clip"))
    my_columns = lax.dynamic_slice_in_dim(
        activated_all, lax.axis_index(("blk", "clip")) * share_rows, share_rows, 1
    )
    modw_share = jnp.einsum("sc,sk->ck", my_columns, d_mod_all, preferred_element_type=jnp.float32)
    summed = (
        lax.psum_scatter(table_part, ("blk", "clip"), scatter_dimension=0, tiled=True),
        lax.psum_scatter(bias_part, ("blk", "clip"), scatter_dimension=0, tiled=True),
        lax.psum_scatter(qkv_part, ("blk", "clip"), scatter_dimension=0, tiled=True),
        lax.psum_scatter(outw_part, ("blk", "clip"), scatter_dimension=0, tiled=True),
        lax.psum_scatter(upper_part, ("blk", "clip"), scatter_dimension=0, tiled=True),
        lax.psum_scatter(lower_part, ("blk", "clip"), scatter_dimension=0, tiled=True),
    )
    return (
        layer_out,
        tokens_grad,
        summed[0].T,
        modw_share,
        summed[1],
        summed[2],
        summed[3],
        summed[4],
        summed[5],
    )


LANES = 128
FF = 4096
AXES = ("blk", "clip")
EXP_SCALE = SCALE * 1.4426950408889634
VMEM_LIMIT = 56 * 1024 * 1024
NT = (((1,), (1,)), ((), ()))
NN = (((1,), (0,)), ((), ()))


def cost(microseconds):
    return pl.CostEstimate(
        flops=int(microseconds * 1e9), bytes_accessed=int(microseconds * 3e6), transcendentals=0
    )


class Shifted:
    def __init__(self, ref, start):
        self.ref, self.start = ref, start

    def __getitem__(self, place):
        return self.ref[self.start + place]


FRAME_COUNT = 2 * D // LANES
BITS_AT, ORDER_AT = 0, 5
FRAMES_AT = ORDER_AT + D // LANES
SLOTS_AT = FRAMES_AT + FRAME_COUNT
GROUP_AT = SLOTS_AT + FRAME_COUNT
MINE_AT = GROUP_AT + FRAME_COUNT
ANYWHERE = pl.BlockSpec(memory_space=pl.ANY)


def full_block(shape):
    return pl.BlockSpec(shape, lambda *ids: (0,) * len(shape))


def rope_tables(frame_count):
    lane = np.arange(LANES) % HEAD
    pieces = []
    for comp_width in (16, 24, 24):
        half_width = comp_width // 2
        frequency = ROPE_BASE ** (-2.0 * np.arange(half_width) / comp_width)
        pieces += [frequency, frequency]
    frequency = np.tile(np.concatenate(pieces), LANES // HEAD)[None, :]
    first = (lane < 8) | ((lane >= 16) & (lane < 28)) | ((lane >= 40) & (lane < 52))
    sign = np.where(first, -1.0, 1.0)[None, :]
    in_frame = (lane < 16)[None, :]
    in_row = (lane < 40)[None, :]
    frame_angle = np.arange(frame_count)[:, None] * frequency
    patch = np.arange(PATCHES)[:, None]
    place_angle = np.where(in_row, patch // GRID_W, patch % GRID_W) * frequency
    tables = (
        np.where(in_frame, np.cos(frame_angle), 0.0),
        np.where(in_frame, sign * np.sin(frame_angle), 0.0),
        np.where(in_frame, 0.0, np.cos(place_angle)),
        np.where(in_frame, 0.0, sign * np.sin(place_angle)),
    )
    return tuple(jnp.asarray(table, jnp.float32) for table in tables)


def partner_lanes(values):
    lane = lax.broadcasted_iota(jnp.int32, values.shape, 1) % HEAD
    ahead_eight = pltpu.roll(values, LANES - 8, 1)
    behind_eight = pltpu.roll(values, 8, 1)
    ahead_twelve = pltpu.roll(values, LANES - 12, 1)
    behind_twelve = pltpu.roll(values, 12, 1)
    ahead = ((lane >= 16) & (lane < 28)) | ((lane >= 40) & (lane < 52))
    return jnp.where(
        lane < 8,
        ahead_eight,
        jnp.where(lane < 16, behind_eight, jnp.where(ahead, ahead_twelve, behind_twelve)),
    )


def modulation_kernel(levels_ref, table_ref, weight_ref, bias_ref, out_ref, activated_ref):
    @pl.when(pl.program_id(0) == 0)
    def _():
        count = levels_ref.shape[1]
        hot = lax.broadcasted_iota(jnp.int32, (LEVELS, count), 0) == levels_ref[...]
        embedded = lax.dot_general(
            jnp.where(hot, 1.0, 0.0).astype(jnp.bfloat16),
            table_ref[...],
            (((0,), (0,)), ((), ())),
            preferred_element_type=jnp.float32,
        )
        activated_ref[...] = jax.nn.silu(embedded).astype(jnp.bfloat16)

    out_ref[...] = lax.dot_general(
        activated_ref[...], weight_ref[...], NN, preferred_element_type=jnp.float32
    ) + bias_ref[...].astype(jnp.float32)[None, :]


def modulate(levels, noise_table, mod_weight, mod_bias):
    frame_count = levels.shape[1]
    return pl.pallas_call(
        modulation_kernel,
        grid=(6,),
        in_specs=[
            full_block(levels.shape),
            full_block(noise_table.shape),
            pl.BlockSpec((D, D), lambda i: (0, i)),
            pl.BlockSpec((D,), lambda i: (i,)),
        ],
        out_specs=pl.BlockSpec((frame_count, D), lambda i: (0, i)),
        out_shape=jax.ShapeDtypeStruct((frame_count, 6 * D), jnp.float32),
        scratch_shapes=[pltpu.VMEM((frame_count, D), jnp.bfloat16)],
        compiler_params=pltpu.CompilerParams(
            vmem_limit_bytes=VMEM_LIMIT, dimension_semantics=("arbitrary",)
        ),
        cost_estimate=cost(7),
        name="modulate",
    )(levels, noise_table, mod_weight, mod_bias)


def copy_kernel(info_ref, source_ref, target_ref):
    target_ref[...] = source_ref[...]


def own_columns(info, weight):
    return pl.pallas_call(
        copy_kernel,
        grid_spec=pltpu.PrefetchScalarGridSpec(
            num_scalar_prefetch=1,
            grid=(3,),
            in_specs=[
                pl.BlockSpec((D, LANES), lambda i, info: (0, i * (D // LANES) + info[ORDER_AT]))
            ],
            out_specs=pl.BlockSpec((D, LANES), lambda i, info: (0, i)),
        ),
        out_shape=jax.ShapeDtypeStruct((D, 3 * LANES), jnp.bfloat16),
        compiler_params=pltpu.CompilerParams(dimension_semantics=("arbitrary",)),
        cost_estimate=cost(2),
        name="own_columns",
    )(info, weight)


def project_kernel(
    count,
    first_piece,
    info_ref,
    mod_ref,
    weight_ref,
    fcos_ref,
    fsin_ref,
    pcos_ref,
    psin_ref,
    *refs,
):
    frames_ref = Shifted(info_ref, FRAMES_AT)
    halves, out_ref, first_ref = refs[: 2 * count], refs[-2], refs[-1]
    for piece in range(count):
        for half in range(2):
            source, place = halves[2 * piece + half]
            rows = slice(half * PATCHES, (half + 1) * PATCHES)
            frame = frames_ref[2 * (first_piece + piece) + half]
            normed, unused = normalize(
                source[place * PATCHES : (place + 1) * PATCHES, :].astype(jnp.float32)
            )
            shift = mod_ref[pl.ds(frame, 1), :D]
            scale = mod_ref[pl.ds(frame, 1), D : 2 * D]
            first_ref[piece, rows, :] = (normed * (1.0 + scale) + shift).astype(jnp.bfloat16)
        linear = lax.dot_general(
            first_ref[piece], weight_ref[...], NN, preferred_element_type=jnp.float32
        )
        for half in range(2):
            rows = slice(half * PATCHES, (half + 1) * PATCHES)
            frame = frames_ref[2 * (first_piece + piece) + half]
            cosine = pcos_ref[...] + fcos_ref[pl.ds(frame, 1), :]
            sine = psin_ref[...] + fsin_ref[pl.ds(frame, 1), :]
            for part in range(2):
                columns = slice(part * LANES, (part + 1) * LANES)
                values = linear[rows, columns]
                turned = values * cosine + partner_lanes(values) * sine
                out_ref[piece, rows, columns] = turned.astype(jnp.bfloat16)
            out_ref[piece, rows, 2 * LANES :] = linear[rows, 2 * LANES :].astype(jnp.bfloat16)


def project(info, modulation, weight, tables, first_piece, pieces):
    vmem = pl.BlockSpec(memory_space=pltpu.VMEM)
    count = len(pieces)
    arrays, sources = [], []
    for piece in pieces:
        if isinstance(piece, tuple):
            sources += [(len(arrays), 0), (len(arrays) + 1, 0)]
            arrays += list(piece)
        else:
            sources += [(len(arrays), 0), (len(arrays), 1)]
            arrays.append(piece)

    def kernel(*refs):
        inputs = refs[7 : 7 + len(arrays)]
        halves = [(inputs[which], place) for which, place in sources]
        project_kernel(count, first_piece, *refs[:7], *halves, *refs[7 + len(arrays) :])

    rows = 2 * PATCHES
    return pl.pallas_call(
        kernel,
        in_specs=[pl.BlockSpec(memory_space=pltpu.SMEM)] + [vmem] * (6 + len(arrays)),
        out_specs=[vmem] * 2,
        out_shape=[
            jax.ShapeDtypeStruct((count, rows, 3 * LANES), jnp.bfloat16),
            jax.ShapeDtypeStruct((count, rows, D), jnp.bfloat16),
        ],
        compiler_params=pltpu.CompilerParams(vmem_limit_bytes=VMEM_LIMIT),
        cost_estimate=cost(2 * count),
        name="project",
    )(info, modulation, weight, *tables, *arrays)


def head_stack(values):
    lane = lax.broadcasted_iota(jnp.int32, values.shape, 1)
    zero = jnp.zeros_like(values)
    return jnp.concatenate(
        [jnp.where(lane < HEAD, values, zero), jnp.where(lane < HEAD, zero, values)], axis=0
    )


def hidden_keys(shape):
    key_row = lax.broadcasted_iota(jnp.int32, shape, 0)
    query_column = lax.broadcasted_iota(jnp.int32, shape, 1) % (2 * PATCHES)
    return (key_row >= PATCHES) & (query_column < PATCHES)


def own_heads(values):
    rows = 2 * PATCHES
    return jnp.concatenate([values[:HEAD, :rows], values[HEAD:LANES, rows:]], axis=0)


def by_frame(frames_ref, source_refs, target_refs):
    pieces = [(ref, piece) for ref in source_refs for piece in range(ref.shape[0])]
    for place, (ref, piece) in enumerate(pieces):
        for half in range(2):
            frame = frames_ref[2 * place + half]
            rows = pl.ds(pl.multiple_of(frame * PATCHES, PATCHES), PATCHES)
            for part, target in enumerate(target_refs):
                target[rows, :] = ref[
                    piece,
                    half * PATCHES : (half + 1) * PATCHES,
                    part * LANES : (part + 1) * LANES,
                ]


def attend_kernel(info_ref, qkv_refs, att_ref, ot_ref, lse_ref, q_ref, k_ref, v_ref, vt_ref):
    token_count = q_ref.shape[0]
    frames_ref, slots_ref = Shifted(info_ref, FRAMES_AT), Shifted(info_ref, SLOTS_AT)
    by_frame(frames_ref, qkv_refs, (q_ref, k_ref, v_ref))
    vt_ref[:LANES, :] = v_ref[...].T
    vt_ref[LANES:, :] = jnp.ones((vt_ref.shape[0] - LANES, token_count), jnp.bfloat16)
    step = 2 * PATCHES
    for turn in range(token_count // step):
        here = slice(turn * step, (turn + 1) * step)
        queries = head_stack(q_ref[here, :])
        ranges = [here] if turn == 0 else [slice(0, turn * step), here]
        raw = [
            lax.dot_general(k_ref[keys, :], queries, NT, preferred_element_type=jnp.float32)
            for keys in ranges
        ]
        raw[-1] = jnp.where(hidden_keys(raw[-1].shape), NEG_LARGE, raw[-1])
        top = jnp.max(raw[-1], axis=0, keepdims=True)
        for part in raw[:-1]:
            top = jnp.maximum(top, jnp.max(part, axis=0, keepdims=True))
        top = top * EXP_SCALE
        summed = None
        for keys, part in zip(ranges, raw):
            weights = jnp.exp2(part * EXP_SCALE - top).astype(jnp.bfloat16)
            update = lax.dot_general(
                vt_ref[:, keys], weights, NN, preferred_element_type=jnp.float32
            )
            summed = update if summed is None else summed + update
        totals = summed[LANES : LANES + 1, :]
        lse_ref[turn : turn + 1, :] = top + jnp.log2(totals)
        out = own_heads(summed[:LANES, :] / totals)
        ot_ref[:, here] = out
        rounded = out.T.astype(jnp.bfloat16)
        for half in range(2):
            slot = slots_ref[2 * turn + half]
            rows = pl.ds(pl.multiple_of(slot % 2 * PATCHES, PATCHES), PATCHES)
            att_ref[slot // 2, rows, :] = rounded[half * PATCHES : (half + 1) * PATCHES, :]


def attend(info, qkv, after):
    token_count = FRAME_COUNT * PATCHES
    turns = token_count // (2 * PATCHES)
    vmem = pl.BlockSpec(memory_space=pltpu.VMEM)

    def kernel(info_ref, *refs):
        attend_kernel(info_ref, refs[: len(qkv)], *refs[len(qkv) + 1 :])

    return pl.pallas_call(
        kernel,
        in_specs=[pl.BlockSpec(memory_space=pltpu.SMEM)] + [vmem] * len(qkv) + [ANYWHERE],
        out_specs=[vmem] * 3,
        out_shape=[
            jax.ShapeDtypeStruct((turns, 2 * PATCHES, LANES), jnp.bfloat16),
            jax.ShapeDtypeStruct((LANES, token_count), jnp.float32),
            jax.ShapeDtypeStruct((turns, 4 * PATCHES), jnp.float32),
        ],
        scratch_shapes=[pltpu.VMEM((token_count, LANES), jnp.bfloat16)] * 3
        + [pltpu.VMEM((LANES + 16, token_count), jnp.bfloat16)],
        compiler_params=pltpu.CompilerParams(vmem_limit_bytes=VMEM_LIMIT),
        cost_estimate=cost(10),
        name="attend",
    )(info, *qkv, after)


def attend_back_kernel(
    info_ref,
    grad_ref,
    ot_ref,
    lse_ref,
    fcos_ref,
    fsin_ref,
    pcos_ref,
    psin_ref,
    qkv_refs,
    out_ref,
    q_ref,
    k_ref,
    v_ref,
    d_ref,
    kt_ref,
    dk_ref,
    dv_ref,
):
    token_count = q_ref.shape[0]
    frames_ref, slot_frames_ref, slots_ref = (
        Shifted(info_ref, place) for place in (FRAMES_AT, GROUP_AT, SLOTS_AT)
    )
    by_frame(frames_ref, qkv_refs, (q_ref, k_ref, v_ref))
    by_frame(slot_frames_ref, (grad_ref,), (d_ref,))
    kt_ref[...] = k_ref[...].T
    step = 2 * PATCHES

    def put(frame, part, values):
        slot = slots_ref[frame]
        rows = pl.ds(pl.multiple_of(slot % 2 * PATCHES, PATCHES), PATCHES)
        out_ref[slot // 2, rows, part * LANES : (part + 1) * LANES] = values

    def turn_back(frame, values):
        values = values.astype(jnp.bfloat16).astype(jnp.float32)
        cosine = pcos_ref[...] + fcos_ref[frame : frame + 1, :]
        sine = psin_ref[...] + fsin_ref[frame : frame + 1, :]
        return (values * cosine - partner_lanes(values) * sine).astype(jnp.bfloat16)

    for turn in range(token_count // step):
        here = slice(turn * step, (turn + 1) * step)
        queries = head_stack(q_ref[here, :])
        grads_here = d_ref[here, :]
        grads = head_stack(grads_here)
        product = grads_here.astype(jnp.float32).T * ot_ref[:, here]
        delta = jnp.concatenate(
            [
                jnp.sum(product[:HEAD, :], axis=0, keepdims=True),
                jnp.sum(product[HEAD:, :], axis=0, keepdims=True),
            ],
            axis=1,
        )
        lse = lse_ref[turn : turn + 1, :]
        ranges = [here] if turn == 0 else [here, slice(0, turn * step)]
        total = None
        for keys in ranges:
            raw = lax.dot_general(
                k_ref[keys, :], queries, NT, preferred_element_type=jnp.float32
            )
            weights = jnp.exp2(raw * EXP_SCALE - lse)
            if keys is here:
                weights = jnp.where(hidden_keys(weights.shape), 0.0, weights)
            weight_grad = lax.dot_general(
                v_ref[keys, :], grads, NT, preferred_element_type=jnp.float32
            )
            score_grad = (weights * (weight_grad - delta)).astype(jnp.bfloat16)
            value_part = lax.dot_general(
                weights.astype(jnp.bfloat16), grads, NN, preferred_element_type=jnp.float32
            )
            key_part = lax.dot_general(
                score_grad, queries, NN, preferred_element_type=jnp.float32
            )
            if keys is here:
                dv_ref[keys, :] = value_part
                dk_ref[keys, :] = key_part
            else:
                dv_ref[keys, :] += value_part
                dk_ref[keys, :] += key_part
            update = lax.dot_general(
                kt_ref[:, keys], score_grad, NN, preferred_element_type=jnp.float32
            )
            total = update if total is None else total + update
        query_grad = own_heads(total).T * SCALE
        for half in range(2):
            put(
                2 * turn + half,
                0,
                turn_back(2 * turn + half, query_grad[half * PATCHES : (half + 1) * PATCHES, :]),
            )
    for frame in range(token_count // PATCHES):
        rows = slice(frame * PATCHES, (frame + 1) * PATCHES)
        put(frame, 1, turn_back(frame, dk_ref[rows, :] * SCALE))
        put(frame, 2, dv_ref[rows, :].astype(jnp.bfloat16))


def attend_back(info, qkv, grads, ot, lse, tables, after):
    token_count = FRAME_COUNT * PATCHES
    smem = pl.BlockSpec(memory_space=pltpu.SMEM)
    vmem = pl.BlockSpec(memory_space=pltpu.VMEM)

    def kernel(*refs):
        outs = 8 + len(qkv) + len(after)
        attend_back_kernel(*refs[:8], refs[8 : 8 + len(qkv)], *refs[outs:])

    return pl.pallas_call(
        kernel,
        in_specs=[smem] + [vmem] * (7 + len(qkv)) + [ANYWHERE] * len(after),
        out_specs=vmem,
        out_shape=jax.ShapeDtypeStruct(
            (token_count // (2 * PATCHES), 2 * PATCHES, 3 * LANES), jnp.bfloat16
        ),
        scratch_shapes=[pltpu.VMEM((token_count, LANES), jnp.bfloat16)] * 4
        + [pltpu.VMEM((LANES, token_count), jnp.bfloat16)]
        + [pltpu.VMEM((token_count, LANES), jnp.float32)] * 2,
        compiler_params=pltpu.CompilerParams(vmem_limit_bytes=VMEM_LIMIT),
        cost_estimate=cost(8),
        name="attend_back",
    )(info, grads, ot, lse, *tables, *qkv, *after)


def swap(values, bit):
    count = lax.axis_size(AXES)
    return lax.ppermute(values, AXES, [(index, index ^ bit) for index in range(count)])


PIECES = (0, 4, 2, 1, 5, 6, 3, 7)


def cross(values, bit):
    count = lax.axis_size("blk")
    return lax.ppermute(values, "blk", [(place, place ^ bit) for place in range(count)])


SECOND_AT, ATTENDED_AT, ATTN_AT, UP_AT, UP_ACTS = 0, D, 2 * D, 3 * D, 3 * D + FF
MLP_AT, HIDDEN_AT, DOWN_ACTS = 0, D, D + FF
FF_TILE = 512


def middle_kernel(
    info_ref,
    att_ref,
    tokens_ref,
    cot_ref,
    mod_ref,
    ow_ref,
    up_ref,
    down_ref,
    layer_ref,
    upper_ref,
    lower_ref,
    datt_ref,
    dmid_ref,
    dmod_ref,
    attn_ref,
    mid_ref,
    mlp_ref,
    dsec_ref,
):
    step = pl.program_id(0)
    slot_rows = [slice(slot * PATCHES, (slot + 1) * PATCHES) for slot in range(2)]

    def member(slot, which):
        return mod_ref[pl.ds(info_ref[MINE_AT + slot], 1), which * D : (which + 1) * D]

    @pl.when(step == 0)
    def _():
        for group in range(D // LANES):
            upper_ref[:, ATTENDED_AT + group * LANES : ATTENDED_AT + (group + 1) * LANES] = att_ref[
                group
            ]
        attn_ref[...] = lax.dot_general(
            upper_ref[:, ATTENDED_AT : ATTENDED_AT + D],
            ow_ref[...],
            NN,
            preferred_element_type=jnp.float32,
        )
        for slot, rows in enumerate(slot_rows):
            middle = tokens_ref[rows, :].astype(jnp.float32) + member(slot, 2) * attn_ref[rows, :]
            mid_ref[rows, :] = middle
            normed, unused = normalize(middle)
            upper_ref[rows, SECOND_AT : SECOND_AT + D] = (
                normed * (1.0 + member(slot, 4)) + member(slot, 3)
            ).astype(jnp.bfloat16)
            lower_ref[rows, MLP_AT : MLP_AT + D] = (
                cot_ref[rows, :].astype(jnp.float32) * member(slot, 5)
            ).astype(jnp.bfloat16)
        mlp_ref[...] = jnp.zeros_like(mlp_ref)
        dsec_ref[...] = jnp.zeros_like(dsec_ref)

    up_lin = lax.dot_general(
        upper_ref[:, SECOND_AT : SECOND_AT + D],
        up_ref[...],
        NN,
        preferred_element_type=jnp.float32,
    )
    below = 0.5 + 0.5 * lax.erf(up_lin * 0.7071067811865476)
    density = jnp.exp(up_lin * up_lin * -0.5) * 0.3989422804014327
    hidden = (up_lin * below).astype(jnp.bfloat16)
    d_hidden = lax.dot_general(
        lower_ref[:, MLP_AT : MLP_AT + D], down_ref[...], NT, preferred_element_type=jnp.float32
    )
    d_up = (d_hidden * (below + up_lin * density)).astype(jnp.bfloat16)
    lower_ref[:, pl.ds(pl.multiple_of(HIDDEN_AT + step * FF_TILE, FF_TILE), FF_TILE)] = hidden
    upper_ref[:, pl.ds(pl.multiple_of(UP_AT + step * FF_TILE, FF_TILE), FF_TILE)] = d_up
    mlp_ref[...] += lax.dot_general(
        hidden, down_ref[...], NN, preferred_element_type=jnp.float32
    )
    dsec_ref[...] += lax.dot_general(d_up, up_ref[...], NT, preferred_element_type=jnp.float32)

    @pl.when(step == pl.num_programs(0) - 1)
    def _():
        for slot, rows in enumerate(slot_rows):
            middle = mid_ref[rows, :]
            mlp_out = mlp_ref[rows, :]
            cotangent = cot_ref[rows, :].astype(jnp.float32)
            layer_ref[rows, :] = (middle + member(slot, 5) * mlp_out).astype(jnp.bfloat16)
            normed, inverse = normalize(middle)
            d_second = dsec_ref[rows, :]
            d_middle = cotangent + norm_backward(
                d_second * (1.0 + member(slot, 4)), normed, inverse
            )
            dmid_ref[rows, :] = d_middle
            upper_ref[rows, ATTN_AT : ATTN_AT + D] = (d_middle * member(slot, 2)).astype(
                jnp.bfloat16
            )
            for place, values in enumerate(
                (d_middle * attn_ref[rows, :], d_second, d_second * normed, cotangent * mlp_out)
            ):
                dmod_ref[slot : slot + 1, place * D : (place + 1) * D] = jnp.sum(
                    values, axis=0, keepdims=True
                )
        d_attended = lax.dot_general(
            upper_ref[:, ATTN_AT : ATTN_AT + D],
            ow_ref[...],
            NT,
            preferred_element_type=jnp.float32,
        ).astype(jnp.bfloat16)
        for group in range(D // LANES):
            datt_ref[group] = d_attended[:, group * LANES : (group + 1) * LANES]


def middle_block(info, att, tokens_here, cot_here, modulation, out_weight, fc1_weight, fc2_weight):
    rows = tokens_here.shape[0]
    return pl.pallas_call(
        middle_kernel,
        grid_spec=pltpu.PrefetchScalarGridSpec(
            num_scalar_prefetch=1,
            grid=(FF // FF_TILE,),
            in_specs=[
                full_block(att.shape),
                full_block((rows, D)),
                full_block((rows, D)),
                full_block(modulation.shape),
                full_block((D, D)),
                pl.BlockSpec((D, FF_TILE), lambda f, frames: (0, f)),
                pl.BlockSpec((FF_TILE, D), lambda f, frames: (f, 0)),
            ],
            out_specs=[
                full_block((rows, D)),
                full_block((rows, UP_ACTS)),
                full_block((rows, DOWN_ACTS)),
                full_block(att.shape),
                full_block((rows, D)),
                full_block((2, 4 * D)),
            ],
            scratch_shapes=[pltpu.VMEM((rows, D), jnp.float32)] * 4,
        ),
        out_shape=[
            jax.ShapeDtypeStruct((rows, D), jnp.bfloat16),
            jax.ShapeDtypeStruct((rows, UP_ACTS), jnp.bfloat16),
            jax.ShapeDtypeStruct((rows, DOWN_ACTS), jnp.bfloat16),
            jax.ShapeDtypeStruct(att.shape, jnp.bfloat16),
            jax.ShapeDtypeStruct((rows, D), jnp.float32),
            jax.ShapeDtypeStruct((2, 4 * D), jnp.float32),
        ],
        compiler_params=pltpu.CompilerParams(
            vmem_limit_bytes=VMEM_LIMIT, dimension_semantics=("arbitrary",)
        ),
        cost_estimate=cost(21),
        name="middle_block",
    )(info, att, tokens_here, cot_here, modulation, out_weight, fc1_weight, fc2_weight)


CHIPS = 16
TILE = 256
FINE = D // CHIPS // 2
UPPER_JOBS = ((SECOND_AT, FINE, UP_AT, FF, 10), (ATTENDED_AT, FINE, ATTN_AT, D, 2))
LOWER_JOBS = ((HIDDEN_AT, LANES, MLP_AT, D, 2),)
RIDER_ROWS = 4 * FINE


def rows_of(jobs):
    first = sum(height * tiles for unused, height, unused_at, width, tiles in jobs)
    return first, sum(job[1] * (job[3] // TILE) for job in jobs) - first


def weight_kernel(jobs, info_ref, mine_ref, theirs_ref, *refs):
    keep_a, send_a, keep_b, send_b = refs[-4 - len(jobs) : -len(jobs)]
    left_refs = refs[-len(jobs) :]
    core, xbit, ybit = (info_ref[BITS_AT + place] for place in range(3))
    rows = mine_ref.shape[0]
    row_a = row_b = 0
    for (left_at, height, right_at, width, tiles), left_ref in zip(jobs, left_refs):
        for place, ref in enumerate((mine_ref, theirs_ref)):
            columns = slice(place * rows, (place + 1) * rows)
            if height == LANES:
                for chip in range(CHIPS):
                    source = pl.multiple_of(left_at + (2 * chip + core) * LANES, LANES)
                    left_ref[chip * LANES : (chip + 1) * LANES, columns] = ref[
                        :, pl.ds(source, LANES)
                    ].T
            else:
                turned = ref[:, left_at : left_at + D].T.reshape(CHIPS, 2, height, rows)
                left_ref[:, columns] = jnp.where(core == 0, turned[:, 0], turned[:, 1]).reshape(
                    CHIPS * height, rows
                )
        for tile in range(width // TILE):
            source = right_at + tile * TILE
            right = jnp.concatenate(
                [mine_ref[:, source : source + TILE], theirs_ref[:, source : source + TILE]],
                axis=0,
            )
            part = lax.dot_general(
                left_ref[...], right, NN, preferred_element_type=jnp.float32
            ).astype(jnp.bfloat16)
            if tile < tiles:
                part = part.reshape(CHIPS // 2, 2, height, TILE)
                low, high = part[:, 0], part[:, 1]
                out_rows = slice(row_a, row_a + height)
                keep_a[:, out_rows, :] = jnp.where(xbit == 0, low, high)
                send_a[:, out_rows, :] = jnp.where(xbit == 0, high, low)
                row_a += height
            else:
                part = part.reshape(CHIPS // 4, 2, 2, height, TILE)
                low, high = part[:, 0], part[:, 1]
                out_rows = slice(row_b, row_b + height)
                keep_b[:, :, out_rows, :] = jnp.where(ybit == 0, low, high)
                send_b[:, :, out_rows, :] = jnp.where(ybit == 0, high, low)
                row_b += height


def weight_parts(jobs, info, mine, theirs, after, expense):
    rows = mine.shape[0]
    vmem = pl.BlockSpec(memory_space=pltpu.VMEM)
    rows_a, rows_b = rows_of(jobs)
    first = jax.ShapeDtypeStruct((CHIPS // 2, rows_a, TILE), jnp.bfloat16)
    second = jax.ShapeDtypeStruct((CHIPS // 4, 2, rows_b, TILE), jnp.bfloat16)
    return pl.pallas_call(
        partial(weight_kernel, jobs),
        in_specs=[pl.BlockSpec(memory_space=pltpu.SMEM), vmem, vmem] + [ANYWHERE] * len(after),
        out_specs=[vmem] * 4,
        out_shape=[first, first, second, second],
        scratch_shapes=[pltpu.VMEM((CHIPS * job[1], 2 * rows), jnp.bfloat16) for job in jobs],
        compiler_params=pltpu.CompilerParams(vmem_limit_bytes=VMEM_LIMIT),
        cost_estimate=cost(expense),
        name="weight_parts",
    )(info, mine, theirs, *after)


WEIGHT_ROWS = 256
QUARTER = 6 * D // 4


def first_back_kernel(
    info_ref,
    dqkv_ref,
    tokens_ref,
    mod_ref,
    dmid_ref,
    early_ref,
    weight_ref,
    *refs,
):
    grad_ref, packed_ref, flat_ref, total_ref, wide_ref = refs[-5:]
    step = pl.program_id(0)

    @pl.when(step == 0)
    def _():
        for group in range(D // LANES):
            for part in range(3):
                column = part * D + group * LANES
                flat_ref[:, column : column + LANES] = dqkv_ref[
                    group, :, part * LANES : (part + 1) * LANES
                ]

    columns = pl.ds(pl.multiple_of(step * WEIGHT_ROWS, WEIGHT_ROWS), WEIGHT_ROWS)
    total_ref[:, columns] = lax.dot_general(
        flat_ref[...], weight_ref[...], NT, preferred_element_type=jnp.float32
    )

    @pl.when(step == pl.num_programs(0) - 1)
    def _():
        for slot in range(2):
            rows = slice(slot * PATCHES, (slot + 1) * PATCHES)
            normed, inverse = normalize(tokens_ref[rows, :].astype(jnp.float32))
            d_first = total_ref[rows, :]
            scale = mod_ref[pl.ds(info_ref[MINE_AT + slot], 1), D : 2 * D]
            grad_ref[rows, :] = (
                dmid_ref[rows, :] + norm_backward(d_first * (1.0 + scale), normed, inverse)
            ).astype(jnp.bfloat16)
            pieces = (
                (0, jnp.sum(d_first, axis=0, keepdims=True)),
                (D, jnp.sum(d_first * normed, axis=0, keepdims=True)),
                (2 * D, early_ref[slot : slot + 1, :]),
            )
            for start, piece in pieces:
                for quarter in range(4):
                    low = max(start, quarter * QUARTER)
                    high = min(start + piece.shape[1], (quarter + 1) * QUARTER)
                    if low < high:
                        wide_ref[
                            2 * quarter + slot : 2 * quarter + slot + 1,
                            low - quarter * QUARTER : high - quarter * QUARTER,
                        ] = piece[:, low - start : high - start]
        packed_ref[...] = wide_ref[...].astype(jnp.bfloat16)


def first_back(info, d_qkv, tokens_here, modulation, d_middle, early, qkv_weight, after):
    rows = tokens_here.shape[0]
    return pl.pallas_call(
        first_back_kernel,
        grid_spec=pltpu.PrefetchScalarGridSpec(
            num_scalar_prefetch=1,
            grid=(D // WEIGHT_ROWS,),
            in_specs=[
                full_block(d_qkv.shape),
                full_block((rows, D)),
                full_block(modulation.shape),
                full_block((rows, D)),
                full_block(early.shape),
                pl.BlockSpec((WEIGHT_ROWS, 3 * D), lambda i, frames: (i, 0)),
            ]
            + [ANYWHERE] * len(after),
            out_specs=[full_block((rows, D)), full_block((8, QUARTER))],
            scratch_shapes=[
                pltpu.VMEM((rows, 3 * D), jnp.bfloat16),
                pltpu.VMEM((rows, D), jnp.float32),
                pltpu.VMEM((8, QUARTER), jnp.float32),
            ],
        ),
        out_shape=[
            jax.ShapeDtypeStruct((rows, D), jnp.bfloat16),
            jax.ShapeDtypeStruct((8, QUARTER), jnp.bfloat16),
        ],
        compiler_params=pltpu.CompilerParams(
            vmem_limit_bytes=VMEM_LIMIT, dimension_semantics=("arbitrary",)
        ),
        cost_estimate=cost(6),
        name="first_back",
    )(info, d_qkv, tokens_here, modulation, d_middle, early, qkv_weight, *after)


def pick_split(values, axis, bit):
    return tuple(
        lax.dynamic_index_in_dim(values, which, axis, keepdims=False) for which in (bit, 1 - bit)
    )


def qkv_part_kernel(info_ref, first_refs, grad_ref, keep_ref, send_ref):
    pieces = [(ref, piece) for ref in first_refs for piece in range(ref.shape[0])]
    total = None
    for place, (ref, piece) in enumerate(pieces):
        update = lax.dot_general(
            ref[piece],
            grad_ref[info_ref[ORDER_AT + place]],
            (((0,), (0,)), ((), ())),
            preferred_element_type=jnp.float32,
        )
        total = update if total is None else total + update
    groups, clip_pairs, share, width = keep_ref.shape
    split = total.astype(jnp.bfloat16).reshape(groups, clip_pairs, 2, share, width)
    low, high = split[:, :, 0], split[:, :, 1]
    keep_ref[...] = jnp.where(info_ref[BITS_AT] == 0, low, high)
    send_ref[...] = jnp.where(info_ref[BITS_AT] == 0, high, low)


def qkv_parts(info, firsts, d_heads, share, after):
    vmem = pl.BlockSpec(memory_space=pltpu.VMEM)
    shape = (D // LANES, 2, share, d_heads.shape[2])

    def kernel(info_ref, *refs):
        count = len(firsts)
        qkv_part_kernel(info_ref, refs[:count], refs[count], *refs[-2:])

    return pl.pallas_call(
        kernel,
        in_specs=[pl.BlockSpec(memory_space=pltpu.SMEM)]
        + [vmem] * (len(firsts) + 1)
        + [ANYWHERE] * len(after),
        out_specs=[vmem] * 2,
        out_shape=[jax.ShapeDtypeStruct(shape, jnp.bfloat16)] * 2,
        compiler_params=pltpu.CompilerParams(vmem_limit_bytes=VMEM_LIMIT),
        cost_estimate=cost(0.2),
        name="qkv_parts",
    )(info, *firsts, d_heads, *after)


def pair_sum(keep, got):
    return (keep.astype(jnp.float32) + got.astype(jnp.float32)).astype(jnp.bfloat16)


def fold_kernel(bits, info_ref, *refs):
    count = len(bits)
    out_refs = refs[-2 * count :]
    for place, bit_at in enumerate(bits):
        keep, got = refs[2 * place : 2 * place + 2]
        low, high = pair_sum(keep[0, 0], got[0, 0]), pair_sum(keep[0, 1], got[0, 1])
        bit = info_ref[BITS_AT + bit_at]
        kept, sent = out_refs[2 * place : 2 * place + 2]
        kept[0] = jnp.where(bit == 0, low, high)
        sent[0] = jnp.where(bit == 0, high, low)


def fold(info, bits, pairs, after, expense):
    count, unused, unused_rows, columns = pairs[0][0].shape
    in_specs, out_specs, out_shape = [], [], []
    for keep, got in pairs:
        rows = keep.shape[2]
        in_specs += [pl.BlockSpec((1, 2, rows, columns), lambda i, info: (i, 0, 0, 0))] * 2
        out_specs += [pl.BlockSpec((1, rows, columns), lambda i, info: (i, 0, 0))] * 2
        out_shape += [jax.ShapeDtypeStruct((count, rows, columns), jnp.bfloat16)] * 2
    return pl.pallas_call(
        partial(fold_kernel, bits),
        grid_spec=pltpu.PrefetchScalarGridSpec(
            num_scalar_prefetch=1,
            grid=(count,),
            in_specs=in_specs + [ANYWHERE] * len(after),
            out_specs=out_specs,
        ),
        out_shape=out_shape,
        compiler_params=pltpu.CompilerParams(
            vmem_limit_bytes=VMEM_LIMIT, dimension_semantics=("arbitrary",)
        ),
        cost_estimate=cost(expense),
        name="fold",
    )(info, *(part for pair in pairs for part in pair), *after)


def blend_kernel(riders, keep_a, got_a, keep_b, got_b, *refs):
    out_ref = refs[-1]
    row = 0
    for keep, got in ((keep_a, got_a), (keep_b, got_b)):
        height = keep.shape[1]
        out_ref[0, row : row + height, :] = pair_sum(keep[0], got[0])
        row += height
    for rider in refs[:riders]:
        height = rider.shape[1]
        out_ref[0, row : row + height, :] = rider[0, :, :TILE]
        out_ref[0, row + height : row + 2 * height, :LANES] = rider[0, :, TILE:]
        out_ref[0, row + height : row + 2 * height, LANES:] = jnp.zeros(
            (height, TILE - LANES), jnp.bfloat16
        )
        row += 2 * height


def blend(parts, riders, after, expense):
    rows = sum(part.shape[1] for part in parts[::2]) + 2 * sum(part.shape[1] for part in riders)
    count, columns = parts[0].shape[0], parts[0].shape[2]
    operands = tuple(parts) + tuple(riders)
    return pl.pallas_call(
        partial(blend_kernel, len(riders)),
        grid=(count,),
        in_specs=[pl.BlockSpec((1,) + part.shape[1:], lambda i: (i, 0, 0)) for part in operands]
        + [ANYWHERE] * len(after),
        out_specs=pl.BlockSpec((1, rows, columns), lambda i: (i, 0, 0)),
        out_shape=jax.ShapeDtypeStruct((count, rows, columns), jnp.bfloat16),
        compiler_params=pltpu.CompilerParams(
            vmem_limit_bytes=VMEM_LIMIT, dimension_semantics=("arbitrary",)
        ),
        cost_estimate=cost(expense),
        name="blend",
    )(*operands, *after)


def join_kernel(mine_ref, theirs_ref, *refs):
    count = mine_ref.shape[0]
    refs[-1][:count] = mine_ref[...]
    refs[-1][count:] = theirs_ref[...]


def join(mine, theirs, after):
    vmem = pl.BlockSpec(memory_space=pltpu.VMEM)
    return pl.pallas_call(
        join_kernel,
        in_specs=[vmem, vmem] + [ANYWHERE] * len(after),
        out_specs=vmem,
        out_shape=jax.ShapeDtypeStruct((2 * mine.shape[0],) + mine.shape[1:], mine.dtype),
        compiler_params=pltpu.CompilerParams(vmem_limit_bytes=VMEM_LIMIT),
        cost_estimate=cost(0.5),
        name="join",
    )(mine, theirs, *after)


def add_kernel(keep_ref, got_ref, *refs):
    refs[-1][...] = (
        keep_ref[...].astype(jnp.float32) + got_ref[...].astype(jnp.float32)
    ).astype(jnp.bfloat16)


def add_pair(keep, got, after):
    vmem = pl.BlockSpec(memory_space=pltpu.VMEM)
    return pl.pallas_call(
        add_kernel,
        in_specs=[vmem, vmem] + [ANYWHERE] * len(after),
        out_specs=vmem,
        out_shape=jax.ShapeDtypeStruct(keep.shape, jnp.bfloat16),
        cost_estimate=cost(1),
        name="add_pair",
    )(keep, got, *after)


def finish_kernel(jobs, riders, info_ref, parts_ref, *refs):
    targets = refs[-len(jobs) - riders :]
    row = [0, rows_of(jobs)[0]]
    for (unused, height, unused_at, width, tiles), target in zip(jobs, targets):
        for tile in range(width // TILE):
            second = tile >= tiles
            rows = slice(row[second], row[second] + height)
            total = parts_ref[0, rows, :].astype(jnp.float32)
            for part in range(1, parts_ref.shape[0]):
                total = total + parts_ref[part, rows, :].astype(jnp.float32)
            target[:, tile * TILE : (tile + 1) * TILE] = total
            row[second] += height
    if riders:
        first_row = sum(rows_of(jobs))
        ybit = info_ref[BITS_AT + 2]
        for place in range(parts_ref.shape[0]):
            for side in range(2):
                group = 2 * place + (ybit if side == 0 else 1 - ybit)
                at = first_row + side * 2 * FINE
                for part in range(3):
                    rows = slice(at + part // 2 * FINE, at + part // 2 * FINE + FINE)
                    lanes = slice(part % 2 * LANES, (part % 2 + 1) * LANES)
                    column = pl.multiple_of(part * D + group * LANES, LANES)
                    targets[-1][:, pl.ds(column, LANES)] = parts_ref[place, rows, lanes].astype(
                        jnp.float32
                    )


def finish(info, jobs, parts, riders, after):
    vmem = pl.BlockSpec(memory_space=pltpu.VMEM)
    shapes = [(job[1], job[3]) for job in jobs] + [(FINE, 3 * D)] * riders
    return pl.pallas_call(
        partial(finish_kernel, jobs, riders),
        in_specs=[pl.BlockSpec(memory_space=pltpu.SMEM), vmem] + [ANYWHERE] * len(after),
        out_specs=[vmem] * len(shapes),
        out_shape=[jax.ShapeDtypeStruct(shape, jnp.float32) for shape in shapes],
        compiler_params=pltpu.CompilerParams(vmem_limit_bytes=VMEM_LIMIT),
        cost_estimate=cost(2),
        name="finish",
    )(info, parts, *after)


def closing_kernel(all_ref, embedded_ref, weight_ref, hot_ref, modw_ref, table_ref, bias_ref):
    rows = all_ref.shape[0]
    slots, share = embedded_ref.shape
    embedded = embedded_ref[...]
    sigmoid = jax.nn.sigmoid(embedded)
    activated = (embedded * sigmoid).astype(jnp.bfloat16)
    row = lax.broadcasted_iota(jnp.int32, (slots, rows), 1)
    slot = lax.broadcasted_iota(jnp.int32, (slots, rows), 0)
    d_activated = None
    for quarter in range(4):
        columns = slice(quarter * QUARTER, (quarter + 1) * QUARTER)
        chosen = jnp.where(row == slot // 2 * 8 + 2 * quarter + slot % 2, 1.0, 0.0)
        spread = lax.dot_general(
            activated,
            chosen.astype(jnp.bfloat16),
            (((0,), (0,)), ((), ())),
            preferred_element_type=jnp.float32,
        ).astype(jnp.bfloat16)
        modw_ref[:, columns] = lax.dot_general(
            spread, all_ref[...], NN, preferred_element_type=jnp.float32
        )
        every = jnp.where(
            lax.broadcasted_iota(jnp.int32, (8, rows), 1) % 8 // 2 == quarter, 1.0, 0.0
        ).astype(jnp.bfloat16)
        bias_ref[:, columns] = lax.dot_general(
            every, all_ref[...], NN, preferred_element_type=jnp.float32
        )[:1, :]
        part = lax.dot_general(
            all_ref[...], weight_ref[:, columns], NT, preferred_element_type=jnp.float32
        )
        part = lax.dot_general(
            chosen,
            part,
            NN,
            precision=lax.Precision.HIGHEST,
            preferred_element_type=jnp.float32,
        )
        d_activated = part if d_activated is None else d_activated + part
    d_embedded = d_activated * (sigmoid * (1.0 + embedded * (1.0 - sigmoid)))
    table_ref[...] = lax.dot_general(
        hot_ref[...],
        d_embedded,
        NN,
        precision=lax.Precision.HIGHEST,
        preferred_element_type=jnp.float32,
    )


def closing(gathered, embedded, weight_rows, level_hot):
    vmem = pl.BlockSpec(memory_space=pltpu.VMEM)
    share = embedded.shape[1]
    return pl.pallas_call(
        closing_kernel,
        in_specs=[vmem] * 4,
        out_specs=[vmem] * 3,
        out_shape=[
            jax.ShapeDtypeStruct((share, 6 * D), jnp.float32),
            jax.ShapeDtypeStruct((LEVELS, share), jnp.float32),
            jax.ShapeDtypeStruct((1, 6 * D), jnp.float32),
        ],
        compiler_params=pltpu.CompilerParams(vmem_limit_bytes=VMEM_LIMIT),
        cost_estimate=cost(3),
        name="closing",
    )(gathered, embedded, weight_rows, level_hot)


def halved(part):
    return part.reshape((-1, 2) + part.shape[-2:])


def across(info, parts, after, expense):
    keep_a, got_a, keep_b, got_b = (halved(part) for part in parts)
    keep_a, send_a, keep_b, send_b = fold(
        info, (2, 1), ((keep_a, got_a), (keep_b, got_b)), after, expense
    )
    return (keep_a, swap(send_a, 4), keep_b, swap(send_b, 2)), send_a


def along(parts, riders, after, expense):
    total = blend(parts, riders, after, expense)
    columns = [[2 * place + side for place in range(4)] for side in range(2)]
    return lax.all_to_all(total, "blk", 0, 0, axis_index_groups=columns, tiled=True), total


def local_heads(
    tokens,
    noise_levels,
    group_map,
    noise_table,
    mod_weight,
    mod_bias,
    qkv_weight,
    out_weight,
    fc1_weight,
    fc2_weight,
    out_cotangent,
):
    rows_here = 2 * PATCHES
    frame_count = group_map.shape[0]
    groups = D // LANES
    device_count = lax.axis_size(AXES)
    index = lax.axis_index(AXES)
    bits = [(index >> place) & 1 for place in range(5)]
    tables = rope_tables(frame_count)
    clip_levels = noise_levels
    for bit in (1, 2):
        clip_levels = jnp.concatenate([clip_levels, swap(clip_levels, bit)], axis=0)
    members = jnp.zeros((1,), jnp.int32)
    for bit in (16, 8, 4, 2, 1):
        members = jnp.concatenate([members, members ^ bit])
    member_slots = (2 * ((index ^ members) >> 2))[:, None] + jnp.arange(2, dtype=jnp.int32)[None, :]
    levels_all = clip_levels[(members & 3)[:, None], group_map[member_slots]].reshape(
        2 * device_count
    )
    tokens_here = tokens.reshape(rows_here, D)
    block = lax.axis_index("blk")
    piece_at = block ^ jnp.array(PIECES, jnp.int32)
    places = jnp.arange(frame_count, dtype=jnp.int32)
    piece_slots = ((2 * piece_at)[:, None] + jnp.arange(2, dtype=jnp.int32)[None, :]).reshape(-1)
    frames = jnp.sum(
        jnp.where(piece_slots[:, None] == places[None, :], group_map[None, :], 0), axis=1
    )
    slots = jnp.sum(jnp.where(group_map[None, :] == places[:, None], places[None, :], 0), axis=1)
    info = jnp.concatenate(
        [jnp.stack(bits), piece_at, frames, slots, group_map, frames[:2]]
    ).astype(jnp.int32)
    far = cross(tokens_here, 4)
    side = cross(tokens_here, 1)
    near = cross(tokens_here, 2)
    far_side, far_near, near_side = cross(far, 1), cross(far, 2), cross(side, 2)
    last = (cross(far_near[:PATCHES], 1), cross(far_side[PATCHES:], 2))
    modulation = modulate(
        noise_levels, noise_table, mod_weight, mod_bias
    )
    weight_here = own_columns(info, qkv_weight)
    projected = []
    for first_piece, pieces in (
        (0, (tokens_here,)),
        (1, (far, near, side)),
        (4, (far_side, far_near, near_side)),
        (7, (last,)),
    ):
        projected.append(project(info, modulation, weight_here, tables, first_piece, pieces))
    qkv_heads = [pair[0] for pair in projected]
    firsts = [pair[1] for pair in projected]
    att_heads, ot, lse = attend(info, qkv_heads, levels_all)
    att = lax.all_to_all(att_heads, "blk", 0, 0, tiled=True)
    layer_out, up_acts, down_acts, d_att, d_middle, d_mod_early = middle_block(
        info,
        att,
        tokens_here,
        out_cotangent.reshape(rows_here, D),
        modulation,
        out_weight,
        fc1_weight,
        fc2_weight,
    )
    grad_heads = lax.all_to_all(d_att, "blk", 0, 0, tiled=True)
    share = D // device_count
    keep_a, send_a, keep_b, send_b = weight_parts(
        UPPER_JOBS, info, up_acts, swap(up_acts, 1), (), 2)
    upper = (keep_a, swap(send_a, 2), keep_b, swap(send_b, 4))
    d_heads = attend_back(info, qkv_heads, grad_heads, ot, lse, tables, (send_a,))
    d_qkv = lax.all_to_all(d_heads, "blk", 0, 0, tiled=True)
    qkv_keep, qkv_send = qkv_parts(info, firsts, d_heads, share, ())
    upper, upper_sent = across(info, upper, (qkv_send,), 10)
    qkv_core = add_pair(qkv_keep, swap(qkv_send, 1), (upper_sent,))
    qkv_keep, qkv_send = pick_split(qkv_core, 1, bits[1])
    qkv_got = swap(qkv_send, 2)
    keep_a, send_a, keep_b, send_b = weight_parts(
        LOWER_JOBS, info, down_acts, swap(down_acts, 1), (upper_sent, qkv_core, upper[3]), 5)
    lower = (keep_a, swap(send_a, 2), keep_b, swap(send_b, 4))
    qkv_sum = add_pair(qkv_keep, qkv_got, (send_a,))
    qkv_keep, qkv_send = pick_split(
        qkv_sum.reshape(groups // 2, 2, share, 3 * LANES), 1, bits[2]
    )
    qkv_got = swap(qkv_send, 4)
    upper, upper_z = along(upper, (), (qkv_send,), 1)
    tokens_grad, d_mod = first_back(
        info, d_qkv, tokens_here, modulation, d_middle, d_mod_early, qkv_weight, (upper_z,)
    )
    got = swap(d_mod, 16)
    lower, lower_sent = across(info, lower, (d_mod,), 15)
    d_mod = join(d_mod, got, (lower_sent,))
    got = swap(d_mod, 8)
    lower, lower_z = along(lower, (qkv_keep, qkv_got), (d_mod,), 5)
    d_mod = join(d_mod, got, (lower_z,))
    for bit in (4, 2, 1):
        d_mod = jnp.concatenate([d_mod, swap(d_mod, bit)])
    level_hot = jnp.arange(LEVELS, dtype=jnp.int32)[:, None] == levels_all[None, :]
    table_columns = lax.dynamic_slice_in_dim(noise_table, index * share, share, 1)
    embedded_columns = jnp.einsum(
        "ls,lc->sc",
        level_hot.astype(jnp.bfloat16),
        table_columns,
        preferred_element_type=jnp.float32,
    )
    weight_rows = lax.dynamic_slice_in_dim(mod_weight, index * share, share, 0)
    modw_share, table_share, bias_sums = closing(
        d_mod, embedded_columns, weight_rows, level_hot.astype(jnp.float32)
    )
    bias_columns = 6 * D // device_count
    bias_share = lax.dynamic_slice_in_dim(bias_sums[0], index * bias_columns, bias_columns)
    upper_share, outw_share = finish(info, UPPER_JOBS, upper, 0, (lower_z,))
    lower_share, qkv_share = finish(
        info, LOWER_JOBS, lower, 1, (upper_share, table_share, modw_share, bias_share)
    )
    return (
        layer_out[None].reshape(1, 2, PATCHES, D),
        tokens_grad.reshape(1, 2, PATCHES, D),
        table_share,
        modw_share,
        bias_share,
        qkv_share,
        outw_share,
        upper_share,
        lower_share,
    )


def solution(mesh):
    pair_split = mesh.shape["blk"] * LANES == D and mesh.shape["clip"] == 4
    return jax.shard_map(
        local_heads if pair_split else local,
        mesh=mesh,
        in_specs=(
            P("clip", "blk", None, None),
            P("clip", None),
            P(),
            P(),
            P(),
            P(),
            P(),
            P(),
            P(),
            P(),
            P("clip", "blk", None, None),
        ),
        out_specs=(
            P("clip", "blk", None, None),
            P("clip", "blk", None, None),
            P(None, ("blk", "clip")),
            P(("blk", "clip"), None),
            P(("blk", "clip")),
            P(("blk", "clip"), None),
            P(("blk", "clip"), None),
            P(("blk", "clip"), None),
            P(("blk", "clip"), None),
        ),
        check_vma=False,
    )
```

```python
from functools import partial

import jax
import jax.numpy as jnp
import numpy as np
from jax import lax
from jax.experimental import pallas as pl
from jax.experimental.pallas import tpu as pltpu
from jax.sharding import PartitionSpec as P

D = 1024
HEAD = 64
HEADS = 16
LEVELS = 1000
GRID_H = 8
GRID_W = 16
PATCHES = 128


SCALE = 0.125
EPSILON = 1e-06
ROPE_BASE = 10000.0
NEG_LARGE = -1e30


def token_positions(frame_ids):
    slot_count = frame_ids.shape[0]
    total_rows = slot_count * GRID_H * GRID_W
    patch_ids = jnp.arange(total_rows, dtype=jnp.int32) % (GRID_H * GRID_W)
    frame_pos = jnp.repeat(frame_ids, GRID_H * GRID_W, total_repeat_length=total_rows)
    return (frame_pos, patch_ids // GRID_W, patch_ids % GRID_W)


def rope_angles(frame_pos, row_pos, col_pos):
    angle_list = []
    for position, comp_width in ((frame_pos, 16), (row_pos, 24), (col_pos, 24)):
        half_width = comp_width // 2
        frequency = ROPE_BASE ** (-2.0 * jnp.arange(half_width, dtype=jnp.float32) / comp_width)
        angle_list.append(position.astype(jnp.float32)[:, None] * frequency[None, :])
    return angle_list


def rotate(values, angle_list, direction):
    pieces = []
    offset = 0
    for angles in angle_list:
        half_width = angles.shape[1]
        first_half = values[:, :, offset : offset + half_width]
        second_half = values[:, :, offset + half_width : offset + 2 * half_width]
        cosine = jnp.cos(angles)[:, None, :]
        sine_part = direction * jnp.sin(angles)[:, None, :]
        pieces.append(first_half * cosine - second_half * sine_part)
        pieces.append(first_half * sine_part + second_half * cosine)
        offset = offset + 2 * half_width
    return jnp.concatenate(pieces, axis=2)


def normalize(values):
    center = values - jnp.mean(values, axis=-1, keepdims=True)
    inverse = lax.rsqrt(jnp.mean(center * center, axis=-1, keepdims=True) + EPSILON)
    return (center * inverse, inverse)


def norm_backward(grad_in, normed, inverse):
    return inverse * (
        grad_in
        - jnp.mean(grad_in, axis=-1, keepdims=True)
        - normed * jnp.mean(grad_in * normed, axis=-1, keepdims=True)
    )


def frames_of(group_map, first_row, row_count):
    slot_frames = lax.dynamic_slice_in_dim(group_map, first_row // PATCHES, row_count // PATCHES)
    return jnp.repeat(slot_frames, PATCHES, total_repeat_length=row_count)


def block_size(row_count, shard_rows):
    return 2 * shard_rows if row_count // shard_rows % 2 == 0 else shard_rows


def keep_same(values):
    return values


def local(
    tokens,
    noise_levels,
    group_map,
    noise_table,
    mod_weight,
    mod_bias,
    qkv_weight,
    out_weight,
    fc1_weight,
    fc2_weight,
    out_cotangent,
):
    rows_here = 2 * PATCHES
    my_frames = lax.dynamic_slice_in_dim(group_map, 2 * lax.axis_index("blk"), 2)
    frame_hot = (
        jnp.arange(group_map.shape[0], dtype=jnp.int32)[None, :] == my_frames[:, None]
    ).astype(jnp.int32)
    my_levels = jnp.sum(frame_hot * noise_levels[0][None, :], axis=1)
    level_hot = jnp.arange(LEVELS, dtype=jnp.int32)[None, :] == my_levels[:, None]
    embedded = jnp.dot(
        level_hot.astype(jnp.bfloat16), noise_table, preferred_element_type=jnp.float32
    )
    activated = jax.nn.silu(embedded).astype(jnp.bfloat16)
    modulation = (
        jnp.dot(activated, mod_weight, preferred_element_type=jnp.float32)
        + mod_bias.astype(jnp.float32)[None, :]
    )
    shift_one, scale_one, gate_one, shift_two, scale_two, gate_two = [
        modulation[:, member * D : (member + 1) * D][:, None, :] for member in range(6)
    ]
    inputs_here = tokens[0].astype(jnp.float32)
    normed_one, inverse_one = normalize(inputs_here)
    first_in = (
        (normed_one * (1.0 + scale_one) + shift_one).astype(jnp.bfloat16).reshape(rows_here, D)
    )
    qkv_lin = jnp.dot(first_in, qkv_weight, preferred_element_type=jnp.float32)
    token_frames, row_pos, col_pos = token_positions(my_frames)
    angle_list = rope_angles(token_frames, row_pos, col_pos)
    query = rotate(qkv_lin[:, :D].reshape(rows_here, HEADS, HEAD), angle_list, 1.0).astype(
        jnp.bfloat16
    )
    key_part = rotate(
        qkv_lin[:, D : 2 * D].reshape(rows_here, HEADS, HEAD), angle_list, 1.0
    ).astype(jnp.bfloat16)
    value_part = qkv_lin[:, 2 * D :].reshape(rows_here, HEADS, HEAD).astype(jnp.bfloat16)
    top_frame = jnp.max(my_frames)
    own_lowest = jnp.min(my_frames)
    forward_start = (
        jnp.full((HEADS, rows_here), NEG_LARGE, jnp.float32),
        jnp.zeros((HEADS, rows_here), jnp.float32),
        jnp.zeros((rows_here, HEADS, HEAD), jnp.float32),
    )
    first_row = jnp.int32(0)
    keys_piece = lax.all_gather(key_part, "blk", axis=0, tiled=True)
    values_piece = lax.all_gather(value_part, "blk", axis=0, tiled=True)
    piece_rows = keys_piece.shape[0]
    block_rows = block_size(piece_rows, rows_here)

    def forward_advance(turn_index, running):
        offset = turn_index * block_rows
        keys_block = lax.dynamic_slice_in_dim(keys_piece, offset, block_rows)
        values_block = lax.dynamic_slice_in_dim(values_piece, offset, block_rows)
        block_frames = frames_of(group_map, first_row + offset, block_rows)

        def attend(previous):
            top_scores, totals, accumulated = previous
            scores = (
                jnp.einsum("qhd,khd->hqk", query, keys_block, preferred_element_type=jnp.float32)
                * SCALE
            )
            allowed = block_frames[None, None, :] <= token_frames[None, :, None]
            new_top = jnp.maximum(
                top_scores, jnp.max(jnp.where(allowed, scores, NEG_LARGE), axis=2)
            )
            weights = jnp.where(allowed, jnp.exp(scores - new_top[:, :, None]), 0.0)
            factor = jnp.exp(top_scores - new_top)
            update = jnp.einsum(
                "hqk,khd->qhd",
                weights.astype(jnp.bfloat16),
                values_block,
                preferred_element_type=jnp.float32,
            )
            return (
                new_top,
                totals * factor + jnp.sum(weights, axis=2),
                accumulated * factor.T[:, :, None] + update,
            )

        return lax.cond(jnp.min(block_frames) > top_frame, keep_same, attend, running)

    top_scores, totals, accumulated = lax.fori_loop(
        0, piece_rows // block_rows, forward_advance, forward_start
    )
    attended = accumulated / totals.T[:, :, None]
    log_total = top_scores + jnp.log(totals)
    attended_low = attended.astype(jnp.bfloat16).reshape(rows_here, D)
    attn_out = jnp.dot(attended_low, out_weight, preferred_element_type=jnp.float32).reshape(
        2, PATCHES, D
    )
    middle = inputs_here + gate_one * attn_out
    normed_two, inverse_two = normalize(middle)
    second_in = (
        (normed_two * (1.0 + scale_two) + shift_two).astype(jnp.bfloat16).reshape(rows_here, D)
    )
    up_lin = jnp.dot(second_in, fc1_weight, preferred_element_type=jnp.float32)
    hidden = jax.nn.gelu(up_lin, approximate=False).astype(jnp.bfloat16)
    mlp_out = jnp.dot(hidden, fc2_weight, preferred_element_type=jnp.float32).reshape(2, PATCHES, D)
    layer_out = (middle + gate_two * mlp_out).astype(jnp.bfloat16)[None]
    cotangent = out_cotangent[0].astype(jnp.float32)
    d_gate_two = jnp.sum(cotangent * mlp_out, axis=1)
    d_mlp = (cotangent * gate_two).astype(jnp.bfloat16).reshape(rows_here, D)
    lower_part = jnp.einsum("rf,rd->fd", hidden, d_mlp, preferred_element_type=jnp.float32)
    d_hidden = jnp.einsum("rd,fd->rf", d_mlp, fc2_weight, preferred_element_type=jnp.float32)
    unused_value, gelu_pull = jax.vjp(partial(jax.nn.gelu, approximate=False), up_lin)
    d_up = gelu_pull(d_hidden)[0].astype(jnp.bfloat16)
    upper_part = jnp.einsum("rc,rf->cf", second_in, d_up, preferred_element_type=jnp.float32)
    d_second = jnp.einsum(
        "rf,cf->rc", d_up, fc1_weight, preferred_element_type=jnp.float32
    ).reshape(2, PATCHES, D)
    d_shift_two = jnp.sum(d_second, axis=1)
    d_scale_two = jnp.sum(d_second * normed_two, axis=1)
    d_middle = cotangent + norm_backward(d_second * (1.0 + scale_two), normed_two, inverse_two)
    d_gate_one = jnp.sum(d_middle * attn_out, axis=1)
    d_attn = (d_middle * gate_one).astype(jnp.bfloat16).reshape(rows_here, D)
    outw_part = jnp.einsum("rc,rd->cd", attended_low, d_attn, preferred_element_type=jnp.float32)
    d_attended = (
        jnp.einsum("rd,cd->rc", d_attn, out_weight, preferred_element_type=jnp.float32)
        .astype(jnp.bfloat16)
        .reshape(rows_here, HEADS, HEAD)
    )
    delta = jnp.sum(d_attended.astype(jnp.float32) * attended, axis=2).T
    grad_start = jnp.zeros((rows_here, HEADS, HEAD), jnp.float32)
    query_first_row = jnp.int32(0)
    query_keys_piece = lax.all_gather(key_part, "blk", axis=0, tiled=True)
    query_values_piece = lax.all_gather(value_part, "blk", axis=0, tiled=True)
    piece_rows = query_keys_piece.shape[0]
    query_block_rows = block_size(piece_rows, rows_here)

    def query_advance(turn_index, running):
        offset = turn_index * query_block_rows
        keys_block = lax.dynamic_slice_in_dim(query_keys_piece, offset, query_block_rows)
        values_block = lax.dynamic_slice_in_dim(query_values_piece, offset, query_block_rows)
        block_frames = frames_of(group_map, query_first_row + offset, query_block_rows)

        def query_accumulate(previous):
            scores = (
                jnp.einsum("qhd,khd->hqk", query, keys_block, preferred_element_type=jnp.float32)
                * SCALE
            )
            allowed = block_frames[None, None, :] <= token_frames[None, :, None]
            weights = jnp.where(allowed, jnp.exp(scores - log_total[:, :, None]), 0.0)
            weight_grad = jnp.einsum(
                "qhd,khd->hqk", d_attended, values_block, preferred_element_type=jnp.float32
            )
            score_grad = (weights * (weight_grad - delta[:, :, None]) * SCALE).astype(jnp.bfloat16)
            return previous + jnp.einsum(
                "hqk,khd->qhd", score_grad, keys_block, preferred_element_type=jnp.float32
            )

        return lax.cond(jnp.min(block_frames) > top_frame, keep_same, query_accumulate, running)

    query_grad = lax.fori_loop(0, piece_rows // query_block_rows, query_advance, grad_start)
    stats_lse, stats_delta = (
        lax.all_gather(log_total.T, "blk", axis=0, tiled=True),
        lax.all_gather(delta.T, "blk", axis=0, tiled=True),
    )
    key_first_row = jnp.int32(0)
    queries_piece = lax.all_gather(query, "blk", axis=0, tiled=True)
    grads_piece = lax.all_gather(d_attended, "blk", axis=0, tiled=True)
    piece_rows = queries_piece.shape[0]
    key_block_rows = block_size(piece_rows, rows_here)

    def key_advance(turn_index, running):
        offset = turn_index * key_block_rows
        query_block = lax.dynamic_slice_in_dim(queries_piece, offset, key_block_rows)
        grad_block = lax.dynamic_slice_in_dim(grads_piece, offset, key_block_rows)
        lse_block = lax.dynamic_slice_in_dim(stats_lse, key_first_row + offset, key_block_rows).T
        delta_block = lax.dynamic_slice_in_dim(
            stats_delta, key_first_row + offset, key_block_rows
        ).T
        block_frames = frames_of(group_map, key_first_row + offset, key_block_rows)

        def key_accumulate(previous):
            key_total, value_total = previous
            scores = (
                jnp.einsum(
                    "qhd,khd->hqk", query_block, key_part, preferred_element_type=jnp.float32
                )
                * SCALE
            )
            allowed = token_frames[None, None, :] <= block_frames[None, :, None]
            weights = jnp.where(allowed, jnp.exp(scores - lse_block[:, :, None]), 0.0)
            value_total = value_total + jnp.einsum(
                "hqk,qhd->khd",
                weights.astype(jnp.bfloat16),
                grad_block,
                preferred_element_type=jnp.float32,
            )
            weight_grad = jnp.einsum(
                "qhd,khd->hqk", grad_block, value_part, preferred_element_type=jnp.float32
            )
            score_grad = (weights * (weight_grad - delta_block[:, :, None]) * SCALE).astype(
                jnp.bfloat16
            )
            key_total = key_total + jnp.einsum(
                "hqk,qhd->khd", score_grad, query_block, preferred_element_type=jnp.float32
            )
            return (key_total, value_total)

        return lax.cond(jnp.max(block_frames) < own_lowest, keep_same, key_accumulate, running)

    key_grad, value_grad = lax.fori_loop(
        0, piece_rows // key_block_rows, key_advance, (grad_start, grad_start)
    )
    query_low = lax.optimization_barrier(query_grad.astype(jnp.bfloat16)).astype(jnp.float32)
    key_low = lax.optimization_barrier(key_grad.astype(jnp.bfloat16)).astype(jnp.float32)
    query_back = rotate(query_low, angle_list, -1.0).reshape(rows_here, D)
    key_back = rotate(key_low, angle_list, -1.0).reshape(rows_here, D)
    d_qkv = jnp.concatenate(
        [query_back, key_back, value_grad.reshape(rows_here, D)], axis=1
    ).astype(jnp.bfloat16)
    qkv_part = jnp.einsum("rc,rk->ck", first_in, d_qkv, preferred_element_type=jnp.float32)
    d_first = jnp.einsum(
        "rk,ck->rc", d_qkv, qkv_weight, preferred_element_type=jnp.float32
    ).reshape(2, PATCHES, D)
    d_shift_one = jnp.sum(d_first, axis=1)
    d_scale_one = jnp.sum(d_first * normed_one, axis=1)
    tokens_grad = (
        d_middle + norm_backward(d_first * (1.0 + scale_one), normed_one, inverse_one)
    ).astype(jnp.bfloat16)[None]
    d_mod = jnp.concatenate(
        [d_shift_one, d_scale_one, d_gate_one, d_shift_two, d_scale_two, d_gate_two], axis=1
    )
    bias_part = jnp.sum(d_mod, axis=0)
    d_mod_low = d_mod.astype(jnp.bfloat16)
    d_activated = jnp.einsum("sk,ck->sc", d_mod_low, mod_weight, preferred_element_type=jnp.float32)
    unused_silu, silu_pull = jax.vjp(jax.nn.silu, embedded)
    d_embedded = silu_pull(d_activated)[0]
    table_part = jnp.einsum(
        "sl,sc->cl", level_hot.astype(jnp.float32), d_embedded, precision=lax.Precision.HIGHEST
    )
    activated_all, d_mod_all = (
        lax.all_gather(activated, ("blk", "clip"), axis=0, tiled=True),
        lax.all_gather(d_mod_low, ("blk", "clip"), axis=0, tiled=True),
    )
    share_rows = D // lax.axis_size(("blk", "clip"))
    my_columns = lax.dynamic_slice_in_dim(
        activated_all, lax.axis_index(("blk", "clip")) * share_rows, share_rows, 1
    )
    modw_share = jnp.einsum("sc,sk->ck", my_columns, d_mod_all, preferred_element_type=jnp.float32)
    summed = (
        lax.psum_scatter(table_part, ("blk", "clip"), scatter_dimension=0, tiled=True),
        lax.psum_scatter(bias_part, ("blk", "clip"), scatter_dimension=0, tiled=True),
        lax.psum_scatter(qkv_part, ("blk", "clip"), scatter_dimension=0, tiled=True),
        lax.psum_scatter(outw_part, ("blk", "clip"), scatter_dimension=0, tiled=True),
        lax.psum_scatter(upper_part, ("blk", "clip"), scatter_dimension=0, tiled=True),
        lax.psum_scatter(lower_part, ("blk", "clip"), scatter_dimension=0, tiled=True),
    )
    return (
        layer_out,
        tokens_grad,
        summed[0].T,
        modw_share,
        summed[1],
        summed[2],
        summed[3],
        summed[4],
        summed[5],
    )


LANES = 128
FF = 4096
AXES = ("blk", "clip")
EXP_SCALE = SCALE * 1.4426950408889634
VMEM_LIMIT = 56 * 1024 * 1024
NT = (((1,), (1,)), ((), ()))
NN = (((1,), (0,)), ((), ()))


def cost(microseconds):
    return pl.CostEstimate(
        flops=int(microseconds * 1e9), bytes_accessed=int(microseconds * 3e6), transcendentals=0
    )


class Shifted:
    def __init__(self, ref, start):
        self.ref, self.start = ref, start

    def __getitem__(self, place):
        return self.ref[self.start + place]


FRAME_COUNT = 2 * D // LANES
BITS_AT, ORDER_AT = 0, 5
FRAMES_AT = ORDER_AT + D // LANES
SLOTS_AT = FRAMES_AT + FRAME_COUNT
GROUP_AT = SLOTS_AT + FRAME_COUNT
MINE_AT = GROUP_AT + FRAME_COUNT
ANYWHERE = pl.BlockSpec(memory_space=pl.ANY)


def full_block(shape):
    return pl.BlockSpec(shape, lambda *ids: (0,) * len(shape))


def rope_tables(frame_count):
    lane = np.arange(LANES) % HEAD
    pieces = []
    for comp_width in (16, 24, 24):
        half_width = comp_width // 2
        frequency = ROPE_BASE ** (-2.0 * np.arange(half_width) / comp_width)
        pieces += [frequency, frequency]
    frequency = np.tile(np.concatenate(pieces), LANES // HEAD)[None, :]
    first = (lane < 8) | ((lane >= 16) & (lane < 28)) | ((lane >= 40) & (lane < 52))
    sign = np.where(first, -1.0, 1.0)[None, :]
    in_frame = (lane < 16)[None, :]
    in_row = (lane < 40)[None, :]
    frame_angle = np.arange(frame_count)[:, None] * frequency
    patch = np.arange(PATCHES)[:, None]
    place_angle = np.where(in_row, patch // GRID_W, patch % GRID_W) * frequency
    tables = (
        np.where(in_frame, np.cos(frame_angle), 0.0),
        np.where(in_frame, sign * np.sin(frame_angle), 0.0),
        np.where(in_frame, 0.0, np.cos(place_angle)),
        np.where(in_frame, 0.0, sign * np.sin(place_angle)),
    )
    return tuple(jnp.asarray(table, jnp.float32) for table in tables)


def partner_lanes(values):
    lane = lax.broadcasted_iota(jnp.int32, values.shape, 1) % HEAD
    ahead_eight = pltpu.roll(values, LANES - 8, 1)
    behind_eight = pltpu.roll(values, 8, 1)
    ahead_twelve = pltpu.roll(values, LANES - 12, 1)
    behind_twelve = pltpu.roll(values, 12, 1)
    ahead = ((lane >= 16) & (lane < 28)) | ((lane >= 40) & (lane < 52))
    return jnp.where(
        lane < 8,
        ahead_eight,
        jnp.where(lane < 16, behind_eight, jnp.where(ahead, ahead_twelve, behind_twelve)),
    )


def modulation_kernel(levels_ref, table_ref, weight_ref, bias_ref, out_ref, activated_ref):
    @pl.when(pl.program_id(0) == 0)
    def _():
        count = levels_ref.shape[1]
        hot = lax.broadcasted_iota(jnp.int32, (LEVELS, count), 0) == levels_ref[...]
        embedded = lax.dot_general(
            jnp.where(hot, 1.0, 0.0).astype(jnp.bfloat16),
            table_ref[...],
            (((0,), (0,)), ((), ())),
            preferred_element_type=jnp.float32,
        )
        activated_ref[...] = jax.nn.silu(embedded).astype(jnp.bfloat16)

    out_ref[...] = lax.dot_general(
        activated_ref[...], weight_ref[...], NN, preferred_element_type=jnp.float32
    ) + bias_ref[...].astype(jnp.float32)[None, :]


def modulate(levels, noise_table, mod_weight, mod_bias):
    frame_count = levels.shape[1]
    return pl.pallas_call(
        modulation_kernel,
        grid=(6,),
        in_specs=[
            full_block(levels.shape),
            full_block(noise_table.shape),
            pl.BlockSpec((D, D), lambda i: (0, i)),
            pl.BlockSpec((D,), lambda i: (i,)),
        ],
        out_specs=pl.BlockSpec((frame_count, D), lambda i: (0, i)),
        out_shape=jax.ShapeDtypeStruct((frame_count, 6 * D), jnp.float32),
        scratch_shapes=[pltpu.VMEM((frame_count, D), jnp.bfloat16)],
        compiler_params=pltpu.CompilerParams(
            vmem_limit_bytes=VMEM_LIMIT, dimension_semantics=("arbitrary",)
        ),
        cost_estimate=cost(7),
        name="modulate",
    )(levels, noise_table, mod_weight, mod_bias)


def copy_kernel(info_ref, source_ref, target_ref):
    target_ref[...] = source_ref[...]


def own_columns(info, weight):
    return pl.pallas_call(
        copy_kernel,
        grid_spec=pltpu.PrefetchScalarGridSpec(
            num_scalar_prefetch=1,
            grid=(3,),
            in_specs=[
                pl.BlockSpec((D, LANES), lambda i, info: (0, i * (D // LANES) + info[ORDER_AT]))
            ],
            out_specs=pl.BlockSpec((D, LANES), lambda i, info: (0, i)),
        ),
        out_shape=jax.ShapeDtypeStruct((D, 3 * LANES), jnp.bfloat16),
        compiler_params=pltpu.CompilerParams(dimension_semantics=("arbitrary",)),
        cost_estimate=cost(2),
        name="own_columns",
    )(info, weight)


def project_kernel(
    count,
    first_piece,
    info_ref,
    mod_ref,
    weight_ref,
    fcos_ref,
    fsin_ref,
    pcos_ref,
    psin_ref,
    *refs,
):
    frames_ref = Shifted(info_ref, FRAMES_AT)
    halves, out_ref, first_ref = refs[: 2 * count], refs[-2], refs[-1]
    for piece in range(count):
        for half in range(2):
            source, place = halves[2 * piece + half]
            rows = slice(half * PATCHES, (half + 1) * PATCHES)
            frame = frames_ref[2 * (first_piece + piece) + half]
            normed, unused = normalize(
                source[place * PATCHES : (place + 1) * PATCHES, :].astype(jnp.float32)
            )
            shift = mod_ref[pl.ds(frame, 1), :D]
            scale = mod_ref[pl.ds(frame, 1), D : 2 * D]
            first_ref[piece, rows, :] = (normed * (1.0 + scale) + shift).astype(jnp.bfloat16)
        linear = lax.dot_general(
            first_ref[piece], weight_ref[...], NN, preferred_element_type=jnp.float32
        )
        for half in range(2):
            rows = slice(half * PATCHES, (half + 1) * PATCHES)
            frame = frames_ref[2 * (first_piece + piece) + half]
            cosine = pcos_ref[...] + fcos_ref[pl.ds(frame, 1), :]
            sine = psin_ref[...] + fsin_ref[pl.ds(frame, 1), :]
            for part in range(2):
                columns = slice(part * LANES, (part + 1) * LANES)
                values = linear[rows, columns]
                turned = values * cosine + partner_lanes(values) * sine
                out_ref[piece, rows, columns] = turned.astype(jnp.bfloat16)
            out_ref[piece, rows, 2 * LANES :] = linear[rows, 2 * LANES :].astype(jnp.bfloat16)


def project(info, modulation, weight, tables, first_piece, pieces):
    vmem = pl.BlockSpec(memory_space=pltpu.VMEM)
    count = len(pieces)
    arrays, sources = [], []
    for piece in pieces:
        if isinstance(piece, tuple):
            sources += [(len(arrays), 0), (len(arrays) + 1, 0)]
            arrays += list(piece)
        else:
            sources += [(len(arrays), 0), (len(arrays), 1)]
            arrays.append(piece)

    def kernel(*refs):
        inputs = refs[7 : 7 + len(arrays)]
        halves = [(inputs[which], place) for which, place in sources]
        project_kernel(count, first_piece, *refs[:7], *halves, *refs[7 + len(arrays) :])

    rows = 2 * PATCHES
    return pl.pallas_call(
        kernel,
        in_specs=[pl.BlockSpec(memory_space=pltpu.SMEM)] + [vmem] * (6 + len(arrays)),
        out_specs=[vmem] * 2,
        out_shape=[
            jax.ShapeDtypeStruct((count, rows, 3 * LANES), jnp.bfloat16),
            jax.ShapeDtypeStruct((count, rows, D), jnp.bfloat16),
        ],
        compiler_params=pltpu.CompilerParams(vmem_limit_bytes=VMEM_LIMIT),
        cost_estimate=cost(2 * count),
        name="project",
    )(info, modulation, weight, *tables, *arrays)


def head_stack(values):
    lane = lax.broadcasted_iota(jnp.int32, values.shape, 1)
    zero = jnp.zeros_like(values)
    return jnp.concatenate(
        [jnp.where(lane < HEAD, values, zero), jnp.where(lane < HEAD, zero, values)], axis=0
    )


def hidden_keys(shape):
    key_row = lax.broadcasted_iota(jnp.int32, shape, 0)
    query_column = lax.broadcasted_iota(jnp.int32, shape, 1) % (2 * PATCHES)
    return (key_row >= PATCHES) & (query_column < PATCHES)


def own_heads(values):
    rows = 2 * PATCHES
    return jnp.concatenate([values[:HEAD, :rows], values[HEAD:LANES, rows:]], axis=0)


def by_frame(frames_ref, source_refs, target_refs):
    pieces = [(ref, piece) for ref in source_refs for piece in range(ref.shape[0])]
    for place, (ref, piece) in enumerate(pieces):
        for half in range(2):
            frame = frames_ref[2 * place + half]
            rows = pl.ds(pl.multiple_of(frame * PATCHES, PATCHES), PATCHES)
            for part, target in enumerate(target_refs):
                target[rows, :] = ref[
                    piece,
                    half * PATCHES : (half + 1) * PATCHES,
                    part * LANES : (part + 1) * LANES,
                ]


def attend_kernel(info_ref, qkv_refs, att_ref, ot_ref, lse_ref, q_ref, k_ref, v_ref, vt_ref):
    token_count = q_ref.shape[0]
    frames_ref, slots_ref = Shifted(info_ref, FRAMES_AT), Shifted(info_ref, SLOTS_AT)
    by_frame(frames_ref, qkv_refs, (q_ref, k_ref, v_ref))
    vt_ref[:LANES, :] = v_ref[...].T
    vt_ref[LANES:, :] = jnp.ones((vt_ref.shape[0] - LANES, token_count), jnp.bfloat16)
    step = 2 * PATCHES
    for turn in range(token_count // step):
        here = slice(turn * step, (turn + 1) * step)
        queries = head_stack(q_ref[here, :])
        ranges = [here] if turn == 0 else [slice(0, turn * step), here]
        raw = [
            lax.dot_general(k_ref[keys, :], queries, NT, preferred_element_type=jnp.float32)
            for keys in ranges
        ]
        raw[-1] = jnp.where(hidden_keys(raw[-1].shape), NEG_LARGE, raw[-1])
        top = jnp.max(raw[-1], axis=0, keepdims=True)
        for part in raw[:-1]:
            top = jnp.maximum(top, jnp.max(part, axis=0, keepdims=True))
        top = top * EXP_SCALE
        summed = None
        for keys, part in zip(ranges, raw):
            weights = jnp.exp2(part * EXP_SCALE - top).astype(jnp.bfloat16)
            update = lax.dot_general(
                vt_ref[:, keys], weights, NN, preferred_element_type=jnp.float32
            )
            summed = update if summed is None else summed + update
        totals = summed[LANES : LANES + 1, :]
        lse_ref[turn : turn + 1, :] = top + jnp.log2(totals)
        out = own_heads(summed[:LANES, :] / totals)
        ot_ref[:, here] = out
        rounded = out.T.astype(jnp.bfloat16)
        for half in range(2):
            slot = slots_ref[2 * turn + half]
            rows = pl.ds(pl.multiple_of(slot % 2 * PATCHES, PATCHES), PATCHES)
            att_ref[slot // 2, rows, :] = rounded[half * PATCHES : (half + 1) * PATCHES, :]


def attend(info, qkv, after):
    token_count = FRAME_COUNT * PATCHES
    turns = token_count // (2 * PATCHES)
    vmem = pl.BlockSpec(memory_space=pltpu.VMEM)

    def kernel(info_ref, *refs):
        attend_kernel(info_ref, refs[: len(qkv)], *refs[len(qkv) + 1 :])

    return pl.pallas_call(
        kernel,
        in_specs=[pl.BlockSpec(memory_space=pltpu.SMEM)] + [vmem] * len(qkv) + [ANYWHERE],
        out_specs=[vmem] * 3,
        out_shape=[
            jax.ShapeDtypeStruct((turns, 2 * PATCHES, LANES), jnp.bfloat16),
            jax.ShapeDtypeStruct((LANES, token_count), jnp.float32),
            jax.ShapeDtypeStruct((turns, 4 * PATCHES), jnp.float32),
        ],
        scratch_shapes=[pltpu.VMEM((token_count, LANES), jnp.bfloat16)] * 3
        + [pltpu.VMEM((LANES + 16, token_count), jnp.bfloat16)],
        compiler_params=pltpu.CompilerParams(vmem_limit_bytes=VMEM_LIMIT),
        cost_estimate=cost(10),
        name="attend",
    )(info, *qkv, after)


def attend_back_kernel(
    info_ref,
    grad_ref,
    ot_ref,
    lse_ref,
    fcos_ref,
    fsin_ref,
    pcos_ref,
    psin_ref,
    qkv_refs,
    out_ref,
    q_ref,
    k_ref,
    v_ref,
    d_ref,
    kt_ref,
    dk_ref,
    dv_ref,
):
    token_count = q_ref.shape[0]
    frames_ref, slot_frames_ref, slots_ref = (
        Shifted(info_ref, place) for place in (FRAMES_AT, GROUP_AT, SLOTS_AT)
    )
    by_frame(frames_ref, qkv_refs, (q_ref, k_ref, v_ref))
    by_frame(slot_frames_ref, (grad_ref,), (d_ref,))
    kt_ref[...] = k_ref[...].T
    step = 2 * PATCHES

    def put(frame, part, values):
        slot = slots_ref[frame]
        rows = pl.ds(pl.multiple_of(slot % 2 * PATCHES, PATCHES), PATCHES)
        out_ref[slot // 2, rows, part * LANES : (part + 1) * LANES] = values

    def turn_back(frame, values):
        values = values.astype(jnp.bfloat16).astype(jnp.float32)
        cosine = pcos_ref[...] + fcos_ref[frame : frame + 1, :]
        sine = psin_ref[...] + fsin_ref[frame : frame + 1, :]
        return (values * cosine - partner_lanes(values) * sine).astype(jnp.bfloat16)

    for turn in range(token_count // step):
        here = slice(turn * step, (turn + 1) * step)
        queries = head_stack(q_ref[here, :])
        grads_here = d_ref[here, :]
        grads = head_stack(grads_here)
        product = grads_here.astype(jnp.float32).T * ot_ref[:, here]
        delta = jnp.concatenate(
            [
                jnp.sum(product[:HEAD, :], axis=0, keepdims=True),
                jnp.sum(product[HEAD:, :], axis=0, keepdims=True),
            ],
            axis=1,
        )
        lse = lse_ref[turn : turn + 1, :]
        ranges = [here] if turn == 0 else [here, slice(0, turn * step)]
        total = None
        for keys in ranges:
            raw = lax.dot_general(
                k_ref[keys, :], queries, NT, preferred_element_type=jnp.float32
            )
            weights = jnp.exp2(raw * EXP_SCALE - lse)
            if keys is here:
                weights = jnp.where(hidden_keys(weights.shape), 0.0, weights)
            weight_grad = lax.dot_general(
                v_ref[keys, :], grads, NT, preferred_element_type=jnp.float32
            )
            score_grad = (weights * (weight_grad - delta)).astype(jnp.bfloat16)
            value_part = lax.dot_general(
                weights.astype(jnp.bfloat16), grads, NN, preferred_element_type=jnp.float32
            )
            key_part = lax.dot_general(
                score_grad, queries, NN, preferred_element_type=jnp.float32
            )
            if keys is here:
                dv_ref[keys, :] = value_part
                dk_ref[keys, :] = key_part
            else:
                dv_ref[keys, :] += value_part
                dk_ref[keys, :] += key_part
            update = lax.dot_general(
                kt_ref[:, keys], score_grad, NN, preferred_element_type=jnp.float32
            )
            total = update if total is None else total + update
        query_grad = own_heads(total).T * SCALE
        for half in range(2):
            put(
                2 * turn + half,
                0,
                turn_back(2 * turn + half, query_grad[half * PATCHES : (half + 1) * PATCHES, :]),
            )
    for frame in range(token_count // PATCHES):
        rows = slice(frame * PATCHES, (frame + 1) * PATCHES)
        put(frame, 1, turn_back(frame, dk_ref[rows, :] * SCALE))
        put(frame, 2, dv_ref[rows, :].astype(jnp.bfloat16))


def attend_back(info, qkv, grads, ot, lse, tables, after):
    token_count = FRAME_COUNT * PATCHES
    smem = pl.BlockSpec(memory_space=pltpu.SMEM)
    vmem = pl.BlockSpec(memory_space=pltpu.VMEM)

    def kernel(*refs):
        outs = 8 + len(qkv) + len(after)
        attend_back_kernel(*refs[:8], refs[8 : 8 + len(qkv)], *refs[outs:])

    return pl.pallas_call(
        kernel,
        in_specs=[smem] + [vmem] * (7 + len(qkv)) + [ANYWHERE] * len(after),
        out_specs=vmem,
        out_shape=jax.ShapeDtypeStruct(
            (token_count // (2 * PATCHES), 2 * PATCHES, 3 * LANES), jnp.bfloat16
        ),
        scratch_shapes=[pltpu.VMEM((token_count, LANES), jnp.bfloat16)] * 4
        + [pltpu.VMEM((LANES, token_count), jnp.bfloat16)]
        + [pltpu.VMEM((token_count, LANES), jnp.float32)] * 2,
        compiler_params=pltpu.CompilerParams(vmem_limit_bytes=VMEM_LIMIT),
        cost_estimate=cost(8),
        name="attend_back",
    )(info, grads, ot, lse, *tables, *qkv, *after)


def swap(values, bit):
    count = lax.axis_size(AXES)
    return lax.ppermute(values, AXES, [(index, index ^ bit) for index in range(count)])


PIECES = (0, 4, 2, 1, 5, 6, 3, 7)


def cross(values, bit):
    count = lax.axis_size("blk")
    return lax.ppermute(values, "blk", [(place, place ^ bit) for place in range(count)])


SECOND_AT, ATTENDED_AT, ATTN_AT, UP_AT, UP_ACTS = 0, D, 2 * D, 3 * D, 3 * D + FF
MLP_AT, HIDDEN_AT, DOWN_ACTS = 0, D, D + FF
FF_TILE = 512


def middle_kernel(
    info_ref,
    att_ref,
    tokens_ref,
    cot_ref,
    mod_ref,
    ow_ref,
    up_ref,
    down_ref,
    layer_ref,
    upper_ref,
    lower_ref,
    datt_ref,
    dmid_ref,
    dmod_ref,
    attn_ref,
    mid_ref,
    mlp_ref,
    dsec_ref,
):
    step = pl.program_id(0)
    slot_rows = [slice(slot * PATCHES, (slot + 1) * PATCHES) for slot in range(2)]

    def member(slot, which):
        return mod_ref[pl.ds(info_ref[MINE_AT + slot], 1), which * D : (which + 1) * D]

    @pl.when(step == 0)
    def _():
        for group in range(D // LANES):
            upper_ref[:, ATTENDED_AT + group * LANES : ATTENDED_AT + (group + 1) * LANES] = att_ref[
                group
            ]
        attn_ref[...] = lax.dot_general(
            upper_ref[:, ATTENDED_AT : ATTENDED_AT + D],
            ow_ref[...],
            NN,
            preferred_element_type=jnp.float32,
        )
        for slot, rows in enumerate(slot_rows):
            middle = tokens_ref[rows, :].astype(jnp.float32) + member(slot, 2) * attn_ref[rows, :]
            mid_ref[rows, :] = middle
            normed, unused = normalize(middle)
            upper_ref[rows, SECOND_AT : SECOND_AT + D] = (
                normed * (1.0 + member(slot, 4)) + member(slot, 3)
            ).astype(jnp.bfloat16)
            lower_ref[rows, MLP_AT : MLP_AT + D] = (
                cot_ref[rows, :].astype(jnp.float32) * member(slot, 5)
            ).astype(jnp.bfloat16)
        mlp_ref[...] = jnp.zeros_like(mlp_ref)
        dsec_ref[...] = jnp.zeros_like(dsec_ref)

    up_lin = lax.dot_general(
        upper_ref[:, SECOND_AT : SECOND_AT + D],
        up_ref[...],
        NN,
        preferred_element_type=jnp.float32,
    )
    below = 0.5 + 0.5 * lax.erf(up_lin * 0.7071067811865476)
    density = jnp.exp(up_lin * up_lin * -0.5) * 0.3989422804014327
    hidden = (up_lin * below).astype(jnp.bfloat16)
    d_hidden = lax.dot_general(
        lower_ref[:, MLP_AT : MLP_AT + D], down_ref[...], NT, preferred_element_type=jnp.float32
    )
    d_up = (d_hidden * (below + up_lin * density)).astype(jnp.bfloat16)
    lower_ref[:, pl.ds(pl.multiple_of(HIDDEN_AT + step * FF_TILE, FF_TILE), FF_TILE)] = hidden
    upper_ref[:, pl.ds(pl.multiple_of(UP_AT + step * FF_TILE, FF_TILE), FF_TILE)] = d_up
    mlp_ref[...] += lax.dot_general(
        hidden, down_ref[...], NN, preferred_element_type=jnp.float32
    )
    dsec_ref[...] += lax.dot_general(d_up, up_ref[...], NT, preferred_element_type=jnp.float32)

    @pl.when(step == pl.num_programs(0) - 1)
    def _():
        for slot, rows in enumerate(slot_rows):
            middle = mid_ref[rows, :]
            mlp_out = mlp_ref[rows, :]
            cotangent = cot_ref[rows, :].astype(jnp.float32)
            layer_ref[rows, :] = (middle + member(slot, 5) * mlp_out).astype(jnp.bfloat16)
            normed, inverse = normalize(middle)
            d_second = dsec_ref[rows, :]
            d_middle = cotangent + norm_backward(
                d_second * (1.0 + member(slot, 4)), normed, inverse
            )
            dmid_ref[rows, :] = d_middle
            upper_ref[rows, ATTN_AT : ATTN_AT + D] = (d_middle * member(slot, 2)).astype(
                jnp.bfloat16
            )
            for place, values in enumerate(
                (d_middle * attn_ref[rows, :], d_second, d_second * normed, cotangent * mlp_out)
            ):
                dmod_ref[slot : slot + 1, place * D : (place + 1) * D] = jnp.sum(
                    values, axis=0, keepdims=True
                )
        d_attended = lax.dot_general(
            upper_ref[:, ATTN_AT : ATTN_AT + D],
            ow_ref[...],
            NT,
            preferred_element_type=jnp.float32,
        ).astype(jnp.bfloat16)
        for group in range(D // LANES):
            datt_ref[group] = d_attended[:, group * LANES : (group + 1) * LANES]


def middle_block(info, att, tokens_here, cot_here, modulation, out_weight, fc1_weight, fc2_weight):
    rows = tokens_here.shape[0]
    return pl.pallas_call(
        middle_kernel,
        grid_spec=pltpu.PrefetchScalarGridSpec(
            num_scalar_prefetch=1,
            grid=(FF // FF_TILE,),
            in_specs=[
                full_block(att.shape),
                full_block((rows, D)),
                full_block((rows, D)),
                full_block(modulation.shape),
                full_block((D, D)),
                pl.BlockSpec((D, FF_TILE), lambda f, frames: (0, f)),
                pl.BlockSpec((FF_TILE, D), lambda f, frames: (f, 0)),
            ],
            out_specs=[
                full_block((rows, D)),
                full_block((rows, UP_ACTS)),
                full_block((rows, DOWN_ACTS)),
                full_block(att.shape),
                full_block((rows, D)),
                full_block((2, 4 * D)),
            ],
            scratch_shapes=[pltpu.VMEM((rows, D), jnp.float32)] * 4,
        ),
        out_shape=[
            jax.ShapeDtypeStruct((rows, D), jnp.bfloat16),
            jax.ShapeDtypeStruct((rows, UP_ACTS), jnp.bfloat16),
            jax.ShapeDtypeStruct((rows, DOWN_ACTS), jnp.bfloat16),
            jax.ShapeDtypeStruct(att.shape, jnp.bfloat16),
            jax.ShapeDtypeStruct((rows, D), jnp.float32),
            jax.ShapeDtypeStruct((2, 4 * D), jnp.float32),
        ],
        compiler_params=pltpu.CompilerParams(
            vmem_limit_bytes=VMEM_LIMIT, dimension_semantics=("arbitrary",)
        ),
        cost_estimate=cost(21),
        name="middle_block",
    )(info, att, tokens_here, cot_here, modulation, out_weight, fc1_weight, fc2_weight)


CHIPS = 16
TILE = 256
FINE = D // CHIPS // 2
UPPER_JOBS = ((SECOND_AT, FINE, UP_AT, FF, 10), (ATTENDED_AT, FINE, ATTN_AT, D, 2))
LOWER_JOBS = ((HIDDEN_AT, LANES, MLP_AT, D, 2),)


def rows_of(jobs):
    first = sum(height * tiles for unused, height, unused_at, width, tiles in jobs)
    return first, sum(job[1] * (job[3] // TILE) for job in jobs) - first


def weight_kernel(jobs, info_ref, mine_ref, theirs_ref, *refs):
    keep_a, send_a, keep_b, send_b = refs[-4 - len(jobs) : -len(jobs)]
    left_refs = refs[-len(jobs) :]
    core, xbit, ybit = (info_ref[BITS_AT + place] for place in range(3))
    rows = mine_ref.shape[0]
    row_a = row_b = 0
    for (left_at, height, right_at, width, tiles), left_ref in zip(jobs, left_refs):
        for place, ref in enumerate((mine_ref, theirs_ref)):
            columns = slice(place * rows, (place + 1) * rows)
            if height == LANES:
                for chip in range(CHIPS):
                    source = pl.multiple_of(left_at + (2 * chip + core) * LANES, LANES)
                    left_ref[chip * LANES : (chip + 1) * LANES, columns] = ref[
                        :, pl.ds(source, LANES)
                    ].T
            else:
                turned = ref[:, left_at : left_at + D].T.reshape(CHIPS, 2, height, rows)
                left_ref[:, columns] = jnp.where(core == 0, turned[:, 0], turned[:, 1]).reshape(
                    CHIPS * height, rows
                )
        for tile in range(width // TILE):
            source = right_at + tile * TILE
            right = jnp.concatenate(
                [mine_ref[:, source : source + TILE], theirs_ref[:, source : source + TILE]],
                axis=0,
            )
            part = lax.dot_general(
                left_ref[...], right, NN, preferred_element_type=jnp.float32
            ).astype(jnp.bfloat16)
            if tile < tiles:
                part = part.reshape(CHIPS // 2, 2, height, TILE)
                low, high = part[:, 0], part[:, 1]
                out_rows = slice(row_a, row_a + height)
                keep_a[:, out_rows, :] = jnp.where(xbit == 0, low, high)
                send_a[:, out_rows, :] = jnp.where(xbit == 0, high, low)
                row_a += height
            else:
                part = part.reshape(CHIPS // 4, 2, 2, height, TILE)
                low, high = part[:, 0], part[:, 1]
                out_rows = slice(row_b, row_b + height)
                keep_b[:, :, out_rows, :] = jnp.where(ybit == 0, low, high)
                send_b[:, :, out_rows, :] = jnp.where(ybit == 0, high, low)
                row_b += height


def weight_parts(jobs, info, mine, theirs, after, expense):
    rows = mine.shape[0]
    vmem = pl.BlockSpec(memory_space=pltpu.VMEM)
    rows_a, rows_b = rows_of(jobs)
    first = jax.ShapeDtypeStruct((CHIPS // 2, rows_a, TILE), jnp.bfloat16)
    second = jax.ShapeDtypeStruct((CHIPS // 4, 2, rows_b, TILE), jnp.bfloat16)
    return pl.pallas_call(
        partial(weight_kernel, jobs),
        in_specs=[pl.BlockSpec(memory_space=pltpu.SMEM), vmem, vmem] + [ANYWHERE] * len(after),
        out_specs=[vmem] * 4,
        out_shape=[first, first, second, second],
        scratch_shapes=[pltpu.VMEM((CHIPS * job[1], 2 * rows), jnp.bfloat16) for job in jobs],
        compiler_params=pltpu.CompilerParams(vmem_limit_bytes=VMEM_LIMIT),
        cost_estimate=cost(expense),
        name="weight_parts",
    )(info, mine, theirs, *after)


WEIGHT_ROWS = 256
QUARTER = 6 * D // 4


def first_back_kernel(
    info_ref,
    dqkv_ref,
    tokens_ref,
    mod_ref,
    dmid_ref,
    early_ref,
    weight_ref,
    *refs,
):
    grad_ref, packed_ref, flat_ref, total_ref, wide_ref = refs[-5:]
    step = pl.program_id(0)

    @pl.when(step == 0)
    def _():
        for group in range(D // LANES):
            for part in range(3):
                column = part * D + group * LANES
                flat_ref[:, column : column + LANES] = dqkv_ref[
                    group, :, part * LANES : (part + 1) * LANES
                ]

    columns = pl.ds(pl.multiple_of(step * WEIGHT_ROWS, WEIGHT_ROWS), WEIGHT_ROWS)
    total_ref[:, columns] = lax.dot_general(
        flat_ref[...], weight_ref[...], NT, preferred_element_type=jnp.float32
    )

    @pl.when(step == pl.num_programs(0) - 1)
    def _():
        for slot in range(2):
            rows = slice(slot * PATCHES, (slot + 1) * PATCHES)
            normed, inverse = normalize(tokens_ref[rows, :].astype(jnp.float32))
            d_first = total_ref[rows, :]
            scale = mod_ref[pl.ds(info_ref[MINE_AT + slot], 1), D : 2 * D]
            grad_ref[rows, :] = (
                dmid_ref[rows, :] + norm_backward(d_first * (1.0 + scale), normed, inverse)
            ).astype(jnp.bfloat16)
            pieces = (
                (0, jnp.sum(d_first, axis=0, keepdims=True)),
                (D, jnp.sum(d_first * normed, axis=0, keepdims=True)),
                (2 * D, early_ref[slot : slot + 1, :]),
            )
            for start, piece in pieces:
                for quarter in range(4):
                    low = max(start, quarter * QUARTER)
                    high = min(start + piece.shape[1], (quarter + 1) * QUARTER)
                    if low < high:
                        wide_ref[
                            2 * quarter + slot : 2 * quarter + slot + 1,
                            low - quarter * QUARTER : high - quarter * QUARTER,
                        ] = piece[:, low - start : high - start]
        packed_ref[...] = wide_ref[...].astype(jnp.bfloat16)


def first_back(info, d_qkv, tokens_here, modulation, d_middle, early, qkv_weight, after):
    rows = tokens_here.shape[0]
    return pl.pallas_call(
        first_back_kernel,
        grid_spec=pltpu.PrefetchScalarGridSpec(
            num_scalar_prefetch=1,
            grid=(D // WEIGHT_ROWS,),
            in_specs=[
                full_block(d_qkv.shape),
                full_block((rows, D)),
                full_block(modulation.shape),
                full_block((rows, D)),
                full_block(early.shape),
                pl.BlockSpec((WEIGHT_ROWS, 3 * D), lambda i, frames: (i, 0)),
            ]
            + [ANYWHERE] * len(after),
            out_specs=[full_block((rows, D)), full_block((8, QUARTER))],
            scratch_shapes=[
                pltpu.VMEM((rows, 3 * D), jnp.bfloat16),
                pltpu.VMEM((rows, D), jnp.float32),
                pltpu.VMEM((8, QUARTER), jnp.float32),
            ],
        ),
        out_shape=[
            jax.ShapeDtypeStruct((rows, D), jnp.bfloat16),
            jax.ShapeDtypeStruct((8, QUARTER), jnp.bfloat16),
        ],
        compiler_params=pltpu.CompilerParams(
            vmem_limit_bytes=VMEM_LIMIT, dimension_semantics=("arbitrary",)
        ),
        cost_estimate=cost(6),
        name="first_back",
    )(info, d_qkv, tokens_here, modulation, d_middle, early, qkv_weight, *after)


def qkv_part_kernel(info_ref, first_refs, grad_ref, keep_ref, send_ref):
    pieces = [(ref, piece) for ref in first_refs for piece in range(ref.shape[0])]
    total = None
    for place, (ref, piece) in enumerate(pieces):
        update = lax.dot_general(
            ref[piece],
            grad_ref[info_ref[ORDER_AT + place]],
            (((0,), (0,)), ((), ())),
            preferred_element_type=jnp.float32,
        )
        total = update if total is None else total + update
    groups, clip_pairs, share, width = keep_ref.shape
    split = total.astype(jnp.bfloat16).reshape(groups, clip_pairs, 2, share, width)
    low, high = split[:, :, 0], split[:, :, 1]
    keep_ref[...] = jnp.where(info_ref[BITS_AT] == 0, low, high)
    send_ref[...] = jnp.where(info_ref[BITS_AT] == 0, high, low)


def qkv_parts(info, firsts, d_heads, share, after):
    vmem = pl.BlockSpec(memory_space=pltpu.VMEM)
    shape = (D // LANES, 2, share, d_heads.shape[2])

    def kernel(info_ref, *refs):
        count = len(firsts)
        qkv_part_kernel(info_ref, refs[:count], refs[count], *refs[-2:])

    return pl.pallas_call(
        kernel,
        in_specs=[pl.BlockSpec(memory_space=pltpu.SMEM)]
        + [vmem] * (len(firsts) + 1)
        + [ANYWHERE] * len(after),
        out_specs=[vmem] * 2,
        out_shape=[jax.ShapeDtypeStruct(shape, jnp.bfloat16)] * 2,
        compiler_params=pltpu.CompilerParams(vmem_limit_bytes=VMEM_LIMIT),
        cost_estimate=cost(0.2),
        name="qkv_parts",
    )(info, *firsts, d_heads, *after)


def pair_sum(keep, got):
    return (keep.astype(jnp.float32) + got.astype(jnp.float32)).astype(jnp.bfloat16)


def fold_kernel(bits, info_ref, *refs):
    count = len(bits)
    out_refs = refs[-2 * count :]
    for place, bit_at in enumerate(bits):
        keep, got = refs[2 * place : 2 * place + 2]
        low, high = pair_sum(keep[:, 0], got[:, 0]), pair_sum(keep[:, 1], got[:, 1])
        bit = info_ref[BITS_AT + bit_at]
        kept, sent = out_refs[2 * place : 2 * place + 2]
        kept[...] = jnp.where(bit == 0, low, high)
        sent[...] = jnp.where(bit == 0, high, low)


def fold(info, bits, pairs, after, expense):
    count, unused, unused_rows, columns = pairs[0][0].shape
    in_specs, out_specs, out_shape = [], [], []
    for keep, got in pairs:
        rows = keep.shape[2]
        in_specs += [full_block((count, 2, rows, columns))] * 2
        out_specs += [full_block((count, rows, columns))] * 2
        out_shape += [jax.ShapeDtypeStruct((count, rows, columns), jnp.bfloat16)] * 2
    return pl.pallas_call(
        partial(fold_kernel, bits),
        grid_spec=pltpu.PrefetchScalarGridSpec(
            num_scalar_prefetch=1,
            grid=(1,),
            in_specs=in_specs + [ANYWHERE] * len(after),
            out_specs=out_specs,
        ),
        out_shape=out_shape,
        compiler_params=pltpu.CompilerParams(
            vmem_limit_bytes=VMEM_LIMIT, dimension_semantics=("arbitrary",)
        ),
        cost_estimate=cost(expense),
        name="fold",
    )(info, *(part for pair in pairs for part in pair), *after)


def blend_kernel(riders, keep_a, got_a, keep_b, got_b, *refs):
    out_ref = refs[-1]
    row = 0
    for keep, got in ((keep_a, got_a), (keep_b, got_b)):
        height = keep.shape[1]
        out_ref[:, row : row + height, :] = pair_sum(keep[...], got[...])
        row += height
    for side, rider in enumerate(refs[:riders]):
        height = rider.shape[1]
        out_ref[:, row + side * height : row + (side + 1) * height, :] = rider[:, :, :TILE]
        last = row + riders * height
        out_ref[:, last : last + height, side * LANES : (side + 1) * LANES] = rider[:, :, TILE:]


def blend(parts, riders, after, expense):
    rows = sum(part.shape[1] for part in parts[::2]) + (3 * FINE if riders else 0)
    count, columns = parts[0].shape[0], parts[0].shape[2]
    operands = tuple(parts) + tuple(riders)
    return pl.pallas_call(
        partial(blend_kernel, len(riders)),
        grid=(1,),
        in_specs=[full_block(part.shape) for part in operands]
        + [ANYWHERE] * len(after),
        out_specs=full_block((count, rows, columns)),
        out_shape=jax.ShapeDtypeStruct((count, rows, columns), jnp.bfloat16),
        compiler_params=pltpu.CompilerParams(
            vmem_limit_bytes=VMEM_LIMIT, dimension_semantics=("arbitrary",)
        ),
        cost_estimate=cost(expense),
        name="blend",
    )(*operands, *after)


def join_kernel(mine_ref, theirs_ref, *refs):
    count = mine_ref.shape[0]
    refs[-1][:count] = mine_ref[...]
    refs[-1][count:] = theirs_ref[...]


def join(mine, theirs, after):
    vmem = pl.BlockSpec(memory_space=pltpu.VMEM)
    return pl.pallas_call(
        join_kernel,
        in_specs=[vmem, vmem] + [ANYWHERE] * len(after),
        out_specs=vmem,
        out_shape=jax.ShapeDtypeStruct((2 * mine.shape[0],) + mine.shape[1:], mine.dtype),
        compiler_params=pltpu.CompilerParams(vmem_limit_bytes=VMEM_LIMIT),
        cost_estimate=cost(0.5),
        name="join",
    )(mine, theirs, *after)


def add_kernel(bit_at, info_ref, keep_ref, got_ref, *refs):
    low, high = (
        (keep_ref[:, half].astype(jnp.float32) + got_ref[:, half].astype(jnp.float32)).astype(
            jnp.bfloat16
        )
        for half in range(2)
    )
    bit = info_ref[BITS_AT + bit_at]
    refs[-2][...] = jnp.where(bit == 0, low, high)
    refs[-1][...] = jnp.where(bit == 0, high, low)


def add_halves(info, keep, got, bit_at, after):
    vmem = pl.BlockSpec(memory_space=pltpu.VMEM)
    out = jax.ShapeDtypeStruct(keep.shape[:1] + keep.shape[2:], jnp.bfloat16)
    return pl.pallas_call(
        partial(add_kernel, bit_at),
        in_specs=[pl.BlockSpec(memory_space=pltpu.SMEM), vmem, vmem] + [ANYWHERE] * len(after),
        out_specs=[vmem] * 2,
        out_shape=[out] * 2,
        cost_estimate=cost(1),
        name="add_halves",
    )(info, keep, got, *after)


def finish_kernel(jobs, riders, info_ref, parts_ref, *refs):
    targets = refs[-len(jobs) - riders :]
    row = [0, rows_of(jobs)[0]]
    for (unused, height, unused_at, width, tiles), target in zip(jobs, targets):
        for tile in range(width // TILE):
            second = tile >= tiles
            rows = slice(row[second], row[second] + height)
            total = parts_ref[0, rows, :].astype(jnp.float32)
            for part in range(1, parts_ref.shape[0]):
                total = total + parts_ref[part, rows, :].astype(jnp.float32)
            target[:, tile * TILE : (tile + 1) * TILE] = total
            row[second] += height
    if riders:
        first_row = sum(rows_of(jobs))
        ybit = info_ref[BITS_AT + 2]
        for place in range(parts_ref.shape[0]):
            for side in range(2):
                group = 2 * place + (ybit if side == 0 else 1 - ybit)
                for part in range(3):
                    row_at, lane_at = ((side, 0), (side, 1), (2, side))[part]
                    rows = slice(first_row + row_at * FINE, first_row + (row_at + 1) * FINE)
                    lanes = slice(lane_at * LANES, (lane_at + 1) * LANES)
                    column = pl.multiple_of(part * D + group * LANES, LANES)
                    targets[-1][:, pl.ds(column, LANES)] = parts_ref[place, rows, lanes].astype(
                        jnp.float32
                    )


def finish(info, jobs, parts, riders, after):
    vmem = pl.BlockSpec(memory_space=pltpu.VMEM)
    shapes = [(job[1], job[3]) for job in jobs] + [(FINE, 3 * D)] * riders
    return pl.pallas_call(
        partial(finish_kernel, jobs, riders),
        in_specs=[pl.BlockSpec(memory_space=pltpu.SMEM), vmem] + [ANYWHERE] * len(after),
        out_specs=[vmem] * len(shapes),
        out_shape=[jax.ShapeDtypeStruct(shape, jnp.float32) for shape in shapes],
        compiler_params=pltpu.CompilerParams(vmem_limit_bytes=VMEM_LIMIT),
        cost_estimate=cost(2),
        name="finish",
    )(info, parts, *after)


def closing_kernel(all_ref, embedded_ref, weight_ref, hot_ref, modw_ref, table_ref, bias_ref):
    rows = all_ref.shape[0]
    slots, share = embedded_ref.shape
    embedded = embedded_ref[...]
    sigmoid = jax.nn.sigmoid(embedded)
    activated = (embedded * sigmoid).astype(jnp.bfloat16)
    row = lax.broadcasted_iota(jnp.int32, (slots, rows), 1)
    slot = lax.broadcasted_iota(jnp.int32, (slots, rows), 0)
    d_activated = None
    for quarter in range(4):
        columns = slice(quarter * QUARTER, (quarter + 1) * QUARTER)
        chosen = jnp.where(row == slot // 2 * 8 + 2 * quarter + slot % 2, 1.0, 0.0)
        spread = lax.dot_general(
            activated,
            chosen.astype(jnp.bfloat16),
            (((0,), (0,)), ((), ())),
            preferred_element_type=jnp.float32,
        ).astype(jnp.bfloat16)
        modw_ref[:, columns] = lax.dot_general(
            spread, all_ref[...], NN, preferred_element_type=jnp.float32
        )
        every = jnp.where(
            lax.broadcasted_iota(jnp.int32, (8, rows), 1) % 8 // 2 == quarter, 1.0, 0.0
        ).astype(jnp.bfloat16)
        bias_ref[:, columns] = lax.dot_general(
            every, all_ref[...], NN, preferred_element_type=jnp.float32
        )[:1, :]
        part = lax.dot_general(
            all_ref[...], weight_ref[:, columns], NT, preferred_element_type=jnp.float32
        )
        part = lax.dot_general(
            chosen,
            part,
            NN,
            precision=lax.Precision.HIGHEST,
            preferred_element_type=jnp.float32,
        )
        d_activated = part if d_activated is None else d_activated + part
    d_embedded = d_activated * (sigmoid * (1.0 + embedded * (1.0 - sigmoid)))
    table_ref[...] = lax.dot_general(
        hot_ref[...],
        d_embedded,
        NN,
        precision=lax.Precision.HIGHEST,
        preferred_element_type=jnp.float32,
    )


def closing(gathered, embedded, weight_rows, level_hot):
    vmem = pl.BlockSpec(memory_space=pltpu.VMEM)
    share = embedded.shape[1]
    return pl.pallas_call(
        closing_kernel,
        in_specs=[vmem] * 4,
        out_specs=[vmem] * 3,
        out_shape=[
            jax.ShapeDtypeStruct((share, 6 * D), jnp.float32),
            jax.ShapeDtypeStruct((LEVELS, share), jnp.float32),
            jax.ShapeDtypeStruct((1, 6 * D), jnp.float32),
        ],
        compiler_params=pltpu.CompilerParams(vmem_limit_bytes=VMEM_LIMIT),
        cost_estimate=cost(3),
        name="closing",
    )(gathered, embedded, weight_rows, level_hot)


def halved(part):
    return part.reshape((-1, 2) + part.shape[-2:])


def across(info, parts, after, expense):
    keep_a, got_a, keep_b, got_b = (halved(part) for part in parts)
    keep_a, send_a, keep_b, send_b = fold(
        info, (2, 1), ((keep_a, got_a), (keep_b, got_b)), after, expense
    )
    return (keep_a, swap(send_a, 4), keep_b, swap(send_b, 2)), send_a


def along(parts, riders, after, expense):
    total = blend(parts, riders, after, expense)
    columns = [[2 * place + side for place in range(4)] for side in range(2)]
    return lax.all_to_all(total, "blk", 0, 0, axis_index_groups=columns, tiled=True), total


def local_heads(
    tokens,
    noise_levels,
    group_map,
    noise_table,
    mod_weight,
    mod_bias,
    qkv_weight,
    out_weight,
    fc1_weight,
    fc2_weight,
    out_cotangent,
):
    rows_here = 2 * PATCHES
    frame_count = group_map.shape[0]
    groups = D // LANES
    device_count = lax.axis_size(AXES)
    index = lax.axis_index(AXES)
    bits = [(index >> place) & 1 for place in range(5)]
    tables = rope_tables(frame_count)
    clip_levels = noise_levels
    for bit in (1, 2):
        clip_levels = jnp.concatenate([clip_levels, swap(clip_levels, bit)], axis=0)
    members = jnp.zeros((1,), jnp.int32)
    for bit in (16, 8, 4, 2, 1):
        members = jnp.concatenate([members, members ^ bit])
    member_slots = (2 * ((index ^ members) >> 2))[:, None] + jnp.arange(2, dtype=jnp.int32)[None, :]
    levels_all = clip_levels[(members & 3)[:, None], group_map[member_slots]].reshape(
        2 * device_count
    )
    tokens_here = tokens.reshape(rows_here, D)
    block = lax.axis_index("blk")
    piece_at = block ^ jnp.array(PIECES, jnp.int32)
    places = jnp.arange(frame_count, dtype=jnp.int32)
    piece_slots = ((2 * piece_at)[:, None] + jnp.arange(2, dtype=jnp.int32)[None, :]).reshape(-1)
    frames = jnp.sum(
        jnp.where(piece_slots[:, None] == places[None, :], group_map[None, :], 0), axis=1
    )
    slots = jnp.sum(jnp.where(group_map[None, :] == places[:, None], places[None, :], 0), axis=1)
    info = jnp.concatenate(
        [jnp.stack(bits), piece_at, frames, slots, group_map, frames[:2]]
    ).astype(jnp.int32)
    far = cross(tokens_here, 4)
    side = cross(tokens_here, 1)
    near = cross(tokens_here, 2)
    far_side, far_near, near_side = cross(far, 1), cross(far, 2), cross(side, 2)
    last = (cross(far_near[:PATCHES], 1), cross(far_side[PATCHES:], 2))
    modulation = modulate(
        noise_levels, noise_table, mod_weight, mod_bias
    )
    weight_here = own_columns(info, qkv_weight)
    projected = []
    for first_piece, pieces in (
        (0, (tokens_here,)),
        (1, (far, near, side)),
        (4, (far_side, far_near, near_side)),
        (7, (last,)),
    ):
        projected.append(project(info, modulation, weight_here, tables, first_piece, pieces))
    qkv_heads = [pair[0] for pair in projected]
    firsts = [pair[1] for pair in projected]
    att_heads, ot, lse = attend(info, qkv_heads, levels_all)
    att = lax.all_to_all(att_heads, "blk", 0, 0, tiled=True)
    layer_out, up_acts, down_acts, d_att, d_middle, d_mod_early = middle_block(
        info,
        att,
        tokens_here,
        out_cotangent.reshape(rows_here, D),
        modulation,
        out_weight,
        fc1_weight,
        fc2_weight,
    )
    grad_heads = lax.all_to_all(d_att, "blk", 0, 0, tiled=True)
    share = D // device_count
    keep_a, send_a, keep_b, send_b = weight_parts(
        UPPER_JOBS, info, up_acts, swap(up_acts, 1), (), 2)
    upper = (keep_a, swap(send_a, 2), keep_b, swap(send_b, 4))
    d_heads = attend_back(info, qkv_heads, grad_heads, ot, lse, tables, (send_a,))
    d_qkv = lax.all_to_all(d_heads, "blk", 0, 0, tiled=True)
    qkv_keep, qkv_send = qkv_parts(info, firsts, d_heads, share, ())
    qkv_keep, qkv_send = add_halves(info, qkv_keep, swap(qkv_send, 1), 1, ())
    qkv_got = swap(qkv_send, 2)
    upper, upper_sent = across(info, upper, (qkv_send,), 6)
    keep_a, send_a, keep_b, send_b = weight_parts(
        LOWER_JOBS, info, down_acts, swap(down_acts, 1), (upper_sent, qkv_got, upper[3]), 3)
    lower = (keep_a, swap(send_a, 2), keep_b, swap(send_b, 4))
    upper, upper_z = along(upper, (), (send_a,), 1)
    tokens_grad, d_mod = first_back(
        info, d_qkv, tokens_here, modulation, d_middle, d_mod_early, qkv_weight, (upper_z,)
    )
    pairs = (groups // 2, 2, share, 3 * LANES)
    qkv_keep, qkv_send = add_halves(
        info, qkv_keep.reshape(pairs), qkv_got.reshape(pairs), 2, (d_mod,)
    )
    qkv_got = swap(qkv_send, 4)
    got = swap(d_mod, 16)
    lower, lower_sent = across(info, lower, (qkv_send,), 15)
    d_mod = join(d_mod, got, (lower_sent,))
    got = swap(d_mod, 8)
    lower, lower_z = along(lower, (qkv_keep, qkv_got), (d_mod,), 5)
    d_mod = join(d_mod, got, (lower_z,))
    for bit in (4, 2, 1):
        d_mod = jnp.concatenate([d_mod, swap(d_mod, bit)])
    level_hot = jnp.arange(LEVELS, dtype=jnp.int32)[:, None] == levels_all[None, :]
    table_columns = lax.dynamic_slice_in_dim(noise_table, index * share, share, 1)
    embedded_columns = jnp.einsum(
        "ls,lc->sc",
        level_hot.astype(jnp.bfloat16),
        table_columns,
        preferred_element_type=jnp.float32,
    )
    weight_rows = lax.dynamic_slice_in_dim(mod_weight, index * share, share, 0)
    modw_share, table_share, bias_sums = closing(
        d_mod, embedded_columns, weight_rows, level_hot.astype(jnp.float32)
    )
    bias_columns = 6 * D // device_count
    bias_share = lax.dynamic_slice_in_dim(bias_sums[0], index * bias_columns, bias_columns)
    upper_share, outw_share = finish(info, UPPER_JOBS, upper, 0, (lower_z,))
    lower_share, qkv_share = finish(
        info, LOWER_JOBS, lower, 1, (upper_share, table_share, modw_share, bias_share)
    )
    return (
        layer_out[None].reshape(1, 2, PATCHES, D),
        tokens_grad.reshape(1, 2, PATCHES, D),
        table_share,
        modw_share,
        bias_share,
        qkv_share,
        outw_share,
        upper_share,
        lower_share,
    )


def solution(mesh):
    pair_split = mesh.shape["blk"] * LANES == D and mesh.shape["clip"] == 4
    return jax.shard_map(
        local_heads if pair_split else local,
        mesh=mesh,
        in_specs=(
            P("clip", "blk", None, None),
            P("clip", None),
            P(),
            P(),
            P(),
            P(),
            P(),
            P(),
            P(),
            P(),
            P("clip", "blk", None, None),
        ),
        out_specs=(
            P("clip", "blk", None, None),
            P("clip", "blk", None, None),
            P(None, ("blk", "clip")),
            P(("blk", "clip"), None),
            P(("blk", "clip")),
            P(("blk", "clip"), None),
            P(("blk", "clip"), None),
            P(("blk", "clip"), None),
            P(("blk", "clip"), None),
        ),
        check_vma=False,
    )
```

```python
from functools import partial

import jax
import jax.numpy as jnp
import numpy as np
from jax import lax
from jax.experimental import pallas as pl
from jax.experimental.pallas import tpu as pltpu
from jax.sharding import PartitionSpec as P

D = 1024
HEAD = 64
HEADS = 16
LEVELS = 1000
GRID_H = 8
GRID_W = 16
PATCHES = 128


SCALE = 0.125
EPSILON = 1e-06
ROPE_BASE = 10000.0
NEG_LARGE = -1e30


def token_positions(frame_ids):
    slot_count = frame_ids.shape[0]
    total_rows = slot_count * GRID_H * GRID_W
    patch_ids = jnp.arange(total_rows, dtype=jnp.int32) % (GRID_H * GRID_W)
    frame_pos = jnp.repeat(frame_ids, GRID_H * GRID_W, total_repeat_length=total_rows)
    return (frame_pos, patch_ids // GRID_W, patch_ids % GRID_W)


def rope_angles(frame_pos, row_pos, col_pos):
    angle_list = []
    for position, comp_width in ((frame_pos, 16), (row_pos, 24), (col_pos, 24)):
        half_width = comp_width // 2
        frequency = ROPE_BASE ** (-2.0 * jnp.arange(half_width, dtype=jnp.float32) / comp_width)
        angle_list.append(position.astype(jnp.float32)[:, None] * frequency[None, :])
    return angle_list


def rotate(values, angle_list, direction):
    pieces = []
    offset = 0
    for angles in angle_list:
        half_width = angles.shape[1]
        first_half = values[:, :, offset : offset + half_width]
        second_half = values[:, :, offset + half_width : offset + 2 * half_width]
        cosine = jnp.cos(angles)[:, None, :]
        sine_part = direction * jnp.sin(angles)[:, None, :]
        pieces.append(first_half * cosine - second_half * sine_part)
        pieces.append(first_half * sine_part + second_half * cosine)
        offset = offset + 2 * half_width
    return jnp.concatenate(pieces, axis=2)


def normalize(values):
    center = values - jnp.mean(values, axis=-1, keepdims=True)
    inverse = lax.rsqrt(jnp.mean(center * center, axis=-1, keepdims=True) + EPSILON)
    return (center * inverse, inverse)


def norm_backward(grad_in, normed, inverse):
    return inverse * (
        grad_in
        - jnp.mean(grad_in, axis=-1, keepdims=True)
        - normed * jnp.mean(grad_in * normed, axis=-1, keepdims=True)
    )


def frames_of(group_map, first_row, row_count):
    slot_frames = lax.dynamic_slice_in_dim(group_map, first_row // PATCHES, row_count // PATCHES)
    return jnp.repeat(slot_frames, PATCHES, total_repeat_length=row_count)


def block_size(row_count, shard_rows):
    return 2 * shard_rows if row_count // shard_rows % 2 == 0 else shard_rows


def keep_same(values):
    return values


def local(
    tokens,
    noise_levels,
    group_map,
    noise_table,
    mod_weight,
    mod_bias,
    qkv_weight,
    out_weight,
    fc1_weight,
    fc2_weight,
    out_cotangent,
):
    rows_here = 2 * PATCHES
    my_frames = lax.dynamic_slice_in_dim(group_map, 2 * lax.axis_index("blk"), 2)
    frame_hot = (
        jnp.arange(group_map.shape[0], dtype=jnp.int32)[None, :] == my_frames[:, None]
    ).astype(jnp.int32)
    my_levels = jnp.sum(frame_hot * noise_levels[0][None, :], axis=1)
    level_hot = jnp.arange(LEVELS, dtype=jnp.int32)[None, :] == my_levels[:, None]
    embedded = jnp.dot(
        level_hot.astype(jnp.bfloat16), noise_table, preferred_element_type=jnp.float32
    )
    activated = jax.nn.silu(embedded).astype(jnp.bfloat16)
    modulation = (
        jnp.dot(activated, mod_weight, preferred_element_type=jnp.float32)
        + mod_bias.astype(jnp.float32)[None, :]
    )
    shift_one, scale_one, gate_one, shift_two, scale_two, gate_two = [
        modulation[:, member * D : (member + 1) * D][:, None, :] for member in range(6)
    ]
    inputs_here = tokens[0].astype(jnp.float32)
    normed_one, inverse_one = normalize(inputs_here)
    first_in = (
        (normed_one * (1.0 + scale_one) + shift_one).astype(jnp.bfloat16).reshape(rows_here, D)
    )
    qkv_lin = jnp.dot(first_in, qkv_weight, preferred_element_type=jnp.float32)
    token_frames, row_pos, col_pos = token_positions(my_frames)
    angle_list = rope_angles(token_frames, row_pos, col_pos)
    query = rotate(qkv_lin[:, :D].reshape(rows_here, HEADS, HEAD), angle_list, 1.0).astype(
        jnp.bfloat16
    )
    key_part = rotate(
        qkv_lin[:, D : 2 * D].reshape(rows_here, HEADS, HEAD), angle_list, 1.0
    ).astype(jnp.bfloat16)
    value_part = qkv_lin[:, 2 * D :].reshape(rows_here, HEADS, HEAD).astype(jnp.bfloat16)
    top_frame = jnp.max(my_frames)
    own_lowest = jnp.min(my_frames)
    forward_start = (
        jnp.full((HEADS, rows_here), NEG_LARGE, jnp.float32),
        jnp.zeros((HEADS, rows_here), jnp.float32),
        jnp.zeros((rows_here, HEADS, HEAD), jnp.float32),
    )
    first_row = jnp.int32(0)
    keys_piece = lax.all_gather(key_part, "blk", axis=0, tiled=True)
    values_piece = lax.all_gather(value_part, "blk", axis=0, tiled=True)
    piece_rows = keys_piece.shape[0]
    block_rows = block_size(piece_rows, rows_here)

    def forward_advance(turn_index, running):
        offset = turn_index * block_rows
        keys_block = lax.dynamic_slice_in_dim(keys_piece, offset, block_rows)
        values_block = lax.dynamic_slice_in_dim(values_piece, offset, block_rows)
        block_frames = frames_of(group_map, first_row + offset, block_rows)

        def attend(previous):
            top_scores, totals, accumulated = previous
            scores = (
                jnp.einsum("qhd,khd->hqk", query, keys_block, preferred_element_type=jnp.float32)
                * SCALE
            )
            allowed = block_frames[None, None, :] <= token_frames[None, :, None]
            new_top = jnp.maximum(
                top_scores, jnp.max(jnp.where(allowed, scores, NEG_LARGE), axis=2)
            )
            weights = jnp.where(allowed, jnp.exp(scores - new_top[:, :, None]), 0.0)
            factor = jnp.exp(top_scores - new_top)
            update = jnp.einsum(
                "hqk,khd->qhd",
                weights.astype(jnp.bfloat16),
                values_block,
                preferred_element_type=jnp.float32,
            )
            return (
                new_top,
                totals * factor + jnp.sum(weights, axis=2),
                accumulated * factor.T[:, :, None] + update,
            )

        return lax.cond(jnp.min(block_frames) > top_frame, keep_same, attend, running)

    top_scores, totals, accumulated = lax.fori_loop(
        0, piece_rows // block_rows, forward_advance, forward_start
    )
    attended = accumulated / totals.T[:, :, None]
    log_total = top_scores + jnp.log(totals)
    attended_low = attended.astype(jnp.bfloat16).reshape(rows_here, D)
    attn_out = jnp.dot(attended_low, out_weight, preferred_element_type=jnp.float32).reshape(
        2, PATCHES, D
    )
    middle = inputs_here + gate_one * attn_out
    normed_two, inverse_two = normalize(middle)
    second_in = (
        (normed_two * (1.0 + scale_two) + shift_two).astype(jnp.bfloat16).reshape(rows_here, D)
    )
    up_lin = jnp.dot(second_in, fc1_weight, preferred_element_type=jnp.float32)
    hidden = jax.nn.gelu(up_lin, approximate=False).astype(jnp.bfloat16)
    mlp_out = jnp.dot(hidden, fc2_weight, preferred_element_type=jnp.float32).reshape(2, PATCHES, D)
    layer_out = (middle + gate_two * mlp_out).astype(jnp.bfloat16)[None]
    cotangent = out_cotangent[0].astype(jnp.float32)
    d_gate_two = jnp.sum(cotangent * mlp_out, axis=1)
    d_mlp = (cotangent * gate_two).astype(jnp.bfloat16).reshape(rows_here, D)
    lower_part = jnp.einsum("rf,rd->fd", hidden, d_mlp, preferred_element_type=jnp.float32)
    d_hidden = jnp.einsum("rd,fd->rf", d_mlp, fc2_weight, preferred_element_type=jnp.float32)
    unused_value, gelu_pull = jax.vjp(partial(jax.nn.gelu, approximate=False), up_lin)
    d_up = gelu_pull(d_hidden)[0].astype(jnp.bfloat16)
    upper_part = jnp.einsum("rc,rf->cf", second_in, d_up, preferred_element_type=jnp.float32)
    d_second = jnp.einsum(
        "rf,cf->rc", d_up, fc1_weight, preferred_element_type=jnp.float32
    ).reshape(2, PATCHES, D)
    d_shift_two = jnp.sum(d_second, axis=1)
    d_scale_two = jnp.sum(d_second * normed_two, axis=1)
    d_middle = cotangent + norm_backward(d_second * (1.0 + scale_two), normed_two, inverse_two)
    d_gate_one = jnp.sum(d_middle * attn_out, axis=1)
    d_attn = (d_middle * gate_one).astype(jnp.bfloat16).reshape(rows_here, D)
    outw_part = jnp.einsum("rc,rd->cd", attended_low, d_attn, preferred_element_type=jnp.float32)
    d_attended = (
        jnp.einsum("rd,cd->rc", d_attn, out_weight, preferred_element_type=jnp.float32)
        .astype(jnp.bfloat16)
        .reshape(rows_here, HEADS, HEAD)
    )
    delta = jnp.sum(d_attended.astype(jnp.float32) * attended, axis=2).T
    grad_start = jnp.zeros((rows_here, HEADS, HEAD), jnp.float32)
    query_first_row = jnp.int32(0)
    query_keys_piece = lax.all_gather(key_part, "blk", axis=0, tiled=True)
    query_values_piece = lax.all_gather(value_part, "blk", axis=0, tiled=True)
    piece_rows = query_keys_piece.shape[0]
    query_block_rows = block_size(piece_rows, rows_here)

    def query_advance(turn_index, running):
        offset = turn_index * query_block_rows
        keys_block = lax.dynamic_slice_in_dim(query_keys_piece, offset, query_block_rows)
        values_block = lax.dynamic_slice_in_dim(query_values_piece, offset, query_block_rows)
        block_frames = frames_of(group_map, query_first_row + offset, query_block_rows)

        def query_accumulate(previous):
            scores = (
                jnp.einsum("qhd,khd->hqk", query, keys_block, preferred_element_type=jnp.float32)
                * SCALE
            )
            allowed = block_frames[None, None, :] <= token_frames[None, :, None]
            weights = jnp.where(allowed, jnp.exp(scores - log_total[:, :, None]), 0.0)
            weight_grad = jnp.einsum(
                "qhd,khd->hqk", d_attended, values_block, preferred_element_type=jnp.float32
            )
            score_grad = (weights * (weight_grad - delta[:, :, None]) * SCALE).astype(jnp.bfloat16)
            return previous + jnp.einsum(
                "hqk,khd->qhd", score_grad, keys_block, preferred_element_type=jnp.float32
            )

        return lax.cond(jnp.min(block_frames) > top_frame, keep_same, query_accumulate, running)

    query_grad = lax.fori_loop(0, piece_rows // query_block_rows, query_advance, grad_start)
    stats_lse, stats_delta = (
        lax.all_gather(log_total.T, "blk", axis=0, tiled=True),
        lax.all_gather(delta.T, "blk", axis=0, tiled=True),
    )
    key_first_row = jnp.int32(0)
    queries_piece = lax.all_gather(query, "blk", axis=0, tiled=True)
    grads_piece = lax.all_gather(d_attended, "blk", axis=0, tiled=True)
    piece_rows = queries_piece.shape[0]
    key_block_rows = block_size(piece_rows, rows_here)

    def key_advance(turn_index, running):
        offset = turn_index * key_block_rows
        query_block = lax.dynamic_slice_in_dim(queries_piece, offset, key_block_rows)
        grad_block = lax.dynamic_slice_in_dim(grads_piece, offset, key_block_rows)
        lse_block = lax.dynamic_slice_in_dim(stats_lse, key_first_row + offset, key_block_rows).T
        delta_block = lax.dynamic_slice_in_dim(
            stats_delta, key_first_row + offset, key_block_rows
        ).T
        block_frames = frames_of(group_map, key_first_row + offset, key_block_rows)

        def key_accumulate(previous):
            key_total, value_total = previous
            scores = (
                jnp.einsum(
                    "qhd,khd->hqk", query_block, key_part, preferred_element_type=jnp.float32
                )
                * SCALE
            )
            allowed = token_frames[None, None, :] <= block_frames[None, :, None]
            weights = jnp.where(allowed, jnp.exp(scores - lse_block[:, :, None]), 0.0)
            value_total = value_total + jnp.einsum(
                "hqk,qhd->khd",
                weights.astype(jnp.bfloat16),
                grad_block,
                preferred_element_type=jnp.float32,
            )
            weight_grad = jnp.einsum(
                "qhd,khd->hqk", grad_block, value_part, preferred_element_type=jnp.float32
            )
            score_grad = (weights * (weight_grad - delta_block[:, :, None]) * SCALE).astype(
                jnp.bfloat16
            )
            key_total = key_total + jnp.einsum(
                "hqk,qhd->khd", score_grad, query_block, preferred_element_type=jnp.float32
            )
            return (key_total, value_total)

        return lax.cond(jnp.max(block_frames) < own_lowest, keep_same, key_accumulate, running)

    key_grad, value_grad = lax.fori_loop(
        0, piece_rows // key_block_rows, key_advance, (grad_start, grad_start)
    )
    query_low = lax.optimization_barrier(query_grad.astype(jnp.bfloat16)).astype(jnp.float32)
    key_low = lax.optimization_barrier(key_grad.astype(jnp.bfloat16)).astype(jnp.float32)
    query_back = rotate(query_low, angle_list, -1.0).reshape(rows_here, D)
    key_back = rotate(key_low, angle_list, -1.0).reshape(rows_here, D)
    d_qkv = jnp.concatenate(
        [query_back, key_back, value_grad.reshape(rows_here, D)], axis=1
    ).astype(jnp.bfloat16)
    qkv_part = jnp.einsum("rc,rk->ck", first_in, d_qkv, preferred_element_type=jnp.float32)
    d_first = jnp.einsum(
        "rk,ck->rc", d_qkv, qkv_weight, preferred_element_type=jnp.float32
    ).reshape(2, PATCHES, D)
    d_shift_one = jnp.sum(d_first, axis=1)
    d_scale_one = jnp.sum(d_first * normed_one, axis=1)
    tokens_grad = (
        d_middle + norm_backward(d_first * (1.0 + scale_one), normed_one, inverse_one)
    ).astype(jnp.bfloat16)[None]
    d_mod = jnp.concatenate(
        [d_shift_one, d_scale_one, d_gate_one, d_shift_two, d_scale_two, d_gate_two], axis=1
    )
    bias_part = jnp.sum(d_mod, axis=0)
    d_mod_low = d_mod.astype(jnp.bfloat16)
    d_activated = jnp.einsum("sk,ck->sc", d_mod_low, mod_weight, preferred_element_type=jnp.float32)
    unused_silu, silu_pull = jax.vjp(jax.nn.silu, embedded)
    d_embedded = silu_pull(d_activated)[0]
    table_part = jnp.einsum(
        "sl,sc->cl", level_hot.astype(jnp.float32), d_embedded, precision=lax.Precision.HIGHEST
    )
    activated_all, d_mod_all = (
        lax.all_gather(activated, ("blk", "clip"), axis=0, tiled=True),
        lax.all_gather(d_mod_low, ("blk", "clip"), axis=0, tiled=True),
    )
    share_rows = D // lax.axis_size(("blk", "clip"))
    my_columns = lax.dynamic_slice_in_dim(
        activated_all, lax.axis_index(("blk", "clip")) * share_rows, share_rows, 1
    )
    modw_share = jnp.einsum("sc,sk->ck", my_columns, d_mod_all, preferred_element_type=jnp.float32)
    summed = (
        lax.psum_scatter(table_part, ("blk", "clip"), scatter_dimension=0, tiled=True),
        lax.psum_scatter(bias_part, ("blk", "clip"), scatter_dimension=0, tiled=True),
        lax.psum_scatter(qkv_part, ("blk", "clip"), scatter_dimension=0, tiled=True),
        lax.psum_scatter(outw_part, ("blk", "clip"), scatter_dimension=0, tiled=True),
        lax.psum_scatter(upper_part, ("blk", "clip"), scatter_dimension=0, tiled=True),
        lax.psum_scatter(lower_part, ("blk", "clip"), scatter_dimension=0, tiled=True),
    )
    return (
        layer_out,
        tokens_grad,
        summed[0].T,
        modw_share,
        summed[1],
        summed[2],
        summed[3],
        summed[4],
        summed[5],
    )


LANES = 128
FF = 4096
AXES = ("blk", "clip")
EXP_SCALE = SCALE * 1.4426950408889634
VMEM_LIMIT = 56 * 1024 * 1024
NT = (((1,), (1,)), ((), ()))
NN = (((1,), (0,)), ((), ()))


def cost(microseconds):
    return pl.CostEstimate(
        flops=int(microseconds * 1e9), bytes_accessed=int(microseconds * 3e6), transcendentals=0
    )


class Shifted:
    def __init__(self, ref, start):
        self.ref, self.start = ref, start

    def __getitem__(self, place):
        return self.ref[self.start + place]


FRAME_COUNT = 2 * D // LANES
BITS_AT, ORDER_AT = 0, 5
FRAMES_AT = ORDER_AT + D // LANES
SLOTS_AT = FRAMES_AT + FRAME_COUNT
GROUP_AT = SLOTS_AT + FRAME_COUNT
MINE_AT = GROUP_AT + FRAME_COUNT
ANYWHERE = pl.BlockSpec(memory_space=pl.ANY)


def full_block(shape):
    return pl.BlockSpec(shape, lambda *ids: (0,) * len(shape))


def rope_tables(frame_count):
    lane = np.arange(LANES) % HEAD
    pieces = []
    for comp_width in (16, 24, 24):
        half_width = comp_width // 2
        frequency = ROPE_BASE ** (-2.0 * np.arange(half_width) / comp_width)
        pieces += [frequency, frequency]
    frequency = np.tile(np.concatenate(pieces), LANES // HEAD)[None, :]
    first = (lane < 8) | ((lane >= 16) & (lane < 28)) | ((lane >= 40) & (lane < 52))
    sign = np.where(first, -1.0, 1.0)[None, :]
    in_frame = (lane < 16)[None, :]
    in_row = (lane < 40)[None, :]
    frame_angle = np.arange(frame_count)[:, None] * frequency
    patch = np.arange(PATCHES)[:, None]
    place_angle = np.where(in_row, patch // GRID_W, patch % GRID_W) * frequency
    tables = (
        np.where(in_frame, np.cos(frame_angle), 0.0),
        np.where(in_frame, sign * np.sin(frame_angle), 0.0),
        np.where(in_frame, 0.0, np.cos(place_angle)),
        np.where(in_frame, 0.0, sign * np.sin(place_angle)),
    )
    return tuple(jnp.asarray(table, jnp.float32) for table in tables)


def partner_lanes(values):
    lane = lax.broadcasted_iota(jnp.int32, values.shape, 1) % HEAD
    ahead_eight = pltpu.roll(values, LANES - 8, 1)
    behind_eight = pltpu.roll(values, 8, 1)
    ahead_twelve = pltpu.roll(values, LANES - 12, 1)
    behind_twelve = pltpu.roll(values, 12, 1)
    ahead = ((lane >= 16) & (lane < 28)) | ((lane >= 40) & (lane < 52))
    return jnp.where(
        lane < 8,
        ahead_eight,
        jnp.where(lane < 16, behind_eight, jnp.where(ahead, ahead_twelve, behind_twelve)),
    )


def modulation_kernel(levels_ref, table_ref, weight_ref, bias_ref, out_ref, activated_ref):
    @pl.when(pl.program_id(0) == 0)
    def _():
        count = levels_ref.shape[1]
        hot = lax.broadcasted_iota(jnp.int32, (LEVELS, count), 0) == levels_ref[...]
        embedded = lax.dot_general(
            jnp.where(hot, 1.0, 0.0).astype(jnp.bfloat16),
            table_ref[...],
            (((0,), (0,)), ((), ())),
            preferred_element_type=jnp.float32,
        )
        activated_ref[...] = jax.nn.silu(embedded).astype(jnp.bfloat16)

    out_ref[...] = lax.dot_general(
        activated_ref[...], weight_ref[...], NN, preferred_element_type=jnp.float32
    ) + bias_ref[...].astype(jnp.float32)[None, :]


def modulate(levels, noise_table, mod_weight, mod_bias):
    frame_count = levels.shape[1]
    return pl.pallas_call(
        modulation_kernel,
        grid=(6,),
        in_specs=[
            full_block(levels.shape),
            full_block(noise_table.shape),
            pl.BlockSpec((D, D), lambda i: (0, i)),
            pl.BlockSpec((D,), lambda i: (i,)),
        ],
        out_specs=pl.BlockSpec((frame_count, D), lambda i: (0, i)),
        out_shape=jax.ShapeDtypeStruct((frame_count, 6 * D), jnp.float32),
        scratch_shapes=[pltpu.VMEM((frame_count, D), jnp.bfloat16)],
        compiler_params=pltpu.CompilerParams(
            vmem_limit_bytes=VMEM_LIMIT, dimension_semantics=("arbitrary",)
        ),
        cost_estimate=cost(7),
        name="modulate",
    )(levels, noise_table, mod_weight, mod_bias)


def copy_kernel(info_ref, source_ref, target_ref):
    target_ref[...] = source_ref[...]


def own_columns(info, weight):
    return pl.pallas_call(
        copy_kernel,
        grid_spec=pltpu.PrefetchScalarGridSpec(
            num_scalar_prefetch=1,
            grid=(3,),
            in_specs=[
                pl.BlockSpec((D, LANES), lambda i, info: (0, i * (D // LANES) + info[ORDER_AT]))
            ],
            out_specs=pl.BlockSpec((D, LANES), lambda i, info: (0, i)),
        ),
        out_shape=jax.ShapeDtypeStruct((D, 3 * LANES), jnp.bfloat16),
        compiler_params=pltpu.CompilerParams(dimension_semantics=("arbitrary",)),
        cost_estimate=cost(2),
        name="own_columns",
    )(info, weight)


def project_kernel(
    count,
    first_piece,
    info_ref,
    mod_ref,
    weight_ref,
    fcos_ref,
    fsin_ref,
    pcos_ref,
    psin_ref,
    *refs,
):
    frames_ref = Shifted(info_ref, FRAMES_AT)
    halves, out_ref, first_ref = refs[: 2 * count], refs[-2], refs[-1]
    for piece in range(count):
        for half in range(2):
            source, place = halves[2 * piece + half]
            rows = slice(half * PATCHES, (half + 1) * PATCHES)
            frame = frames_ref[2 * (first_piece + piece) + half]
            normed, unused = normalize(
                source[place * PATCHES : (place + 1) * PATCHES, :].astype(jnp.float32)
            )
            shift = mod_ref[pl.ds(frame, 1), :D]
            scale = mod_ref[pl.ds(frame, 1), D : 2 * D]
            first_ref[piece, rows, :] = (normed * (1.0 + scale) + shift).astype(jnp.bfloat16)
        linear = lax.dot_general(
            first_ref[piece], weight_ref[...], NN, preferred_element_type=jnp.float32
        )
        for half in range(2):
            rows = slice(half * PATCHES, (half + 1) * PATCHES)
            frame = frames_ref[2 * (first_piece + piece) + half]
            cosine = pcos_ref[...] + fcos_ref[pl.ds(frame, 1), :]
            sine = psin_ref[...] + fsin_ref[pl.ds(frame, 1), :]
            for part in range(2):
                columns = slice(part * LANES, (part + 1) * LANES)
                values = linear[rows, columns]
                turned = values * cosine + partner_lanes(values) * sine
                out_ref[piece, rows, columns] = turned.astype(jnp.bfloat16)
            out_ref[piece, rows, 2 * LANES :] = linear[rows, 2 * LANES :].astype(jnp.bfloat16)


def project(info, modulation, weight, tables, first_piece, pieces):
    vmem = pl.BlockSpec(memory_space=pltpu.VMEM)
    count = len(pieces)
    arrays, sources = [], []
    for piece in pieces:
        if isinstance(piece, tuple):
            sources += [(len(arrays), 0), (len(arrays) + 1, 0)]
            arrays += list(piece)
        else:
            sources += [(len(arrays), 0), (len(arrays), 1)]
            arrays.append(piece)

    def kernel(*refs):
        inputs = refs[7 : 7 + len(arrays)]
        halves = [(inputs[which], place) for which, place in sources]
        project_kernel(count, first_piece, *refs[:7], *halves, *refs[7 + len(arrays) :])

    rows = 2 * PATCHES
    return pl.pallas_call(
        kernel,
        in_specs=[pl.BlockSpec(memory_space=pltpu.SMEM)] + [vmem] * (6 + len(arrays)),
        out_specs=[vmem] * 2,
        out_shape=[
            jax.ShapeDtypeStruct((count, rows, 3 * LANES), jnp.bfloat16),
            jax.ShapeDtypeStruct((count, rows, D), jnp.bfloat16),
        ],
        compiler_params=pltpu.CompilerParams(vmem_limit_bytes=VMEM_LIMIT),
        cost_estimate=cost(2 * count),
        name="project",
    )(info, modulation, weight, *tables, *arrays)


def head_stack(values):
    lane = lax.broadcasted_iota(jnp.int32, values.shape, 1)
    zero = jnp.zeros_like(values)
    return jnp.concatenate(
        [jnp.where(lane < HEAD, values, zero), jnp.where(lane < HEAD, zero, values)], axis=0
    )


def hidden_keys(shape):
    key_row = lax.broadcasted_iota(jnp.int32, shape, 0)
    query_column = lax.broadcasted_iota(jnp.int32, shape, 1) % (2 * PATCHES)
    return (key_row >= PATCHES) & (query_column < PATCHES)


def own_heads(values):
    rows = 2 * PATCHES
    return jnp.concatenate([values[:HEAD, :rows], values[HEAD:LANES, rows:]], axis=0)


def by_frame(frames_ref, source_refs, target_refs):
    pieces = [(ref, piece) for ref in source_refs for piece in range(ref.shape[0])]
    for place, (ref, piece) in enumerate(pieces):
        for half in range(2):
            frame = frames_ref[2 * place + half]
            rows = pl.ds(pl.multiple_of(frame * PATCHES, PATCHES), PATCHES)
            for part, target in enumerate(target_refs):
                target[rows, :] = ref[
                    piece,
                    half * PATCHES : (half + 1) * PATCHES,
                    part * LANES : (part + 1) * LANES,
                ]


def attend_kernel(info_ref, qkv_refs, att_ref, ot_ref, lse_ref, q_ref, k_ref, v_ref, vt_ref):
    token_count = q_ref.shape[0]
    frames_ref, slots_ref = Shifted(info_ref, FRAMES_AT), Shifted(info_ref, SLOTS_AT)
    by_frame(frames_ref, qkv_refs, (q_ref, k_ref, v_ref))
    vt_ref[:LANES, :] = v_ref[...].T
    vt_ref[LANES:, :] = jnp.ones((vt_ref.shape[0] - LANES, token_count), jnp.bfloat16)
    step = 2 * PATCHES
    for turn in range(token_count // step):
        here = slice(turn * step, (turn + 1) * step)
        queries = head_stack(q_ref[here, :])
        ranges = [here] if turn == 0 else [slice(0, turn * step), here]
        raw = [
            lax.dot_general(k_ref[keys, :], queries, NT, preferred_element_type=jnp.float32)
            for keys in ranges
        ]
        raw[-1] = jnp.where(hidden_keys(raw[-1].shape), NEG_LARGE, raw[-1])
        top = jnp.max(raw[-1], axis=0, keepdims=True)
        for part in raw[:-1]:
            top = jnp.maximum(top, jnp.max(part, axis=0, keepdims=True))
        top = top * EXP_SCALE
        summed = None
        for keys, part in zip(ranges, raw):
            weights = jnp.exp2(part * EXP_SCALE - top).astype(jnp.bfloat16)
            update = lax.dot_general(
                vt_ref[:, keys], weights, NN, preferred_element_type=jnp.float32
            )
            summed = update if summed is None else summed + update
        totals = summed[LANES : LANES + 1, :]
        lse_ref[turn : turn + 1, :] = top + jnp.log2(totals)
        out = own_heads(summed[:LANES, :] / totals)
        ot_ref[:, here] = out
        rounded = out.T.astype(jnp.bfloat16)
        for half in range(2):
            slot = slots_ref[2 * turn + half]
            rows = pl.ds(pl.multiple_of(slot % 2 * PATCHES, PATCHES), PATCHES)
            att_ref[slot // 2, rows, :] = rounded[half * PATCHES : (half + 1) * PATCHES, :]


def attend(info, qkv, after):
    token_count = FRAME_COUNT * PATCHES
    turns = token_count // (2 * PATCHES)
    vmem = pl.BlockSpec(memory_space=pltpu.VMEM)

    def kernel(info_ref, *refs):
        attend_kernel(info_ref, refs[: len(qkv)], *refs[len(qkv) + 1 :])

    return pl.pallas_call(
        kernel,
        in_specs=[pl.BlockSpec(memory_space=pltpu.SMEM)] + [vmem] * len(qkv) + [ANYWHERE],
        out_specs=[vmem] * 3,
        out_shape=[
            jax.ShapeDtypeStruct((turns, 2 * PATCHES, LANES), jnp.bfloat16),
            jax.ShapeDtypeStruct((LANES, token_count), jnp.float32),
            jax.ShapeDtypeStruct((turns, 4 * PATCHES), jnp.float32),
        ],
        scratch_shapes=[pltpu.VMEM((token_count, LANES), jnp.bfloat16)] * 3
        + [pltpu.VMEM((LANES + 16, token_count), jnp.bfloat16)],
        compiler_params=pltpu.CompilerParams(vmem_limit_bytes=VMEM_LIMIT),
        cost_estimate=cost(10),
        name="attend",
    )(info, *qkv, after)


def attend_back_kernel(
    info_ref,
    grad_ref,
    ot_ref,
    lse_ref,
    fcos_ref,
    fsin_ref,
    pcos_ref,
    psin_ref,
    qkv_refs,
    out_ref,
    q_ref,
    k_ref,
    v_ref,
    d_ref,
    kt_ref,
    dk_ref,
    dv_ref,
):
    token_count = q_ref.shape[0]
    frames_ref, slot_frames_ref, slots_ref = (
        Shifted(info_ref, place) for place in (FRAMES_AT, GROUP_AT, SLOTS_AT)
    )
    by_frame(frames_ref, qkv_refs, (q_ref, k_ref, v_ref))
    by_frame(slot_frames_ref, (grad_ref,), (d_ref,))
    kt_ref[...] = k_ref[...].T
    step = 2 * PATCHES

    def put(frame, part, values):
        slot = slots_ref[frame]
        rows = pl.ds(pl.multiple_of(slot % 2 * PATCHES, PATCHES), PATCHES)
        out_ref[slot // 2, rows, part * LANES : (part + 1) * LANES] = values

    def turn_back(frame, values):
        values = values.astype(jnp.bfloat16).astype(jnp.float32)
        cosine = pcos_ref[...] + fcos_ref[frame : frame + 1, :]
        sine = psin_ref[...] + fsin_ref[frame : frame + 1, :]
        return (values * cosine - partner_lanes(values) * sine).astype(jnp.bfloat16)

    for turn in range(token_count // step):
        here = slice(turn * step, (turn + 1) * step)
        queries = head_stack(q_ref[here, :])
        grads_here = d_ref[here, :]
        grads = head_stack(grads_here)
        product = grads_here.astype(jnp.float32).T * ot_ref[:, here]
        delta = jnp.concatenate(
            [
                jnp.sum(product[:HEAD, :], axis=0, keepdims=True),
                jnp.sum(product[HEAD:, :], axis=0, keepdims=True),
            ],
            axis=1,
        )
        lse = lse_ref[turn : turn + 1, :]
        ranges = [here] if turn == 0 else [here, slice(0, turn * step)]
        total = None
        for keys in ranges:
            raw = lax.dot_general(
                k_ref[keys, :], queries, NT, preferred_element_type=jnp.float32
            )
            weights = jnp.exp2(raw * EXP_SCALE - lse)
            if keys is here:
                weights = jnp.where(hidden_keys(weights.shape), 0.0, weights)
            weight_grad = lax.dot_general(
                v_ref[keys, :], grads, NT, preferred_element_type=jnp.float32
            )
            score_grad = (weights * (weight_grad - delta)).astype(jnp.bfloat16)
            value_part = lax.dot_general(
                weights.astype(jnp.bfloat16), grads, NN, preferred_element_type=jnp.float32
            )
            key_part = lax.dot_general(
                score_grad, queries, NN, preferred_element_type=jnp.float32
            )
            if keys is here:
                dv_ref[keys, :] = value_part
                dk_ref[keys, :] = key_part
            else:
                dv_ref[keys, :] += value_part
                dk_ref[keys, :] += key_part
            update = lax.dot_general(
                kt_ref[:, keys], score_grad, NN, preferred_element_type=jnp.float32
            )
            total = update if total is None else total + update
        query_grad = own_heads(total).T * SCALE
        for half in range(2):
            put(
                2 * turn + half,
                0,
                turn_back(2 * turn + half, query_grad[half * PATCHES : (half + 1) * PATCHES, :]),
            )
    for frame in range(token_count // PATCHES):
        rows = slice(frame * PATCHES, (frame + 1) * PATCHES)
        put(frame, 1, turn_back(frame, dk_ref[rows, :] * SCALE))
        put(frame, 2, dv_ref[rows, :].astype(jnp.bfloat16))


def attend_back(info, qkv, grads, ot, lse, tables, after):
    token_count = FRAME_COUNT * PATCHES
    smem = pl.BlockSpec(memory_space=pltpu.SMEM)
    vmem = pl.BlockSpec(memory_space=pltpu.VMEM)

    def kernel(*refs):
        outs = 8 + len(qkv) + len(after)
        attend_back_kernel(*refs[:8], refs[8 : 8 + len(qkv)], *refs[outs:])

    return pl.pallas_call(
        kernel,
        in_specs=[smem] + [vmem] * (7 + len(qkv)) + [ANYWHERE] * len(after),
        out_specs=vmem,
        out_shape=jax.ShapeDtypeStruct(
            (token_count // (2 * PATCHES), 2 * PATCHES, 3 * LANES), jnp.bfloat16
        ),
        scratch_shapes=[pltpu.VMEM((token_count, LANES), jnp.bfloat16)] * 4
        + [pltpu.VMEM((LANES, token_count), jnp.bfloat16)]
        + [pltpu.VMEM((token_count, LANES), jnp.float32)] * 2,
        compiler_params=pltpu.CompilerParams(vmem_limit_bytes=VMEM_LIMIT),
        cost_estimate=cost(8),
        name="attend_back",
    )(info, grads, ot, lse, *tables, *qkv, *after)


def swap(values, bit):
    count = lax.axis_size(AXES)
    return lax.ppermute(values, AXES, [(index, index ^ bit) for index in range(count)])


PIECES = (0, 4, 2, 1, 5, 6, 3, 7)


def cross(values, bit):
    count = lax.axis_size("blk")
    return lax.ppermute(values, "blk", [(place, place ^ bit) for place in range(count)])


SECOND_AT, ATTENDED_AT, ATTN_AT, UP_AT, UP_ACTS = 0, D, 2 * D, 3 * D, 3 * D + FF
MLP_AT, HIDDEN_AT, DOWN_ACTS = 0, D, D + FF
FF_TILE = 1024
PARTS = 2


def middle_kernel(
    info_ref,
    att_ref,
    tokens_ref,
    cot_ref,
    mod_ref,
    ow_ref,
    up_ref,
    down_ref,
    layer_ref,
    upper_ref,
    lower_ref,
    datt_ref,
    dmid_ref,
    dmod_ref,
    attn_ref,
    mid_ref,
    mlp_ref,
    dsec_ref,
    second_ref,
    dmlp_ref,
):
    step = pl.program_id(0)
    slot_rows = [slice(slot * PATCHES, (slot + 1) * PATCHES) for slot in range(2)]

    def member(slot, which):
        return mod_ref[pl.ds(info_ref[MINE_AT + slot], 1), which * D : (which + 1) * D]

    @pl.when(step == 0)
    def _():
        for group in range(D // LANES):
            upper_ref[:, ATTENDED_AT + group * LANES : ATTENDED_AT + (group + 1) * LANES] = att_ref[
                group
            ]
        attn_ref[...] = lax.dot_general(
            upper_ref[:, ATTENDED_AT : ATTENDED_AT + D],
            ow_ref[...],
            NN,
            preferred_element_type=jnp.float32,
        )
        for slot, rows in enumerate(slot_rows):
            middle = tokens_ref[rows, :].astype(jnp.float32) + member(slot, 2) * attn_ref[rows, :]
            mid_ref[rows, :] = middle
            normed, unused = normalize(middle)
            upper_ref[rows, SECOND_AT : SECOND_AT + D] = (
                normed * (1.0 + member(slot, 4)) + member(slot, 3)
            ).astype(jnp.bfloat16)
            lower_ref[rows, MLP_AT : MLP_AT + D] = (
                cot_ref[rows, :].astype(jnp.float32) * member(slot, 5)
            ).astype(jnp.bfloat16)
        second_ref[...] = upper_ref[:, SECOND_AT : SECOND_AT + D]
        dmlp_ref[...] = lower_ref[:, MLP_AT : MLP_AT + D]
        mlp_ref[...] = jnp.zeros_like(mlp_ref)
        dsec_ref[...] = jnp.zeros_like(dsec_ref)

    width = FF_TILE // PARTS
    linear = []
    for part in range(PARTS):
        columns = slice(part * width, (part + 1) * width)
        up_lin = lax.dot_general(
            second_ref[...], up_ref[:, columns], NN, preferred_element_type=jnp.float32
        )
        d_hidden = lax.dot_general(
            dmlp_ref[...], down_ref[columns, :], NT, preferred_element_type=jnp.float32
        )
        linear.append((up_lin, d_hidden))
    hidden, d_up = [], []
    for up_lin, d_hidden in linear:
        below = 0.5 + 0.5 * lax.erf(up_lin * 0.7071067811865476)
        density = jnp.exp(up_lin * up_lin * -0.5) * 0.3989422804014327
        hidden.append((up_lin * below).astype(jnp.bfloat16))
        d_up.append((d_hidden * (below + up_lin * density)).astype(jnp.bfloat16))
    hidden, d_up = jnp.concatenate(hidden, axis=1), jnp.concatenate(d_up, axis=1)
    mlp_ref[...] += lax.dot_general(
        hidden, down_ref[...], NN, preferred_element_type=jnp.float32
    )
    dsec_ref[...] += lax.dot_general(d_up, up_ref[...], NT, preferred_element_type=jnp.float32)
    lower_ref[:, pl.ds(pl.multiple_of(HIDDEN_AT + step * FF_TILE, FF_TILE), FF_TILE)] = hidden
    upper_ref[:, pl.ds(pl.multiple_of(UP_AT + step * FF_TILE, FF_TILE), FF_TILE)] = d_up

    @pl.when(step == pl.num_programs(0) - 1)
    def _():
        for slot, rows in enumerate(slot_rows):
            middle = mid_ref[rows, :]
            mlp_out = mlp_ref[rows, :]
            cotangent = cot_ref[rows, :].astype(jnp.float32)
            layer_ref[rows, :] = (middle + member(slot, 5) * mlp_out).astype(jnp.bfloat16)
            normed, inverse = normalize(middle)
            d_second = dsec_ref[rows, :]
            d_middle = cotangent + norm_backward(
                d_second * (1.0 + member(slot, 4)), normed, inverse
            )
            dmid_ref[rows, :] = d_middle
            upper_ref[rows, ATTN_AT : ATTN_AT + D] = (d_middle * member(slot, 2)).astype(
                jnp.bfloat16
            )
            for place, values in enumerate(
                (d_middle * attn_ref[rows, :], d_second, d_second * normed, cotangent * mlp_out)
            ):
                dmod_ref[slot : slot + 1, place * D : (place + 1) * D] = jnp.sum(
                    values, axis=0, keepdims=True
                )
        d_attended = lax.dot_general(
            upper_ref[:, ATTN_AT : ATTN_AT + D],
            ow_ref[...],
            NT,
            preferred_element_type=jnp.float32,
        ).astype(jnp.bfloat16)
        for group in range(D // LANES):
            datt_ref[group] = d_attended[:, group * LANES : (group + 1) * LANES]


def middle_block(info, att, tokens_here, cot_here, modulation, out_weight, fc1_weight, fc2_weight):
    rows = tokens_here.shape[0]
    return pl.pallas_call(
        middle_kernel,
        grid_spec=pltpu.PrefetchScalarGridSpec(
            num_scalar_prefetch=1,
            grid=(FF // FF_TILE,),
            in_specs=[
                full_block(att.shape),
                full_block((rows, D)),
                full_block((rows, D)),
                full_block(modulation.shape),
                full_block((D, D)),
                pl.BlockSpec((D, FF_TILE), lambda f, frames: (0, f)),
                pl.BlockSpec((FF_TILE, D), lambda f, frames: (f, 0)),
            ],
            out_specs=[
                full_block((rows, D)),
                full_block((rows, UP_ACTS)),
                full_block((rows, DOWN_ACTS)),
                full_block(att.shape),
                full_block((rows, D)),
                full_block((2, 4 * D)),
            ],
            scratch_shapes=[pltpu.VMEM((rows, D), jnp.float32)] * 4
            + [pltpu.VMEM((rows, D), jnp.bfloat16)] * 2,
        ),
        out_shape=[
            jax.ShapeDtypeStruct((rows, D), jnp.bfloat16),
            jax.ShapeDtypeStruct((rows, UP_ACTS), jnp.bfloat16),
            jax.ShapeDtypeStruct((rows, DOWN_ACTS), jnp.bfloat16),
            jax.ShapeDtypeStruct(att.shape, jnp.bfloat16),
            jax.ShapeDtypeStruct((rows, D), jnp.float32),
            jax.ShapeDtypeStruct((2, 4 * D), jnp.float32),
        ],
        compiler_params=pltpu.CompilerParams(
            vmem_limit_bytes=VMEM_LIMIT, dimension_semantics=("arbitrary",)
        ),
        cost_estimate=cost(21),
        name="middle_block",
    )(info, att, tokens_here, cot_here, modulation, out_weight, fc1_weight, fc2_weight)


CHIPS = 16
TILE = 256
FINE = D // CHIPS // 2
UPPER_JOBS = ((SECOND_AT, FINE, UP_AT, FF, 10), (ATTENDED_AT, FINE, ATTN_AT, D, 2))
LOWER_JOBS = ((HIDDEN_AT, LANES, MLP_AT, D, 2),)


def rows_of(jobs):
    first = sum(height * tiles for unused, height, unused_at, width, tiles in jobs)
    return first, sum(job[1] * (job[3] // TILE) for job in jobs) - first


def weight_kernel(jobs, info_ref, mine_ref, theirs_ref, *refs):
    keep_a, send_a, keep_b, send_b = refs[-4 - len(jobs) : -len(jobs)]
    left_refs = refs[-len(jobs) :]
    core, xbit, ybit = (info_ref[BITS_AT + place] for place in range(3))
    rows = mine_ref.shape[0]
    row_a = row_b = 0
    for (left_at, height, right_at, width, tiles), left_ref in zip(jobs, left_refs):
        for place, ref in enumerate((mine_ref, theirs_ref)):
            columns = slice(place * rows, (place + 1) * rows)
            if height == LANES:
                for chip in range(CHIPS):
                    source = pl.multiple_of(left_at + (2 * chip + core) * LANES, LANES)
                    left_ref[chip * LANES : (chip + 1) * LANES, columns] = ref[
                        :, pl.ds(source, LANES)
                    ].T
            else:
                turned = ref[:, left_at : left_at + D].T.reshape(CHIPS, 2, height, rows)
                left_ref[:, columns] = jnp.where(core == 0, turned[:, 0], turned[:, 1]).reshape(
                    CHIPS * height, rows
                )
        for tile in range(width // TILE):
            source = right_at + tile * TILE
            right = jnp.concatenate(
                [mine_ref[:, source : source + TILE], theirs_ref[:, source : source + TILE]],
                axis=0,
            )
            part = lax.dot_general(
                left_ref[...], right, NN, preferred_element_type=jnp.float32
            ).astype(jnp.bfloat16)
            if tile < tiles:
                part = part.reshape(CHIPS // 2, 2, height, TILE)
                low, high = part[:, 0], part[:, 1]
                out_rows = slice(row_a, row_a + height)
                keep_a[:, out_rows, :] = jnp.where(xbit == 0, low, high)
                send_a[:, out_rows, :] = jnp.where(xbit == 0, high, low)
                row_a += height
            else:
                part = part.reshape(CHIPS // 4, 2, 2, height, TILE)
                low, high = part[:, 0], part[:, 1]
                out_rows = slice(row_b, row_b + height)
                keep_b[:, :, out_rows, :] = jnp.where(ybit == 0, low, high)
                send_b[:, :, out_rows, :] = jnp.where(ybit == 0, high, low)
                row_b += height


def weight_parts(jobs, info, mine, theirs, after, expense):
    rows = mine.shape[0]
    vmem = pl.BlockSpec(memory_space=pltpu.VMEM)
    rows_a, rows_b = rows_of(jobs)
    first = jax.ShapeDtypeStruct((CHIPS // 2, rows_a, TILE), jnp.bfloat16)
    second = jax.ShapeDtypeStruct((CHIPS // 4, 2, rows_b, TILE), jnp.bfloat16)
    return pl.pallas_call(
        partial(weight_kernel, jobs),
        in_specs=[pl.BlockSpec(memory_space=pltpu.SMEM), vmem, vmem] + [ANYWHERE] * len(after),
        out_specs=[vmem] * 4,
        out_shape=[first, first, second, second],
        scratch_shapes=[pltpu.VMEM((CHIPS * job[1], 2 * rows), jnp.bfloat16) for job in jobs],
        compiler_params=pltpu.CompilerParams(vmem_limit_bytes=VMEM_LIMIT),
        cost_estimate=cost(expense),
        name="weight_parts",
    )(info, mine, theirs, *after)


WEIGHT_ROWS = 256
QUARTER = 6 * D // 4


def first_back_kernel(
    info_ref,
    dqkv_ref,
    tokens_ref,
    mod_ref,
    dmid_ref,
    early_ref,
    weight_ref,
    *refs,
):
    grad_ref, packed_ref, flat_ref, total_ref, wide_ref = refs[-5:]
    step = pl.program_id(0)

    @pl.when(step == 0)
    def _():
        for group in range(D // LANES):
            for part in range(3):
                column = part * D + group * LANES
                flat_ref[:, column : column + LANES] = dqkv_ref[
                    group, :, part * LANES : (part + 1) * LANES
                ]

    columns = pl.ds(pl.multiple_of(step * WEIGHT_ROWS, WEIGHT_ROWS), WEIGHT_ROWS)
    total_ref[:, columns] = lax.dot_general(
        flat_ref[...], weight_ref[...], NT, preferred_element_type=jnp.float32
    )

    @pl.when(step == pl.num_programs(0) - 1)
    def _():
        for slot in range(2):
            rows = slice(slot * PATCHES, (slot + 1) * PATCHES)
            normed, inverse = normalize(tokens_ref[rows, :].astype(jnp.float32))
            d_first = total_ref[rows, :]
            scale = mod_ref[pl.ds(info_ref[MINE_AT + slot], 1), D : 2 * D]
            grad_ref[rows, :] = (
                dmid_ref[rows, :] + norm_backward(d_first * (1.0 + scale), normed, inverse)
            ).astype(jnp.bfloat16)
            pieces = (
                (0, jnp.sum(d_first, axis=0, keepdims=True)),
                (D, jnp.sum(d_first * normed, axis=0, keepdims=True)),
                (2 * D, early_ref[slot : slot + 1, :]),
            )
            for start, piece in pieces:
                for quarter in range(4):
                    low = max(start, quarter * QUARTER)
                    high = min(start + piece.shape[1], (quarter + 1) * QUARTER)
                    if low < high:
                        wide_ref[
                            2 * quarter + slot : 2 * quarter + slot + 1,
                            low - quarter * QUARTER : high - quarter * QUARTER,
                        ] = piece[:, low - start : high - start]
        packed_ref[...] = wide_ref[...].astype(jnp.bfloat16)


def first_back(info, d_qkv, tokens_here, modulation, d_middle, early, qkv_weight, after):
    rows = tokens_here.shape[0]
    return pl.pallas_call(
        first_back_kernel,
        grid_spec=pltpu.PrefetchScalarGridSpec(
            num_scalar_prefetch=1,
            grid=(D // WEIGHT_ROWS,),
            in_specs=[
                full_block(d_qkv.shape),
                full_block((rows, D)),
                full_block(modulation.shape),
                full_block((rows, D)),
                full_block(early.shape),
                pl.BlockSpec((WEIGHT_ROWS, 3 * D), lambda i, frames: (i, 0)),
            ]
            + [ANYWHERE] * len(after),
            out_specs=[full_block((rows, D)), full_block((8, QUARTER))],
            scratch_shapes=[
                pltpu.VMEM((rows, 3 * D), jnp.bfloat16),
                pltpu.VMEM((rows, D), jnp.float32),
                pltpu.VMEM((8, QUARTER), jnp.float32),
            ],
        ),
        out_shape=[
            jax.ShapeDtypeStruct((rows, D), jnp.bfloat16),
            jax.ShapeDtypeStruct((8, QUARTER), jnp.bfloat16),
        ],
        compiler_params=pltpu.CompilerParams(
            vmem_limit_bytes=VMEM_LIMIT, dimension_semantics=("arbitrary",)
        ),
        cost_estimate=cost(6),
        name="first_back",
    )(info, d_qkv, tokens_here, modulation, d_middle, early, qkv_weight, *after)


def qkv_part_kernel(info_ref, first_refs, grad_ref, keep_ref, send_ref):
    pieces = [(ref, piece) for ref in first_refs for piece in range(ref.shape[0])]
    total = None
    for place, (ref, piece) in enumerate(pieces):
        update = lax.dot_general(
            ref[piece],
            grad_ref[info_ref[ORDER_AT + place]],
            (((0,), (0,)), ((), ())),
            preferred_element_type=jnp.float32,
        )
        total = update if total is None else total + update
    groups, clip_pairs, share, width = keep_ref.shape
    split = total.astype(jnp.bfloat16).reshape(groups, clip_pairs, 2, share, width)
    low, high = split[:, :, 0], split[:, :, 1]
    keep_ref[...] = jnp.where(info_ref[BITS_AT] == 0, low, high)
    send_ref[...] = jnp.where(info_ref[BITS_AT] == 0, high, low)


def qkv_parts(info, firsts, d_heads, share, after):
    vmem = pl.BlockSpec(memory_space=pltpu.VMEM)
    shape = (D // LANES, 2, share, d_heads.shape[2])

    def kernel(info_ref, *refs):
        count = len(firsts)
        qkv_part_kernel(info_ref, refs[:count], refs[count], *refs[-2:])

    return pl.pallas_call(
        kernel,
        in_specs=[pl.BlockSpec(memory_space=pltpu.SMEM)]
        + [vmem] * (len(firsts) + 1)
        + [ANYWHERE] * len(after),
        out_specs=[vmem] * 2,
        out_shape=[jax.ShapeDtypeStruct(shape, jnp.bfloat16)] * 2,
        compiler_params=pltpu.CompilerParams(vmem_limit_bytes=VMEM_LIMIT),
        cost_estimate=cost(0.2),
        name="qkv_parts",
    )(info, *firsts, d_heads, *after)


def pair_sum(keep, got):
    return (keep.astype(jnp.float32) + got.astype(jnp.float32)).astype(jnp.bfloat16)


def fold_kernel(bits, info_ref, *refs):
    count = len(bits)
    out_refs = refs[-2 * count :]
    for place, bit_at in enumerate(bits):
        keep, got = refs[2 * place : 2 * place + 2]
        low, high = pair_sum(keep[:, 0], got[:, 0]), pair_sum(keep[:, 1], got[:, 1])
        bit = info_ref[BITS_AT + bit_at]
        kept, sent = out_refs[2 * place : 2 * place + 2]
        kept[...] = jnp.where(bit == 0, low, high)
        sent[...] = jnp.where(bit == 0, high, low)


def fold(info, bits, pairs, after, expense):
    count, unused, unused_rows, columns = pairs[0][0].shape
    in_specs, out_specs, out_shape = [], [], []
    for keep, got in pairs:
        rows = keep.shape[2]
        in_specs += [full_block((count, 2, rows, columns))] * 2
        out_specs += [full_block((count, rows, columns))] * 2
        out_shape += [jax.ShapeDtypeStruct((count, rows, columns), jnp.bfloat16)] * 2
    return pl.pallas_call(
        partial(fold_kernel, bits),
        grid_spec=pltpu.PrefetchScalarGridSpec(
            num_scalar_prefetch=1,
            grid=(1,),
            in_specs=in_specs + [ANYWHERE] * len(after),
            out_specs=out_specs,
        ),
        out_shape=out_shape,
        compiler_params=pltpu.CompilerParams(
            vmem_limit_bytes=VMEM_LIMIT, dimension_semantics=("arbitrary",)
        ),
        cost_estimate=cost(expense),
        name="fold",
    )(info, *(part for pair in pairs for part in pair), *after)


def blend_kernel(riders, keep_a, got_a, keep_b, got_b, *refs):
    out_ref = refs[-1]
    row = 0
    for keep, got in ((keep_a, got_a), (keep_b, got_b)):
        height = keep.shape[1]
        out_ref[:, row : row + height, :] = pair_sum(keep[...], got[...])
        row += height
    for side, rider in enumerate(refs[:riders]):
        height = rider.shape[1]
        out_ref[:, row + side * height : row + (side + 1) * height, :] = rider[:, :, :TILE]
        last = row + riders * height
        out_ref[:, last : last + height, side * LANES : (side + 1) * LANES] = rider[:, :, TILE:]


def blend(parts, riders, after, expense):
    rows = sum(part.shape[1] for part in parts[::2]) + (3 * FINE if riders else 0)
    count, columns = parts[0].shape[0], parts[0].shape[2]
    operands = tuple(parts) + tuple(riders)
    return pl.pallas_call(
        partial(blend_kernel, len(riders)),
        grid=(1,),
        in_specs=[full_block(part.shape) for part in operands]
        + [ANYWHERE] * len(after),
        out_specs=full_block((count, rows, columns)),
        out_shape=jax.ShapeDtypeStruct((count, rows, columns), jnp.bfloat16),
        compiler_params=pltpu.CompilerParams(
            vmem_limit_bytes=VMEM_LIMIT, dimension_semantics=("arbitrary",)
        ),
        cost_estimate=cost(expense),
        name="blend",
    )(*operands, *after)


def join_kernel(mine_ref, theirs_ref, *refs):
    count = mine_ref.shape[0]
    refs[-1][:count] = mine_ref[...]
    refs[-1][count:] = theirs_ref[...]


def join(mine, theirs, after):
    vmem = pl.BlockSpec(memory_space=pltpu.VMEM)
    return pl.pallas_call(
        join_kernel,
        in_specs=[vmem, vmem] + [ANYWHERE] * len(after),
        out_specs=vmem,
        out_shape=jax.ShapeDtypeStruct((2 * mine.shape[0],) + mine.shape[1:], mine.dtype),
        compiler_params=pltpu.CompilerParams(vmem_limit_bytes=VMEM_LIMIT),
        cost_estimate=cost(0.5),
        name="join",
    )(mine, theirs, *after)


def add_kernel(bit_at, info_ref, keep_ref, got_ref, *refs):
    low, high = (
        (keep_ref[:, half].astype(jnp.float32) + got_ref[:, half].astype(jnp.float32)).astype(
            jnp.bfloat16
        )
        for half in range(2)
    )
    bit = info_ref[BITS_AT + bit_at]
    refs[-2][...] = jnp.where(bit == 0, low, high)
    refs[-1][...] = jnp.where(bit == 0, high, low)


def add_halves(info, keep, got, bit_at, after):
    vmem = pl.BlockSpec(memory_space=pltpu.VMEM)
    out = jax.ShapeDtypeStruct(keep.shape[:1] + keep.shape[2:], jnp.bfloat16)
    return pl.pallas_call(
        partial(add_kernel, bit_at),
        in_specs=[pl.BlockSpec(memory_space=pltpu.SMEM), vmem, vmem] + [ANYWHERE] * len(after),
        out_specs=[vmem] * 2,
        out_shape=[out] * 2,
        cost_estimate=cost(1),
        name="add_halves",
    )(info, keep, got, *after)


def finish_kernel(jobs, riders, info_ref, parts_ref, *refs):
    targets = refs[-len(jobs) - riders :]
    row = [0, rows_of(jobs)[0]]
    for (unused, height, unused_at, width, tiles), target in zip(jobs, targets):
        for tile in range(width // TILE):
            second = tile >= tiles
            rows = slice(row[second], row[second] + height)
            total = parts_ref[0, rows, :].astype(jnp.float32)
            for part in range(1, parts_ref.shape[0]):
                total = total + parts_ref[part, rows, :].astype(jnp.float32)
            target[:, tile * TILE : (tile + 1) * TILE] = total
            row[second] += height
    if riders:
        first_row = sum(rows_of(jobs))
        ybit = info_ref[BITS_AT + 2]
        for place in range(parts_ref.shape[0]):
            for side in range(2):
                group = 2 * place + (ybit if side == 0 else 1 - ybit)
                for part in range(3):
                    row_at, lane_at = ((side, 0), (side, 1), (2, side))[part]
                    rows = slice(first_row + row_at * FINE, first_row + (row_at + 1) * FINE)
                    lanes = slice(lane_at * LANES, (lane_at + 1) * LANES)
                    column = pl.multiple_of(part * D + group * LANES, LANES)
                    targets[-1][:, pl.ds(column, LANES)] = parts_ref[place, rows, lanes].astype(
                        jnp.float32
                    )


def finish(info, jobs, parts, riders, after):
    vmem = pl.BlockSpec(memory_space=pltpu.VMEM)
    shapes = [(job[1], job[3]) for job in jobs] + [(FINE, 3 * D)] * riders
    return pl.pallas_call(
        partial(finish_kernel, jobs, riders),
        in_specs=[pl.BlockSpec(memory_space=pltpu.SMEM), vmem] + [ANYWHERE] * len(after),
        out_specs=[vmem] * len(shapes),
        out_shape=[jax.ShapeDtypeStruct(shape, jnp.float32) for shape in shapes],
        compiler_params=pltpu.CompilerParams(vmem_limit_bytes=VMEM_LIMIT),
        cost_estimate=cost(2),
        name="finish",
    )(info, parts, *after)


def closing_kernel(all_ref, embedded_ref, weight_ref, hot_ref, modw_ref, table_ref, bias_ref):
    rows = all_ref.shape[0]
    slots, share = embedded_ref.shape
    embedded = embedded_ref[...]
    sigmoid = jax.nn.sigmoid(embedded)
    activated = (embedded * sigmoid).astype(jnp.bfloat16)
    row = lax.broadcasted_iota(jnp.int32, (slots, rows), 1)
    slot = lax.broadcasted_iota(jnp.int32, (slots, rows), 0)
    d_activated = None
    for quarter in range(4):
        columns = slice(quarter * QUARTER, (quarter + 1) * QUARTER)
        chosen = jnp.where(row == slot // 2 * 8 + 2 * quarter + slot % 2, 1.0, 0.0)
        spread = lax.dot_general(
            activated,
            chosen.astype(jnp.bfloat16),
            (((0,), (0,)), ((), ())),
            preferred_element_type=jnp.float32,
        ).astype(jnp.bfloat16)
        modw_ref[:, columns] = lax.dot_general(
            spread, all_ref[...], NN, preferred_element_type=jnp.float32
        )
        every = jnp.where(
            lax.broadcasted_iota(jnp.int32, (8, rows), 1) % 8 // 2 == quarter, 1.0, 0.0
        ).astype(jnp.bfloat16)
        bias_ref[:, columns] = lax.dot_general(
            every, all_ref[...], NN, preferred_element_type=jnp.float32
        )[:1, :]
        part = lax.dot_general(
            all_ref[...], weight_ref[:, columns], NT, preferred_element_type=jnp.float32
        )
        part = lax.dot_general(
            chosen,
            part,
            NN,
            precision=lax.Precision.HIGHEST,
            preferred_element_type=jnp.float32,
        )
        d_activated = part if d_activated is None else d_activated + part
    d_embedded = d_activated * (sigmoid * (1.0 + embedded * (1.0 - sigmoid)))
    table_ref[...] = lax.dot_general(
        hot_ref[...],
        d_embedded,
        NN,
        precision=lax.Precision.HIGHEST,
        preferred_element_type=jnp.float32,
    )


def closing(gathered, embedded, weight_rows, level_hot):
    vmem = pl.BlockSpec(memory_space=pltpu.VMEM)
    share = embedded.shape[1]
    return pl.pallas_call(
        closing_kernel,
        in_specs=[vmem] * 4,
        out_specs=[vmem] * 3,
        out_shape=[
            jax.ShapeDtypeStruct((share, 6 * D), jnp.float32),
            jax.ShapeDtypeStruct((LEVELS, share), jnp.float32),
            jax.ShapeDtypeStruct((1, 6 * D), jnp.float32),
        ],
        compiler_params=pltpu.CompilerParams(vmem_limit_bytes=VMEM_LIMIT),
        cost_estimate=cost(3),
        name="closing",
    )(gathered, embedded, weight_rows, level_hot)


def halved(part):
    return part.reshape((-1, 2) + part.shape[-2:])


def across(info, parts, after, expense):
    keep_a, got_a, keep_b, got_b = (halved(part) for part in parts)
    keep_a, send_a, keep_b, send_b = fold(
        info, (2, 1), ((keep_a, got_a), (keep_b, got_b)), after, expense
    )
    return (keep_a, swap(send_a, 4), keep_b, swap(send_b, 2)), send_a


def along(parts, riders, after, expense):
    total = blend(parts, riders, after, expense)
    columns = [[2 * place + side for place in range(4)] for side in range(2)]
    return lax.all_to_all(total, "blk", 0, 0, axis_index_groups=columns, tiled=True), total


def local_heads(
    tokens,
    noise_levels,
    group_map,
    noise_table,
    mod_weight,
    mod_bias,
    qkv_weight,
    out_weight,
    fc1_weight,
    fc2_weight,
    out_cotangent,
):
    rows_here = 2 * PATCHES
    frame_count = group_map.shape[0]
    groups = D // LANES
    device_count = lax.axis_size(AXES)
    index = lax.axis_index(AXES)
    bits = [(index >> place) & 1 for place in range(5)]
    tables = rope_tables(frame_count)
    clip_levels = noise_levels
    for bit in (1, 2):
        clip_levels = jnp.concatenate([clip_levels, swap(clip_levels, bit)], axis=0)
    members = jnp.zeros((1,), jnp.int32)
    for bit in (16, 8, 4, 2, 1):
        members = jnp.concatenate([members, members ^ bit])
    member_slots = (2 * ((index ^ members) >> 2))[:, None] + jnp.arange(2, dtype=jnp.int32)[None, :]
    levels_all = clip_levels[(members & 3)[:, None], group_map[member_slots]].reshape(
        2 * device_count
    )
    tokens_here = tokens.reshape(rows_here, D)
    block = lax.axis_index("blk")
    piece_at = block ^ jnp.array(PIECES, jnp.int32)
    places = jnp.arange(frame_count, dtype=jnp.int32)
    piece_slots = ((2 * piece_at)[:, None] + jnp.arange(2, dtype=jnp.int32)[None, :]).reshape(-1)
    frames = jnp.sum(
        jnp.where(piece_slots[:, None] == places[None, :], group_map[None, :], 0), axis=1
    )
    slots = jnp.sum(jnp.where(group_map[None, :] == places[:, None], places[None, :], 0), axis=1)
    info = jnp.concatenate(
        [jnp.stack(bits), piece_at, frames, slots, group_map, frames[:2]]
    ).astype(jnp.int32)
    far = cross(tokens_here, 4)
    side = cross(tokens_here, 1)
    near = cross(tokens_here, 2)
    far_side, far_near, near_side = cross(far, 1), cross(far, 2), cross(side, 2)
    last = (cross(far_near[:PATCHES], 1), cross(far_side[PATCHES:], 2))
    modulation = modulate(
        noise_levels, noise_table, mod_weight, mod_bias
    )
    weight_here = own_columns(info, qkv_weight)
    projected = []
    for first_piece, pieces in (
        (0, (tokens_here,)),
        (1, (far, near, side)),
        (4, (far_side, far_near, near_side)),
        (7, (last,)),
    ):
        projected.append(project(info, modulation, weight_here, tables, first_piece, pieces))
    qkv_heads = [pair[0] for pair in projected]
    firsts = [pair[1] for pair in projected]
    att_heads, ot, lse = attend(info, qkv_heads, levels_all)
    att = lax.all_to_all(att_heads, "blk", 0, 0, tiled=True)
    layer_out, up_acts, down_acts, d_att, d_middle, d_mod_early = middle_block(
        info,
        att,
        tokens_here,
        out_cotangent.reshape(rows_here, D),
        modulation,
        out_weight,
        fc1_weight,
        fc2_weight,
    )
    grad_heads = lax.all_to_all(d_att, "blk", 0, 0, tiled=True)
    share = D // device_count
    keep_a, send_a, keep_b, send_b = weight_parts(
        UPPER_JOBS, info, up_acts, swap(up_acts, 1), (), 2)
    upper = (keep_a, swap(send_a, 2), keep_b, swap(send_b, 4))
    d_heads = attend_back(info, qkv_heads, grad_heads, ot, lse, tables, (send_a,))
    d_qkv = lax.all_to_all(d_heads, "blk", 0, 0, tiled=True)
    qkv_keep, qkv_send = qkv_parts(info, firsts, d_heads, share, ())
    qkv_keep, qkv_send = add_halves(info, qkv_keep, swap(qkv_send, 1), 1, ())
    qkv_got = swap(qkv_send, 2)
    upper, upper_sent = across(info, upper, (qkv_send,), 6)
    keep_a, send_a, keep_b, send_b = weight_parts(
        LOWER_JOBS, info, down_acts, swap(down_acts, 1), (upper_sent, qkv_got, upper[3]), 3)
    lower = (keep_a, swap(send_a, 2), keep_b, swap(send_b, 4))
    upper, upper_z = along(upper, (), (send_a,), 1)
    tokens_grad, d_mod = first_back(
        info, d_qkv, tokens_here, modulation, d_middle, d_mod_early, qkv_weight, (upper_z,)
    )
    pairs = (groups // 2, 2, share, 3 * LANES)
    qkv_keep, qkv_send = add_halves(
        info, qkv_keep.reshape(pairs), qkv_got.reshape(pairs), 2, (d_mod,)
    )
    qkv_got = swap(qkv_send, 4)
    got = swap(d_mod, 16)
    lower, lower_sent = across(info, lower, (qkv_send,), 15)
    d_mod = join(d_mod, got, (lower_sent,))
    got = swap(d_mod, 8)
    lower, lower_z = along(lower, (qkv_keep, qkv_got), (d_mod,), 5)
    d_mod = join(d_mod, got, (lower_z,))
    for bit in (4, 2, 1):
        d_mod = jnp.concatenate([d_mod, swap(d_mod, bit)])
    level_hot = jnp.arange(LEVELS, dtype=jnp.int32)[:, None] == levels_all[None, :]
    table_columns = lax.dynamic_slice_in_dim(noise_table, index * share, share, 1)
    embedded_columns = jnp.einsum(
        "ls,lc->sc",
        level_hot.astype(jnp.bfloat16),
        table_columns,
        preferred_element_type=jnp.float32,
    )
    weight_rows = lax.dynamic_slice_in_dim(mod_weight, index * share, share, 0)
    modw_share, table_share, bias_sums = closing(
        d_mod, embedded_columns, weight_rows, level_hot.astype(jnp.float32)
    )
    bias_columns = 6 * D // device_count
    bias_share = lax.dynamic_slice_in_dim(bias_sums[0], index * bias_columns, bias_columns)
    upper_share, outw_share = finish(info, UPPER_JOBS, upper, 0, (lower_z,))
    lower_share, qkv_share = finish(
        info, LOWER_JOBS, lower, 1, (upper_share, table_share, modw_share, bias_share)
    )
    return (
        layer_out[None].reshape(1, 2, PATCHES, D),
        tokens_grad.reshape(1, 2, PATCHES, D),
        table_share,
        modw_share,
        bias_share,
        qkv_share,
        outw_share,
        upper_share,
        lower_share,
    )


def solution(mesh):
    pair_split = mesh.shape["blk"] * LANES == D and mesh.shape["clip"] == 4
    return jax.shard_map(
        local_heads if pair_split else local,
        mesh=mesh,
        in_specs=(
            P("clip", "blk", None, None),
            P("clip", None),
            P(),
            P(),
            P(),
            P(),
            P(),
            P(),
            P(),
            P(),
            P("clip", "blk", None, None),
        ),
        out_specs=(
            P("clip", "blk", None, None),
            P("clip", "blk", None, None),
            P(None, ("blk", "clip")),
            P(("blk", "clip"), None),
            P(("blk", "clip")),
            P(("blk", "clip"), None),
            P(("blk", "clip"), None),
            P(("blk", "clip"), None),
            P(("blk", "clip"), None),
        ),
        check_vma=False,
    )
```

```python
from functools import partial

import jax
import jax.numpy as jnp
import numpy as np
from jax import lax
from jax.experimental import pallas as pl
from jax.experimental.pallas import tpu as pltpu
from jax.sharding import PartitionSpec as P

D = 1024
HEAD = 64
HEADS = 16
LEVELS = 1000
GRID_H = 8
GRID_W = 16
PATCHES = 128


SCALE = 0.125
EPSILON = 1e-06
ROPE_BASE = 10000.0
NEG_LARGE = -1e30


def token_positions(frame_ids):
    slot_count = frame_ids.shape[0]
    total_rows = slot_count * GRID_H * GRID_W
    patch_ids = jnp.arange(total_rows, dtype=jnp.int32) % (GRID_H * GRID_W)
    frame_pos = jnp.repeat(frame_ids, GRID_H * GRID_W, total_repeat_length=total_rows)
    return (frame_pos, patch_ids // GRID_W, patch_ids % GRID_W)


def rope_angles(frame_pos, row_pos, col_pos):
    angle_list = []
    for position, comp_width in ((frame_pos, 16), (row_pos, 24), (col_pos, 24)):
        half_width = comp_width // 2
        frequency = ROPE_BASE ** (-2.0 * jnp.arange(half_width, dtype=jnp.float32) / comp_width)
        angle_list.append(position.astype(jnp.float32)[:, None] * frequency[None, :])
    return angle_list


def rotate(values, angle_list, direction):
    pieces = []
    offset = 0
    for angles in angle_list:
        half_width = angles.shape[1]
        first_half = values[:, :, offset : offset + half_width]
        second_half = values[:, :, offset + half_width : offset + 2 * half_width]
        cosine = jnp.cos(angles)[:, None, :]
        sine_part = direction * jnp.sin(angles)[:, None, :]
        pieces.append(first_half * cosine - second_half * sine_part)
        pieces.append(first_half * sine_part + second_half * cosine)
        offset = offset + 2 * half_width
    return jnp.concatenate(pieces, axis=2)


def normalize(values):
    center = values - jnp.mean(values, axis=-1, keepdims=True)
    inverse = lax.rsqrt(jnp.mean(center * center, axis=-1, keepdims=True) + EPSILON)
    return (center * inverse, inverse)


def norm_backward(grad_in, normed, inverse):
    return inverse * (
        grad_in
        - jnp.mean(grad_in, axis=-1, keepdims=True)
        - normed * jnp.mean(grad_in * normed, axis=-1, keepdims=True)
    )


def frames_of(group_map, first_row, row_count):
    slot_frames = lax.dynamic_slice_in_dim(group_map, first_row // PATCHES, row_count // PATCHES)
    return jnp.repeat(slot_frames, PATCHES, total_repeat_length=row_count)


def block_size(row_count, shard_rows):
    return 2 * shard_rows if row_count // shard_rows % 2 == 0 else shard_rows


def keep_same(values):
    return values


def local(
    tokens,
    noise_levels,
    group_map,
    noise_table,
    mod_weight,
    mod_bias,
    qkv_weight,
    out_weight,
    fc1_weight,
    fc2_weight,
    out_cotangent,
):
    rows_here = 2 * PATCHES
    my_frames = lax.dynamic_slice_in_dim(group_map, 2 * lax.axis_index("blk"), 2)
    frame_hot = (
        jnp.arange(group_map.shape[0], dtype=jnp.int32)[None, :] == my_frames[:, None]
    ).astype(jnp.int32)
    my_levels = jnp.sum(frame_hot * noise_levels[0][None, :], axis=1)
    level_hot = jnp.arange(LEVELS, dtype=jnp.int32)[None, :] == my_levels[:, None]
    embedded = jnp.dot(
        level_hot.astype(jnp.bfloat16), noise_table, preferred_element_type=jnp.float32
    )
    activated = jax.nn.silu(embedded).astype(jnp.bfloat16)
    modulation = (
        jnp.dot(activated, mod_weight, preferred_element_type=jnp.float32)
        + mod_bias.astype(jnp.float32)[None, :]
    )
    shift_one, scale_one, gate_one, shift_two, scale_two, gate_two = [
        modulation[:, member * D : (member + 1) * D][:, None, :] for member in range(6)
    ]
    inputs_here = tokens[0].astype(jnp.float32)
    normed_one, inverse_one = normalize(inputs_here)
    first_in = (
        (normed_one * (1.0 + scale_one) + shift_one).astype(jnp.bfloat16).reshape(rows_here, D)
    )
    qkv_lin = jnp.dot(first_in, qkv_weight, preferred_element_type=jnp.float32)
    token_frames, row_pos, col_pos = token_positions(my_frames)
    angle_list = rope_angles(token_frames, row_pos, col_pos)
    query = rotate(qkv_lin[:, :D].reshape(rows_here, HEADS, HEAD), angle_list, 1.0).astype(
        jnp.bfloat16
    )
    key_part = rotate(
        qkv_lin[:, D : 2 * D].reshape(rows_here, HEADS, HEAD), angle_list, 1.0
    ).astype(jnp.bfloat16)
    value_part = qkv_lin[:, 2 * D :].reshape(rows_here, HEADS, HEAD).astype(jnp.bfloat16)
    top_frame = jnp.max(my_frames)
    own_lowest = jnp.min(my_frames)
    forward_start = (
        jnp.full((HEADS, rows_here), NEG_LARGE, jnp.float32),
        jnp.zeros((HEADS, rows_here), jnp.float32),
        jnp.zeros((rows_here, HEADS, HEAD), jnp.float32),
    )
    first_row = jnp.int32(0)
    keys_piece = lax.all_gather(key_part, "blk", axis=0, tiled=True)
    values_piece = lax.all_gather(value_part, "blk", axis=0, tiled=True)
    piece_rows = keys_piece.shape[0]
    block_rows = block_size(piece_rows, rows_here)

    def forward_advance(turn_index, running):
        offset = turn_index * block_rows
        keys_block = lax.dynamic_slice_in_dim(keys_piece, offset, block_rows)
        values_block = lax.dynamic_slice_in_dim(values_piece, offset, block_rows)
        block_frames = frames_of(group_map, first_row + offset, block_rows)

        def attend(previous):
            top_scores, totals, accumulated = previous
            scores = (
                jnp.einsum("qhd,khd->hqk", query, keys_block, preferred_element_type=jnp.float32)
                * SCALE
            )
            allowed = block_frames[None, None, :] <= token_frames[None, :, None]
            new_top = jnp.maximum(
                top_scores, jnp.max(jnp.where(allowed, scores, NEG_LARGE), axis=2)
            )
            weights = jnp.where(allowed, jnp.exp(scores - new_top[:, :, None]), 0.0)
            factor = jnp.exp(top_scores - new_top)
            update = jnp.einsum(
                "hqk,khd->qhd",
                weights.astype(jnp.bfloat16),
                values_block,
                preferred_element_type=jnp.float32,
            )
            return (
                new_top,
                totals * factor + jnp.sum(weights, axis=2),
                accumulated * factor.T[:, :, None] + update,
            )

        return lax.cond(jnp.min(block_frames) > top_frame, keep_same, attend, running)

    top_scores, totals, accumulated = lax.fori_loop(
        0, piece_rows // block_rows, forward_advance, forward_start
    )
    attended = accumulated / totals.T[:, :, None]
    log_total = top_scores + jnp.log(totals)
    attended_low = attended.astype(jnp.bfloat16).reshape(rows_here, D)
    attn_out = jnp.dot(attended_low, out_weight, preferred_element_type=jnp.float32).reshape(
        2, PATCHES, D
    )
    middle = inputs_here + gate_one * attn_out
    normed_two, inverse_two = normalize(middle)
    second_in = (
        (normed_two * (1.0 + scale_two) + shift_two).astype(jnp.bfloat16).reshape(rows_here, D)
    )
    up_lin = jnp.dot(second_in, fc1_weight, preferred_element_type=jnp.float32)
    hidden = jax.nn.gelu(up_lin, approximate=False).astype(jnp.bfloat16)
    mlp_out = jnp.dot(hidden, fc2_weight, preferred_element_type=jnp.float32).reshape(2, PATCHES, D)
    layer_out = (middle + gate_two * mlp_out).astype(jnp.bfloat16)[None]
    cotangent = out_cotangent[0].astype(jnp.float32)
    d_gate_two = jnp.sum(cotangent * mlp_out, axis=1)
    d_mlp = (cotangent * gate_two).astype(jnp.bfloat16).reshape(rows_here, D)
    lower_part = jnp.einsum("rf,rd->fd", hidden, d_mlp, preferred_element_type=jnp.float32)
    d_hidden = jnp.einsum("rd,fd->rf", d_mlp, fc2_weight, preferred_element_type=jnp.float32)
    unused_value, gelu_pull = jax.vjp(partial(jax.nn.gelu, approximate=False), up_lin)
    d_up = gelu_pull(d_hidden)[0].astype(jnp.bfloat16)
    upper_part = jnp.einsum("rc,rf->cf", second_in, d_up, preferred_element_type=jnp.float32)
    d_second = jnp.einsum(
        "rf,cf->rc", d_up, fc1_weight, preferred_element_type=jnp.float32
    ).reshape(2, PATCHES, D)
    d_shift_two = jnp.sum(d_second, axis=1)
    d_scale_two = jnp.sum(d_second * normed_two, axis=1)
    d_middle = cotangent + norm_backward(d_second * (1.0 + scale_two), normed_two, inverse_two)
    d_gate_one = jnp.sum(d_middle * attn_out, axis=1)
    d_attn = (d_middle * gate_one).astype(jnp.bfloat16).reshape(rows_here, D)
    outw_part = jnp.einsum("rc,rd->cd", attended_low, d_attn, preferred_element_type=jnp.float32)
    d_attended = (
        jnp.einsum("rd,cd->rc", d_attn, out_weight, preferred_element_type=jnp.float32)
        .astype(jnp.bfloat16)
        .reshape(rows_here, HEADS, HEAD)
    )
    delta = jnp.sum(d_attended.astype(jnp.float32) * attended, axis=2).T
    grad_start = jnp.zeros((rows_here, HEADS, HEAD), jnp.float32)
    query_first_row = jnp.int32(0)
    query_keys_piece = lax.all_gather(key_part, "blk", axis=0, tiled=True)
    query_values_piece = lax.all_gather(value_part, "blk", axis=0, tiled=True)
    piece_rows = query_keys_piece.shape[0]
    query_block_rows = block_size(piece_rows, rows_here)

    def query_advance(turn_index, running):
        offset = turn_index * query_block_rows
        keys_block = lax.dynamic_slice_in_dim(query_keys_piece, offset, query_block_rows)
        values_block = lax.dynamic_slice_in_dim(query_values_piece, offset, query_block_rows)
        block_frames = frames_of(group_map, query_first_row + offset, query_block_rows)

        def query_accumulate(previous):
            scores = (
                jnp.einsum("qhd,khd->hqk", query, keys_block, preferred_element_type=jnp.float32)
                * SCALE
            )
            allowed = block_frames[None, None, :] <= token_frames[None, :, None]
            weights = jnp.where(allowed, jnp.exp(scores - log_total[:, :, None]), 0.0)
            weight_grad = jnp.einsum(
                "qhd,khd->hqk", d_attended, values_block, preferred_element_type=jnp.float32
            )
            score_grad = (weights * (weight_grad - delta[:, :, None]) * SCALE).astype(jnp.bfloat16)
            return previous + jnp.einsum(
                "hqk,khd->qhd", score_grad, keys_block, preferred_element_type=jnp.float32
            )

        return lax.cond(jnp.min(block_frames) > top_frame, keep_same, query_accumulate, running)

    query_grad = lax.fori_loop(0, piece_rows // query_block_rows, query_advance, grad_start)
    stats_lse, stats_delta = (
        lax.all_gather(log_total.T, "blk", axis=0, tiled=True),
        lax.all_gather(delta.T, "blk", axis=0, tiled=True),
    )
    key_first_row = jnp.int32(0)
    queries_piece = lax.all_gather(query, "blk", axis=0, tiled=True)
    grads_piece = lax.all_gather(d_attended, "blk", axis=0, tiled=True)
    piece_rows = queries_piece.shape[0]
    key_block_rows = block_size(piece_rows, rows_here)

    def key_advance(turn_index, running):
        offset = turn_index * key_block_rows
        query_block = lax.dynamic_slice_in_dim(queries_piece, offset, key_block_rows)
        grad_block = lax.dynamic_slice_in_dim(grads_piece, offset, key_block_rows)
        lse_block = lax.dynamic_slice_in_dim(stats_lse, key_first_row + offset, key_block_rows).T
        delta_block = lax.dynamic_slice_in_dim(
            stats_delta, key_first_row + offset, key_block_rows
        ).T
        block_frames = frames_of(group_map, key_first_row + offset, key_block_rows)

        def key_accumulate(previous):
            key_total, value_total = previous
            scores = (
                jnp.einsum(
                    "qhd,khd->hqk", query_block, key_part, preferred_element_type=jnp.float32
                )
                * SCALE
            )
            allowed = token_frames[None, None, :] <= block_frames[None, :, None]
            weights = jnp.where(allowed, jnp.exp(scores - lse_block[:, :, None]), 0.0)
            value_total = value_total + jnp.einsum(
                "hqk,qhd->khd",
                weights.astype(jnp.bfloat16),
                grad_block,
                preferred_element_type=jnp.float32,
            )
            weight_grad = jnp.einsum(
                "qhd,khd->hqk", grad_block, value_part, preferred_element_type=jnp.float32
            )
            score_grad = (weights * (weight_grad - delta_block[:, :, None]) * SCALE).astype(
                jnp.bfloat16
            )
            key_total = key_total + jnp.einsum(
                "hqk,qhd->khd", score_grad, query_block, preferred_element_type=jnp.float32
            )
            return (key_total, value_total)

        return lax.cond(jnp.max(block_frames) < own_lowest, keep_same, key_accumulate, running)

    key_grad, value_grad = lax.fori_loop(
        0, piece_rows // key_block_rows, key_advance, (grad_start, grad_start)
    )
    query_low = lax.optimization_barrier(query_grad.astype(jnp.bfloat16)).astype(jnp.float32)
    key_low = lax.optimization_barrier(key_grad.astype(jnp.bfloat16)).astype(jnp.float32)
    query_back = rotate(query_low, angle_list, -1.0).reshape(rows_here, D)
    key_back = rotate(key_low, angle_list, -1.0).reshape(rows_here, D)
    d_qkv = jnp.concatenate(
        [query_back, key_back, value_grad.reshape(rows_here, D)], axis=1
    ).astype(jnp.bfloat16)
    qkv_part = jnp.einsum("rc,rk->ck", first_in, d_qkv, preferred_element_type=jnp.float32)
    d_first = jnp.einsum(
        "rk,ck->rc", d_qkv, qkv_weight, preferred_element_type=jnp.float32
    ).reshape(2, PATCHES, D)
    d_shift_one = jnp.sum(d_first, axis=1)
    d_scale_one = jnp.sum(d_first * normed_one, axis=1)
    tokens_grad = (
        d_middle + norm_backward(d_first * (1.0 + scale_one), normed_one, inverse_one)
    ).astype(jnp.bfloat16)[None]
    d_mod = jnp.concatenate(
        [d_shift_one, d_scale_one, d_gate_one, d_shift_two, d_scale_two, d_gate_two], axis=1
    )
    bias_part = jnp.sum(d_mod, axis=0)
    d_mod_low = d_mod.astype(jnp.bfloat16)
    d_activated = jnp.einsum("sk,ck->sc", d_mod_low, mod_weight, preferred_element_type=jnp.float32)
    unused_silu, silu_pull = jax.vjp(jax.nn.silu, embedded)
    d_embedded = silu_pull(d_activated)[0]
    table_part = jnp.einsum(
        "sl,sc->cl", level_hot.astype(jnp.float32), d_embedded, precision=lax.Precision.HIGHEST
    )
    activated_all, d_mod_all = (
        lax.all_gather(activated, ("blk", "clip"), axis=0, tiled=True),
        lax.all_gather(d_mod_low, ("blk", "clip"), axis=0, tiled=True),
    )
    share_rows = D // lax.axis_size(("blk", "clip"))
    my_columns = lax.dynamic_slice_in_dim(
        activated_all, lax.axis_index(("blk", "clip")) * share_rows, share_rows, 1
    )
    modw_share = jnp.einsum("sc,sk->ck", my_columns, d_mod_all, preferred_element_type=jnp.float32)
    summed = (
        lax.psum_scatter(table_part, ("blk", "clip"), scatter_dimension=0, tiled=True),
        lax.psum_scatter(bias_part, ("blk", "clip"), scatter_dimension=0, tiled=True),
        lax.psum_scatter(qkv_part, ("blk", "clip"), scatter_dimension=0, tiled=True),
        lax.psum_scatter(outw_part, ("blk", "clip"), scatter_dimension=0, tiled=True),
        lax.psum_scatter(upper_part, ("blk", "clip"), scatter_dimension=0, tiled=True),
        lax.psum_scatter(lower_part, ("blk", "clip"), scatter_dimension=0, tiled=True),
    )
    return (
        layer_out,
        tokens_grad,
        summed[0].T,
        modw_share,
        summed[1],
        summed[2],
        summed[3],
        summed[4],
        summed[5],
    )


LANES = 128
FF = 4096
AXES = ("blk", "clip")
EXP_SCALE = SCALE * 1.4426950408889634
VMEM_LIMIT = 56 * 1024 * 1024
NT = (((1,), (1,)), ((), ()))
NN = (((1,), (0,)), ((), ()))


def cost(microseconds):
    return pl.CostEstimate(
        flops=int(microseconds * 1e9), bytes_accessed=int(microseconds * 3e6), transcendentals=0
    )


class Shifted:
    def __init__(self, ref, start):
        self.ref, self.start = ref, start

    def __getitem__(self, place):
        return self.ref[self.start + place]


FRAME_COUNT = 2 * D // LANES
BITS_AT, ORDER_AT = 0, 5
FRAMES_AT = ORDER_AT + D // LANES
SLOTS_AT = FRAMES_AT + FRAME_COUNT
GROUP_AT = SLOTS_AT + FRAME_COUNT
MINE_AT = GROUP_AT + FRAME_COUNT
ANYWHERE = pl.BlockSpec(memory_space=pl.ANY)


def full_block(shape):
    return pl.BlockSpec(shape, lambda *ids: (0,) * len(shape))


def rope_tables(frame_count):
    lane = np.arange(LANES) % HEAD
    pieces = []
    for comp_width in (16, 24, 24):
        half_width = comp_width // 2
        frequency = ROPE_BASE ** (-2.0 * np.arange(half_width) / comp_width)
        pieces += [frequency, frequency]
    frequency = np.tile(np.concatenate(pieces), LANES // HEAD)[None, :]
    first = (lane < 8) | ((lane >= 16) & (lane < 28)) | ((lane >= 40) & (lane < 52))
    sign = np.where(first, -1.0, 1.0)[None, :]
    in_frame = (lane < 16)[None, :]
    in_row = (lane < 40)[None, :]
    frame_angle = np.arange(frame_count)[:, None] * frequency
    patch = np.arange(PATCHES)[:, None]
    place_angle = np.where(in_row, patch // GRID_W, patch % GRID_W) * frequency
    tables = (
        np.where(in_frame, np.cos(frame_angle), 0.0),
        np.where(in_frame, sign * np.sin(frame_angle), 0.0),
        np.where(in_frame, 0.0, np.cos(place_angle)),
        np.where(in_frame, 0.0, sign * np.sin(place_angle)),
    )
    return tuple(jnp.asarray(table, jnp.float32) for table in tables)


def partner_lanes(values):
    lane = lax.broadcasted_iota(jnp.int32, values.shape, 1) % HEAD
    ahead_eight = pltpu.roll(values, LANES - 8, 1)
    behind_eight = pltpu.roll(values, 8, 1)
    ahead_twelve = pltpu.roll(values, LANES - 12, 1)
    behind_twelve = pltpu.roll(values, 12, 1)
    ahead = ((lane >= 16) & (lane < 28)) | ((lane >= 40) & (lane < 52))
    return jnp.where(
        lane < 8,
        ahead_eight,
        jnp.where(lane < 16, behind_eight, jnp.where(ahead, ahead_twelve, behind_twelve)),
    )


def modulation_kernel(levels_ref, table_ref, weight_ref, bias_ref, out_ref, activated_ref):
    @pl.when(pl.program_id(0) == 0)
    def _():
        count = levels_ref.shape[1]
        hot = lax.broadcasted_iota(jnp.int32, (LEVELS, count), 0) == levels_ref[...]
        embedded = lax.dot_general(
            jnp.where(hot, 1.0, 0.0).astype(jnp.bfloat16),
            table_ref[...],
            (((0,), (0,)), ((), ())),
            preferred_element_type=jnp.float32,
        )
        activated_ref[...] = jax.nn.silu(embedded).astype(jnp.bfloat16)

    out_ref[...] = lax.dot_general(
        activated_ref[...], weight_ref[...], NN, preferred_element_type=jnp.float32
    ) + bias_ref[...].astype(jnp.float32)[None, :]


def modulate(levels, noise_table, mod_weight, mod_bias, first, count):
    frame_count = levels.shape[1]
    return pl.pallas_call(
        modulation_kernel,
        grid=(count,),
        in_specs=[
            full_block(levels.shape),
            full_block(noise_table.shape),
            pl.BlockSpec((D, D), lambda i: (0, first + i)),
            pl.BlockSpec((D,), lambda i: (first + i,)),
        ],
        out_specs=pl.BlockSpec((frame_count, D), lambda i: (0, i)),
        out_shape=jax.ShapeDtypeStruct((frame_count, count * D), jnp.float32),
        scratch_shapes=[pltpu.VMEM((frame_count, D), jnp.bfloat16)],
        compiler_params=pltpu.CompilerParams(
            vmem_limit_bytes=VMEM_LIMIT, dimension_semantics=("arbitrary",)
        ),
        cost_estimate=cost(count),
        name="modulate",
    )(levels, noise_table, mod_weight, mod_bias)


def copy_kernel(info_ref, source_ref, target_ref):
    target_ref[...] = source_ref[...]


def own_columns(info, weight):
    return pl.pallas_call(
        copy_kernel,
        grid_spec=pltpu.PrefetchScalarGridSpec(
            num_scalar_prefetch=1,
            grid=(3,),
            in_specs=[
                pl.BlockSpec((D, LANES), lambda i, info: (0, i * (D // LANES) + info[ORDER_AT]))
            ],
            out_specs=pl.BlockSpec((D, LANES), lambda i, info: (0, i)),
        ),
        out_shape=jax.ShapeDtypeStruct((D, 3 * LANES), jnp.bfloat16),
        compiler_params=pltpu.CompilerParams(dimension_semantics=("arbitrary",)),
        cost_estimate=cost(2),
        name="own_columns",
    )(info, weight)


def project_kernel(
    count,
    first_piece,
    info_ref,
    mod_ref,
    weight_ref,
    fcos_ref,
    fsin_ref,
    pcos_ref,
    psin_ref,
    *refs,
):
    frames_ref = Shifted(info_ref, FRAMES_AT)
    halves, out_ref, first_ref = refs[: 2 * count], refs[-2], refs[-1]
    for piece in range(count):
        for half in range(2):
            source, place = halves[2 * piece + half]
            rows = slice(half * PATCHES, (half + 1) * PATCHES)
            frame = frames_ref[2 * (first_piece + piece) + half]
            normed, unused = normalize(
                source[place * PATCHES : (place + 1) * PATCHES, :].astype(jnp.float32)
            )
            shift = mod_ref[pl.ds(frame, 1), :D]
            scale = mod_ref[pl.ds(frame, 1), D : 2 * D]
            first_ref[piece, rows, :] = (normed * (1.0 + scale) + shift).astype(jnp.bfloat16)
        linear = lax.dot_general(
            first_ref[piece], weight_ref[...], NN, preferred_element_type=jnp.float32
        )
        for half in range(2):
            rows = slice(half * PATCHES, (half + 1) * PATCHES)
            frame = frames_ref[2 * (first_piece + piece) + half]
            cosine = pcos_ref[...] + fcos_ref[pl.ds(frame, 1), :]
            sine = psin_ref[...] + fsin_ref[pl.ds(frame, 1), :]
            for part in range(2):
                columns = slice(part * LANES, (part + 1) * LANES)
                values = linear[rows, columns]
                turned = values * cosine + partner_lanes(values) * sine
                out_ref[piece, rows, columns] = turned.astype(jnp.bfloat16)
            out_ref[piece, rows, 2 * LANES :] = linear[rows, 2 * LANES :].astype(jnp.bfloat16)


def project(info, modulation, weight, tables, first_piece, pieces, after):
    vmem = pl.BlockSpec(memory_space=pltpu.VMEM)
    count = len(pieces)
    arrays, sources = [], []
    for piece in pieces:
        if isinstance(piece, tuple):
            sources += [(len(arrays), 0), (len(arrays) + 1, 0)]
            arrays += list(piece)
        else:
            sources += [(len(arrays), 0), (len(arrays), 1)]
            arrays.append(piece)

    def kernel(*refs):
        inputs = refs[7 : 7 + len(arrays)]
        halves = [(inputs[which], place) for which, place in sources]
        project_kernel(count, first_piece, *refs[:7], *halves, *refs[-2:])

    rows = 2 * PATCHES
    return pl.pallas_call(
        kernel,
        in_specs=[pl.BlockSpec(memory_space=pltpu.SMEM)]
        + [vmem] * (6 + len(arrays))
        + [ANYWHERE] * len(after),
        out_specs=[vmem] * 2,
        out_shape=[
            jax.ShapeDtypeStruct((count, rows, 3 * LANES), jnp.bfloat16),
            jax.ShapeDtypeStruct((count, rows, D), jnp.bfloat16),
        ],
        compiler_params=pltpu.CompilerParams(vmem_limit_bytes=VMEM_LIMIT),
        cost_estimate=cost(2 * count),
        name="project",
    )(info, modulation, weight, *tables, *arrays, *after)


def head_stack(values):
    lane = lax.broadcasted_iota(jnp.int32, values.shape, 1)
    zero = jnp.zeros_like(values)
    return jnp.concatenate(
        [jnp.where(lane < HEAD, values, zero), jnp.where(lane < HEAD, zero, values)], axis=0
    )


def hidden_keys(shape):
    key_row = lax.broadcasted_iota(jnp.int32, shape, 0)
    query_column = lax.broadcasted_iota(jnp.int32, shape, 1) % (2 * PATCHES)
    return (key_row >= PATCHES) & (query_column < PATCHES)


def own_heads(values):
    rows = 2 * PATCHES
    return jnp.concatenate([values[:HEAD, :rows], values[HEAD:LANES, rows:]], axis=0)


def by_frame(frames_ref, source_refs, target_refs):
    pieces = [(ref, piece) for ref in source_refs for piece in range(ref.shape[0])]
    for place, (ref, piece) in enumerate(pieces):
        for half in range(2):
            frame = frames_ref[2 * place + half]
            rows = pl.ds(pl.multiple_of(frame * PATCHES, PATCHES), PATCHES)
            for part, target in enumerate(target_refs):
                target[rows, :] = ref[
                    piece,
                    half * PATCHES : (half + 1) * PATCHES,
                    part * LANES : (part + 1) * LANES,
                ]


def attend_kernel(info_ref, qkv_refs, att_ref, ot_ref, lse_ref, q_ref, k_ref, v_ref, vt_ref):
    token_count = q_ref.shape[0]
    frames_ref, slots_ref = Shifted(info_ref, FRAMES_AT), Shifted(info_ref, SLOTS_AT)
    by_frame(frames_ref, qkv_refs, (q_ref, k_ref, v_ref))
    vt_ref[:LANES, :] = v_ref[...].T
    vt_ref[LANES:, :] = jnp.ones((vt_ref.shape[0] - LANES, token_count), jnp.bfloat16)
    step = 2 * PATCHES
    for turn in range(token_count // step):
        here = slice(turn * step, (turn + 1) * step)
        queries = head_stack(q_ref[here, :])
        ranges = [here] if turn == 0 else [slice(0, turn * step), here]
        raw = [
            lax.dot_general(k_ref[keys, :], queries, NT, preferred_element_type=jnp.float32)
            for keys in ranges
        ]
        raw[-1] = jnp.where(hidden_keys(raw[-1].shape), NEG_LARGE, raw[-1])
        top = jnp.max(raw[-1], axis=0, keepdims=True)
        for part in raw[:-1]:
            top = jnp.maximum(top, jnp.max(part, axis=0, keepdims=True))
        top = top * EXP_SCALE
        summed = None
        for keys, part in zip(ranges, raw):
            weights = jnp.exp2(part * EXP_SCALE - top).astype(jnp.bfloat16)
            update = lax.dot_general(
                vt_ref[:, keys], weights, NN, preferred_element_type=jnp.float32
            )
            summed = update if summed is None else summed + update
        totals = summed[LANES : LANES + 1, :]
        lse_ref[turn : turn + 1, :] = top + jnp.log2(totals)
        out = own_heads(summed[:LANES, :] / totals)
        ot_ref[:, here] = out
        rounded = out.T.astype(jnp.bfloat16)
        for half in range(2):
            slot = slots_ref[2 * turn + half]
            rows = pl.ds(pl.multiple_of(slot % 2 * PATCHES, PATCHES), PATCHES)
            att_ref[slot // 2, rows, :] = rounded[half * PATCHES : (half + 1) * PATCHES, :]


def attend(info, qkv, after):
    token_count = FRAME_COUNT * PATCHES
    turns = token_count // (2 * PATCHES)
    vmem = pl.BlockSpec(memory_space=pltpu.VMEM)

    def kernel(info_ref, *refs):
        attend_kernel(info_ref, refs[: len(qkv)], *refs[len(qkv) + 1 :])

    return pl.pallas_call(
        kernel,
        in_specs=[pl.BlockSpec(memory_space=pltpu.SMEM)] + [vmem] * len(qkv) + [ANYWHERE],
        out_specs=[vmem] * 3,
        out_shape=[
            jax.ShapeDtypeStruct((turns, 2 * PATCHES, LANES), jnp.bfloat16),
            jax.ShapeDtypeStruct((LANES, token_count), jnp.float32),
            jax.ShapeDtypeStruct((turns, 4 * PATCHES), jnp.float32),
        ],
        scratch_shapes=[pltpu.VMEM((token_count, LANES), jnp.bfloat16)] * 3
        + [pltpu.VMEM((LANES + 16, token_count), jnp.bfloat16)],
        compiler_params=pltpu.CompilerParams(vmem_limit_bytes=VMEM_LIMIT),
        cost_estimate=cost(10),
        name="attend",
    )(info, *qkv, after)


def attend_back_kernel(
    info_ref,
    grad_ref,
    ot_ref,
    lse_ref,
    fcos_ref,
    fsin_ref,
    pcos_ref,
    psin_ref,
    qkv_refs,
    out_ref,
    q_ref,
    k_ref,
    v_ref,
    d_ref,
    kt_ref,
    dk_ref,
    dv_ref,
):
    token_count = q_ref.shape[0]
    frames_ref, slot_frames_ref, slots_ref = (
        Shifted(info_ref, place) for place in (FRAMES_AT, GROUP_AT, SLOTS_AT)
    )
    by_frame(frames_ref, qkv_refs, (q_ref, k_ref, v_ref))
    by_frame(slot_frames_ref, (grad_ref,), (d_ref,))
    kt_ref[...] = k_ref[...].T
    step = 2 * PATCHES

    def put(frame, part, values):
        slot = slots_ref[frame]
        rows = pl.ds(pl.multiple_of(slot % 2 * PATCHES, PATCHES), PATCHES)
        out_ref[slot // 2, rows, part * LANES : (part + 1) * LANES] = values

    def turn_back(frame, values):
        values = values.astype(jnp.bfloat16).astype(jnp.float32)
        cosine = pcos_ref[...] + fcos_ref[frame : frame + 1, :]
        sine = psin_ref[...] + fsin_ref[frame : frame + 1, :]
        return (values * cosine - partner_lanes(values) * sine).astype(jnp.bfloat16)

    for turn in range(token_count // step):
        here = slice(turn * step, (turn + 1) * step)
        queries = head_stack(q_ref[here, :])
        grads_here = d_ref[here, :]
        grads = head_stack(grads_here)
        product = grads_here.astype(jnp.float32).T * ot_ref[:, here]
        delta = jnp.concatenate(
            [
                jnp.sum(product[:HEAD, :], axis=0, keepdims=True),
                jnp.sum(product[HEAD:, :], axis=0, keepdims=True),
            ],
            axis=1,
        )
        lse = lse_ref[turn : turn + 1, :]
        ranges = [here] if turn == 0 else [here, slice(0, turn * step)]
        total = None
        for keys in ranges:
            raw = lax.dot_general(
                k_ref[keys, :], queries, NT, preferred_element_type=jnp.float32
            )
            weights = jnp.exp2(raw * EXP_SCALE - lse)
            if keys is here:
                weights = jnp.where(hidden_keys(weights.shape), 0.0, weights)
            weight_grad = lax.dot_general(
                v_ref[keys, :], grads, NT, preferred_element_type=jnp.float32
            )
            score_grad = (weights * (weight_grad - delta)).astype(jnp.bfloat16)
            value_part = lax.dot_general(
                weights.astype(jnp.bfloat16), grads, NN, preferred_element_type=jnp.float32
            )
            key_part = lax.dot_general(
                score_grad, queries, NN, preferred_element_type=jnp.float32
            )
            if keys is here:
                dv_ref[keys, :] = value_part
                dk_ref[keys, :] = key_part
            else:
                dv_ref[keys, :] += value_part
                dk_ref[keys, :] += key_part
            update = lax.dot_general(
                kt_ref[:, keys], score_grad, NN, preferred_element_type=jnp.float32
            )
            total = update if total is None else total + update
        query_grad = own_heads(total).T * SCALE
        for half in range(2):
            put(
                2 * turn + half,
                0,
                turn_back(2 * turn + half, query_grad[half * PATCHES : (half + 1) * PATCHES, :]),
            )
    for frame in range(token_count // PATCHES):
        rows = slice(frame * PATCHES, (frame + 1) * PATCHES)
        put(frame, 1, turn_back(frame, dk_ref[rows, :] * SCALE))
        put(frame, 2, dv_ref[rows, :].astype(jnp.bfloat16))


def attend_back(info, qkv, grads, ot, lse, tables, after):
    token_count = FRAME_COUNT * PATCHES
    smem = pl.BlockSpec(memory_space=pltpu.SMEM)
    vmem = pl.BlockSpec(memory_space=pltpu.VMEM)

    def kernel(*refs):
        outs = 8 + len(qkv) + len(after)
        attend_back_kernel(*refs[:8], refs[8 : 8 + len(qkv)], *refs[outs:])

    return pl.pallas_call(
        kernel,
        in_specs=[smem] + [vmem] * (7 + len(qkv)) + [ANYWHERE] * len(after),
        out_specs=vmem,
        out_shape=jax.ShapeDtypeStruct(
            (token_count // (2 * PATCHES), 2 * PATCHES, 3 * LANES), jnp.bfloat16
        ),
        scratch_shapes=[pltpu.VMEM((token_count, LANES), jnp.bfloat16)] * 4
        + [pltpu.VMEM((LANES, token_count), jnp.bfloat16)]
        + [pltpu.VMEM((token_count, LANES), jnp.float32)] * 2,
        compiler_params=pltpu.CompilerParams(vmem_limit_bytes=VMEM_LIMIT),
        cost_estimate=cost(8),
        name="attend_back",
    )(info, grads, ot, lse, *tables, *qkv, *after)


def swap(values, bit):
    count = lax.axis_size(AXES)
    return lax.ppermute(values, AXES, [(index, index ^ bit) for index in range(count)])


PIECES = (0, 4, 2, 1, 5, 6, 3, 7)


def cross(values, bit):
    count = lax.axis_size("blk")
    return lax.ppermute(values, "blk", [(place, place ^ bit) for place in range(count)])


SECOND_AT, ATTENDED_AT, ATTN_AT, UP_AT, UP_ACTS = 0, D, 2 * D, 3 * D, 3 * D + FF
MLP_AT, HIDDEN_AT, DOWN_ACTS = 0, D, D + FF
FF_TILE = 1024
PARTS = 2


def middle_kernel(
    info_ref,
    att_ref,
    tokens_ref,
    cot_ref,
    mod_ref,
    ow_ref,
    up_ref,
    down_ref,
    layer_ref,
    upper_ref,
    lower_ref,
    datt_ref,
    dmid_ref,
    dmod_ref,
    attn_ref,
    mid_ref,
    mlp_ref,
    dsec_ref,
    second_ref,
    dmlp_ref,
):
    step = pl.program_id(0)
    slot_rows = [slice(slot * PATCHES, (slot + 1) * PATCHES) for slot in range(2)]

    def member(slot, which):
        return mod_ref[pl.ds(info_ref[MINE_AT + slot], 1), (which - 2) * D : (which - 1) * D]

    @pl.when(step == 0)
    def _():
        for group in range(D // LANES):
            upper_ref[:, ATTENDED_AT + group * LANES : ATTENDED_AT + (group + 1) * LANES] = att_ref[
                group
            ]
        attn_ref[...] = lax.dot_general(
            upper_ref[:, ATTENDED_AT : ATTENDED_AT + D],
            ow_ref[...],
            NN,
            preferred_element_type=jnp.float32,
        )
        for slot, rows in enumerate(slot_rows):
            middle = tokens_ref[rows, :].astype(jnp.float32) + member(slot, 2) * attn_ref[rows, :]
            mid_ref[rows, :] = middle
            normed, unused = normalize(middle)
            upper_ref[rows, SECOND_AT : SECOND_AT + D] = (
                normed * (1.0 + member(slot, 4)) + member(slot, 3)
            ).astype(jnp.bfloat16)
            lower_ref[rows, MLP_AT : MLP_AT + D] = (
                cot_ref[rows, :].astype(jnp.float32) * member(slot, 5)
            ).astype(jnp.bfloat16)
        second_ref[...] = upper_ref[:, SECOND_AT : SECOND_AT + D]
        dmlp_ref[...] = lower_ref[:, MLP_AT : MLP_AT + D]
        mlp_ref[...] = jnp.zeros_like(mlp_ref)
        dsec_ref[...] = jnp.zeros_like(dsec_ref)

    width = FF_TILE // PARTS
    linear = []
    for part in range(PARTS):
        columns = slice(part * width, (part + 1) * width)
        up_lin = lax.dot_general(
            second_ref[...], up_ref[:, columns], NN, preferred_element_type=jnp.float32
        )
        d_hidden = lax.dot_general(
            dmlp_ref[...], down_ref[columns, :], NT, preferred_element_type=jnp.float32
        )
        linear.append((up_lin, d_hidden))
    hidden, d_up = [], []
    for up_lin, d_hidden in linear:
        below = 0.5 + 0.5 * lax.erf(up_lin * 0.7071067811865476)
        density = jnp.exp(up_lin * up_lin * -0.5) * 0.3989422804014327
        hidden.append((up_lin * below).astype(jnp.bfloat16))
        d_up.append((d_hidden * (below + up_lin * density)).astype(jnp.bfloat16))
    hidden, d_up = jnp.concatenate(hidden, axis=1), jnp.concatenate(d_up, axis=1)
    mlp_ref[...] += lax.dot_general(
        hidden, down_ref[...], NN, preferred_element_type=jnp.float32
    )
    dsec_ref[...] += lax.dot_general(d_up, up_ref[...], NT, preferred_element_type=jnp.float32)
    lower_ref[:, pl.ds(pl.multiple_of(HIDDEN_AT + step * FF_TILE, FF_TILE), FF_TILE)] = hidden
    upper_ref[:, pl.ds(pl.multiple_of(UP_AT + step * FF_TILE, FF_TILE), FF_TILE)] = d_up

    @pl.when(step == pl.num_programs(0) - 1)
    def _():
        for slot, rows in enumerate(slot_rows):
            middle = mid_ref[rows, :]
            mlp_out = mlp_ref[rows, :]
            cotangent = cot_ref[rows, :].astype(jnp.float32)
            layer_ref[rows, :] = (middle + member(slot, 5) * mlp_out).astype(jnp.bfloat16)
            normed, inverse = normalize(middle)
            d_second = dsec_ref[rows, :]
            d_middle = cotangent + norm_backward(
                d_second * (1.0 + member(slot, 4)), normed, inverse
            )
            dmid_ref[rows, :] = d_middle
            upper_ref[rows, ATTN_AT : ATTN_AT + D] = (d_middle * member(slot, 2)).astype(
                jnp.bfloat16
            )
            for place, values in enumerate(
                (d_middle * attn_ref[rows, :], d_second, d_second * normed, cotangent * mlp_out)
            ):
                dmod_ref[slot : slot + 1, place * D : (place + 1) * D] = jnp.sum(
                    values, axis=0, keepdims=True
                )
        d_attended = lax.dot_general(
            upper_ref[:, ATTN_AT : ATTN_AT + D],
            ow_ref[...],
            NT,
            preferred_element_type=jnp.float32,
        ).astype(jnp.bfloat16)
        for group in range(D // LANES):
            datt_ref[group] = d_attended[:, group * LANES : (group + 1) * LANES]


def middle_block(info, att, tokens_here, cot_here, modulation, out_weight, fc1_weight, fc2_weight):
    rows = tokens_here.shape[0]
    return pl.pallas_call(
        middle_kernel,
        grid_spec=pltpu.PrefetchScalarGridSpec(
            num_scalar_prefetch=1,
            grid=(FF // FF_TILE,),
            in_specs=[
                full_block(att.shape),
                full_block((rows, D)),
                full_block((rows, D)),
                full_block(modulation.shape),
                full_block((D, D)),
                pl.BlockSpec((D, FF_TILE), lambda f, frames: (0, f)),
                pl.BlockSpec((FF_TILE, D), lambda f, frames: (f, 0)),
            ],
            out_specs=[
                full_block((rows, D)),
                full_block((rows, UP_ACTS)),
                full_block((rows, DOWN_ACTS)),
                full_block(att.shape),
                full_block((rows, D)),
                full_block((2, 4 * D)),
            ],
            scratch_shapes=[pltpu.VMEM((rows, D), jnp.float32)] * 4
            + [pltpu.VMEM((rows, D), jnp.bfloat16)] * 2,
        ),
        out_shape=[
            jax.ShapeDtypeStruct((rows, D), jnp.bfloat16),
            jax.ShapeDtypeStruct((rows, UP_ACTS), jnp.bfloat16),
            jax.ShapeDtypeStruct((rows, DOWN_ACTS), jnp.bfloat16),
            jax.ShapeDtypeStruct(att.shape, jnp.bfloat16),
            jax.ShapeDtypeStruct((rows, D), jnp.float32),
            jax.ShapeDtypeStruct((2, 4 * D), jnp.float32),
        ],
        compiler_params=pltpu.CompilerParams(
            vmem_limit_bytes=VMEM_LIMIT, dimension_semantics=("arbitrary",)
        ),
        cost_estimate=cost(21),
        name="middle_block",
    )(info, att, tokens_here, cot_here, modulation, out_weight, fc1_weight, fc2_weight)


CHIPS = 16
TILE = 256
FINE = D // CHIPS // 2
UPPER_JOBS = ((SECOND_AT, FINE, UP_AT, FF, 10), (ATTENDED_AT, FINE, ATTN_AT, D, 2))
LOWER_JOBS = ((HIDDEN_AT, LANES, MLP_AT, D, 2),)


def rows_of(jobs):
    first = sum(height * tiles for unused, height, unused_at, width, tiles in jobs)
    return first, sum(job[1] * (job[3] // TILE) for job in jobs) - first


def weight_kernel(jobs, info_ref, mine_ref, theirs_ref, *refs):
    keep_a, send_a, keep_b, send_b = refs[-4 - len(jobs) : -len(jobs)]
    left_refs = refs[-len(jobs) :]
    core, xbit, ybit = (info_ref[BITS_AT + place] for place in range(3))
    rows = mine_ref.shape[0]
    row_a = row_b = 0
    for (left_at, height, right_at, width, tiles), left_ref in zip(jobs, left_refs):
        for place, ref in enumerate((mine_ref, theirs_ref)):
            columns = slice(place * rows, (place + 1) * rows)
            if height == LANES:
                for chip in range(CHIPS):
                    source = pl.multiple_of(left_at + (2 * chip + core) * LANES, LANES)
                    left_ref[chip * LANES : (chip + 1) * LANES, columns] = ref[
                        :, pl.ds(source, LANES)
                    ].T
            else:
                turned = ref[:, left_at : left_at + D].T.reshape(CHIPS, 2, height, rows)
                left_ref[:, columns] = jnp.where(core == 0, turned[:, 0], turned[:, 1]).reshape(
                    CHIPS * height, rows
                )
        for tile in range(width // TILE):
            source = right_at + tile * TILE
            right = jnp.concatenate(
                [mine_ref[:, source : source + TILE], theirs_ref[:, source : source + TILE]],
                axis=0,
            )
            part = lax.dot_general(
                left_ref[...], right, NN, preferred_element_type=jnp.float32
            ).astype(jnp.bfloat16)
            if tile < tiles:
                part = part.reshape(CHIPS // 2, 2, height, TILE)
                low, high = part[:, 0], part[:, 1]
                out_rows = slice(row_a, row_a + height)
                keep_a[:, out_rows, :] = jnp.where(xbit == 0, low, high)
                send_a[:, out_rows, :] = jnp.where(xbit == 0, high, low)
                row_a += height
            else:
                part = part.reshape(CHIPS // 4, 2, 2, height, TILE)
                low, high = part[:, 0], part[:, 1]
                out_rows = slice(row_b, row_b + height)
                keep_b[:, :, out_rows, :] = jnp.where(ybit == 0, low, high)
                send_b[:, :, out_rows, :] = jnp.where(ybit == 0, high, low)
                row_b += height


def weight_parts(jobs, info, mine, theirs, after, expense):
    rows = mine.shape[0]
    vmem = pl.BlockSpec(memory_space=pltpu.VMEM)
    rows_a, rows_b = rows_of(jobs)
    first = jax.ShapeDtypeStruct((CHIPS // 2, rows_a, TILE), jnp.bfloat16)
    second = jax.ShapeDtypeStruct((CHIPS // 4, 2, rows_b, TILE), jnp.bfloat16)
    return pl.pallas_call(
        partial(weight_kernel, jobs),
        in_specs=[pl.BlockSpec(memory_space=pltpu.SMEM), vmem, vmem] + [ANYWHERE] * len(after),
        out_specs=[vmem] * 4,
        out_shape=[first, first, second, second],
        scratch_shapes=[pltpu.VMEM((CHIPS * job[1], 2 * rows), jnp.bfloat16) for job in jobs],
        compiler_params=pltpu.CompilerParams(vmem_limit_bytes=VMEM_LIMIT),
        cost_estimate=cost(expense),
        name="weight_parts",
    )(info, mine, theirs, *after)


WEIGHT_ROWS = 256
QUARTER = 6 * D // 4


def first_back_kernel(
    info_ref,
    dqkv_ref,
    tokens_ref,
    mod_ref,
    dmid_ref,
    early_ref,
    weight_ref,
    *refs,
):
    grad_ref, packed_ref, flat_ref, total_ref, wide_ref = refs[-5:]
    step = pl.program_id(0)

    @pl.when(step == 0)
    def _():
        for group in range(D // LANES):
            for part in range(3):
                column = part * D + group * LANES
                flat_ref[:, column : column + LANES] = dqkv_ref[
                    group, :, part * LANES : (part + 1) * LANES
                ]

    columns = pl.ds(pl.multiple_of(step * WEIGHT_ROWS, WEIGHT_ROWS), WEIGHT_ROWS)
    total_ref[:, columns] = lax.dot_general(
        flat_ref[...], weight_ref[...], NT, preferred_element_type=jnp.float32
    )

    @pl.when(step == pl.num_programs(0) - 1)
    def _():
        for slot in range(2):
            rows = slice(slot * PATCHES, (slot + 1) * PATCHES)
            normed, inverse = normalize(tokens_ref[rows, :].astype(jnp.float32))
            d_first = total_ref[rows, :]
            scale = mod_ref[pl.ds(info_ref[MINE_AT + slot], 1), D : 2 * D]
            grad_ref[rows, :] = (
                dmid_ref[rows, :] + norm_backward(d_first * (1.0 + scale), normed, inverse)
            ).astype(jnp.bfloat16)
            pieces = (
                (0, jnp.sum(d_first, axis=0, keepdims=True)),
                (D, jnp.sum(d_first * normed, axis=0, keepdims=True)),
                (2 * D, early_ref[slot : slot + 1, :]),
            )
            for start, piece in pieces:
                for quarter in range(4):
                    low = max(start, quarter * QUARTER)
                    high = min(start + piece.shape[1], (quarter + 1) * QUARTER)
                    if low < high:
                        wide_ref[
                            2 * quarter + slot : 2 * quarter + slot + 1,
                            low - quarter * QUARTER : high - quarter * QUARTER,
                        ] = piece[:, low - start : high - start]
        packed_ref[...] = wide_ref[...].astype(jnp.bfloat16)


def first_back(info, d_qkv, tokens_here, modulation, d_middle, early, qkv_weight, after):
    rows = tokens_here.shape[0]
    return pl.pallas_call(
        first_back_kernel,
        grid_spec=pltpu.PrefetchScalarGridSpec(
            num_scalar_prefetch=1,
            grid=(D // WEIGHT_ROWS,),
            in_specs=[
                full_block(d_qkv.shape),
                full_block((rows, D)),
                full_block(modulation.shape),
                full_block((rows, D)),
                full_block(early.shape),
                pl.BlockSpec((WEIGHT_ROWS, 3 * D), lambda i, frames: (i, 0)),
            ]
            + [ANYWHERE] * len(after),
            out_specs=[full_block((rows, D)), full_block((8, QUARTER))],
            scratch_shapes=[
                pltpu.VMEM((rows, 3 * D), jnp.bfloat16),
                pltpu.VMEM((rows, D), jnp.float32),
                pltpu.VMEM((8, QUARTER), jnp.float32),
            ],
        ),
        out_shape=[
            jax.ShapeDtypeStruct((rows, D), jnp.bfloat16),
            jax.ShapeDtypeStruct((8, QUARTER), jnp.bfloat16),
        ],
        compiler_params=pltpu.CompilerParams(
            vmem_limit_bytes=VMEM_LIMIT, dimension_semantics=("arbitrary",)
        ),
        cost_estimate=cost(6),
        name="first_back",
    )(info, d_qkv, tokens_here, modulation, d_middle, early, qkv_weight, *after)


def qkv_part_kernel(info_ref, first_refs, grad_ref, keep_ref, send_ref):
    pieces = [(ref, piece) for ref in first_refs for piece in range(ref.shape[0])]
    total = None
    for place, (ref, piece) in enumerate(pieces):
        update = lax.dot_general(
            ref[piece],
            grad_ref[info_ref[ORDER_AT + place]],
            (((0,), (0,)), ((), ())),
            preferred_element_type=jnp.float32,
        )
        total = update if total is None else total + update
    groups, clip_pairs, share, width = keep_ref.shape
    split = total.astype(jnp.bfloat16).reshape(groups, clip_pairs, 2, share, width)
    low, high = split[:, :, 0], split[:, :, 1]
    keep_ref[...] = jnp.where(info_ref[BITS_AT] == 0, low, high)
    send_ref[...] = jnp.where(info_ref[BITS_AT] == 0, high, low)


def qkv_parts(info, firsts, d_heads, share, after):
    vmem = pl.BlockSpec(memory_space=pltpu.VMEM)
    shape = (D // LANES, 2, share, d_heads.shape[2])

    def kernel(info_ref, *refs):
        count = len(firsts)
        qkv_part_kernel(info_ref, refs[:count], refs[count], *refs[-2:])

    return pl.pallas_call(
        kernel,
        in_specs=[pl.BlockSpec(memory_space=pltpu.SMEM)]
        + [vmem] * (len(firsts) + 1)
        + [ANYWHERE] * len(after),
        out_specs=[vmem] * 2,
        out_shape=[jax.ShapeDtypeStruct(shape, jnp.bfloat16)] * 2,
        compiler_params=pltpu.CompilerParams(vmem_limit_bytes=VMEM_LIMIT),
        cost_estimate=cost(0.2),
        name="qkv_parts",
    )(info, *firsts, d_heads, *after)


def pair_sum(keep, got):
    return (keep.astype(jnp.float32) + got.astype(jnp.float32)).astype(jnp.bfloat16)


def fold_kernel(bits, info_ref, *refs):
    count = len(bits)
    out_refs = refs[-2 * count :]
    for place, bit_at in enumerate(bits):
        keep, got = refs[2 * place : 2 * place + 2]
        low, high = pair_sum(keep[:, 0], got[:, 0]), pair_sum(keep[:, 1], got[:, 1])
        bit = info_ref[BITS_AT + bit_at]
        kept, sent = out_refs[2 * place : 2 * place + 2]
        kept[...] = jnp.where(bit == 0, low, high)
        sent[...] = jnp.where(bit == 0, high, low)


def fold(info, bits, pairs, after, expense):
    count, unused, unused_rows, columns = pairs[0][0].shape
    in_specs, out_specs, out_shape = [], [], []
    for keep, got in pairs:
        rows = keep.shape[2]
        in_specs += [full_block((count, 2, rows, columns))] * 2
        out_specs += [full_block((count, rows, columns))] * 2
        out_shape += [jax.ShapeDtypeStruct((count, rows, columns), jnp.bfloat16)] * 2
    return pl.pallas_call(
        partial(fold_kernel, bits),
        grid_spec=pltpu.PrefetchScalarGridSpec(
            num_scalar_prefetch=1,
            grid=(1,),
            in_specs=in_specs + [ANYWHERE] * len(after),
            out_specs=out_specs,
        ),
        out_shape=out_shape,
        compiler_params=pltpu.CompilerParams(
            vmem_limit_bytes=VMEM_LIMIT, dimension_semantics=("arbitrary",)
        ),
        cost_estimate=cost(expense),
        name="fold",
    )(info, *(part for pair in pairs for part in pair), *after)


def blend_kernel(riders, keep_a, got_a, keep_b, got_b, *refs):
    out_ref = refs[-1]
    row = 0
    for keep, got in ((keep_a, got_a), (keep_b, got_b)):
        height = keep.shape[1]
        out_ref[:, row : row + height, :] = pair_sum(keep[...], got[...])
        row += height
    for side, rider in enumerate(refs[:riders]):
        height = rider.shape[1]
        out_ref[:, row + side * height : row + (side + 1) * height, :] = rider[:, :, :TILE]
        last = row + riders * height
        out_ref[:, last : last + height, side * LANES : (side + 1) * LANES] = rider[:, :, TILE:]


def blend(parts, riders, after, expense):
    rows = sum(part.shape[1] for part in parts[::2]) + (3 * FINE if riders else 0)
    count, columns = parts[0].shape[0], parts[0].shape[2]
    operands = tuple(parts) + tuple(riders)
    return pl.pallas_call(
        partial(blend_kernel, len(riders)),
        grid=(1,),
        in_specs=[full_block(part.shape) for part in operands]
        + [ANYWHERE] * len(after),
        out_specs=full_block((count, rows, columns)),
        out_shape=jax.ShapeDtypeStruct((count, rows, columns), jnp.bfloat16),
        compiler_params=pltpu.CompilerParams(
            vmem_limit_bytes=VMEM_LIMIT, dimension_semantics=("arbitrary",)
        ),
        cost_estimate=cost(expense),
        name="blend",
    )(*operands, *after)


def join_kernel(mine_ref, theirs_ref, *refs):
    count = mine_ref.shape[0]
    refs[-1][:count] = mine_ref[...]
    refs[-1][count:] = theirs_ref[...]


def join(mine, theirs, after):
    vmem = pl.BlockSpec(memory_space=pltpu.VMEM)
    return pl.pallas_call(
        join_kernel,
        in_specs=[vmem, vmem] + [ANYWHERE] * len(after),
        out_specs=vmem,
        out_shape=jax.ShapeDtypeStruct((2 * mine.shape[0],) + mine.shape[1:], mine.dtype),
        compiler_params=pltpu.CompilerParams(vmem_limit_bytes=VMEM_LIMIT),
        cost_estimate=cost(0.5),
        name="join",
    )(mine, theirs, *after)


def add_kernel(bit_at, info_ref, keep_ref, got_ref, *refs):
    low, high = (
        (keep_ref[:, half].astype(jnp.float32) + got_ref[:, half].astype(jnp.float32)).astype(
            jnp.bfloat16
        )
        for half in range(2)
    )
    bit = info_ref[BITS_AT + bit_at]
    refs[-2][...] = jnp.where(bit == 0, low, high)
    refs[-1][...] = jnp.where(bit == 0, high, low)


def add_halves(info, keep, got, bit_at, after):
    vmem = pl.BlockSpec(memory_space=pltpu.VMEM)
    out = jax.ShapeDtypeStruct(keep.shape[:1] + keep.shape[2:], jnp.bfloat16)
    return pl.pallas_call(
        partial(add_kernel, bit_at),
        in_specs=[pl.BlockSpec(memory_space=pltpu.SMEM), vmem, vmem] + [ANYWHERE] * len(after),
        out_specs=[vmem] * 2,
        out_shape=[out] * 2,
        cost_estimate=cost(1),
        name="add_halves",
    )(info, keep, got, *after)


def finish_kernel(jobs, riders, info_ref, parts_ref, *refs):
    targets = refs[-len(jobs) - riders :]
    row = [0, rows_of(jobs)[0]]
    for (unused, height, unused_at, width, tiles), target in zip(jobs, targets):
        for tile in range(width // TILE):
            second = tile >= tiles
            rows = slice(row[second], row[second] + height)
            total = parts_ref[0, rows, :].astype(jnp.float32)
            for part in range(1, parts_ref.shape[0]):
                total = total + parts_ref[part, rows, :].astype(jnp.float32)
            target[:, tile * TILE : (tile + 1) * TILE] = total
            row[second] += height
    if riders:
        first_row = sum(rows_of(jobs))
        ybit = info_ref[BITS_AT + 2]
        for place in range(parts_ref.shape[0]):
            for side in range(2):
                group = 2 * place + (ybit if side == 0 else 1 - ybit)
                for part in range(3):
                    row_at, lane_at = ((side, 0), (side, 1), (2, side))[part]
                    rows = slice(first_row + row_at * FINE, first_row + (row_at + 1) * FINE)
                    lanes = slice(lane_at * LANES, (lane_at + 1) * LANES)
                    column = pl.multiple_of(part * D + group * LANES, LANES)
                    targets[-1][:, pl.ds(column, LANES)] = parts_ref[place, rows, lanes].astype(
                        jnp.float32
                    )


def finish(info, jobs, parts, riders, after):
    vmem = pl.BlockSpec(memory_space=pltpu.VMEM)
    shapes = [(job[1], job[3]) for job in jobs] + [(FINE, 3 * D)] * riders
    return pl.pallas_call(
        partial(finish_kernel, jobs, riders),
        in_specs=[pl.BlockSpec(memory_space=pltpu.SMEM), vmem] + [ANYWHERE] * len(after),
        out_specs=[vmem] * len(shapes),
        out_shape=[jax.ShapeDtypeStruct(shape, jnp.float32) for shape in shapes],
        compiler_params=pltpu.CompilerParams(vmem_limit_bytes=VMEM_LIMIT),
        cost_estimate=cost(2),
        name="finish",
    )(info, parts, *after)


def closing_kernel(all_ref, embedded_ref, weight_ref, hot_ref, modw_ref, table_ref, bias_ref):
    rows = all_ref.shape[0]
    slots, share = embedded_ref.shape
    embedded = embedded_ref[...]
    sigmoid = jax.nn.sigmoid(embedded)
    activated = (embedded * sigmoid).astype(jnp.bfloat16)
    row = lax.broadcasted_iota(jnp.int32, (slots, rows), 1)
    slot = lax.broadcasted_iota(jnp.int32, (slots, rows), 0)
    d_activated = None
    for quarter in range(4):
        columns = slice(quarter * QUARTER, (quarter + 1) * QUARTER)
        chosen = jnp.where(row == slot // 2 * 8 + 2 * quarter + slot % 2, 1.0, 0.0)
        spread = lax.dot_general(
            activated,
            chosen.astype(jnp.bfloat16),
            (((0,), (0,)), ((), ())),
            preferred_element_type=jnp.float32,
        ).astype(jnp.bfloat16)
        modw_ref[:, columns] = lax.dot_general(
            spread, all_ref[...], NN, preferred_element_type=jnp.float32
        )
        every = jnp.where(
            lax.broadcasted_iota(jnp.int32, (8, rows), 1) % 8 // 2 == quarter, 1.0, 0.0
        ).astype(jnp.bfloat16)
        bias_ref[:, columns] = lax.dot_general(
            every, all_ref[...], NN, preferred_element_type=jnp.float32
        )[:1, :]
        part = lax.dot_general(
            all_ref[...], weight_ref[:, columns], NT, preferred_element_type=jnp.float32
        )
        part = lax.dot_general(
            chosen,
            part,
            NN,
            precision=lax.Precision.HIGHEST,
            preferred_element_type=jnp.float32,
        )
        d_activated = part if d_activated is None else d_activated + part
    d_embedded = d_activated * (sigmoid * (1.0 + embedded * (1.0 - sigmoid)))
    table_ref[...] = lax.dot_general(
        hot_ref[...],
        d_embedded,
        NN,
        precision=lax.Precision.HIGHEST,
        preferred_element_type=jnp.float32,
    )


def closing(gathered, embedded, weight_rows, level_hot):
    vmem = pl.BlockSpec(memory_space=pltpu.VMEM)
    share = embedded.shape[1]
    return pl.pallas_call(
        closing_kernel,
        in_specs=[vmem] * 4,
        out_specs=[vmem] * 3,
        out_shape=[
            jax.ShapeDtypeStruct((share, 6 * D), jnp.float32),
            jax.ShapeDtypeStruct((LEVELS, share), jnp.float32),
            jax.ShapeDtypeStruct((1, 6 * D), jnp.float32),
        ],
        compiler_params=pltpu.CompilerParams(vmem_limit_bytes=VMEM_LIMIT),
        cost_estimate=cost(3),
        name="closing",
    )(gathered, embedded, weight_rows, level_hot)


def halved(part):
    return part.reshape((-1, 2) + part.shape[-2:])


def across(info, parts, after, expense):
    keep_a, got_a, keep_b, got_b = (halved(part) for part in parts)
    keep_a, send_a, keep_b, send_b = fold(
        info, (2, 1), ((keep_a, got_a), (keep_b, got_b)), after, expense
    )
    return (keep_a, swap(send_a, 4), keep_b, swap(send_b, 2)), send_a


def along(parts, riders, after, expense):
    total = blend(parts, riders, after, expense)
    columns = [[2 * place + side for place in range(4)] for side in range(2)]
    return lax.all_to_all(total, "blk", 0, 0, axis_index_groups=columns, tiled=True), total


def local_heads(
    tokens,
    noise_levels,
    group_map,
    noise_table,
    mod_weight,
    mod_bias,
    qkv_weight,
    out_weight,
    fc1_weight,
    fc2_weight,
    out_cotangent,
):
    rows_here = 2 * PATCHES
    frame_count = group_map.shape[0]
    groups = D // LANES
    device_count = lax.axis_size(AXES)
    index = lax.axis_index(AXES)
    bits = [(index >> place) & 1 for place in range(5)]
    tables = rope_tables(frame_count)
    clip_levels = noise_levels
    for bit in (1, 2):
        clip_levels = jnp.concatenate([clip_levels, swap(clip_levels, bit)], axis=0)
    members = jnp.zeros((1,), jnp.int32)
    for bit in (16, 8, 4, 2, 1):
        members = jnp.concatenate([members, members ^ bit])
    member_slots = (2 * ((index ^ members) >> 2))[:, None] + jnp.arange(2, dtype=jnp.int32)[None, :]
    levels_all = clip_levels[(members & 3)[:, None], group_map[member_slots]].reshape(
        2 * device_count
    )
    tokens_here = tokens.reshape(rows_here, D)
    block = lax.axis_index("blk")
    piece_at = block ^ jnp.array(PIECES, jnp.int32)
    places = jnp.arange(frame_count, dtype=jnp.int32)
    piece_slots = ((2 * piece_at)[:, None] + jnp.arange(2, dtype=jnp.int32)[None, :]).reshape(-1)
    frames = jnp.sum(
        jnp.where(piece_slots[:, None] == places[None, :], group_map[None, :], 0), axis=1
    )
    slots = jnp.sum(jnp.where(group_map[None, :] == places[:, None], places[None, :], 0), axis=1)
    info = jnp.concatenate(
        [jnp.stack(bits), piece_at, frames, slots, group_map, frames[:2]]
    ).astype(jnp.int32)
    far = cross(tokens_here, 4)
    side = cross(tokens_here, 1)
    near = cross(tokens_here, 2)
    far_side, far_near, near_side = cross(far, 1), cross(far, 2), cross(side, 2)
    last = (cross(far_near[:PATCHES], 1), cross(far_side[PATCHES:], 2))
    mod_first, mod_rest = (
        modulate(noise_levels, noise_table, mod_weight, mod_bias, first, count)
        for first, count in ((0, 2), (2, 4))
    )
    weight_here = own_columns(info, qkv_weight)
    projected = []
    for first_piece, pieces in (
        (0, (tokens_here,)),
        (1, (far, near, side)),
        (4, (far_side, far_near, near_side)),
        (7, (last,)),
    ):
        projected.append(project(
                info,
                mod_first,
                weight_here,
                tables,
                first_piece,
                pieces,
                (mod_rest,) if first_piece == 4 else (),
            ))
    qkv_heads = [pair[0] for pair in projected]
    firsts = [pair[1] for pair in projected]
    att_heads, ot, lse = attend(info, qkv_heads, levels_all)
    att = lax.all_to_all(att_heads, "blk", 0, 0, tiled=True)
    layer_out, up_acts, down_acts, d_att, d_middle, d_mod_early = middle_block(
        info,
        att,
        tokens_here,
        out_cotangent.reshape(rows_here, D),
        mod_rest,
        out_weight,
        fc1_weight,
        fc2_weight,
    )
    grad_heads = lax.all_to_all(d_att, "blk", 0, 0, tiled=True)
    share = D // device_count
    keep_a, send_a, keep_b, send_b = weight_parts(
        UPPER_JOBS, info, up_acts, swap(up_acts, 1), (), 2)
    upper = (keep_a, swap(send_a, 2), keep_b, swap(send_b, 4))
    d_heads = attend_back(info, qkv_heads, grad_heads, ot, lse, tables, (send_a,))
    d_qkv = lax.all_to_all(d_heads, "blk", 0, 0, tiled=True)
    qkv_keep, qkv_send = qkv_parts(info, firsts, d_heads, share, ())
    qkv_keep, qkv_send = add_halves(info, qkv_keep, swap(qkv_send, 1), 1, ())
    qkv_got = swap(qkv_send, 2)
    upper, upper_sent = across(info, upper, (qkv_send,), 6)
    keep_a, send_a, keep_b, send_b = weight_parts(
        LOWER_JOBS, info, down_acts, swap(down_acts, 1), (upper_sent, qkv_got, upper[3]), 3)
    lower = (keep_a, swap(send_a, 2), keep_b, swap(send_b, 4))
    upper, upper_z = along(upper, (), (send_a,), 1)
    tokens_grad, d_mod = first_back(
        info, d_qkv, tokens_here, mod_first, d_middle, d_mod_early, qkv_weight, (upper_z,)
    )
    pairs = (groups // 2, 2, share, 3 * LANES)
    qkv_keep, qkv_send = add_halves(
        info, qkv_keep.reshape(pairs), qkv_got.reshape(pairs), 2, (d_mod,)
    )
    qkv_got = swap(qkv_send, 4)
    got = swap(d_mod, 16)
    lower, lower_sent = across(info, lower, (qkv_send,), 15)
    d_mod = join(d_mod, got, (lower_sent,))
    got = swap(d_mod, 8)
    lower, lower_z = along(lower, (qkv_keep, qkv_got), (d_mod,), 5)
    d_mod = join(d_mod, got, (lower_z,))
    for bit in (4, 2, 1):
        d_mod = jnp.concatenate([d_mod, swap(d_mod, bit)])
    level_hot = jnp.arange(LEVELS, dtype=jnp.int32)[:, None] == levels_all[None, :]
    table_columns = lax.dynamic_slice_in_dim(noise_table, index * share, share, 1)
    embedded_columns = jnp.einsum(
        "ls,lc->sc",
        level_hot.astype(jnp.bfloat16),
        table_columns,
        preferred_element_type=jnp.float32,
    )
    weight_rows = lax.dynamic_slice_in_dim(mod_weight, index * share, share, 0)
    modw_share, table_share, bias_sums = closing(
        d_mod, embedded_columns, weight_rows, level_hot.astype(jnp.float32)
    )
    bias_columns = 6 * D // device_count
    bias_share = lax.dynamic_slice_in_dim(bias_sums[0], index * bias_columns, bias_columns)
    upper_share, outw_share = finish(info, UPPER_JOBS, upper, 0, (lower_z,))
    lower_share, qkv_share = finish(
        info, LOWER_JOBS, lower, 1, (upper_share, table_share, modw_share, bias_share)
    )
    return (
        layer_out[None].reshape(1, 2, PATCHES, D),
        tokens_grad.reshape(1, 2, PATCHES, D),
        table_share,
        modw_share,
        bias_share,
        qkv_share,
        outw_share,
        upper_share,
        lower_share,
    )


def solution(mesh):
    pair_split = mesh.shape["blk"] * LANES == D and mesh.shape["clip"] == 4
    return jax.shard_map(
        local_heads if pair_split else local,
        mesh=mesh,
        in_specs=(
            P("clip", "blk", None, None),
            P("clip", None),
            P(),
            P(),
            P(),
            P(),
            P(),
            P(),
            P(),
            P(),
            P("clip", "blk", None, None),
        ),
        out_specs=(
            P("clip", "blk", None, None),
            P("clip", "blk", None, None),
            P(None, ("blk", "clip")),
            P(("blk", "clip"), None),
            P(("blk", "clip")),
            P(("blk", "clip"), None),
            P(("blk", "clip"), None),
            P(("blk", "clip"), None),
            P(("blk", "clip"), None),
        ),
        check_vma=False,
    )
```
